32 devices in a mesh: wide: 8 (over z, y), narrow: 4 (over x, core).
Axes of the slice: x: 2, y: 2, z: 4, core: 2. Of those that a mesh axis runs over, the one named last changes fastest.
Arguments:
- inputs: bfloat16 [4096, 1024], P(('wide', 'narrow')), may hold values from -6 to 6
- memory: bfloat16 [8192, 1024], P(('wide', 'narrow')), may hold values from -6 to 6
- cotangent: bfloat16 [4096, 1024], P(('wide', 'narrow')), may hold values from -6 to 6
- segments: int32 [4096], P(('wide', 'narrow')), may hold values from 0 to 3, as said below
- memory_segments: int32 [8192], P(('wide', 'narrow')), may hold values from 0 to 3, as said below
- query_self: bfloat16 [1024, 1024], P(('wide', 'narrow')), may hold values from -0.1875 to 0.1875
- key_self: bfloat16 [1024, 1024], P(('wide', 'narrow')), may hold values from -0.1875 to 0.1875
- value_self: bfloat16 [1024, 1024], P(('wide', 'narrow')), may hold values from -0.1875 to 0.1875
- output_self: bfloat16 [1024, 1024], P(('wide', 'narrow')), may hold values from -1 to 1
- query_cross: bfloat16 [1024, 1024], P(('wide', 'narrow')), may hold values from -0.1875 to 0.1875
- key_cross: bfloat16 [1024, 1024], P(('wide', 'narrow')), may hold values from -0.1875 to 0.1875
- value_cross: bfloat16 [1024, 1024], P(('wide', 'narrow')), may hold values from -0.1875 to 0.1875
- output_cross: bfloat16 [1024, 1024], P(('wide', 'narrow')), may hold values from -1 to 1
- self_gain: bfloat16 [1024], P(('wide', 'narrow')), may hold values from 0.099609375 to 1.8984375
- self_shift: bfloat16 [1024], P(('wide', 'narrow')), may hold values from -3 to 3
- cross_gain: bfloat16 [1024], P(('wide', 'narrow')), may hold values from 0.099609375 to 1.8984375
- cross_shift: bfloat16 [1024], P(('wide', 'narrow')), may hold values from -3 to 3
- final_gain: bfloat16 [1024], P(('wide', 'narrow')), may hold values from 0.099609375 to 1.8984375
- final_shift: bfloat16 [1024], P(('wide', 'narrow')), may hold values from -3 to 3
- feed_in: bfloat16 [1024, 4096], P(None, 'wide'), may hold values from -0.1875 to 0.1875
- feed_out: bfloat16 [4096, 1024], P('wide'), may hold values from -0.09375 to 0.09375
- adapter_down: bfloat16 [1024, 512], P(None, 'narrow'), may hold values from -0.1875 to 0.1875
- adapter_up: bfloat16 [512, 1024], P('narrow'), may hold values from -0.0625 to 0.0625
- prefix_embed: bfloat16 [30, 1024], P(None, ('wide', 'narrow')), may hold values from -6 to 6
- prefix_inner: bfloat16 [1024, 512], P(('wide', 'narrow')), may hold values from -0.1875 to 0.1875
- prefix_outer: bfloat16 [512, 2048], P(None, ('wide', 'narrow')), may hold values from -0.375 to 0.375
Outputs:
- output: bfloat16 [4096, 1024], P(('wide', 'narrow'))
- inputs_grad: bfloat16 [4096, 1024], P(('wide', 'narrow'))
- memory_grad: bfloat16 [8192, 1024], P(('wide', 'narrow'))
- query_self_grad: float32 [1024, 1024], P(('wide', 'narrow'))
- key_self_grad: float32 [1024, 1024], P(('wide', 'narrow'))
- value_self_grad: float32 [1024, 1024], P(('wide', 'narrow'))
- output_self_grad: float32 [1024, 1024], P(('wide', 'narrow'))
- query_cross_grad: float32 [1024, 1024], P(('wide', 'narrow'))
- key_cross_grad: float32 [1024, 1024], P(('wide', 'narrow'))
- value_cross_grad: float32 [1024, 1024], P(('wide', 'narrow'))
- output_cross_grad: float32 [1024, 1024], P(('wide', 'narrow'))
- self_gain_grad: float32 [1024], P(('wide', 'narrow'))
- self_shift_grad: float32 [1024], P(('wide', 'narrow'))
- cross_gain_grad: float32 [1024], P(('wide', 'narrow'))
- cross_shift_grad: float32 [1024], P(('wide', 'narrow'))
- final_gain_grad: float32 [1024], P(('wide', 'narrow'))
- final_shift_grad: float32 [1024], P(('wide', 'narrow'))
- feed_in_grad: float32 [1024, 4096], P('narrow', 'wide')
- feed_out_grad: float32 [4096, 1024], P('wide', 'narrow')
- adapter_down_grad: float32 [1024, 512], P('wide', 'narrow')
- adapter_up_grad: float32 [512, 1024], P('narrow', 'wide')
- prefix_embed_grad: float32 [30, 1024], P(None, ('wide', 'narrow'))
- prefix_inner_grad: float32 [1024, 512], P(('wide', 'narrow'))
- prefix_outer_grad: float32 [512, 2048], P(None, ('wide', 'narrow'))
The draws below stay inside these ranges and needn't reach their ends.
Inputs may be any that keep to these rules, and one draw needn't show every extreme that they name: `segments`: within each sequence's 128 target tokens the ids never fall; the first is 0 and the last is 3. `memory_segments`: within each sequence's 256 encoder tokens the ids never fall, and every id of 0 to 3 names at least one of them.
All inputs are finite; a program needn't handle non-finite values.
Results may differ from the reference program's by a relative error of at most 0.024.
Values may be sent and summed in bfloat16 or wider, within the bound.
A program may use at most 256 MiB of HBM per device.

```python
import math
import jax
import jax.numpy as jnp
from jax import lax

D = 1024
HEADS = 16
HEAD = 64
FF = 4096
AD = 512
PREFIX = 30
PHID = 512
SEQ = 128
MEM = 256
DOCS = 4
TOKENS = 4096
MEM_TOKENS = 8192


def documents(key):
    count = TOKENS // SEQ
    first_key = jax.random.fold_in(key, 101)
    second_key = jax.random.fold_in(key, 202)
    cuts = jax.random.randint(first_key, (count, DOCS - 1), 1, SEQ)
    places = jnp.arange(SEQ)
    target = jnp.sum((places[None, :, None] >= cuts[:, None, :]).astype(jnp.int32), axis=2)
    stride = MEM // DOCS
    offsets = jax.random.randint(second_key, (count, DOCS - 1), 1, stride + 1)
    bounds = jnp.arange(DOCS - 1)[None, :] * stride + offsets
    spots = jnp.arange(MEM)
    source = jnp.sum((spots[None, :, None] >= bounds[:, None, :]).astype(jnp.int32), axis=2)
    return (target.reshape(TOKENS).astype(jnp.int32), source.reshape(MEM_TOKENS).astype(jnp.int32))


def draw_segments(key, part):
    return documents(key)[0]


def draw_memory_segments(key, part):
    return documents(key)[1]


def levels(key, shape, shards, low, high):
    def one(axis_at, blocks):
        draws = jax.random.uniform(jax.random.fold_in(jax.random.fold_in(key, 6), axis_at), (blocks,), jnp.float32, low / len(shards), high / len(shards))
        return jnp.repeat(jnp.exp(draws), shape[axis_at] // blocks).reshape((-1,) + (1,) * (len(shape) - axis_at - 1))

    factor_of = one(*shards[0])
    for cut in shards[1:]:
        factor_of = factor_of * one(*cut)
    return factor_of


def scatter_about(key, extent, width, bound, split=(), kind=jnp.bfloat16):
    values = width * jax.random.normal(key, extent, jnp.float32)
    if split:
        values = values * levels(key, extent, split, -0.22, 0.18)
    return jnp.clip(values, -bound, bound).astype(kind)


def setup_inputs(seed: int = 0) -> dict:
    keys = jax.random.split(jax.random.key(seed), 27)
    inputs = scatter_about(keys[0], (TOKENS, D), 1.0, 6.0, ((0, 32),))
    memory = scatter_about(keys[1], (MEM_TOKENS, D), 1.0, 6.0, ((0, 32),))
    cotangent = scatter_about(keys[2], (TOKENS, D), 1.0, 6.0, ((0, 32),))
    segments = draw_segments(jax.random.fold_in(keys[26], 71), 0)
    memory_segments = draw_memory_segments(jax.random.fold_in(keys[26], 71), 0)
    query_self = scatter_about(keys[5], (D, D), D ** -0.5, 0.1875, ((0, 32),))
    key_self = scatter_about(keys[6], (D, D), D ** -0.5, 0.1875, ((0, 32),))
    value_self = scatter_about(keys[7], (D, D), D ** -0.5, 0.1875, ((0, 32),))
    output_self = scatter_about(keys[8], (D, D), (D // 32) ** -0.5, 1.0, ((0, 32),))
    query_cross = scatter_about(keys[9], (D, D), D ** -0.5, 0.1875, ((0, 32),))
    key_cross = scatter_about(keys[10], (D, D), D ** -0.5, 0.1875, ((0, 32),))
    value_cross = scatter_about(keys[11], (D, D), D ** -0.5, 0.1875, ((0, 32),))
    output_cross = scatter_about(keys[12], (D, D), (D // 32) ** -0.5, 1.0, ((0, 32),))
    self_gain = jnp.clip(1.0 + 0.18 * jax.random.normal(keys[13], (D,), jnp.float32), 0.099609375, 1.8984375).astype(jnp.bfloat16)
    self_shift = scatter_about(keys[14], (D,), 0.5, 3.0, ((0, 32),))
    cross_gain = jnp.clip(1.0 + 0.18 * jax.random.normal(keys[15], (D,), jnp.float32), 0.099609375, 1.8984375).astype(jnp.bfloat16)
    cross_shift = scatter_about(keys[16], (D,), 0.5, 3.0, ((0, 32),))
    final_gain = jnp.clip(1.0 + 0.18 * jax.random.normal(keys[17], (D,), jnp.float32), 0.099609375, 1.8984375).astype(jnp.bfloat16)
    final_shift = scatter_about(keys[18], (D,), 0.5, 3.0, ((0, 32),))
    feed_in = scatter_about(keys[19], (D, FF), D ** -0.5, 0.1875, ((1, 8),))
    feed_out = scatter_about(keys[20], (FF, D), FF ** -0.5, 0.09375, ((0, 8),))
    adapter_down = scatter_about(keys[21], (D, AD), D ** -0.5, 0.1875, ((1, 4),))
    adapter_up = scatter_about(keys[22], (AD, D), (16 * AD) ** -0.5, 0.0625, ((0, 4),))
    prefix_embed = scatter_about(keys[23], (PREFIX, D), 1.0, 6.0, ((1, 32),))
    prefix_inner = scatter_about(keys[24], (D, PHID), D ** -0.5, 0.1875, ((0, 32),))
    prefix_outer = scatter_about(keys[25], (PHID, 2 * D), (PHID // 2) ** -0.5, 0.375, ((1, 32),))
    return {"inputs": inputs, "memory": memory, "cotangent": cotangent, "segments": segments, "memory_segments": memory_segments, "query_self": query_self, "key_self": key_self, "value_self": value_self, "output_self": output_self, "query_cross": query_cross, "key_cross": key_cross, "value_cross": value_cross, "output_cross": output_cross, "self_gain": self_gain, "self_shift": self_shift, "cross_gain": cross_gain, "cross_shift": cross_shift, "final_gain": final_gain, "final_shift": final_shift, "feed_in": feed_in, "feed_out": feed_out, "adapter_down": adapter_down, "adapter_up": adapter_up, "prefix_embed": prefix_embed, "prefix_inner": prefix_inner, "prefix_outer": prefix_outer}


HIGHEST = lax.Precision.HIGHEST
EPSILON = 1e-05
MASKED = -1000000000.0
ADAPT_SCALE = 4.0

@jax.custom_vjp
def low(v):
    return lax.optimization_barrier(v.astype(jnp.bfloat16)).astype(jnp.float32)

@jax.custom_vjp
def low_back(v):
    return v

def low_keep(v):
    return (low(v), None)

def low_pass(kept, grad):
    return (grad,)

def back_keep(v):
    return (v, None)

def back_low(kept, grad):
    return (low(grad),)
low.defvjp(low_keep, low_pass)
low_back.defvjp(back_keep, back_low)

def product(left, right):
    return jnp.matmul(left, right, precision=HIGHEST)

def layer_norm(values, factor, offset):
    average = lax.optimization_barrier(jnp.mean(values, axis=-1, keepdims=True))
    center = values - average
    inverse = lax.rsqrt(lax.optimization_barrier(jnp.mean(center * center, axis=-1, keepdims=True)) + EPSILON)
    return center * inverse * factor + offset

def attend(queries, key_rows, value_rows, allowed):
    batch = queries.shape[0]
    length = queries.shape[1]
    count = key_rows.shape[1]
    query_heads = queries.reshape(batch, length, HEADS, HEAD)
    key_heads = key_rows.reshape(batch, count, HEADS, HEAD)
    value_heads = value_rows.reshape(batch, count, HEADS, HEAD)
    scores = jnp.einsum('bshd,bkhd->bhsk', query_heads, key_heads, precision=HIGHEST) * HEAD ** (-0.5)
    scores = low_back(scores)
    scores = jnp.where(allowed[:, None], scores, MASKED)
    largest = lax.optimization_barrier(jnp.max(scores, axis=-1, keepdims=True))
    expon = jnp.exp(scores - largest)
    probs = low(expon / lax.optimization_barrier(jnp.sum(expon, axis=-1, keepdims=True)))
    mixed = jnp.einsum('bhsk,bkhd->bshd', probs, value_heads, precision=HIGHEST)
    return mixed.reshape(batch, length, HEADS * HEAD)

def block(weights, prefix_keys, prefix_values, inputs, memory, segments, memory_segments):
    query_self, key_self, value_self, output_self, query_cross, key_cross, value_cross, output_cross, self_gain, self_shift, cross_gain, cross_shift, final_gain, final_shift, feed_in, feed_out, adapter_down, adapter_up = weights
    batch = inputs.shape[0]
    places = jnp.arange(SEQ)
    causal = places[:, None] >= places[None, :]
    local_mask = (segments[:, :, None] == segments[:, None, :]) & causal[None]
    prefix_mask = jnp.ones((batch, SEQ, PREFIX), dtype=jnp.bool_)
    self_mask = jnp.concatenate([prefix_mask, local_mask], axis=2)
    queries = low_back(low(product(inputs, query_self)))
    key_rows = low_back(low(product(inputs, key_self)))
    value_rows = low_back(low(product(inputs, value_self)))
    all_keys = jnp.concatenate([jnp.broadcast_to(prefix_keys[None], (batch, PREFIX, D)), key_rows], axis=1)
    all_values = jnp.concatenate([jnp.broadcast_to(prefix_values[None], (batch, PREFIX, D)), value_rows], axis=1)
    attended = low_back(low(attend(queries, all_keys, all_values, self_mask)))
    first = layer_norm(inputs + low_back(product(attended, output_self)), self_gain, self_shift)
    cross_queries = low_back(low(product(low(first), query_cross)))
    cross_keys = low_back(low(product(memory, key_cross)))
    cross_values = low_back(low(product(memory, value_cross)))
    cross_mask = segments[:, :, None] == memory_segments[:, None, :]
    crossed = low_back(low(attend(cross_queries, cross_keys, cross_values, cross_mask)))
    second = layer_norm(first + low_back(product(crossed, output_cross)), cross_gain, cross_shift)
    second_low = low(second)
    hidden_pre = low_back(product(second_low, feed_in))
    hidden = low(jax.nn.gelu(hidden_pre, approximate=False))
    bottle_pre = low_back(product(second_low, adapter_down))
    bottle = low(jax.nn.gelu(bottle_pre, approximate=False))
    branch = low_back(product(hidden, feed_out) + ADAPT_SCALE * product(bottle, adapter_up))
    return layer_norm(second + branch, final_gain, final_shift)

def forward(inputs, memory, query_self, key_self, value_self, output_self, query_cross, key_cross, value_cross, output_cross, self_gain, self_shift, cross_gain, cross_shift, final_gain, final_shift, feed_in, feed_out, adapter_down, adapter_up, prefix_embed, prefix_inner, prefix_outer, segments, memory_segments):
    weights = (query_self, key_self, value_self, output_self, query_cross, key_cross, value_cross, output_cross, self_gain, self_shift, cross_gain, cross_shift, final_gain, final_shift, feed_in, feed_out, adapter_down, adapter_up)
    tangent = jnp.tanh(product(prefix_embed, prefix_inner))
    prefix_rows = low(product(low(tangent), prefix_outer))
    prefix_keys = prefix_rows[:, :D]
    prefix_values = prefix_rows[:, D:]
    count = TOKENS // SEQ
    group = math.gcd(count, max(1, 4096 // SEQ))
    steps_count = count // group
    pieces = (inputs.reshape(steps_count, group, SEQ, D), memory.reshape(steps_count, group, MEM, D), segments.reshape(steps_count, group, SEQ), memory_segments.reshape(steps_count, group, MEM))

    def one_group(items):
        return block(weights, prefix_keys, prefix_values, items[0], items[1], items[2], items[3])
    outputs = lax.map(jax.checkpoint(one_group), pieces)
    return outputs.reshape(TOKENS, D)

def reference(inputs, memory, cotangent, segments, memory_segments, query_self, key_self, value_self, output_self, query_cross, key_cross, value_cross, output_cross, self_gain, self_shift, cross_gain, cross_shift, final_gain, final_shift, feed_in, feed_out, adapter_down, adapter_up, prefix_embed, prefix_inner, prefix_outer):
    floats = [array.astype(jnp.float32) for array in (inputs, memory, query_self, key_self, value_self, output_self, query_cross, key_cross, value_cross, output_cross, self_gain, self_shift, cross_gain, cross_shift, final_gain, final_shift, feed_in, feed_out, adapter_down, adapter_up, prefix_embed, prefix_inner, prefix_outer)]

    def wrapped(*arrays):
        return forward(*arrays, segments, memory_segments)
    result, pullback = jax.vjp(wrapped, *floats)
    grads = pullback(cotangent.astype(jnp.float32))
    return (result.astype(jnp.bfloat16), grads[0].astype(jnp.bfloat16), grads[1].astype(jnp.bfloat16), grads[2], grads[3], grads[4], grads[5], grads[6], grads[7], grads[8], grads[9], grads[10], grads[11], grads[12], grads[13], grads[14], grads[15], grads[16], grads[17], grads[18], grads[19], grads[20], grads[21], grads[22])
```

```python
import functools
from functools import reduce

import jax
import jax.numpy as jnp
from jax import lax
from jax.experimental import pallas as pl
from jax.experimental.pallas import tpu as pltpu
from jax.sharding import PartitionSpec as P

MESH = pl.DeviceIdType.MESH
bf16, f32 = jnp.bfloat16, jnp.float32
WIDE, NARROW = "wide", "narrow"
BOTH = (WIDE, NARROW)


HEADS = 16
HEAD = 64
PREFIX = 30


HIGHEST = lax.Precision.HIGHEST
EPSILON = 1e-05
MASKED = -1000000000.0
ADAPT_SCALE = 4.0


def matmul(left, right):
    return jnp.dot(left, right, preferred_element_type=jnp.float32)


def left_product(left, right):
    return lax.dot_general(
        left, right, (((0,), (0,)), ((), ())), preferred_element_type=jnp.float32
    )


def right_product(left, right):
    return lax.dot_general(
        left, right, (((1,), (1,)), ((), ())), preferred_element_type=jnp.float32
    )


def exact_left(left, right):
    return lax.dot_general(
        left, right, (((0,), (0,)), ((), ())), precision=HIGHEST, preferred_element_type=jnp.float32
    )


def exact_right(left, right):
    return lax.dot_general(
        left, right, (((1,), (1,)), ((), ())), precision=HIGHEST, preferred_element_type=jnp.float32
    )


def norm_forward(values, factor, offset):
    average = jnp.mean(values, axis=-1, keepdims=True)
    center = values - average
    inverse = lax.rsqrt(jnp.mean(center * center, axis=-1, keepdims=True) + EPSILON)
    normed = center * inverse
    return (normed * factor + offset, normed, inverse)


def norm_backward(grad_out, normed, inverse, factor):
    scaled = grad_out * factor
    grad_in = inverse * (
        scaled
        - jnp.mean(scaled, axis=-1, keepdims=True)
        - normed * jnp.mean(scaled * normed, axis=-1, keepdims=True)
    )
    return (grad_in, jnp.sum(grad_out * normed, axis=0), jnp.sum(grad_out, axis=0))


def head_view(rows):
    return rows.reshape(rows.shape[0], HEADS, HEAD)


def scored(queries, key_rows, allowed):
    raw = jnp.einsum(
        "shd,khd->hsk", head_view(queries), head_view(key_rows), preferred_element_type=jnp.float32
    )
    return jnp.where(allowed[None], raw * HEAD ** (-0.5), MASKED)


def attend_forward(queries, parts):
    scores = [scored(queries, member[0], member[2]) for member in parts]
    largest = reduce(jnp.maximum, [jnp.max(matrix, axis=-1, keepdims=True) for matrix in scores])
    total = reduce(
        jnp.add, [jnp.sum(jnp.exp(matrix - largest), axis=-1, keepdims=True) for matrix in scores]
    )
    logsum = largest + jnp.log(total)
    mixed = reduce(
        jnp.add,
        [
            jnp.einsum(
                "hsk,khd->shd",
                jnp.exp(matrix - logsum).astype(jnp.bfloat16),
                head_view(member[1]),
                preferred_element_type=jnp.float32,
            )
            for matrix, member in zip(scores, parts)
        ],
    )
    return (mixed.reshape(queries.shape[0], HEADS * HEAD), logsum)


def attend_backward(queries, parts, logsum, grad_low):
    grad_heads = head_view(grad_low)
    chances = [jnp.exp(scored(queries, member[0], member[2]) - logsum) for member in parts]
    slopes = [
        jnp.einsum(
            "shd,khd->hsk", grad_heads, head_view(member[1]), preferred_element_type=jnp.float32
        )
        for member in parts
    ]
    row_dot = reduce(
        jnp.add,
        [jnp.sum(chance * slope, axis=-1, keepdims=True) for chance, slope in zip(chances, slopes)],
    )
    scale = HEAD ** (-0.5)
    grad_query = jnp.zeros((queries.shape[0], HEADS, HEAD), jnp.float32)
    results = []
    for member, chance, slope in zip(parts, chances, slopes):
        dscore = (chance * (slope - row_dot)).astype(jnp.bfloat16)
        grad_query = grad_query + jnp.einsum(
            "hsk,khd->shd", dscore, head_view(member[0]), preferred_element_type=jnp.float32
        )
        grad_key = (
            jnp.einsum(
                "hsk,shd->khd", dscore, head_view(queries), preferred_element_type=jnp.float32
            )
            * scale
        )
        grad_value = jnp.einsum(
            "hsk,shd->khd",
            chance.astype(jnp.bfloat16),
            grad_heads,
            preferred_element_type=jnp.float32,
        )
        results.append(
            (
                grad_key.reshape(grad_key.shape[0], HEADS * HEAD),
                grad_value.reshape(grad_value.shape[0], HEADS * HEAD),
            )
        )
    return ((grad_query * scale).reshape(queries.shape[0], HEADS * HEAD), results)


def gelu_back(pre_values, grad_values):
    return jax.vjp(lambda inner: jax.nn.gelu(inner, approximate=False), pre_values)[1](grad_values)[
        0
    ]


def plain_body(
    inputs,
    memory,
    cotangent,
    segments,
    memory_segments,
    query_self,
    key_self,
    value_self,
    output_self,
    query_cross,
    key_cross,
    value_cross,
    output_cross,
    self_gain,
    self_shift,
    cross_gain,
    cross_shift,
    final_gain,
    final_shift,
    feed_in,
    feed_out,
    adapter_down,
    adapter_up,
    prefix_embed,
    prefix_inner,
    prefix_outer,
):
    (
        query_one,
        key_one,
        value_one,
        output_one,
        query_two,
        key_two,
        value_two,
        output_two,
        gain_one,
        shift_one,
        gain_two,
        shift_two,
        gain_three,
        shift_three,
        embed_full,
        inner_full,
        outer_full,
    ) = (
        lax.all_gather(query_self, BOTH, axis=0, tiled=True),
        lax.all_gather(key_self, BOTH, axis=0, tiled=True),
        lax.all_gather(value_self, BOTH, axis=0, tiled=True),
        lax.all_gather(output_self, BOTH, axis=0, tiled=True),
        lax.all_gather(query_cross, BOTH, axis=0, tiled=True),
        lax.all_gather(key_cross, BOTH, axis=0, tiled=True),
        lax.all_gather(value_cross, BOTH, axis=0, tiled=True),
        lax.all_gather(output_cross, BOTH, axis=0, tiled=True),
        lax.all_gather(self_gain, BOTH, axis=0, tiled=True),
        lax.all_gather(self_shift, BOTH, axis=0, tiled=True),
        lax.all_gather(cross_gain, BOTH, axis=0, tiled=True),
        lax.all_gather(cross_shift, BOTH, axis=0, tiled=True),
        lax.all_gather(final_gain, BOTH, axis=0, tiled=True),
        lax.all_gather(final_shift, BOTH, axis=0, tiled=True),
        lax.all_gather(prefix_embed, BOTH, axis=1, tiled=True),
        lax.all_gather(prefix_inner, BOTH, axis=0, tiled=True),
        lax.all_gather(prefix_outer, BOTH, axis=1, tiled=True),
    )
    factor_one = gain_one.astype(jnp.float32)
    factor_two = gain_two.astype(jnp.float32)
    factor_three = gain_three.astype(jnp.float32)
    length = inputs.shape[0]
    width = inputs.shape[1]
    places = jnp.arange(length)
    causal = places[:, None] >= places[None, :]
    local_mask = (segments[:, None] == segments[None, :]) & causal
    prefix_mask = jnp.ones((length, PREFIX), jnp.bool_)
    cross_mask = segments[:, None] == memory_segments[None, :]
    tangent = jnp.tanh(matmul(embed_full, inner_full))
    tangent_low = tangent.astype(jnp.bfloat16)
    prefix_rows = matmul(tangent_low, outer_full).astype(jnp.bfloat16)
    prefix_keys = prefix_rows[:, :width]
    prefix_values = prefix_rows[:, width:]
    queries = matmul(inputs, query_one).astype(jnp.bfloat16)
    key_rows = matmul(inputs, key_one).astype(jnp.bfloat16)
    value_rows = matmul(inputs, value_one).astype(jnp.bfloat16)
    self_parts = ((prefix_keys, prefix_values, prefix_mask), (key_rows, value_rows, local_mask))
    attended, self_logsum = attend_forward(queries, self_parts)
    attended_low = attended.astype(jnp.bfloat16)
    first, normed_one, inverse_one = norm_forward(
        inputs.astype(jnp.float32) + matmul(attended_low, output_one),
        factor_one,
        shift_one.astype(jnp.float32),
    )
    first_low = first.astype(jnp.bfloat16)
    cross_queries = matmul(first_low, query_two).astype(jnp.bfloat16)
    cross_keys = matmul(memory, key_two).astype(jnp.bfloat16)
    cross_values = matmul(memory, value_two).astype(jnp.bfloat16)
    cross_parts = ((cross_keys, cross_values, cross_mask),)
    crossed, cross_logsum = attend_forward(cross_queries, cross_parts)
    crossed_low = crossed.astype(jnp.bfloat16)
    second, normed_two, inverse_two = norm_forward(
        first + matmul(crossed_low, output_two), factor_two, shift_two.astype(jnp.float32)
    )
    second_low = second.astype(jnp.bfloat16)
    feed_rows = lax.all_gather(second_low, WIDE, axis=0, tiled=True)
    hidden_pre = matmul(feed_rows, feed_in)
    hidden_low = jax.nn.gelu(hidden_pre, approximate=False).astype(jnp.bfloat16)
    feed_sum = lax.psum_scatter(
        matmul(hidden_low, feed_out), WIDE, scatter_dimension=0, tiled=True
    )
    adapt_rows = lax.all_gather(second_low, NARROW, axis=0, tiled=True)
    bottle_pre = matmul(adapt_rows, adapter_down)
    bottle_low = jax.nn.gelu(bottle_pre, approximate=False).astype(jnp.bfloat16)
    adapt_sum = lax.psum_scatter(
        matmul(bottle_low, adapter_up).astype(jnp.bfloat16),
        NARROW,
        scatter_dimension=0,
        tiled=True,
    ).astype(jnp.float32)
    branch = feed_sum + ADAPT_SCALE * adapt_sum
    result, normed_three, inverse_three = norm_forward(
        second + branch, factor_three, shift_three.astype(jnp.float32)
    )
    grad_branch, gain_three_grad, shift_three_grad = norm_backward(
        cotangent.astype(jnp.float32), normed_three, inverse_three, factor_three
    )
    branch_low = grad_branch.astype(jnp.bfloat16)
    branch_rows = lax.all_gather(branch_low, WIDE, axis=0, tiled=True)
    grad_hidden = right_product(branch_rows, feed_out)
    grad_pre = gelu_back(hidden_pre, grad_hidden).astype(jnp.bfloat16)
    grad_out_part = left_product(hidden_low, branch_rows)
    grad_in_part = left_product(feed_rows, grad_pre)
    grad_feed = lax.psum_scatter(
        right_product(grad_pre, feed_in), WIDE, scatter_dimension=0, tiled=True
    )
    feed_in_total, feed_out_total = (
        lax.psum_scatter(
            grad_in_part.astype(jnp.bfloat16), NARROW, scatter_dimension=0, tiled=True
        ).astype(jnp.float32),
        lax.psum_scatter(
            grad_out_part.astype(jnp.bfloat16), NARROW, scatter_dimension=1, tiled=True
        ).astype(jnp.float32),
    )
    branch_narrow = lax.all_gather(branch_low, NARROW, axis=0, tiled=True)
    grad_bottle = ADAPT_SCALE * right_product(branch_narrow, adapter_up)
    grad_bottle_pre = gelu_back(bottle_pre, grad_bottle).astype(jnp.bfloat16)
    grad_up_part = ADAPT_SCALE * left_product(bottle_low, branch_narrow)
    grad_down_part = left_product(adapt_rows, grad_bottle_pre)
    grad_adapt = lax.psum_scatter(
        right_product(grad_bottle_pre, adapter_down).astype(jnp.bfloat16),
        NARROW,
        scatter_dimension=0,
        tiled=True,
    ).astype(jnp.float32)
    down_total, up_total = (
        lax.psum_scatter(grad_down_part, WIDE, scatter_dimension=0, tiled=True),
        lax.psum_scatter(grad_up_part, WIDE, scatter_dimension=1, tiled=True),
    )
    grad_second = grad_branch + grad_feed + grad_adapt
    grad_mid, gain_two_grad, shift_two_grad = norm_backward(
        grad_second, normed_two, inverse_two, factor_two
    )
    mid_low = grad_mid.astype(jnp.bfloat16)
    output_two_grad = left_product(crossed_low, mid_low)
    crossed_grad = right_product(mid_low, output_two).astype(jnp.bfloat16)
    cross_query_grad, cross_results = attend_backward(
        cross_queries, cross_parts, cross_logsum, crossed_grad
    )
    cross_query_low = cross_query_grad.astype(jnp.bfloat16)
    cross_key_low = cross_results[0][0].astype(jnp.bfloat16)
    cross_value_low = cross_results[0][1].astype(jnp.bfloat16)
    query_two_grad = left_product(first_low, cross_query_low)
    key_two_grad = left_product(memory, cross_key_low)
    value_two_grad = left_product(memory, cross_value_low)
    memory_grad = (
        right_product(cross_key_low, key_two) + right_product(cross_value_low, value_two)
    ).astype(jnp.bfloat16)
    grad_first = grad_mid + right_product(cross_query_low, query_two)
    grad_start, gain_one_grad, shift_one_grad = norm_backward(
        grad_first, normed_one, inverse_one, factor_one
    )
    start_low = grad_start.astype(jnp.bfloat16)
    output_one_grad = left_product(attended_low, start_low)
    attended_grad = right_product(start_low, output_one).astype(jnp.bfloat16)
    self_query_grad, self_results = attend_backward(queries, self_parts, self_logsum, attended_grad)
    self_query_low = self_query_grad.astype(jnp.bfloat16)
    self_key_low = self_results[1][0].astype(jnp.bfloat16)
    self_value_low = self_results[1][1].astype(jnp.bfloat16)
    query_one_grad = left_product(inputs, self_query_low)
    key_one_grad = left_product(inputs, self_key_low)
    value_one_grad = left_product(inputs, self_value_low)
    inputs_grad = (
        grad_start
        + right_product(self_query_low, query_one)
        + right_product(self_key_low, key_one)
        + right_product(self_value_low, value_one)
    ).astype(jnp.bfloat16)
    prefix_grad = jnp.concatenate([self_results[0][0], self_results[0][1]], axis=1)
    outer_grad = exact_left(tangent_low.astype(jnp.float32), prefix_grad)
    tangent_grad = exact_right(prefix_grad, outer_full.astype(jnp.float32)) * (
        1.0 - tangent * tangent
    )
    inner_grad = exact_left(embed_full.astype(jnp.float32), tangent_grad)
    embed_grad = exact_right(tangent_grad, inner_full.astype(jnp.float32))
    (
        query_one_sum,
        key_one_sum,
        value_one_sum,
        output_one_sum,
        query_two_sum,
        key_two_sum,
        value_two_sum,
        output_two_sum,
        gain_one_sum,
        shift_one_sum,
        gain_two_sum,
        shift_two_sum,
        gain_three_sum,
        shift_three_sum,
        embed_sum,
        inner_sum,
        outer_sum,
    ) = (
        lax.psum_scatter(query_one_grad, BOTH, scatter_dimension=0, tiled=True),
        lax.psum_scatter(key_one_grad, BOTH, scatter_dimension=0, tiled=True),
        lax.psum_scatter(value_one_grad, BOTH, scatter_dimension=0, tiled=True),
        lax.psum_scatter(output_one_grad, BOTH, scatter_dimension=0, tiled=True),
        lax.psum_scatter(query_two_grad, BOTH, scatter_dimension=0, tiled=True),
        lax.psum_scatter(key_two_grad, BOTH, scatter_dimension=0, tiled=True),
        lax.psum_scatter(value_two_grad, BOTH, scatter_dimension=0, tiled=True),
        lax.psum_scatter(output_two_grad, BOTH, scatter_dimension=0, tiled=True),
        lax.psum_scatter(gain_one_grad, BOTH, scatter_dimension=0, tiled=True),
        lax.psum_scatter(shift_one_grad, BOTH, scatter_dimension=0, tiled=True),
        lax.psum_scatter(gain_two_grad, BOTH, scatter_dimension=0, tiled=True),
        lax.psum_scatter(shift_two_grad, BOTH, scatter_dimension=0, tiled=True),
        lax.psum_scatter(gain_three_grad, BOTH, scatter_dimension=0, tiled=True),
        lax.psum_scatter(shift_three_grad, BOTH, scatter_dimension=0, tiled=True),
        lax.psum_scatter(embed_grad, BOTH, scatter_dimension=1, tiled=True),
        lax.psum_scatter(inner_grad, BOTH, scatter_dimension=0, tiled=True),
        lax.psum_scatter(outer_grad, BOTH, scatter_dimension=1, tiled=True),
    )
    return (
        result.astype(jnp.bfloat16),
        inputs_grad,
        memory_grad,
        query_one_sum,
        key_one_sum,
        value_one_sum,
        output_one_sum,
        query_two_sum,
        key_two_sum,
        value_two_sum,
        output_two_sum,
        gain_one_sum,
        shift_one_sum,
        gain_two_sum,
        shift_two_sum,
        gain_three_sum,
        shift_three_sum,
        feed_in_total,
        feed_out_total,
        down_total,
        up_total,
        embed_sum,
        inner_sum,
        outer_sum,
    )


def place():
    w = lax.axis_index(WIDE); n = lax.axis_index(NARROW)
    return w // 2, w % 2, n // 2, n % 2

def device(a, b, x, c):
    return (a * 2 + b, x * 2 + c)

def greet(peers):
    barrier = pltpu.get_barrier_semaphore()
    for p in peers:
        pl.semaphore_signal(barrier, inc=1, device_id=p, device_id_type=MESH)
    pl.semaphore_wait(barrier, len(peers))

def remote(src, dst, send, recv, dev):
    return pltpu.make_async_remote_copy(src_ref=src, dst_ref=dst, send_sem=send, recv_sem=recv, device_id=dev, device_id_type=MESH)

def gather_kernel(A, r, s_ref, fin, fout, down, up, g_ref, fin2, fout2, down4, up4, f_s, f_r, own_sem, own_s, own_r, z_s, z_r, m_s, m_r, l_s, l_r, d_s, d_r):
    a, b, x, c = place()
    core, xp, yp = device(a, b, x, 1 - c), device(a, b, 1 - x, c), device(a, 1 - b, x, c)
    zp = [device((a + j) % A, b, x, c) for j in range(A)]
    greet([core, xp, yp] + zp[1:])
    width = g_ref.shape[2]
    half = width // 2
    def row(a_, b_, x_):
        return pl.multiple_of(((a_ * 2 + b_) * 2 + x_) * 2 * r, 2 * r)
    mine = row(a, b, x)
    pairs = s_ref.shape[0] // 2
    local, cross = [], []
    for i in range(pairs):
        k, o = 2 * i + c, 2 * i + 1 - c
        at = pl.multiple_of(mine + c * r, r)
        l = pltpu.make_async_copy(s_ref.at[k], g_ref.at[k, pl.ds(at, r)], own_sem.at[i])
        q = remote(s_ref.at[o], g_ref.at[o, pl.ds(at, r)], own_s.at[i], own_r.at[i], core)
        q.start(); l.start()
        local.append(l); cross.append(q)
    def block(i, h, a_, b_, x_):
        return g_ref.at[2 * i + c, pl.ds(row(a_, b_, x_), 2 * r), pl.ds(h * half, half)]
    sent = []
    def send(i, h, where, sems, idx, dev):
        ss, rr = sems
        cp = remote(block(i, h, *where), block(i, h, *where), ss.at[idx], rr.at[idx], dev)
        cp.start(); sent.append(cp)
    arr = {}
    def wait(i, h, where, rr, idx):
        pltpu.make_async_copy(block(i, h, *where), block(i, h, *where), rr.at[idx]).wait()
    def first(i):
        local[i].wait(); cross[i].wait()
        for h in range(2):
            send(i, h, (a, b, x), (m_s, m_r), (i * 2 + h) * A, (yp, xp)[h])
        for h in range(2):
            send(i, h, (a, b, x), (l_s, l_r), 2 * (i * 2 + h) * A, (xp, yp)[h])
        for j in range(1, A):
            for h in range(2):
                send(i, h, (a, b, x), (z_s, z_r), (i * 2 + h) * A + j, zp[j])
    def third(i, j):
        aj = (a + A - j) % A
        for h in range(2):
            idx = (i * 2 + h) * A + j
            other = (aj, 1 - b, x) if h == 0 else (aj, b, 1 - x)
            wait(i, h, other, m_r, idx)
            send(i, h, other, (l_s, l_r), 2 * idx + 1, (xp, yp)[h])
    def middle(i):
        third(i, 0)
        for j in range(1, A):
            aj = (a + A - j) % A
            for h in range(2):
                wait(i, h, (aj, b, x), z_r, (i * 2 + h) * A + j)
                send(i, h, (aj, b, x), (m_s, m_r), (i * 2 + h) * A + j, (yp, xp)[h])
            for h in range(2):
                send(i, h, (aj, b, x), (l_s, l_r), 2 * ((i * 2 + h) * A + j), (xp, yp)[h])
    def last(i):
        for j in range(1, A):
            third(i, j)
    def finish(i):
        for j in range(A):
            aj = (a + A - j) % A
            for h in range(2):
                idx = (i * 2 + h) * A + j
                one = (aj, b, 1 - x) if h == 0 else (aj, 1 - b, x)
                wait(i, h, one, l_r, 2 * idx)
                wait(i, h, (aj, 1 - b, 1 - x), l_r, 2 * idx + 1)
        k = 2 * i + c
        q = remote(g_ref.at[k], g_ref.at[k], d_s.at[i], d_r.at[i], core)
        q.start(); cross.append(q)
    za = a + 1 - 2 * (a % 2)
    zq = device(za, b, x, c)
    H, AD = fin.shape[1], down.shape[1]
    D = fin.shape[0]
    extra = []
    def put(src, dst, dev):
        q = remote(src, dst, f_s.at[len(extra)], f_r.at[len(extra)], dev)
        q.start(); extra.append(q)
        return q
    def keep(src, dst):
        q = pltpu.make_async_copy(src, dst, f_s.at[len(extra)])
        q.start(); extra.append(None)
        return q
    kept = []
    def feeds():
        kept.append(keep(fin, fin2.at[:, pl.ds(0, H)]))
        kept.append(keep(fout, fout2.at[pl.ds(0, H)]))
        ri, ro = pl.ds(pl.multiple_of(c * (D // 2), D // 2), D // 2), pl.ds(pl.multiple_of(c * (H // 2), H // 2), H // 2)
        ro2 = pl.ds(pl.multiple_of(H + c * (H // 2), H // 2), H // 2)
        return ([put(fin.at[ri], fin2.at[ri, pl.ds(H, H)], zq), put(fout.at[ro], fout2.at[ro2], zq)],
                [(fin2.at[ri, pl.ds(H, H)],) * 2, (fout2.at[ro2],) * 2])
    def adapter():
        n = pl.ds(pl.multiple_of((x * 2 + c) * AD, AD), AD)
        m = pl.ds(pl.multiple_of((2 - 2 * x + c) * AD, AD), AD)
        kept.append(keep(down, down4.at[:, n]))
        kept.append(keep(up, up4.at[n]))
        q = [put(down, down4.at[:, n], xp), put(up, up4.at[n], xp), put(down, down4.at[:, n], core), put(up, up4.at[n], core)]
        return q[:2], [(down4.at[:, m],) * 2, (up4.at[m],) * 2]
    def onward(waits, pairs_):
        for q, (src, dst) in zip(waits, pairs_):
            q.wait_recv()
            put(src, dst, core)
    first(0)
    for i in range(pairs):
        if i + 1 < pairs:
            first(i + 1)
        if i == 1:
            ad = adapter()
        if i == 2:
            fe = feeds()
        middle(i)
        last(i)
        if i: finish(i - 1)
    onward(*ad)
    onward(*fe)
    finish(pairs - 1)
    for i in range(pairs):
        cross[pairs + i].wait()
    for cp in sent:
        cp.wait_send()
    for cp in kept:
        cp.wait()
    for cp in extra:
        if cp is not None:
            cp.wait_send()
            if not any(cp is q for q in ad[0] + fe[0]):
                cp.wait_recv()

def gather(A, shards, fin, fout, down, up):
    K, r, width = shards.shape
    pairs = K // 2
    sem = pltpu.SemaphoreType.DMA
    n = pairs * 2 * A
    sds = jax.ShapeDtypeStruct
    D, H = fin.shape
    AD = down.shape[1]
    any_ = pl.BlockSpec(memory_space=pl.ANY)
    return pl.pallas_call(
        functools.partial(gather_kernel, A, r),
        out_shape=(sds((K, A * 8 * r, width), bf16), sds((D, 2 * H), bf16), sds((2 * H, D), bf16), sds((D, 4 * AD), bf16), sds((4 * AD, D), bf16)),
        in_specs=[any_] * 5, out_specs=(any_,) * 5,
        scratch_shapes=[sem((16,)), sem((16,)), sem((pairs,)), sem((pairs,)), sem((pairs,)), sem((n,)), sem((n,)), sem((n,)), sem((n,)), sem((2 * n,)), sem((2 * n,)), sem((pairs,)), sem((pairs,))],
        compiler_params=pltpu.CompilerParams(collective_id=1, has_side_effects=True),
        name="weights_in")(shards, fin, fout, down, up)


def dot_left(l, r):
    return lax.dot_general(l, r, (((0,), (0,)), ((), ())), preferred_element_type=f32)

class Copies:
    def __init__(self, send, recv):
        self.send, self.recv, self.count, self.all = send, recv, 0, []
    def __call__(self, src, dst, dev):
        cp = remote(src, dst, self.send.at[self.count], self.recv.at[self.count], dev)
        self.count += 1
        cp.start(); self.all.append(cp)
        return cp
    def local(self, src, dst):
        cp = pltpu.make_async_copy(src, dst, self.send.at[self.count])
        self.count += 1
        cp.start()
        return cp
    def sent(self, some):
        for cp in some:
            cp.wait_send()
            self.all = [o for o in self.all if o is not cp]
    def close(self):
        for cp in self.all: cp.wait_send()

def reduce_kernel(A, r, xs, ys, mem, ym, ax, ay, fi, fo, out, aout, fi_out, fo_out,
                  xb, yb, mb, mby, axb, ayb, pb, apb, fib, fob, r1, r2, r3, ra1, ra2, ra3, rfi, rfo, rzi, rzo, rxi, rxo, ob, aob, fib2, fob2, ssem, rsem):
    a, b, x, c = place()
    core, xp, yp = device(a, b, x, 1 - c), device(a, b, 1 - x, c), device(a, 1 - b, x, c)
    zp = [device((a + j) % A, b, x, c) for j in range(A)]
    za = a + 1 - 2 * (a % 2)
    zq = device(za, b, x, c)
    greet([core, xp, yp] + zp[1:])
    cp = Copies(ssem, rsem)
    o = 1 - c
    T = 128
    D = pb.shape[-1]; HID = fi.shape[1] // 2
    st0 = []
    fcopies = []
    Q = fi.shape[0] // 4
    for xx in range(2):
        dq = pl.ds(pl.multiple_of((xx * 2 + o) * Q, Q), Q)
        fcopies.append(cp(fi.at[dq, :], rfi.at[xx], core))
        fcopies.append(cp(fo.at[:, dq], rfo.at[xx], core))
    for i in range(3):
        e = [cp(xs.at[2 * i + o], xb.at[i, pl.ds(T, T)], core), cp(ys.at[2 * i + o], yb.at[i, pl.ds(T, T)], core)]
        l = [cp.local(xs.at[2 * i + c], xb.at[i, pl.ds(0, T)]), cp.local(ys.at[2 * i + c], yb.at[i, pl.ds(0, T)])]
        st0.append((e, l))
    M = mem.shape[0]
    e = [cp(mem, mb.at[pl.ds(M, M)], core), cp(ym.at[o], mby.at[pl.ds(M, M)], core)]
    l = [cp.local(mem, mb.at[pl.ds(0, M)]), cp.local(ym.at[c], mby.at[pl.ds(0, M)])]
    st0.append((e, l))
    e = [cp(ax.at[o], axb.at[pl.ds(T, T)], core), cp(ay.at[o], ayb.at[pl.ds(T, T)], core)]
    l = [cp.local(ax.at[c], axb.at[pl.ds(0, T)]), cp.local(ay.at[c], ayb.at[pl.ds(0, T)])]
    st0.append((e, l))
    def ready(i):
        for q in st0[i][0]: q.wait_recv()
        for q in st0[i][1]: q.wait()
    for q in fcopies: q.wait_recv()
    for xx in range(2):
        dq = pl.ds(pl.multiple_of((xx * 2 + c) * Q, Q), Q)
        def rows_fi(t, _):
            fib[xx, pl.ds(t * 32, 32), :] = fi[pl.ds(pl.multiple_of((xx * 2 + c) * Q + t * 32, 32), 32), :] + rfi[xx, pl.ds(t * 32, 32), :]
            return 0
        lax.fori_loop(0, Q // 32, rows_fi, 0)
        def rows_fo(t, _):
            fob[xx, pl.ds(t * 64, 64), :] = fo[pl.ds(t * 64, 64), dq] + rfo[xx, pl.ds(t * 64, 64), :]
            return 0
        lax.fori_loop(0, fo.shape[0] // 64, rows_fo, 0)
    zf = [cp(fib.at[:, :, pl.ds(HID, HID)], rzi, zq), cp(fob.at[:, pl.ds(HID, HID), :], rzo, zq)]

    half = D // 2
    first, second, third = {}, {}, {}
    def compute(i):
        ready(i)
        for h in range(2):
            def tile(t, _):
                cols = pl.ds(pl.multiple_of(h * half + t * 256, 256), 256)
                if i < 3:
                    p = dot_left(xb[i], yb[i, :, cols])
                else:
                    p = dot_left(mb[...], mby[:, cols])
                pb[i, :, :, :, :, cols] = p.astype(bf16).reshape(A, 2, 2, 2 * r, 256)
                return 0
            lax.fori_loop(0, half // 256, tile, 0)
            cols = pl.ds(h * half, half)
            if h == 0:
                first[i, h] = cp(pb.at[i, :, :, 1 - x, :, cols], r1.at[i, h], xp)
            else:
                first[i, h] = cp(pb.at[i, :, 1 - b, :, :, cols], r1.at[i, h], yp)
    def one(i, h):
        cols = pl.ds(h * half, half)
        first[i, h].wait_recv()
        def add(side):
            def row(z, _):
                if h == 0:
                    pb[i, z, side, x, :, cols] = pb[i, z, side, x, :, cols] + r1[i, h, z, side]
                else:
                    pb[i, z, b, side, :, cols] = pb[i, z, b, side, :, cols] + r1[i, h, z, side]
                return 0
            lax.fori_loop(0, A, row, 0)
        add(1 - b if h == 0 else 1 - x)
        if h == 0:
            second[i, h] = cp(pb.at[i, :, 1 - b, x, :, cols], r2.at[i, h], yp)
        else:
            second[i, h] = cp(pb.at[i, :, b, 1 - x, :, cols], r2.at[i, h], xp)
        add(b if h == 0 else x)
    def two(i, h):
        cols = pl.ds(h * half, half)
        second[i, h].wait_recv()
        for j in range(1, A):
            aj = (a + j) % A
            pb[i, aj, b, x, :, cols] = pb[i, aj, b, x, :, cols] + r2[i, h, aj]
            third[i, h, j] = cp(pb.at[i, aj, b, x, :, cols], r3.at[i, h, j - 1], zp[j])
        pb[i, a, b, x, :, cols] = pb[i, a, b, x, :, cols] + r2[i, h, a]
    outs = []
    def three(i, h):
        cols = pl.ds(h * half, half)
        for j in range(1, A): third[i, h, j].wait_recv()
        t = pb[i, a, b, x, :, cols].astype(f32)
        for j in range(1, A): t = t + r3[i, h, j - 1].astype(f32)
        ob[i, :, cols] = t
        if h == 1:
            outs.append(cp.local(ob.at[i, pl.ds(pl.multiple_of(c * r, r), r)], out.at[2 * i + c]).wait)
            q = cp(ob.at[i, pl.ds(pl.multiple_of(o * r, r), r)], out.at[2 * i + c], core)
            outs.append(q.wait_recv)
    def adapt0():
        ready(4)
        for t in range(2):
            cols = pl.ds(t * 256, 256)
            apb[t] = dot_left(axb[...], ayb[:, cols]).astype(bf16).reshape(A, 2, D // (2 * A), 256)
        first["a"] = cp(apb.at[1 - x], ra1, xp)
    def adapt1():
        first["a"].wait_recv()
        def row(z, _):
            for s in range(2):
                apb[x, z, s] = apb[x, z, s] + ra1[z, s]
            return 0
        lax.fori_loop(0, A, row, 0)
        second["a"] = cp(apb.at[x, :, 1 - b], ra2, yp)
    def adapt2():
        second["a"].wait_recv()
        for j in range(1, A):
            aj = (a + j) % A
            apb[x, aj, b] = apb[x, aj, b] + ra2[aj]
            third["a", j] = cp(apb.at[x, aj, b], ra3.at[j - 1], zp[j])
        apb[x, a, b] = apb[x, a, b] + ra2[a]
    def adapt3():
        for j in range(1, A): third["a", j].wait_recv()
        t = apb[x, a, b].astype(f32)
        for j in range(1, A): t = t + ra3[j - 1].astype(f32)
        aob[0] = t[:, :128]
        aob[1] = t[:, 128:]
        outs.append(cp.local(aob.at[c], aout.at[c]).wait)
        outs.append(cp(aob.at[o], aout.at[c], core).wait_recv)
    xf = []
    def feed1():
        for q in zf: q.wait_recv()
        def rows_fi(t, _):
            for xx in range(2):
                rows = pl.ds(t * 32, 32)
                fib[xx, rows, pl.ds(0, HID)] = fib[xx, rows, pl.ds(0, HID)] + rzi[xx, rows, :]
            return 0
        lax.fori_loop(0, Q // 32, rows_fi, 0)
        def rows_fo(t, _):
            for xx in range(2):
                rows = pl.ds(t * 64, 64)
                fob[xx, rows, :] = fob[xx, rows, :] + rzo[xx, rows, :]
            return 0
        lax.fori_loop(0, HID // 64, rows_fo, 0)
        xf.append(cp(fib.at[1 - x, :, pl.ds(0, HID)], rxi, xp))
        xf.append(cp(fob.at[1 - x, pl.ds(0, HID), :], rxo, xp))
    def feed2():
        for q in xf: q.wait_recv()
        def rows_fi(t, _):
            rows = pl.ds(t * 32, 32)
            fib2[rows, :] = fib[x, rows, pl.ds(0, HID)].astype(f32) + rxi[rows, :].astype(f32)
            return 0
        lax.fori_loop(0, Q // 32, rows_fi, 0)
        def rows_fo(t, _):
            rows = pl.ds(t * 64, 64)
            fob2[rows, :] = fob[x, rows, :].astype(f32) + rxo[rows, :].astype(f32)
            return 0
        lax.fori_loop(0, HID // 64, rows_fo, 0)
        outs.append(cp.local(fib2, fi_out).wait)
        outs.append(cp.local(fob2, fo_out).wait)
    compute(0)
    compute(1)
    compute(2)
    one(0, 0); one(0, 1)
    compute(3)
    one(1, 0); one(1, 1)
    feed1()
    adapt0()
    two(0, 0); two(0, 1)
    one(2, 0); one(2, 1)
    two(1, 0); two(1, 1)
    one(3, 0); one(3, 1)
    two(2, 0); two(2, 1)
    three(0, 0); three(0, 1)
    adapt1()
    two(3, 0); two(3, 1)
    adapt2()
    three(1, 0); three(1, 1)
    feed2()
    three(2, 0); three(2, 1)
    adapt3()
    three(3, 0); three(3, 1)
    for q in outs: q()
    cp.close()

def reduce_grads(A, r, xs, ys, mem, ym, ax, ay, fi, fo):
    D = xs.shape[2]; T = xs.shape[1]; M = mem.shape[0]; Q = fi.shape[0] // 4; H2 = fi.shape[1]; H = H2 // 2
    v = lambda *s: pltpu.VMEM(s, bf16)
    vf = lambda *s: pltpu.VMEM(s, f32)
    any_ = pl.BlockSpec(memory_space=pl.ANY)
    vm = pl.BlockSpec(memory_space=pltpu.VMEM)
    half = D // 2
    sds = jax.ShapeDtypeStruct
    return pl.pallas_call(
        functools.partial(reduce_kernel, A, r),
        out_shape=(sds((8, r, D), f32), sds((2, D // (2 * A), 128), f32), sds((Q, H), f32), sds((H, Q), f32)),
        in_specs=[vm] * 8, out_specs=(any_,) * 4,
        scratch_shapes=[v(3, 2 * T, D), v(3, 2 * T, D), v(2 * M, D), v(2 * M, D), v(2 * T, D), v(2 * T, 512),
            v(4, A, 2, 2, 2 * r, D), v(2, A, 2, D // (2 * A), 256), v(2, Q, H2), v(2, H2, Q),
            v(4, 2, A, 2, 2 * r, half), v(4, 2, A, 2 * r, half), v(4, 2, A - 1, 2 * r, half),
            v(A, 2, D // (2 * A), 256), v(A, D // (2 * A), 256), v(A - 1, D // (2 * A), 256),
            v(2, Q, H2), v(2, H2, Q), v(2, Q, H), v(2, H, Q), v(Q, H), v(H, Q),
            vf(4, 2 * r, D), vf(2, D // (2 * A), 128), vf(Q, H), vf(H, Q),
            pltpu.SemaphoreType.DMA((128,)), pltpu.SemaphoreType.DMA((128,))],
        compiler_params=pltpu.CompilerParams(collective_id=2, has_side_effects=True, vmem_limit_bytes=60 << 20),
        name="weight_grads")(xs, ys, mem, ym, ax, ay, fi, fo)


EPSILON = 1e-05
ADAPT_SCALE = 4.0

def dot(l, r):
    return jnp.dot(l, r, preferred_element_type=f32)

def dot_right(l, r):
    return lax.dot_general(l, r, (((1,), (1,)), ((), ())), preferred_element_type=f32)

def gelu_both(v):
    phi = 0.5 + 0.5 * lax.erf(v * 0.7071067811865476)
    return v * phi, phi + v * (0.3989422804014327 * jnp.exp(-0.5 * v * v))

def norm(v):
    center = v - jnp.mean(v, axis=-1, keepdims=True)
    inverse = lax.rsqrt(jnp.mean(center * center, axis=-1, keepdims=True) + EPSILON)
    return center * inverse, inverse

def norm_back(e, n, inverse, factor):
    s = e * factor
    return inverse * (s - jnp.mean(s, axis=-1, keepdims=True) - n * jnp.mean(s * n, axis=-1, keepdims=True))

def feed_kernel(A, second, cot, fin, fout, down, up, gain, shift, result, gsec, fi, fo, ay, blow, ngrad,
                rows, brow, hid, slope, gpre, part, q1, q2, q3, bslope, acc, ssem, rsem):
    a, b, x, c = place()
    yp = device(a, 1 - b, x, c)
    zp = device((a + A // 2) % A, b, x, c)
    greet([yp, zp])
    cp = Copies(ssem, rsem)
    T, D = second.shape
    NC = 2
    R = T // NC
    HID = fin.shape[1]; TW = 256

    def spread(buf):
        zs, ys = [], []
        for q in range(NC):
            s = pl.ds(q * R, R)
            zs.append(cp(buf.at[0, s], buf.at[2, s], zp))
            ys.append(cp(buf.at[0, s], buf.at[1, s], yp))
        def forward():
            f = []
            for q in range(NC):
                s = pl.ds(q * R, R)
                zs[q].wait_recv()
                f.append(cp(buf.at[2, s], buf.at[3, s], yp))
            return f
        return zs, ys, forward

    p3_sent = []
    def collect(level):
        p3, p1 = [], []
        for q in range(NC):
            p3.append(cp(part.at[3, pl.ds(q * R, R)], q3.at[level, pl.ds(q * R, R)], yp))
        for q in range(NC):
            p1.append(cp(part.at[1, pl.ds(q * R, R)], q1.at[level, pl.ds(q * R, R)], yp))
        p2 = []
        for q in range(NC):
            s = pl.ds(q * R, R)
            p3[q].wait_recv()
            part[2, s] = part[2, s] + q3[level, s]
            p2.append(cp(part.at[2, s], q2.at[level, s], zp))
        p3_sent.append(p3)
        return p1, p2

    def gather_up(level, p1, p2):
        for q in range(NC):
            s = pl.ds(q * R, R)
            p1[q].wait_recv(); p2[q].wait_recv()
            acc[s] = acc[s] + q1[level, s].astype(f32) + q2[level, s].astype(f32)
        cp.sent(p1 + p2 + p3_sent.pop())

    rows[0] = second[...].astype(bf16)
    zs, ys, forward = spread(rows)
    for t in range(2):
        cols = pl.ds(t * 256, 256)
        g, s = gelu_both(dot(rows[0], down[:, cols]))
        ay[1, :, cols] = (ADAPT_SCALE * g.astype(bf16).astype(f32)).astype(bf16)
        bslope[:, cols] = s
    def enter(j):
        def tile(t, _):
            cols = pl.ds(pl.multiple_of(t * TW, TW), TW)
            g, s = gelu_both(dot(rows[j], fin[:, cols]))
            hid[j, :, cols] = g.astype(bf16)
            slope[j, :, cols] = s
            return 0
        lax.fori_loop(0, HID // TW, tile, 0)
        def tile2(t, _):
            cols = pl.ds(pl.multiple_of(t * TW, TW), TW)
            p = dot(hid[j], fout[:, cols])
            if j == 0:
                acc[:, cols] = p + dot(ay[1], up[:, cols])
            else:
                part[j, :, cols] = p.astype(bf16)
            return 0
        lax.fori_loop(0, D // TW, tile2, 0)
    enter(0)
    for q in ys: q.wait_recv()
    fw = forward()
    enter(1)
    enter(2)
    for q in fw: q.wait_recv()
    enter(3)
    p1, p2 = collect(0)
    gather_up(0, p1, p2)
    n3, inv3 = norm(second[...] + acc[...])
    fac = gain[...].astype(f32)
    result[...] = (n3 * fac + shift[...].astype(f32)).astype(bf16)
    e = cot[...].astype(f32)
    gb = norm_back(e, n3, inv3, fac)
    gbl = gb.astype(bf16)
    brow[0] = gbl
    zs, ys, forward = spread(brow)
    blow[...] = gbl
    acc[...] = gb
    ngrad[0:1, :] = jnp.sum(e * n3, axis=0, keepdims=True)
    ngrad[1:2, :] = jnp.sum(e, axis=0, keepdims=True)
    def adapt_tile(t, _):
        cols = pl.ds(pl.multiple_of(t * 256, 256), 256)
        gbot = bslope[:, cols] * (ADAPT_SCALE * dot_right(brow[0], up[cols, :]))
        ay[0, :, cols] = gbot.astype(bf16)
        return 0
    lax.fori_loop(0, down.shape[1] // 256, adapt_tile, 0)
    def leave(j):
        def tile(t, _):
            cols = pl.ds(pl.multiple_of(t * TW, TW), TW)
            gh = dot_right(brow[j], fout[cols, :])
            gpre[j, :, cols] = (slope[j, :, cols] * gh).astype(bf16)
            return 0
        lax.fori_loop(0, HID // TW, tile, 0)
        def tile2(t, _):
            cols = pl.ds(pl.multiple_of(t * TW, TW), TW)
            p = dot_right(gpre[j], fin[cols, :])
            if j == 0:
                acc[:, cols] = acc[:, cols] + p + dot_right(ay[0], down[cols, :])
            else:
                part[j, :, cols] = p.astype(bf16)
            return 0
        lax.fori_loop(0, D // TW, tile2, 0)
    leave(0)
    for q in ys: q.wait_recv()
    fw = forward()
    leave(1)
    leave(2)
    for q in fw: q.wait_recv()
    leave(3)
    p1, p2 = collect(1)
    def wtile(t, _):
        cols = pl.ds(pl.multiple_of(t * TW, TW), TW)
        fi[:, cols] = dot_left(rows[...].reshape(4 * T, D), gpre[:, :, cols].reshape(4 * T, TW)).astype(bf16)
        fo[:, cols] = dot_left(hid[...].reshape(4 * T, HID), brow[:, :, cols].reshape(4 * T, TW)).astype(bf16)
        return 0
    lax.fori_loop(0, HID // TW, wtile, 0)
    gather_up(1, p1, p2)
    gsec[...] = acc[...]
    cp.close()

def feed(A, second, cot, fin, fout, down, up, gain, shift):
    T, D = second.shape; HID = fin.shape[1]; AD = down.shape[1]
    v = lambda *s: pltpu.VMEM(s, bf16)
    vf = lambda *s: pltpu.VMEM(s, f32)
    vm = pl.BlockSpec(memory_space=pltpu.VMEM)
    sds = jax.ShapeDtypeStruct
    return pl.pallas_call(
        functools.partial(feed_kernel, A),
        out_shape=(sds((T, D), bf16), sds((T, D), f32), sds((D, HID), bf16), sds((HID, D), bf16), sds((2, T, AD), bf16), sds((T, D), bf16), sds((2, D), f32)),
        in_specs=[vm] * 8, out_specs=(vm,) * 7,
        scratch_shapes=[v(4, T, D), v(4, T, D), v(4, T, HID), vf(4, T, HID), v(4, T, HID), v(4, T, D),
            v(2, T, D), v(2, T, D), v(2, T, D), vf(T, AD), vf(T, D),
            pltpu.SemaphoreType.DMA((64,)), pltpu.SemaphoreType.DMA((64,))],
        compiler_params=pltpu.CompilerParams(collective_id=3, has_side_effects=True, vmem_limit_bytes=60 << 20),
        name="feed_forward")(second, cot, fin, fout, down, up, gain, shift)


def all_add(cp, A, peers, buf, got, zbuf, value):
    a = place()[0]
    core, xp, yp, zp = peers
    for k, p in enumerate((core, xp, yp)):
        buf[k] = value
        q = cp(buf.at[k], got.at[k], p)
        q.wait_recv()
        value = value + got[k]
    zbuf[a] = value
    qs = [cp(zbuf.at[a], zbuf.at[a], zp[j]) for j in range(1, A)]
    for q in qs: q.wait_recv()
    value = zbuf[0]
    for k in range(1, A): value = value + zbuf[k]
    return value

def neighbours(A):
    a, b, x, c = place()
    return device(a, b, x, 1 - c), device(a, b, 1 - x, c), device(a, 1 - b, x, c), [device((a + j) % A, b, x, c) for j in range(A)]

def prefix_kernel(A, part, outer2, norms, tangent, prows, nout, buf, got, zbuf, r0, r1, ssem, rsem):
    a, b, x, c = place()
    peers = neighbours(A)
    core, xp, yp, zp = peers
    greet([core, xp, yp] + zp[1:])
    cp = Copies(ssem, rsem)
    G = norms.shape[0]
    me = ((a * 2 + b) * 2 + x) * 2 + c
    def nrows(start, count): return nout.at[pl.ds(pl.multiple_of(start * G, G), count * G)]
    nout[pl.ds(pl.multiple_of(me * G, G), G), :] = norms[...]
    n0 = cp(nrows(me, 1), nrows(me, 1), core)
    t = jnp.tanh(all_add(cp, A, peers, buf, got, zbuf, part[...]))
    tangent[...] = t
    n0.wait_recv()
    n1 = cp(nrows(me - c, 2), nrows(me - c, 2), xp)
    mine = jnp.dot(t.astype(bf16), outer2[...], preferred_element_type=f32).astype(bf16)
    r0[...] = mine
    q = cp(r0, r1, core)
    q.wait_recv()
    lane = lax.broadcasted_iota(jnp.int32, mine.shape, 1)
    chip = (a * 2 + b) * 2 + x
    def lanes(start, count): return prows.at[:, pl.ds(pl.multiple_of(start * 128, 128), count * 128)]
    prows[:, pl.ds(pl.multiple_of(chip * 128, 128), 128)] = jnp.where((lane // 64) == c, mine.astype(f32), r1[...].astype(f32)).astype(bf16)
    q = cp(lanes(chip, 1), lanes(chip, 1), xp)
    n1.wait_recv()
    n2 = cp(nrows(me - c - 2 * x, 4), nrows(me - c - 2 * x, 4), yp)
    q.wait_recv()
    q = cp(lanes(chip - x, 2), lanes(chip - x, 2), yp)
    n2.wait_recv(); q.wait_recv()
    qs = [cp(lanes(a * 4, 4), lanes(a * 4, 4), zp[j]) for j in range(1, A)] + [cp(nrows(a * 8, 8), nrows(a * 8, 8), zp[j]) for j in range(1, A)]
    for q in qs: q.wait_recv()
    cp.close()

def prefix(A, part, outer2, norms):
    v = lambda *s: pltpu.VMEM(s, bf16)
    vf = lambda *s: pltpu.VMEM(s, f32)
    vm = pl.BlockSpec(memory_space=pltpu.VMEM)
    sds = jax.ShapeDtypeStruct
    S = part.shape; n = A * 4
    return pl.pallas_call(functools.partial(prefix_kernel, A),
        out_shape=(sds(S, f32), sds((S[0], n * 128), bf16), sds((2 * n * norms.shape[0], 128), bf16)),
        in_specs=[vm] * 3, out_specs=(vm,) * 3,
        scratch_shapes=[vf(3, *S), vf(3, *S), vf(A, *S), v(S[0], 128), v(S[0], 128), pltpu.SemaphoreType.DMA((32,)), pltpu.SemaphoreType.DMA((32,))],
        compiler_params=pltpu.CompilerParams(collective_id=4, has_side_effects=True), name="prefix_in")(part, outer2, norms)

def tail_kernel(A, pg, outer2, ng, pown, tgrad, nsum, buf, got, zbuf, nbuf, ngot, nz, w0, w1, w2, w3, s0, s1, s2, c0, ssem, rsem):
    a, b, x, c = place()
    peers = neighbours(A)
    core, xp, yp, zp = peers
    greet([core, xp, yp] + zp[1:])
    cp = Copies(ssem, rsem)
    def lanes(start, count): return pl.ds(pl.multiple_of(start * 128, 128), count * 128)
    qs = [cp(pg.at[:, lanes((a + j) % A * 4, 4)], w0.at[j - 1], zp[j]) for j in range(1, A)]
    nsum[...] = all_add(cp, A, peers, nbuf, ngot, nz, ng[...])
    t = pg[:, lanes(a * 4, 4)]
    for j, q in enumerate(qs):
        q.wait_recv()
        t = t + w0[j]
    s0[...] = t
    q = cp(s0.at[:, lanes((1 - b) * 2, 2)], w1, yp)
    q.wait_recv()
    s1[...] = s0[:, lanes(b * 2, 2)] + w1[...]
    q = cp(s1.at[:, lanes(1 - x, 1)], w2, xp)
    q.wait_recv()
    s2[...] = s1[:, lanes(x, 1)] + w2[...]
    q = cp(s2, w3, core)
    q.wait_recv()
    t = s2[...] + w3[...]
    pown[...] = t
    lane = lax.broadcasted_iota(jnp.int32, t.shape, 1)
    t = jnp.where((lane // 64) == c, t, 0.0)
    p = lax.dot_general(t, outer2[...].astype(f32), (((1,), (1,)), ((), ())), precision=lax.Precision.HIGHEST, preferred_element_type=f32)
    tgrad[...] = all_add(cp, A, peers, buf, got, zbuf, p)
    cp.close()

def tail(A, pg, outer2, ng):
    vf = lambda *s: pltpu.VMEM(s, f32)
    vm = pl.BlockSpec(memory_space=pltpu.VMEM)
    sds = jax.ShapeDtypeStruct
    K = pg.shape[0]; H = outer2.shape[0]; S = (K, H); N = ng.shape
    return pl.pallas_call(functools.partial(tail_kernel, A),
        out_shape=(sds((K, 128), f32), sds(S, f32), sds(N, f32)),
        in_specs=[vm] * 3, out_specs=(vm,) * 3,
        scratch_shapes=[vf(3, *S), vf(3, *S), vf(A, *S), vf(3, *N), vf(3, *N), vf(A, *N), vf(A - 1, K, 512), vf(K, 256), vf(K, 128), vf(K, 128), vf(K, 512), vf(K, 256), vf(K, 128), vf(8, 128), pltpu.SemaphoreType.DMA((32,)), pltpu.SemaphoreType.DMA((32,))],
        compiler_params=pltpu.CompilerParams(collective_id=5, has_side_effects=True), name="prefix_out")(pg, outer2, ng)


NEGATIVE = -1000000000.0
PADDED = 32

def project(x, weight, out, tile=256):
    def step(t, _):
        cols = pl.ds(pl.multiple_of(t * tile, tile), tile)
        out[:, cols] = dot(x[...], weight[:, cols]).astype(out.dtype)
        return 0
    lax.fori_loop(0, out.shape[1] // tile, step, 0)

def project_back(x, weight, out, tile=256):
    def step(t, _):
        cols = pl.ds(pl.multiple_of(t * tile, tile), tile)
        out[:, cols] = dot_right(x[...], weight[cols, :]).astype(out.dtype)
        return 0
    lax.fori_loop(0, out.shape[1] // tile, step, 0)

def lane_half(rows):
    return lax.broadcasted_iota(jnp.int32, (rows, 128), 1) < 64

def split_heads(v):
    low = lane_half(v.shape[0])
    zero = jnp.zeros_like(v)
    return jnp.where(low, v, zero), jnp.where(low, zero, v)

def self_mask(seg_col, seg_row):
    T = seg_col.shape[0]
    row = lax.broadcasted_iota(jnp.int32, (T, T), 0)
    col = lax.broadcasted_iota(jnp.int32, (T, T), 1)
    own = jnp.where((row >= col) & (seg_col[...] == seg_row[...]), 0.0, NEGATIVE)
    lane = lax.broadcasted_iota(jnp.int32, (T, PADDED), 1)
    return jnp.concatenate([own, jnp.where(lane < 30, 0.0, NEGATIVE)], axis=1)

def attend(q, keys, values, penalty, probs, out, pairs=8):
    def step(p, _):
        cols = pl.ds(pl.multiple_of(p * 128, 128), 128)
        kk, vv = keys(cols), values(cols)
        qs = split_heads(q[:, cols])
        vs = split_heads(vv)
        total = None
        for s in range(2):
            score = jnp.where(penalty[...] < -1.0, NEGATIVE, dot_right(qs[s], kk) * 0.125)
            e = jnp.exp(score - jnp.max(score, axis=-1, keepdims=True))
            prob = (e * (1.0 / jnp.sum(e, axis=-1, keepdims=True))).astype(bf16)
            probs[2 * p + s] = prob
            mixed = dot(prob, vs[s])
            total = mixed if total is None else total + mixed
        out[:, cols] = total.astype(bf16)
        return 0
    lax.fori_loop(0, pairs, step, 0)

def attend_back(grad, q, keys, values, probs, emit, pairs=8):
    def step(p, _):
        cols = pl.ds(pl.multiple_of(p * 128, 128), 128)
        kk, vv = keys(cols), values(cols)
        qs = split_heads(q[:, cols])
        ks = split_heads(kk)
        gs = split_heads(grad[:, cols])
        dq = dk = dv = None
        for s in range(2):
            low = probs[2 * p + s]
            prob = low.astype(f32)
            t = prob * dot_right(gs[s], vv)
            ds = (t - prob * jnp.sum(t, axis=-1, keepdims=True)).astype(bf16)
            a, b, c = dot(ds, ks[s]), dot_left(ds, qs[s]), dot_left(low, gs[s])
            dq, dk, dv = (a, b, c) if dq is None else (dq + a, dk + b, dv + c)
        emit(cols, dq * 0.125, dk * 0.125, dv)
        return 0
    lax.fori_loop(0, pairs, step, 0)

def both_keys(own, prows, offset):
    def get(cols):
        shifted = pl.ds(pl.multiple_of(cols.start + offset, 128), 128)
        return jnp.concatenate([own[:, cols], prows[:, shifted]], axis=0)
    return get

def whole(ref):
    return lambda cols: ref[:, cols]

def add_norm(base, low, weight, gain, shift, out, normed, inverse, tile=256):
    def step(t, _):
        cols = pl.ds(pl.multiple_of(t * tile, tile), tile)
        out[:, cols] = base[:, cols].astype(f32) + dot(low[...], weight[:, cols])
        return 0
    lax.fori_loop(0, out.shape[1] // tile, step, 0)
    n, i = norm(out[...])
    normed[...] = n
    inverse[...] = i
    out[...] = n * gain + shift

def forward_kernel(inputs, memory, seg_col, seg_row, mem_row, weights, prows, vecs,
                   q, k, v, probs, attended, first, n1, i1, cq, ck, cv, cprobs, crossed, second, n2, i2, pen, cpen):
    width = inputs.shape[1]
    pen[...] = self_mask(seg_col, seg_row)
    cpen[...] = jnp.where(seg_col[...] == mem_row[...], 0.0, NEGATIVE)
    project(inputs, weights.at[0], q); project(inputs, weights.at[1], k); project(inputs, weights.at[2], v)
    project(memory, weights.at[6], ck); project(memory, weights.at[7], cv)
    attend(q, both_keys(k, prows, 0), both_keys(v, prows, width), pen, probs, attended)
    add_norm(inputs, attended, weights.at[3], vecs[0:1, :], vecs[1:2, :], first, n1, i1)
    q[...] = q[...]
    def step(t, _):
        cols = pl.ds(pl.multiple_of(t * 256, 256), 256)
        cq[:, cols] = dot(first[...].astype(bf16), weights[4, :, cols]).astype(bf16)
        return 0
    lax.fori_loop(0, width // 256, step, 0)
    attend(cq, whole(ck), whole(cv), cpen, cprobs, crossed)
    add_norm(first, crossed, weights.at[5], vecs[2:3, :], vecs[3:4, :], second, n2, i2)

def forward(inputs, memory, seg_col, seg_row, mem_row, weights, prows, vecs):
    T, D = inputs.shape; M = memory.shape[0]
    vm = pl.BlockSpec(memory_space=pltpu.VMEM)
    sds = jax.ShapeDtypeStruct
    row, mrow, full, one = sds((T, D), bf16), sds((M, D), bf16), sds((T, D), f32), sds((T, 1), f32)
    return pl.pallas_call(forward_kernel,
        out_shape=(row, row, row, sds((16, T, T + PADDED), bf16), row, full, full, one, row, mrow, mrow, sds((16, T, M), bf16), row, full, full, one),
        in_specs=[vm] * 8, out_specs=(vm,) * 16,
        scratch_shapes=[pltpu.VMEM((T, T + PADDED), f32), pltpu.VMEM((T, M), f32)],
        compiler_params=pltpu.CompilerParams(vmem_limit_bytes=60 << 20), name="attention_forward")(
            inputs, memory, seg_col, seg_row, mem_row, weights, prows, vecs)

def norm_back_into(e, n, i, gain, out, ngrad, at):
    ee = e[...]
    nn = n[...]
    out[...] = norm_back(ee, nn, i[...], gain)
    ngrad[at:at + 1, :] = jnp.sum(ee * nn, axis=0, keepdims=True)
    ngrad[at + 1:at + 2, :] = jnp.sum(ee, axis=0, keepdims=True)

def backward_kernel(gsec, q, k, v, probs, n1, i1, cq, ck, cv, cprobs, n2, i2, weights, prows, vecs,
                    igrad, mgrad, dq, dk, dv, start_low, dcq, dck, dcv, mid_low, pgrad, ngrad, gmid, gfirst, og):
    T, D = gsec.shape
    norm_back_into(gsec, n2, i2, vecs[2:3, :], gmid, ngrad, 2)
    mid_low[...] = gmid[...].astype(bf16)
    project_back(mid_low, weights.at[5], og)
    def emit(cols, a, b, c):
        dcq[:, cols] = a.astype(bf16)
        dck[:, cols] = b.astype(bf16)
        dcv[:, cols] = c.astype(bf16)
    attend_back(og, cq, whole(ck), whole(cv), cprobs, emit)
    def step(t, _):
        cols = pl.ds(pl.multiple_of(t * 256, 256), 256)
        gfirst[:, cols] = gmid[:, cols] + dot_right(dcq[...], weights[4, cols, :])
        return 0
    lax.fori_loop(0, D // 256, step, 0)
    norm_back_into(gfirst, n1, i1, vecs[0:1, :], gmid, ngrad, 0)
    start_low[...] = gmid[...].astype(bf16)
    project_back(start_low, weights.at[3], og)
    def emit2(cols, a, b, c):
        dq[:, cols] = a.astype(bf16)
        dk[:, cols] = b[:T].astype(bf16)
        dv[:, cols] = c[:T].astype(bf16)
        pgrad[:, cols] = b[T:]
        pgrad[:, pl.ds(pl.multiple_of(cols.start + D, 128), 128)] = c[T:]
    attend_back(og, q, both_keys(k, prows, 0), both_keys(v, prows, D), probs, emit2)
    def step2(t, _):
        cols = pl.ds(pl.multiple_of(t * 256, 256), 256)
        s = gmid[:, cols] + dot_right(dq[...], weights[0, cols, :]) + dot_right(dk[...], weights[1, cols, :]) + dot_right(dv[...], weights[2, cols, :])
        igrad[:, cols] = s.astype(bf16)
        mgrad[:, cols] = (dot_right(dck[...], weights[6, cols, :]) + dot_right(dcv[...], weights[7, cols, :])).astype(bf16)
        return 0
    lax.fori_loop(0, D // 256, step2, 0)

def backward(gsec, q, k, v, probs, n1, i1, cq, ck, cv, cprobs, n2, i2, weights, prows, vecs):
    T, D = gsec.shape; M = ck.shape[0]
    vm = pl.BlockSpec(memory_space=pltpu.VMEM)
    sds = jax.ShapeDtypeStruct
    row, mrow = sds((T, D), bf16), sds((M, D), bf16)
    return pl.pallas_call(backward_kernel,
        out_shape=(row, mrow, row, row, row, row, row, mrow, mrow, row, sds((PADDED, 2 * D), f32), sds((8, D), f32)),
        in_specs=[vm] * 16, out_specs=(vm,) * 12,
        scratch_shapes=[pltpu.VMEM((T, D), f32), pltpu.VMEM((T, D), f32), pltpu.VMEM((T, D), bf16)],
        compiler_params=pltpu.CompilerParams(vmem_limit_bytes=60 << 20), name="attention_backward")(
            gsec, q, k, v, probs, n1, i1, cq, ck, cv, cprobs, n2, i2, weights, prows, vecs)

def fast_body(A, inputs, memory, cotangent, segments, memory_segments, query_self, key_self, value_self, output_self,
              query_cross, key_cross, value_cross, output_cross, self_gain, self_shift, cross_gain, cross_shift,
              final_gain, final_shift, feed_in, feed_out, adapter_down, adapter_up, prefix_embed, prefix_inner, prefix_outer):
    r = query_self.shape[0]
    length, width = inputs.shape
    w, n = lax.axis_index(WIDE), lax.axis_index(NARROW)
    part = jnp.pad(matmul(prefix_embed, prefix_inner), ((0, 2), (0, 0)))
    norms = jnp.pad(jnp.stack([self_gain, self_shift, cross_gain, cross_shift, final_gain, final_shift]), ((0, 10), (0, 128 - r)))
    outer2 = jnp.concatenate([prefix_outer, prefix_outer], axis=1)
    tangent, prefix_rows, nblocks = prefix(A, part, outer2, norms)
    vecs = nblocks.reshape(-1, 16, 128)[:, :8, :r].transpose(1, 0, 2).reshape(8, width).astype(f32)
    weights, fin2, fout2, down4, up4 = gather(A, jnp.stack([query_self, key_self, value_self, output_self, query_cross, output_cross, key_cross, value_cross]),
        feed_in, feed_out, adapter_down, adapter_up)
    q, k, v, probs, attended, first, n1, i1, cq, ck, cv, cprobs, crossed, second, n2, i2 = forward(
        inputs, memory, segments.reshape(-1, 1), segments.reshape(1, -1), memory_segments.reshape(1, -1), weights, prefix_rows, vecs)
    result, grad_second, fi, fo, ay, branch_low, ngrad3 = feed(A, second, cotangent, fin2, fout2, down4, up4, vecs[4:5], vecs[5:6])
    inputs_grad, memory_grad, dq, dk, dv, start_low, dcq, dck, dcv, mid_low, pgrad, ngrad = backward(
        grad_second, q, k, v, probs, n1, i1, cq, ck, cv, cprobs, n2, i2, weights, prefix_rows, vecs)
    ng = jnp.concatenate([ngrad[:4], ngrad3, jnp.zeros((2, width), jnp.float32)])
    pown, tgrad, nsum = tail(A, pgrad, outer2, ng)
    xs = jnp.stack([inputs, inputs, inputs, attended, first.astype(bf16), crossed])
    ys = jnp.stack([dq, dk, dv, start_low, dcq, mid_low])
    sums, adapt, fi_sum, fo_sum = reduce_grads(A, r, xs, ys, memory, jnp.stack([dck, dcv]),
        jnp.stack([second.astype(jnp.bfloat16), branch_low]), ay, fi, fo)
    return (result, inputs_grad, memory_grad) + finish_outputs(
        sums, adapt, fi_sum, fo_sum, pown, tgrad, nsum, tangent, prefix_embed, prefix_inner, r, w, n)

def finish_outputs(sums, adapt, fi_sum, fo_sum, pown, tgrad, nsum, tangent, prefix_embed, prefix_inner, r, w, n):
    mine = lax.dynamic_slice_in_dim(pown[:PREFIX], (n % 2) * 64, 64, 1)
    tangent = tangent[:PREFIX]
    tangent_grad = tgrad[:PREFIX] * (1.0 - tangent * tangent)
    outer_grad = exact_left(tangent.astype(jnp.bfloat16).astype(jnp.float32), mine)
    inner_grad = exact_left(prefix_embed.astype(jnp.float32), tangent_grad)
    embed_grad = exact_right(tangent_grad, prefix_inner.astype(jnp.float32))
    norm_grads = lax.dynamic_slice_in_dim(nsum, (w * 4 + n) * r, r, 1)
    return (
        sums[0], sums[1], sums[2], sums[3], sums[4], sums[6], sums[7], sums[5],
        norm_grads[0], norm_grads[1], norm_grads[2], norm_grads[3], norm_grads[4], norm_grads[5],
        fi_sum, fo_sum, adapt[0], adapt[1].T, embed_grad, inner_grad, outer_grad,
    )

def solution(mesh):
    wide, narrow = mesh.shape[WIDE], mesh.shape[NARROW]
    fits = narrow == 4 and wide == 8
    body = functools.partial(fast_body, wide // 2) if fits else plain_body
    return jax.shard_map(
        body,
        mesh=mesh,
        in_specs=(
            P(BOTH, None),
            P(BOTH, None),
            P(BOTH, None),
            P(BOTH),
            P(BOTH),
            P(BOTH, None),
            P(BOTH, None),
            P(BOTH, None),
            P(BOTH, None),
            P(BOTH, None),
            P(BOTH, None),
            P(BOTH, None),
            P(BOTH, None),
            P(BOTH),
            P(BOTH),
            P(BOTH),
            P(BOTH),
            P(BOTH),
            P(BOTH),
            P(None, WIDE),
            P(WIDE, None),
            P(None, NARROW),
            P(NARROW, None),
            P(None, BOTH),
            P(BOTH, None),
            P(None, BOTH),
        ),
        out_specs=(
            P(BOTH, None),
            P(BOTH, None),
            P(BOTH, None),
            P(BOTH, None),
            P(BOTH, None),
            P(BOTH, None),
            P(BOTH, None),
            P(BOTH, None),
            P(BOTH, None),
            P(BOTH, None),
            P(BOTH, None),
            P(BOTH),
            P(BOTH),
            P(BOTH),
            P(BOTH),
            P(BOTH),
            P(BOTH),
            P(NARROW, WIDE),
            P(WIDE, NARROW),
            P(WIDE, NARROW),
            P(NARROW, WIDE),
            P(None, BOTH),
            P(BOTH, None),
            P(None, BOTH),
        ),
        check_vma=False,
    )
```

```python
import functools
from functools import reduce

import jax
import jax.numpy as jnp
from jax import lax
from jax.experimental import pallas as pl
from jax.experimental.pallas import tpu as pltpu
from jax.sharding import PartitionSpec as P

MESH = pl.DeviceIdType.MESH
bf16, f32 = jnp.bfloat16, jnp.float32
WIDE, NARROW = "wide", "narrow"
BOTH = (WIDE, NARROW)


HEADS = 16
HEAD = 64
PREFIX = 30


HIGHEST = lax.Precision.HIGHEST
EPSILON = 1e-05
MASKED = -1000000000.0
ADAPT_SCALE = 4.0


def matmul(left, right):
    return jnp.dot(left, right, preferred_element_type=jnp.float32)


def left_product(left, right):
    return lax.dot_general(
        left, right, (((0,), (0,)), ((), ())), preferred_element_type=jnp.float32
    )


def right_product(left, right):
    return lax.dot_general(
        left, right, (((1,), (1,)), ((), ())), preferred_element_type=jnp.float32
    )


def exact_left(left, right):
    return lax.dot_general(
        left, right, (((0,), (0,)), ((), ())), precision=HIGHEST, preferred_element_type=jnp.float32
    )


def exact_right(left, right):
    return lax.dot_general(
        left, right, (((1,), (1,)), ((), ())), precision=HIGHEST, preferred_element_type=jnp.float32
    )


def norm_forward(values, factor, offset):
    average = jnp.mean(values, axis=-1, keepdims=True)
    center = values - average
    inverse = lax.rsqrt(jnp.mean(center * center, axis=-1, keepdims=True) + EPSILON)
    normed = center * inverse
    return (normed * factor + offset, normed, inverse)


def norm_backward(grad_out, normed, inverse, factor):
    scaled = grad_out * factor
    grad_in = inverse * (
        scaled
        - jnp.mean(scaled, axis=-1, keepdims=True)
        - normed * jnp.mean(scaled * normed, axis=-1, keepdims=True)
    )
    return (grad_in, jnp.sum(grad_out * normed, axis=0), jnp.sum(grad_out, axis=0))


def head_view(rows):
    return rows.reshape(rows.shape[0], HEADS, HEAD)


def scored(queries, key_rows, allowed):
    raw = jnp.einsum(
        "shd,khd->hsk", head_view(queries), head_view(key_rows), preferred_element_type=jnp.float32
    )
    return jnp.where(allowed[None], raw * HEAD ** (-0.5), MASKED)


def attend_forward(queries, parts):
    scores = [scored(queries, member[0], member[2]) for member in parts]
    largest = reduce(jnp.maximum, [jnp.max(matrix, axis=-1, keepdims=True) for matrix in scores])
    total = reduce(
        jnp.add, [jnp.sum(jnp.exp(matrix - largest), axis=-1, keepdims=True) for matrix in scores]
    )
    logsum = largest + jnp.log(total)
    mixed = reduce(
        jnp.add,
        [
            jnp.einsum(
                "hsk,khd->shd",
                jnp.exp(matrix - logsum).astype(jnp.bfloat16),
                head_view(member[1]),
                preferred_element_type=jnp.float32,
            )
            for matrix, member in zip(scores, parts)
        ],
    )
    return (mixed.reshape(queries.shape[0], HEADS * HEAD), logsum)


def attend_backward(queries, parts, logsum, grad_low):
    grad_heads = head_view(grad_low)
    chances = [jnp.exp(scored(queries, member[0], member[2]) - logsum) for member in parts]
    slopes = [
        jnp.einsum(
            "shd,khd->hsk", grad_heads, head_view(member[1]), preferred_element_type=jnp.float32
        )
        for member in parts
    ]
    row_dot = reduce(
        jnp.add,
        [jnp.sum(chance * slope, axis=-1, keepdims=True) for chance, slope in zip(chances, slopes)],
    )
    scale = HEAD ** (-0.5)
    grad_query = jnp.zeros((queries.shape[0], HEADS, HEAD), jnp.float32)
    results = []
    for member, chance, slope in zip(parts, chances, slopes):
        dscore = (chance * (slope - row_dot)).astype(jnp.bfloat16)
        grad_query = grad_query + jnp.einsum(
            "hsk,khd->shd", dscore, head_view(member[0]), preferred_element_type=jnp.float32
        )
        grad_key = (
            jnp.einsum(
                "hsk,shd->khd", dscore, head_view(queries), preferred_element_type=jnp.float32
            )
            * scale
        )
        grad_value = jnp.einsum(
            "hsk,shd->khd",
            chance.astype(jnp.bfloat16),
            grad_heads,
            preferred_element_type=jnp.float32,
        )
        results.append(
            (
                grad_key.reshape(grad_key.shape[0], HEADS * HEAD),
                grad_value.reshape(grad_value.shape[0], HEADS * HEAD),
            )
        )
    return ((grad_query * scale).reshape(queries.shape[0], HEADS * HEAD), results)


def gelu_back(pre_values, grad_values):
    return jax.vjp(lambda inner: jax.nn.gelu(inner, approximate=False), pre_values)[1](grad_values)[
        0
    ]


def plain_body(
    inputs,
    memory,
    cotangent,
    segments,
    memory_segments,
    query_self,
    key_self,
    value_self,
    output_self,
    query_cross,
    key_cross,
    value_cross,
    output_cross,
    self_gain,
    self_shift,
    cross_gain,
    cross_shift,
    final_gain,
    final_shift,
    feed_in,
    feed_out,
    adapter_down,
    adapter_up,
    prefix_embed,
    prefix_inner,
    prefix_outer,
):
    (
        query_one,
        key_one,
        value_one,
        output_one,
        query_two,
        key_two,
        value_two,
        output_two,
        gain_one,
        shift_one,
        gain_two,
        shift_two,
        gain_three,
        shift_three,
        embed_full,
        inner_full,
        outer_full,
    ) = (
        lax.all_gather(query_self, BOTH, axis=0, tiled=True),
        lax.all_gather(key_self, BOTH, axis=0, tiled=True),
        lax.all_gather(value_self, BOTH, axis=0, tiled=True),
        lax.all_gather(output_self, BOTH, axis=0, tiled=True),
        lax.all_gather(query_cross, BOTH, axis=0, tiled=True),
        lax.all_gather(key_cross, BOTH, axis=0, tiled=True),
        lax.all_gather(value_cross, BOTH, axis=0, tiled=True),
        lax.all_gather(output_cross, BOTH, axis=0, tiled=True),
        lax.all_gather(self_gain, BOTH, axis=0, tiled=True),
        lax.all_gather(self_shift, BOTH, axis=0, tiled=True),
        lax.all_gather(cross_gain, BOTH, axis=0, tiled=True),
        lax.all_gather(cross_shift, BOTH, axis=0, tiled=True),
        lax.all_gather(final_gain, BOTH, axis=0, tiled=True),
        lax.all_gather(final_shift, BOTH, axis=0, tiled=True),
        lax.all_gather(prefix_embed, BOTH, axis=1, tiled=True),
        lax.all_gather(prefix_inner, BOTH, axis=0, tiled=True),
        lax.all_gather(prefix_outer, BOTH, axis=1, tiled=True),
    )
    factor_one = gain_one.astype(jnp.float32)
    factor_two = gain_two.astype(jnp.float32)
    factor_three = gain_three.astype(jnp.float32)
    length = inputs.shape[0]
    width = inputs.shape[1]
    places = jnp.arange(length)
    causal = places[:, None] >= places[None, :]
    local_mask = (segments[:, None] == segments[None, :]) & causal
    prefix_mask = jnp.ones((length, PREFIX), jnp.bool_)
    cross_mask = segments[:, None] == memory_segments[None, :]
    tangent = jnp.tanh(matmul(embed_full, inner_full))
    tangent_low = tangent.astype(jnp.bfloat16)
    prefix_rows = matmul(tangent_low, outer_full).astype(jnp.bfloat16)
    prefix_keys = prefix_rows[:, :width]
    prefix_values = prefix_rows[:, width:]
    queries = matmul(inputs, query_one).astype(jnp.bfloat16)
    key_rows = matmul(inputs, key_one).astype(jnp.bfloat16)
    value_rows = matmul(inputs, value_one).astype(jnp.bfloat16)
    self_parts = ((prefix_keys, prefix_values, prefix_mask), (key_rows, value_rows, local_mask))
    attended, self_logsum = attend_forward(queries, self_parts)
    attended_low = attended.astype(jnp.bfloat16)
    first, normed_one, inverse_one = norm_forward(
        inputs.astype(jnp.float32) + matmul(attended_low, output_one),
        factor_one,
        shift_one.astype(jnp.float32),
    )
    first_low = first.astype(jnp.bfloat16)
    cross_queries = matmul(first_low, query_two).astype(jnp.bfloat16)
    cross_keys = matmul(memory, key_two).astype(jnp.bfloat16)
    cross_values = matmul(memory, value_two).astype(jnp.bfloat16)
    cross_parts = ((cross_keys, cross_values, cross_mask),)
    crossed, cross_logsum = attend_forward(cross_queries, cross_parts)
    crossed_low = crossed.astype(jnp.bfloat16)
    second, normed_two, inverse_two = norm_forward(
        first + matmul(crossed_low, output_two), factor_two, shift_two.astype(jnp.float32)
    )
    second_low = second.astype(jnp.bfloat16)
    feed_rows = lax.all_gather(second_low, WIDE, axis=0, tiled=True)
    hidden_pre = matmul(feed_rows, feed_in)
    hidden_low = jax.nn.gelu(hidden_pre, approximate=False).astype(jnp.bfloat16)
    feed_sum = lax.psum_scatter(
        matmul(hidden_low, feed_out), WIDE, scatter_dimension=0, tiled=True
    )
    adapt_rows = lax.all_gather(second_low, NARROW, axis=0, tiled=True)
    bottle_pre = matmul(adapt_rows, adapter_down)
    bottle_low = jax.nn.gelu(bottle_pre, approximate=False).astype(jnp.bfloat16)
    adapt_sum = lax.psum_scatter(
        matmul(bottle_low, adapter_up).astype(jnp.bfloat16),
        NARROW,
        scatter_dimension=0,
        tiled=True,
    ).astype(jnp.float32)
    branch = feed_sum + ADAPT_SCALE * adapt_sum
    result, normed_three, inverse_three = norm_forward(
        second + branch, factor_three, shift_three.astype(jnp.float32)
    )
    grad_branch, gain_three_grad, shift_three_grad = norm_backward(
        cotangent.astype(jnp.float32), normed_three, inverse_three, factor_three
    )
    branch_low = grad_branch.astype(jnp.bfloat16)
    branch_rows = lax.all_gather(branch_low, WIDE, axis=0, tiled=True)
    grad_hidden = right_product(branch_rows, feed_out)
    grad_pre = gelu_back(hidden_pre, grad_hidden).astype(jnp.bfloat16)
    grad_out_part = left_product(hidden_low, branch_rows)
    grad_in_part = left_product(feed_rows, grad_pre)
    grad_feed = lax.psum_scatter(
        right_product(grad_pre, feed_in), WIDE, scatter_dimension=0, tiled=True
    )
    feed_in_total, feed_out_total = (
        lax.psum_scatter(
            grad_in_part.astype(jnp.bfloat16), NARROW, scatter_dimension=0, tiled=True
        ).astype(jnp.float32),
        lax.psum_scatter(
            grad_out_part.astype(jnp.bfloat16), NARROW, scatter_dimension=1, tiled=True
        ).astype(jnp.float32),
    )
    branch_narrow = lax.all_gather(branch_low, NARROW, axis=0, tiled=True)
    grad_bottle = ADAPT_SCALE * right_product(branch_narrow, adapter_up)
    grad_bottle_pre = gelu_back(bottle_pre, grad_bottle).astype(jnp.bfloat16)
    grad_up_part = ADAPT_SCALE * left_product(bottle_low, branch_narrow)
    grad_down_part = left_product(adapt_rows, grad_bottle_pre)
    grad_adapt = lax.psum_scatter(
        right_product(grad_bottle_pre, adapter_down).astype(jnp.bfloat16),
        NARROW,
        scatter_dimension=0,
        tiled=True,
    ).astype(jnp.float32)
    down_total, up_total = (
        lax.psum_scatter(grad_down_part, WIDE, scatter_dimension=0, tiled=True),
        lax.psum_scatter(grad_up_part, WIDE, scatter_dimension=1, tiled=True),
    )
    grad_second = grad_branch + grad_feed + grad_adapt
    grad_mid, gain_two_grad, shift_two_grad = norm_backward(
        grad_second, normed_two, inverse_two, factor_two
    )
    mid_low = grad_mid.astype(jnp.bfloat16)
    output_two_grad = left_product(crossed_low, mid_low)
    crossed_grad = right_product(mid_low, output_two).astype(jnp.bfloat16)
    cross_query_grad, cross_results = attend_backward(
        cross_queries, cross_parts, cross_logsum, crossed_grad
    )
    cross_query_low = cross_query_grad.astype(jnp.bfloat16)
    cross_key_low = cross_results[0][0].astype(jnp.bfloat16)
    cross_value_low = cross_results[0][1].astype(jnp.bfloat16)
    query_two_grad = left_product(first_low, cross_query_low)
    key_two_grad = left_product(memory, cross_key_low)
    value_two_grad = left_product(memory, cross_value_low)
    memory_grad = (
        right_product(cross_key_low, key_two) + right_product(cross_value_low, value_two)
    ).astype(jnp.bfloat16)
    grad_first = grad_mid + right_product(cross_query_low, query_two)
    grad_start, gain_one_grad, shift_one_grad = norm_backward(
        grad_first, normed_one, inverse_one, factor_one
    )
    start_low = grad_start.astype(jnp.bfloat16)
    output_one_grad = left_product(attended_low, start_low)
    attended_grad = right_product(start_low, output_one).astype(jnp.bfloat16)
    self_query_grad, self_results = attend_backward(queries, self_parts, self_logsum, attended_grad)
    self_query_low = self_query_grad.astype(jnp.bfloat16)
    self_key_low = self_results[1][0].astype(jnp.bfloat16)
    self_value_low = self_results[1][1].astype(jnp.bfloat16)
    query_one_grad = left_product(inputs, self_query_low)
    key_one_grad = left_product(inputs, self_key_low)
    value_one_grad = left_product(inputs, self_value_low)
    inputs_grad = (
        grad_start
        + right_product(self_query_low, query_one)
        + right_product(self_key_low, key_one)
        + right_product(self_value_low, value_one)
    ).astype(jnp.bfloat16)
    prefix_grad = jnp.concatenate([self_results[0][0], self_results[0][1]], axis=1)
    outer_grad = exact_left(tangent_low.astype(jnp.float32), prefix_grad)
    tangent_grad = exact_right(prefix_grad, outer_full.astype(jnp.float32)) * (
        1.0 - tangent * tangent
    )
    inner_grad = exact_left(embed_full.astype(jnp.float32), tangent_grad)
    embed_grad = exact_right(tangent_grad, inner_full.astype(jnp.float32))
    (
        query_one_sum,
        key_one_sum,
        value_one_sum,
        output_one_sum,
        query_two_sum,
        key_two_sum,
        value_two_sum,
        output_two_sum,
        gain_one_sum,
        shift_one_sum,
        gain_two_sum,
        shift_two_sum,
        gain_three_sum,
        shift_three_sum,
        embed_sum,
        inner_sum,
        outer_sum,
    ) = (
        lax.psum_scatter(query_one_grad, BOTH, scatter_dimension=0, tiled=True),
        lax.psum_scatter(key_one_grad, BOTH, scatter_dimension=0, tiled=True),
        lax.psum_scatter(value_one_grad, BOTH, scatter_dimension=0, tiled=True),
        lax.psum_scatter(output_one_grad, BOTH, scatter_dimension=0, tiled=True),
        lax.psum_scatter(query_two_grad, BOTH, scatter_dimension=0, tiled=True),
        lax.psum_scatter(key_two_grad, BOTH, scatter_dimension=0, tiled=True),
        lax.psum_scatter(value_two_grad, BOTH, scatter_dimension=0, tiled=True),
        lax.psum_scatter(output_two_grad, BOTH, scatter_dimension=0, tiled=True),
        lax.psum_scatter(gain_one_grad, BOTH, scatter_dimension=0, tiled=True),
        lax.psum_scatter(shift_one_grad, BOTH, scatter_dimension=0, tiled=True),
        lax.psum_scatter(gain_two_grad, BOTH, scatter_dimension=0, tiled=True),
        lax.psum_scatter(shift_two_grad, BOTH, scatter_dimension=0, tiled=True),
        lax.psum_scatter(gain_three_grad, BOTH, scatter_dimension=0, tiled=True),
        lax.psum_scatter(shift_three_grad, BOTH, scatter_dimension=0, tiled=True),
        lax.psum_scatter(embed_grad, BOTH, scatter_dimension=1, tiled=True),
        lax.psum_scatter(inner_grad, BOTH, scatter_dimension=0, tiled=True),
        lax.psum_scatter(outer_grad, BOTH, scatter_dimension=1, tiled=True),
    )
    return (
        result.astype(jnp.bfloat16),
        inputs_grad,
        memory_grad,
        query_one_sum,
        key_one_sum,
        value_one_sum,
        output_one_sum,
        query_two_sum,
        key_two_sum,
        value_two_sum,
        output_two_sum,
        gain_one_sum,
        shift_one_sum,
        gain_two_sum,
        shift_two_sum,
        gain_three_sum,
        shift_three_sum,
        feed_in_total,
        feed_out_total,
        down_total,
        up_total,
        embed_sum,
        inner_sum,
        outer_sum,
    )


def place():
    w = lax.axis_index(WIDE); n = lax.axis_index(NARROW)
    return w // 2, w % 2, n // 2, n % 2

def device(a, b, x, c):
    return (a * 2 + b, x * 2 + c)

def greet(peers):
    barrier = pltpu.get_barrier_semaphore()
    for p in peers:
        pl.semaphore_signal(barrier, inc=1, device_id=p, device_id_type=MESH)
    pl.semaphore_wait(barrier, len(peers))

def remote(src, dst, send, recv, dev):
    return pltpu.make_async_remote_copy(src_ref=src, dst_ref=dst, send_sem=send, recv_sem=recv, device_id=dev, device_id_type=MESH)


def dot_left(l, r):
    return lax.dot_general(l, r, (((0,), (0,)), ((), ())), preferred_element_type=f32)

class Copies:
    def __init__(self, send, recv):
        self.send, self.recv, self.count, self.all = send, recv, 0, []
    def __call__(self, src, dst, dev):
        cp = remote(src, dst, self.send.at[self.count], self.recv.at[self.count], dev)
        self.count += 1
        cp.start(); self.all.append(cp)
        return cp
    def local(self, src, dst):
        cp = pltpu.make_async_copy(src, dst, self.send.at[self.count])
        self.count += 1
        cp.start()
        return cp
    def sent(self, some):
        for cp in some:
            cp.wait_send()
            self.all = [o for o in self.all if o is not cp]
    def close(self):
        for cp in self.all: cp.wait_send()


EPSILON = 1e-05
ADAPT_SCALE = 4.0

def dot(l, r):
    return jnp.dot(l, r, preferred_element_type=f32)

def dot_right(l, r):
    return lax.dot_general(l, r, (((1,), (1,)), ((), ())), preferred_element_type=f32)

def gelu_both(v):
    phi = 0.5 + 0.5 * lax.erf(v * 0.7071067811865476)
    return v * phi, phi + v * (0.3989422804014327 * jnp.exp(-0.5 * v * v))

def norm(v):
    center = v - jnp.mean(v, axis=-1, keepdims=True)
    inverse = lax.rsqrt(jnp.mean(center * center, axis=-1, keepdims=True) + EPSILON)
    return center * inverse, inverse

def norm_back(e, n, inverse, factor):
    s = e * factor
    return inverse * (s - jnp.mean(s, axis=-1, keepdims=True) - n * jnp.mean(s * n, axis=-1, keepdims=True))

def feed_kernel(A, second, cot, fin, fout, down, up, gain, shift, result, gsec, fi, fo, ay, blow, ngrad,
                rows, brow, hid, slope, gpre, part, q1, q2, q3, bslope, acc, ssem, rsem):
    a, b, x, c = place()
    yp = device(a, 1 - b, x, c)
    zp = device((a + A // 2) % A, b, x, c)
    greet([yp, zp])
    cp = Copies(ssem, rsem)
    T, D = second.shape
    NC = 2
    R = T // NC
    HID = fin.shape[1]; TW = 256

    def spread(buf):
        zs, ys = [], []
        for q in range(NC):
            s = pl.ds(q * R, R)
            zs.append(cp(buf.at[0, s], buf.at[2, s], zp))
            ys.append(cp(buf.at[0, s], buf.at[1, s], yp))
        def forward():
            f = []
            for q in range(NC):
                s = pl.ds(q * R, R)
                zs[q].wait_recv()
                f.append(cp(buf.at[2, s], buf.at[3, s], yp))
            return f
        return zs, ys, forward

    p3_sent = []
    def collect(level):
        p3, p1 = [], []
        for q in range(NC):
            p3.append(cp(part.at[3, pl.ds(q * R, R)], q3.at[level, pl.ds(q * R, R)], yp))
        for q in range(NC):
            p1.append(cp(part.at[1, pl.ds(q * R, R)], q1.at[level, pl.ds(q * R, R)], yp))
        p2 = []
        for q in range(NC):
            s = pl.ds(q * R, R)
            p3[q].wait_recv()
            part[2, s] = part[2, s] + q3[level, s]
            p2.append(cp(part.at[2, s], q2.at[level, s], zp))
        p3_sent.append(p3)
        return p1, p2

    def gather_up(level, p1, p2):
        for q in range(NC):
            s = pl.ds(q * R, R)
            p1[q].wait_recv(); p2[q].wait_recv()
            acc[s] = acc[s] + q1[level, s].astype(f32) + q2[level, s].astype(f32)
        cp.sent(p1 + p2 + p3_sent.pop())

    rows[0] = second[...].astype(bf16)
    zs, ys, forward = spread(rows)
    for t in range(2):
        cols = pl.ds(t * 256, 256)
        g, s = gelu_both(dot(rows[0], down[:, cols]))
        ay[1, :, cols] = (ADAPT_SCALE * g.astype(bf16).astype(f32)).astype(bf16)
        bslope[:, cols] = s
    def enter(j):
        def tile(t, _):
            cols = pl.ds(pl.multiple_of(t * TW, TW), TW)
            g, s = gelu_both(dot(rows[j], fin[:, cols]))
            hid[j, :, cols] = g.astype(bf16)
            slope[j, :, cols] = s
            return 0
        lax.fori_loop(0, HID // TW, tile, 0)
        def tile2(t, _):
            cols = pl.ds(pl.multiple_of(t * TW, TW), TW)
            p = dot(hid[j], fout[:, cols])
            if j == 0:
                acc[:, cols] = p + dot(ay[1], up[:, cols])
            else:
                part[j, :, cols] = p.astype(bf16)
            return 0
        lax.fori_loop(0, D // TW, tile2, 0)
    enter(0)
    for q in ys: q.wait_recv()
    fw = forward()
    enter(1)
    enter(2)
    for q in fw: q.wait_recv()
    enter(3)
    p1, p2 = collect(0)
    gather_up(0, p1, p2)
    n3, inv3 = norm(second[...] + acc[...])
    fac = gain[...].astype(f32)
    result[...] = (n3 * fac + shift[...].astype(f32)).astype(bf16)
    e = cot[...].astype(f32)
    gb = norm_back(e, n3, inv3, fac)
    gbl = gb.astype(bf16)
    brow[0] = gbl
    zs, ys, forward = spread(brow)
    blow[...] = gbl
    acc[...] = gb
    ngrad[0:1, :] = jnp.sum(e * n3, axis=0, keepdims=True)
    ngrad[1:2, :] = jnp.sum(e, axis=0, keepdims=True)
    def adapt_tile(t, _):
        cols = pl.ds(pl.multiple_of(t * 256, 256), 256)
        gbot = bslope[:, cols] * (ADAPT_SCALE * dot_right(brow[0], up[cols, :]))
        ay[0, :, cols] = gbot.astype(bf16)
        return 0
    lax.fori_loop(0, down.shape[1] // 256, adapt_tile, 0)
    def leave(j):
        def tile(t, _):
            cols = pl.ds(pl.multiple_of(t * TW, TW), TW)
            gh = dot_right(brow[j], fout[cols, :])
            gpre[j, :, cols] = (slope[j, :, cols] * gh).astype(bf16)
            return 0
        lax.fori_loop(0, HID // TW, tile, 0)
        def tile2(t, _):
            cols = pl.ds(pl.multiple_of(t * TW, TW), TW)
            p = dot_right(gpre[j], fin[cols, :])
            if j == 0:
                acc[:, cols] = acc[:, cols] + p + dot_right(ay[0], down[cols, :])
            else:
                part[j, :, cols] = p.astype(bf16)
            return 0
        lax.fori_loop(0, D // TW, tile2, 0)
    leave(0)
    for q in ys: q.wait_recv()
    fw = forward()
    leave(1)
    leave(2)
    for q in fw: q.wait_recv()
    leave(3)
    p1, p2 = collect(1)
    def wtile(t, _):
        cols = pl.ds(pl.multiple_of(t * TW, TW), TW)
        fi[:, cols] = dot_left(rows[...].reshape(4 * T, D), gpre[:, :, cols].reshape(4 * T, TW)).astype(bf16)
        fo[:, cols] = dot_left(hid[...].reshape(4 * T, HID), brow[:, :, cols].reshape(4 * T, TW)).astype(bf16)
        return 0
    lax.fori_loop(0, HID // TW, wtile, 0)
    gather_up(1, p1, p2)
    gsec[...] = acc[...]
    cp.close()

def feed(A, second, cot, fin, fout, down, up, gain, shift):
    T, D = second.shape; HID = fin.shape[1]; AD = down.shape[1]
    v = lambda *s: pltpu.VMEM(s, bf16)
    vf = lambda *s: pltpu.VMEM(s, f32)
    vm = pl.BlockSpec(memory_space=pltpu.VMEM)
    sds = jax.ShapeDtypeStruct
    return pl.pallas_call(
        functools.partial(feed_kernel, A),
        out_shape=(sds((T, D), bf16), sds((T, D), f32), sds((D, HID), bf16), sds((HID, D), bf16), sds((2, T, AD), bf16), sds((T, D), bf16), sds((2, D), f32)),
        in_specs=[vm] * 8, out_specs=(vm,) * 7,
        scratch_shapes=[v(4, T, D), v(4, T, D), v(4, T, HID), vf(4, T, HID), v(4, T, HID), v(4, T, D),
            v(2, T, D), v(2, T, D), v(2, T, D), vf(T, AD), vf(T, D),
            pltpu.SemaphoreType.DMA((64,)), pltpu.SemaphoreType.DMA((64,))],
        compiler_params=pltpu.CompilerParams(collective_id=3, has_side_effects=True, vmem_limit_bytes=60 << 20),
        name="feed_forward")(second, cot, fin, fout, down, up, gain, shift)


NEGATIVE = -1000000000.0
PADDED = 32

def project(x, weight, out, tile=256):
    def step(t, _):
        cols = pl.ds(pl.multiple_of(t * tile, tile), tile)
        out[:, cols] = dot(x[...], weight[:, cols]).astype(out.dtype)
        return 0
    lax.fori_loop(0, out.shape[1] // tile, step, 0)


def lane_half(rows):
    return lax.broadcasted_iota(jnp.int32, (rows, 128), 1) < 64

def split_heads(v):
    low = lane_half(v.shape[0])
    zero = jnp.zeros_like(v)
    return jnp.where(low, v, zero), jnp.where(low, zero, v)

def self_mask(seg_col, seg_row):
    T = seg_col.shape[0]
    row = lax.broadcasted_iota(jnp.int32, (T, T), 0)
    col = lax.broadcasted_iota(jnp.int32, (T, T), 1)
    own = jnp.where((row >= col) & (seg_col[...] == seg_row[...]), 0.0, NEGATIVE)
    lane = lax.broadcasted_iota(jnp.int32, (T, PADDED), 1)
    return jnp.concatenate([own, jnp.where(lane < 30, 0.0, NEGATIVE)], axis=1)

def attend(q, keys, values, penalty, probs, out, pairs=8):
    def step(p, _):
        cols = pl.ds(pl.multiple_of(p * 128, 128), 128)
        kk, vv = keys(cols), values(cols)
        qs = split_heads(q[:, cols])
        vs = split_heads(vv)
        total = None
        for s in range(2):
            score = jnp.where(penalty[...] < -1.0, NEGATIVE, dot_right(qs[s], kk) * 0.125)
            e = jnp.exp(score - jnp.max(score, axis=-1, keepdims=True))
            prob = (e * (1.0 / jnp.sum(e, axis=-1, keepdims=True))).astype(bf16)
            probs[2 * p + s] = prob
            mixed = dot(prob, vs[s])
            total = mixed if total is None else total + mixed
        out[:, cols] = total.astype(bf16)
        return 0
    lax.fori_loop(0, pairs, step, 0)


def both_keys(own, prows, offset):
    def get(cols):
        shifted = pl.ds(pl.multiple_of(cols.start + offset, 128), 128)
        return jnp.concatenate([own[:, cols], prows[:, shifted]], axis=0)
    return get

def whole(ref):
    return lambda cols: ref[:, cols]

def add_norm(base, low, weight, gain, shift, out, normed, inverse, tile=256):
    def step(t, _):
        cols = pl.ds(pl.multiple_of(t * tile, tile), tile)
        out[:, cols] = base[:, cols].astype(f32) + dot(low[...], weight[:, cols])
        return 0
    lax.fori_loop(0, out.shape[1] // tile, step, 0)
    n, i = norm(out[...])
    normed[...] = n
    inverse[...] = i
    out[...] = n * gain + shift

def forward_kernel(inputs, memory, seg_col, seg_row, mem_row, weights, prows, vecs,
                   q, k, v, probs, attended, first, n1, i1, cq, ck, cv, cprobs, crossed, second, n2, i2, pen, cpen):
    width = inputs.shape[1]
    pen[...] = self_mask(seg_col, seg_row)
    cpen[...] = jnp.where(seg_col[...] == mem_row[...], 0.0, NEGATIVE)
    project(inputs, weights.at[0], q); project(inputs, weights.at[1], k); project(inputs, weights.at[2], v)
    project(memory, weights.at[6], ck); project(memory, weights.at[7], cv)
    attend(q, both_keys(k, prows, 0), both_keys(v, prows, width), pen, probs, attended)
    add_norm(inputs, attended, weights.at[3], vecs[0:1, :], vecs[1:2, :], first, n1, i1)
    q[...] = q[...]
    def step(t, _):
        cols = pl.ds(pl.multiple_of(t * 256, 256), 256)
        cq[:, cols] = dot(first[...].astype(bf16), weights[4, :, cols]).astype(bf16)
        return 0
    lax.fori_loop(0, width // 256, step, 0)
    attend(cq, whole(ck), whole(cv), cpen, cprobs, crossed)
    add_norm(first, crossed, weights.at[5], vecs[2:3, :], vecs[3:4, :], second, n2, i2)

def forward(inputs, memory, seg_col, seg_row, mem_row, weights, prows, vecs):
    T, D = inputs.shape; M = memory.shape[0]
    vm = pl.BlockSpec(memory_space=pltpu.VMEM)
    sds = jax.ShapeDtypeStruct
    row, mrow, full, one = sds((T, D), bf16), sds((M, D), bf16), sds((T, D), f32), sds((T, 1), f32)
    return pl.pallas_call(forward_kernel,
        out_shape=(row, row, row, sds((16, T, T + PADDED), bf16), row, full, full, one, row, mrow, mrow, sds((16, T, M), bf16), row, full, full, one),
        in_specs=[vm] * 8, out_specs=(vm,) * 16,
        scratch_shapes=[pltpu.VMEM((T, T + PADDED), f32), pltpu.VMEM((T, M), f32)],
        compiler_params=pltpu.CompilerParams(vmem_limit_bytes=60 << 20), name="attention_forward")(
            inputs, memory, seg_col, seg_row, mem_row, weights, prows, vecs)

def norm_back_into(e, n, i, gain, out, ngrad, at):
    ee = e[...]
    nn = n[...]
    out[...] = norm_back(ee, nn, i[...], gain)
    ngrad[at:at + 1, :] = jnp.sum(ee * nn, axis=0, keepdims=True)
    ngrad[at + 1:at + 2, :] = jnp.sum(ee, axis=0, keepdims=True)


def columns(t, tile=256):
    return pl.ds(pl.multiple_of(t * tile, tile), tile)

def loop(start, stop, step):
    lax.fori_loop(start, stop, lambda t, z: (step(t), z)[1], 0)

def front_kernel(A, r, inputs, memory, seg_col, seg_row, mem_row, embed, inner, outer2, norms, *refs):
    ws, (fin, fout, down, up) = refs[:8], refs[8:12]
    (wout, fin2, fout2, down4, up4, tangent, prows_o, vecs_o, q_o, k_o, v_o, probs_o, att_o, first_o, n1_o, i1_o, cq_o, ck_o, cv_o, cprobs_o, crossed_o,
     second_o, slow_o, n2_o, i2_o) = refs[12:37]
    (g, q, k, v, probs, att, first, flow, n1, i1, cq, ck, cv, cprobs, crossed, second, slow, n2, i2, pen, cpen,
     buf, got, zbuf, r0, r1, prows, nout, vecs, tan, ssem, rsem) = refs[37:]
    a, b, x, c = place()
    core, xp, yp = device(a, b, x, 1 - c), device(a, b, 1 - x, c), device(a, 1 - b, x, c)
    zp = [device((a + j) % A, b, x, c) for j in range(A)]
    za = a + 1 - 2 * (a % 2)
    zq = device(za, b, x, c)
    greet([core, xp, yp] + zp[1:])
    cp = Copies(ssem, rsem)
    T, D = inputs.shape
    pairs = 4
    def row(a_, b_, x_):
        return pl.multiple_of(((a_ * 2 + b_) * 2 + x_) * 2 * r, 2 * r)
    at = pl.ds(pl.multiple_of(row(a, b, x) + c * r, r), r)
    cut = (pl.ds(0, 3 * D // 8), pl.ds(3 * D // 8, 5 * D // 8))
    def block(i, h, a_, b_, x_):
        return g.at[2 * i + c, pl.ds(row(a_, b_, x_), 2 * r), cut[h]]
    kept = []
    own, cross = [], []
    base = cp.count
    for i in range(pairs):
        s1, s2, rr = ssem.at[cp.count], ssem.at[cp.count + 1], rsem.at[cp.count]
        cp.count += 2
        def start(keep, give):
            pltpu.make_async_copy(ws[2 * i + keep], g.at[2 * i + keep, at], s2).start()
            remote(ws[2 * i + give], g.at[2 * i + give, at], s1, rr, core).start()
        pl.when(c == 0)(functools.partial(start, 0, 1))
        pl.when(c == 1)(functools.partial(start, 1, 0))
        own.append(pltpu.make_async_copy(ws[2 * i], g.at[2 * i, at], s2))
        cross.append(remote(ws[2 * i], g.at[2 * i, at], s1, rr, core))
    G = norms.shape[0]
    me = ((a * 2 + b) * 2 + x) * 2 + c
    chip = (a * 2 + b) * 2 + x
    def nrows(start, count): return nout.at[pl.ds(pl.multiple_of(start * G, G), count * G)]
    def lanes(start, count): return prows.at[:, pl.ds(pl.multiple_of(start * 128, 128), count * 128)]
    nout[pl.ds(pl.multiple_of(me * G, G), G), :] = norms[...]
    small = {}
    peers = (core, xp, yp)
    def pre0():
        small["t"] = dot(embed[...], inner[...])
        buf[0] = small["t"]
        small["s"] = [cp(buf.at[0], got.at[0], core), cp(nrows(me, 1), nrows(me, 1), core)]
    def pre(n):
        def go():
            for e in small["s"]: e.wait_recv()
            buf[n] = buf[n - 1] + got[n - 1]
            start, count = (me - c, 2) if n == 1 else (me - c - 2 * x, 4)
            small["s"] = [cp(buf.at[n], got.at[n], peers[n]), cp(nrows(start, count), nrows(start, count), peers[n])]
        return go
    def pre3():
        for e in small["s"]: e.wait_recv()
        zbuf[a] = buf[2] + got[2]
        small["s"] = [cp(zbuf.at[a], zbuf.at[a], zp[j]) for j in range(1, A)] + [cp(nrows(a * 8, 8), nrows(a * 8, 8), zp[j]) for j in range(1, A)]
    def pre4():
        for e in small["s"]: e.wait_recv()
        t = zbuf[0]
        for n in range(1, A): t = t + zbuf[n]
        t = jnp.tanh(t)
        tan[...] = t
        r0[...] = dot(t.astype(bf16), outer2[...]).astype(bf16)
        small["s"] = [cp(r0, r1, core)]
        lane = lax.broadcasted_iota(jnp.int32, (G, 128), 1) // 32
        for w in range(2 * A):
            s = nout[pl.ds(w * 4 * G, G), :].astype(f32)
            for n in range(1, 4):
                s = jnp.where(lane == n, nout[pl.ds((w * 4 + n) * G, G), :].astype(f32), s)
            vecs[:, pl.ds(w * 128, 128)] = s[:8]
        kept.append(cp.local(tan, tangent))
        kept.append(cp.local(vecs, vecs_o))
    def pre5():
        small["s"][0].wait_recv()
        lane = lax.broadcasted_iota(jnp.int32, (PADDED, 128), 1)
        prows[:, pl.ds(pl.multiple_of(chip * 128, 128), 128)] = jnp.where((lane // 64) == c, r0[...].astype(f32), r1[...].astype(f32)).astype(bf16)
        small["s"] = [cp(lanes(chip, 1), lanes(chip, 1), xp)]
    def pre6():
        small["s"][0].wait_recv()
        small["s"] = [cp(lanes(chip - x, 2), lanes(chip - x, 2), yp)]
    def pre7():
        small["s"][0].wait_recv()
        small["s"] = [cp(lanes(a * 4, 4), lanes(a * 4, 4), zp[j]) for j in range(1, A)]
    def pre8():
        for e in small["s"]: e.wait_recv()
        kept.append(cp.local(prows, prows_o))
    H, AD = fin.shape[1], down.shape[1]
    kept += [cp.local(fin, fin2.at[:, pl.ds(0, H)]), cp.local(fout, fout2.at[pl.ds(0, H)])]
    nd = pl.ds(pl.multiple_of((x * 2 + c) * AD, AD), AD)
    md = pl.ds(pl.multiple_of((2 - 2 * x + c) * AD, AD), AD)
    kept += [cp.local(down, down4.at[:, nd]), cp.local(up, up4.at[nd])]
    feeds, passed = {}, []
    def feed_send(i):
        n = D // 8
        ri = pl.ds(pl.multiple_of(c * (D // 2) + i * n, n), n)
        m = H // 8
        ro = pl.ds(pl.multiple_of(c * (H // 2) + i * m, m), m)
        ro2 = pl.ds(pl.multiple_of(H + c * (H // 2) + i * m, m), m)
        feeds[i] = [(cp(fin.at[ri], fin2.at[ri, pl.ds(H, H)], zq), fin2.at[ri, pl.ds(H, H)]),
                    (cp(fout.at[ro], fout2.at[ro2], zq), fout2.at[ro2])]
    def adapter_send():
        feeds["a"] = [(cp(down, down4.at[:, nd], xp), down4.at[:, md]), (cp(up, up4.at[nd], xp), up4.at[md])]
        passed.extend([cp(down, down4.at[:, nd], core), cp(up, up4.at[nd], core)])
    def feed_pass(i):
        for e, ref in feeds[i]:
            e.wait_recv()
            passed.append(cp(ref, ref, core))
    zc, mc, lc, dc = {}, {}, {}, {}
    two, three = (yp, xp), (xp, yp)
    def first_send(i):
        own[i].wait(); cross[i].wait()
        for h in range(2):
            mc[i, h, 0] = cp(block(i, h, a, b, x), block(i, h, a, b, x), two[h])
        for h in range(2):
            lc[i, h, 0, 0] = cp(block(i, h, a, b, x), block(i, h, a, b, x), three[h])
        for j in range(1, A):
            for h in range(2):
                zc[i, h, j] = cp(block(i, h, a, b, x), block(i, h, a, b, x), zp[j])
    def mid(i, j):
        aj = (a + A - j) % A
        for h in range(2):
            zc[i, h, j].wait_recv()
            mc[i, h, j] = cp(block(i, h, aj, b, x), block(i, h, aj, b, x), two[h])
        for h in range(2):
            lc[i, h, j, 0] = cp(block(i, h, aj, b, x), block(i, h, aj, b, x), three[h])
    def third(i, j):
        aj = (a + A - j) % A
        for h in range(2):
            w = (aj, 1 - b, x) if h == 0 else (aj, b, 1 - x)
            mc[i, h, j].wait_recv()
            lc[i, h, j, 1] = cp(block(i, h, *w), block(i, h, *w), three[h])
    def fin_wait(i):
        for j in range(A):
            for h in range(2):
                lc[i, h, j, 0].wait_recv(); lc[i, h, j, 1].wait_recv()
        dc[i] = cp(g.at[2 * i + c], g.at[2 * i + c], core)
        kept.append(cp.local(g.at[2 * i + c], wout.at[2 * i + c]))
    def arrive(i):
        dc[i].wait_recv()
        kept.append(cp.local(g.at[2 * i + 1 - c], wout.at[2 * i + 1 - c]))
    def halves(src, w, out):
        def part(n):
            def go():
                xv = src[...]
                def step(t):
                    out[:, columns(t)] = dot(xv, g[w, :, columns(t)]).astype(bf16)
                loop(2 * n, 2 * n + 2, step)
            return go
        return [part(0), part(1)]
    def keep(src, dst):
        def go(): kept.append(cp.local(src, dst))
        return go
    def masks():
        pen[...] = self_mask(seg_col, seg_row)
        cpen[...] = jnp.where(seg_col[...] == mem_row[...], 0.0, NEGATIVE)
    def softmax(qv, kk, penalty):
        score = jnp.where(penalty[...] < -1.0, NEGATIVE, dot_right(qv, kk) * 0.125)
        e = jnp.exp(score - jnp.max(score, axis=-1, keepdims=True))
        return (e * (1.0 / jnp.sum(e, axis=-1, keepdims=True))).astype(bf16)
    def own_attend(n):
        def go():
            def step(p):
                cols = columns(p, 128)
                kk = jnp.concatenate([k[:, cols], prows[:, cols]], axis=0)
                vv = jnp.concatenate([v[:, cols], prows[:, pl.ds(pl.multiple_of(D + p * 128, 128), 128)]], axis=0)
                qs, vs = split_heads(q[:, cols]), split_heads(vv)
                total = None
                for s in range(2):
                    prob = softmax(qs[s], kk, pen)
                    probs[2 * p + s] = prob
                    m = dot(prob, vs[s])
                    total = m if total is None else total + m
                att[:, cols] = total.astype(bf16)
            loop(2 * n, 2 * n + 2, step)
        return go
    def cross_scores(n):
        def go():
            def step(p):
                cols = columns(p, 128)
                qs = split_heads(cq[:, cols])
                for s in range(2):
                    cprobs[2 * p + s] = softmax(qs[s], ck[:, cols], cpen)
            loop(2 * n, 2 * n + 2, step)
        return go
    def cross_mix(n):
        def go():
            def step(p):
                cols = columns(p, 128)
                vs = split_heads(cv[:, cols])
                crossed[:, cols] = (dot(cprobs[2 * p], vs[0]) + dot(cprobs[2 * p + 1], vs[1])).astype(bf16)
            loop(4 * n, 4 * n + 4, step)
        return go
    def normed(base, low, w, at, out, nn, ii, olow):
        def part(n):
            def go():
                lv = low[...]
                def step(t):
                    out[:, columns(t)] = base[:, columns(t)].astype(f32) + dot(lv, g[w, :, columns(t)])
                loop(2 * n, 2 * n + 2, step)
            return go
        def last():
            m, inv = norm(out[...])
            nn[...] = m
            ii[...] = inv
            s = m * vecs[at:at + 1, :] + vecs[at + 1:at + 2, :]
            out[...] = s
            olow[...] = s.astype(bf16)
        return [part(0), part(1), last]
    comp = {
        0: halves(inputs, 0, q) + halves(inputs, 1, k) + [keep(q, q_o), keep(k, k_o), masks],
        1: halves(inputs, 2, v) + [keep(v, v_o)] + [own_attend(n) for n in range(4)] + [keep(probs, probs_o), keep(att, att_o)]
           + normed(inputs, att, 3, 0, first, n1, i1, flow) + [keep(flow, first_o), keep(n1, n1_o), keep(i1, i1_o)],
        2: halves(memory, 4, ck) + [keep(ck, ck_o)] + halves(flow, 5, cq) + [keep(cq, cq_o)] + [cross_scores(n) for n in range(4)] + [keep(cprobs, cprobs_o)],
        3: halves(memory, 6, cv) + [keep(cv, cv_o)] + [cross_mix(n) for n in range(2)] + [keep(crossed, crossed_o)]
           + normed(first, crossed, 7, 2, second, n2, i2, slow) + [keep(second, second_o), keep(slow, slow_o), keep(n2, n2_o), keep(i2, i2_o)],
    }
    queue = [pre0, pre(1), pre(2), pre3, pre4, pre5, pre6, pre7, pre8]
    def turn(count=1):
        for _ in range(count):
            if queue: queue.pop(0)()
    first_send(0)
    turn()
    for i in range(pairs):
        if i + 1 < pairs:
            first_send(i + 1)
        feed_send(i)
        if i == 1:
            adapter_send()
        turn()
        third(i, 0)
        turn()
        for j in range(1, A):
            mid(i, j)
            turn(1)
        if i:
            fin_wait(i - 1)
            feed_pass(i - 1)
            turn()
        for j in range(1, A):
            third(i, j)
            turn(1)
        if i:
            arrive(i - 1)
            queue += comp[i - 1]
        turn(3)
    feed_pass(3); feed_pass("a")
    turn(6)
    fin_wait(3)
    turn(100)
    arrive(3)
    queue += comp[3]
    turn(100)
    for e in kept: e.wait()
    for e in passed: e.wait_recv()
    own_ids = None
    cp.close()

def front(A, r, inputs, memory, seg_col, seg_row, mem_row, embed, inner, outer2, norms, ws, fin, fout, down, up):
    T, D = inputs.shape; M = memory.shape[0]; H = fin.shape[1]; AD = down.shape[1]
    vm = pl.BlockSpec(memory_space=pltpu.VMEM)
    any_ = pl.BlockSpec(memory_space=pl.ANY)
    sds = jax.ShapeDtypeStruct
    v = lambda *s: pltpu.VMEM(s, bf16)
    vf = lambda *s: pltpu.VMEM(s, f32)
    row, mrow, full, one = sds((T, D), bf16), sds((M, D), bf16), sds((T, D), f32), sds((T, 1), f32)
    S = (PADDED, inner.shape[1])
    probs, cprobs = (16, T, T + PADDED), (16, T, M)
    return pl.pallas_call(functools.partial(front_kernel, A, r),
        out_shape=(sds((8, D, D), bf16), sds((D, 2 * H), bf16), sds((2 * H, D), bf16), sds((D, 4 * AD), bf16), sds((4 * AD, D), bf16),
            sds(S, f32), sds((PADDED, 2 * D), bf16), sds((8, D), f32), row, row, row, sds(probs, bf16), row, row, full, one, row, mrow, mrow, sds(cprobs, bf16), row,
            full, row, full, one),
        in_specs=[vm] * 9 + [any_] * 12, out_specs=(any_,) * 25,
        scratch_shapes=[v(8, D, D), v(T, D), v(T, D), v(T, D), v(*probs), v(T, D), vf(T, D), v(T, D), vf(T, D), vf(T, 1), v(T, D), v(M, D), v(M, D), v(*cprobs), v(T, D),
            vf(T, D), v(T, D), vf(T, D), vf(T, 1), vf(T, T + PADDED), vf(T, M),
            vf(3, *S), vf(3, *S), vf(A, *S), v(PADDED, 128), v(PADDED, 128), v(PADDED, 2 * D), v(8 * A * norms.shape[0], 128), vf(8, D), vf(*S),
            pltpu.SemaphoreType.DMA((320,)), pltpu.SemaphoreType.DMA((320,))],
        compiler_params=pltpu.CompilerParams(collective_id=1, has_side_effects=True, vmem_limit_bytes=60 << 20), name="front")(
            inputs, memory, seg_col, seg_row, mem_row, embed, inner, outer2, norms, *ws, fin, fout, down, up)


def exact(l, r, dims):
    return lax.dot_general(l, r, (dims, ((), ())), precision=lax.Precision.HIGHEST, preferred_element_type=f32)

def back_kernel(A, r, gsec, n1, i1, n2, i2, vecs, ngrad3, q, k, v, probs, cq, ck, cv, cprobs, prows, inputs, memory, att, flow, crossed, slow, blow, ay,
                tangent, embed, inner, outer2, weights, fi, fo,
                igrad, mgrad, out, aout, fi_out, fo_out, outer_o, inner_o, embed_o, nsum,
                ws, gmid, gfirst, og, mid, dcq, dck, dcv, startl, dq, dk, dv, pg,
                xb, yb, mb, mby, axb, ayb, pb, apb, fib, fob, r1, r2, r3, ra1, ra2, ra3, rfi, rfo, rzi, rzo, rxi, rxo, ob, aob, fib2, fob2,
                buf, got, zbuf, nbuf, ngot, nz, w0, w1, w2, w3, s0, s1, s2, ssem, rsem):
    a, b, x, c = place()
    o = 1 - c
    core, xp, yp = device(a, b, x, o), device(a, b, 1 - x, c), device(a, 1 - b, x, c)
    zp = [device((a + j) % A, b, x, c) for j in range(A)]
    za = a + 1 - 2 * (a % 2)
    zq = device(za, b, x, c)
    peers = (core, xp, yp)
    T, D = gsec.shape
    M = memory.shape[0]
    HID = fi.shape[1] // 2
    Q = fi.shape[0] // 4
    half = D // 2
    cp = Copies(ssem, rsem)
    loads = {}
    def fetch(slot, w):
        loads[slot] = cp.local(weights.at[w], ws.at[slot])
    fetch(0, 7); fetch(1, 5); fetch(2, 3); fetch(3, 4)
    fown = []
    for xx in range(2):
        dq_ = pl.ds(pl.multiple_of((xx * 2 + c) * Q, Q), Q)
        fown += [cp.local(fi.at[dq_, :], fib.at[xx]), cp.local(fo.at[:, dq_], fob.at[xx])]
    greet([core, xp, yp] + zp[1:])
    def offer(srcs, mine, theirs):
        n = cp.count
        cp.count += 2
        def start(keep, give):
            pltpu.make_async_copy(srcs[keep], mine, ssem.at[n]).start()
            remote(srcs[give], theirs, ssem.at[n + 1], rsem.at[n], core).start()
        pl.when(c == 0)(functools.partial(start, 0, 1))
        pl.when(c == 1)(functools.partial(start, 1, 0))
        e = remote(srcs[0], theirs, ssem.at[n + 1], rsem.at[n], core)
        cp.all.append(e)
        return pltpu.make_async_copy(srcs[0], mine, ssem.at[n]).wait, e.wait_recv
    lowT, highT = pl.ds(0, T), pl.ds(T, T)
    waits = {}
    aw = offer((slow, blow), axb.at[lowT], axb.at[highT]) + offer((ay.at[0], ay.at[1]), ayb.at[lowT], ayb.at[highT])
    waits[0] = offer((crossed, flow), xb.at[0, lowT], xb.at[0, highT])
    fcopies = []
    for xx in range(2):
        dq_ = pl.ds(pl.multiple_of((xx * 2 + o) * Q, Q), Q)
        fcopies += [cp(fi.at[dq_, :], rfi.at[xx], core), cp(fo.at[:, dq_], rfo.at[xx], core)]
    waits[1] = offer((memory, memory), mb.at[pl.ds(0, M)], mb.at[pl.ds(M, M)])
    waits[2] = offer((att, inputs), xb.at[1, lowT], xb.at[1, highT])
    waits[3] = offer((inputs, inputs), xb.at[2, lowT], xb.at[2, highT])

    zf, xf, outs = [], [], []
    def feed0():
        for e in fown: e.wait()
        for e in fcopies: e.wait_recv()
        for xx in range(2):
            def rows_fi(t):
                s = pl.ds(t * 32, 32)
                fib[xx, s, :] = fib[xx, s, :] + rfi[xx, s, :]
            loop(0, Q // 32, rows_fi)
            def rows_fo(t):
                s = pl.ds(t * 64, 64)
                fob[xx, s, :] = fob[xx, s, :] + rfo[xx, s, :]
            loop(0, 2 * HID // 64, rows_fo)
        zf.extend([cp(fib.at[:, :, pl.ds(HID, HID)], rzi, zq), cp(fob.at[:, pl.ds(HID, HID), :], rzo, zq)])
    def feed1():
        for e in zf: e.wait_recv()
        for xx in range(2):
            def rows_fi(t):
                s = pl.ds(t * 32, 32)
                fib[xx, s, pl.ds(0, HID)] = fib[xx, s, pl.ds(0, HID)] + rzi[xx, s, :]
            loop(0, Q // 32, rows_fi)
            def rows_fo(t):
                s = pl.ds(t * 64, 64)
                fob[xx, s, :] = fob[xx, s, :] + rzo[xx, s, :]
            loop(0, HID // 64, rows_fo)
        xf.extend([cp(fib.at[1 - x, :, pl.ds(0, HID)], rxi, xp), cp(fob.at[1 - x, pl.ds(0, HID), :], rxo, xp)])
    def feed2():
        for e in xf: e.wait_recv()
        def rows_fi(t):
            s = pl.ds(t * 32, 32)
            fib2[s, :] = fib[x, s, pl.ds(0, HID)].astype(f32) + rxi[s, :].astype(f32)
        loop(0, Q // 32, rows_fi)
        def rows_fo(t):
            s = pl.ds(t * 64, 64)
            fob2[s, :] = fob[x, s, :].astype(f32) + rxo[s, :].astype(f32)
        loop(0, HID // 64, rows_fo)
        outs.extend([cp.local(fib2, fi_out).wait, cp.local(fob2, fo_out).wait])

    first, second, third = {}, {}, {}
    numbers = {}
    for i in range(4):
        for h in range(2):
            numbers[i, h] = cp.count
            cp.count += 1
    def level1(i, h):
        cols = pl.ds(h * half, half)
        n = numbers[i, h]
        if h == 0:
            return remote(pb.at[i, :, :, 1 - x, :, cols], r1.at[i, h], ssem.at[n], rsem.at[n], xp)
        return remote(pb.at[i, :, 1 - b, :, :, cols], r1.at[i, h], ssem.at[n], rsem.at[n], yp)
    def product(i):
        for h in range(2):
            def tile(t):
                cols = pl.ds(pl.multiple_of(h * half + t * 256, 256), 256)
                if i == 1:
                    p = dot_left(mb[...], mby[:, cols])
                else:
                    n = (0, None, 1, 2)[i]
                    p = dot_left(xb[n], yb[n, :, cols])
                pb[i, :, :, :, :, cols] = p.astype(bf16).reshape(A, 2, 2, 2 * r, 256)
            loop(0, half // 256, tile)
            level1(i, h).start()
    for i in range(4):
        for h in range(2):
            first[i, h] = level1(i, h)
            cp.all.append(first[i, h])
    def compute(i):
        for e in waits[i]: e()
        product(i)
    def one(i, h):
        def go():
            cols = pl.ds(h * half, half)
            first[i, h].wait_recv()
            def add(side):
                def row(z):
                    if h == 0:
                        pb[i, z, side, x, :, cols] = pb[i, z, side, x, :, cols] + r1[i, h, z, side]
                    else:
                        pb[i, z, b, side, :, cols] = pb[i, z, b, side, :, cols] + r1[i, h, z, side]
                loop(0, A, row)
            add(1 - b if h == 0 else 1 - x)
            if h == 0:
                second[i, h] = cp(pb.at[i, :, 1 - b, x, :, cols], r2.at[i, h], yp)
            else:
                second[i, h] = cp(pb.at[i, :, b, 1 - x, :, cols], r2.at[i, h], xp)
            add(b if h == 0 else x)
        return go
    def two(i, h):
        def go():
            cols = pl.ds(h * half, half)
            second[i, h].wait_recv()
            for j in range(1, A):
                aj = (a + j) % A
                pb[i, aj, b, x, :, cols] = pb[i, aj, b, x, :, cols] + r2[i, h, aj]
                third[i, h, j] = cp(pb.at[i, aj, b, x, :, cols], r3.at[i, h, j - 1], zp[j])
            pb[i, a, b, x, :, cols] = pb[i, a, b, x, :, cols] + r2[i, h, a]
        return go
    def three(i, h):
        def go():
            cols = pl.ds(h * half, half)
            for j in range(1, A): third[i, h, j].wait_recv()
            t = pb[i, a, b, x, :, cols].astype(f32)
            for j in range(1, A): t = t + r3[i, h, j - 1].astype(f32)
            ob[i, :, cols] = t
            if h == 1:
                outs.append(cp.local(ob.at[i, pl.ds(pl.multiple_of(c * r, r), r)], out.at[2 * i + c]).wait)
                outs.append(cp(ob.at[i, pl.ds(pl.multiple_of(o * r, r), r)], out.at[2 * i + c], core).wait_recv)
        return go
    def adapt0():
        for e in aw: e()
        for t in range(2):
            apb[t] = dot_left(axb[...], ayb[:, pl.ds(t * 256, 256)]).astype(bf16).reshape(A, 2, D // (2 * A), 256)
        first["a"] = cp(apb.at[1 - x], ra1, xp)
    def adapt1():
        first["a"].wait_recv()
        def row(z):
            for s in range(2):
                apb[x, z, s] = apb[x, z, s] + ra1[z, s]
        loop(0, A, row)
        second["a"] = cp(apb.at[x, :, 1 - b], ra2, yp)
    def adapt2():
        second["a"].wait_recv()
        for j in range(1, A):
            aj = (a + j) % A
            apb[x, aj, b] = apb[x, aj, b] + ra2[aj]
            third["a", j] = cp(apb.at[x, aj, b], ra3.at[j - 1], zp[j])
        apb[x, a, b] = apb[x, a, b] + ra2[a]
    def adapt3():
        for j in range(1, A): third["a", j].wait_recv()
        t = apb[x, a, b].astype(f32)
        for j in range(1, A): t = t + ra3[j - 1].astype(f32)
        aob[0] = t[:, :128]
        aob[1] = t[:, 128:]
        outs.append(cp.local(aob.at[c], aout.at[c]).wait)
        outs.append(cp(aob.at[o], aout.at[c], core).wait_recv)
    small = {}
    def lanes(start, count): return pl.ds(pl.multiple_of(start * 128, 128), count * 128)
    def tail0():
        small["w"] = [cp(pg.at[:, lanes((a + j) % A * 4, 4)], w0.at[j - 1], zp[j]) for j in range(1, A)]
        small["n"] = [cp(nbuf.at[0], ngot.at[0], core)]
    def tail_norm(n):
        def go():
            for e in small["n"]: e.wait_recv()
            nbuf[n] = nbuf[n - 1] + ngot[n - 1]
            small["n"] = [cp(nbuf.at[n], ngot.at[n], peers[n])]
        return go
    def tail_norm3():
        for e in small["n"]: e.wait_recv()
        nz[a] = nbuf[2] + ngot[2]
        small["n"] = [cp(nz.at[a], nz.at[a], zp[j]) for j in range(1, A)]
    def tail_norm4():
        for e in small["n"]: e.wait_recv()
        t = nz[0]
        for n in range(1, A): t = t + nz[n]
        nsum[...] = t
    def tail1():
        t = pg[:, lanes(a * 4, 4)]
        for j, e in enumerate(small["w"]):
            e.wait_recv()
            t = t + w0[j]
        s0[...] = t
        small["w"] = [cp(s0.at[:, lanes((1 - b) * 2, 2)], w1, yp)]
    def tail2():
        small["w"][0].wait_recv()
        s1[...] = s0[:, lanes(b * 2, 2)] + w1[...]
        small["w"] = [cp(s1.at[:, lanes(1 - x, 1)], w2, xp)]
    def tail3():
        small["w"][0].wait_recv()
        s2[...] = s1[:, lanes(x, 1)] + w2[...]
        small["w"] = [cp(s2, w3, core)]
    def tail4():
        small["w"][0].wait_recv()
        t = s2[...] + w3[...]
        lane = lax.broadcasted_iota(jnp.int32, t.shape, 1)
        mine = jnp.where((lane // 64) == c, t, 0.0)
        buf[0] = exact(mine, outer2[...].astype(f32), ((1,), (1,)))
        small["w"] = [cp(buf.at[0], got.at[0], core)]
        grad = exact(tangent[...].astype(bf16).astype(f32), t, ((0,), (0,)))
        outer_o[...] = jnp.where(c == 0, grad[:, :64], grad[:, 64:])
    def tail5(n):
        def go():
            small["w"][0].wait_recv()
            buf[n] = buf[n - 1] + got[n - 1]
            small["w"] = [cp(buf.at[n], got.at[n], peers[n])]
        return go
    def tail6():
        small["w"][0].wait_recv()
        zbuf[a] = buf[2] + got[2]
        small["w"] = [cp(zbuf.at[a], zbuf.at[a], zp[j]) for j in range(1, A)]
    def tail7():
        for e in small["w"]: e.wait_recv()
        t = zbuf[0]
        for n in range(1, A): t = t + zbuf[n]
        tan = tangent[...]
        t = t * (1.0 - tan * tan)
        inner_o[...] = exact(embed[...].astype(f32), t, ((0,), (0,)))
        embed_o[...] = exact(t, inner[...].astype(f32), ((1,), (1,)))
    def norm_two():
        norm_back_into(gsec, n2, i2, vecs[2:3, :], gmid, nbuf.at[0], 2)
        mid[...] = gmid[...].astype(bf16)
    def back_project(src, slot, n):
        def go():
            s = src[...]
            loop(2 * n, 2 * n + 2, lambda t: og.__setitem__((slice(None), columns(t)), dot_right(s, ws[slot, columns(t), :]).astype(bf16)))
        return go
    def wait_slot(slot):
        def go(): loads[slot].wait()
        return go
    def pair_back(p, grad, qr, kk, vv, pr):
        cols = columns(p, 128)
        qs, ks, gs = split_heads(qr[:, cols]), split_heads(kk), split_heads(grad[:, cols])
        res = None
        for s in range(2):
            low = pr[2 * p + s]
            prob = low.astype(f32)
            t = prob * dot_right(gs[s], vv)
            ds = (t - prob * jnp.sum(t, axis=-1, keepdims=True)).astype(bf16)
            m = (dot(ds, ks[s]), dot_left(ds, qs[s]), dot_left(low, gs[s]))
            res = m if res is None else tuple(e + f for e, f in zip(res, m))
        return cols, res[0] * 0.125, res[1] * 0.125, res[2]
    def cross_back(n):
        def go():
            def step(p):
                cs = columns(p, 128)
                cols, m1, m2, m3 = pair_back(p, og, cq, ck[:, cs], cv[:, cs], cprobs)
                dcq[:, cols] = m1.astype(bf16)
                dck[:, cols] = m2.astype(bf16)
                dcv[:, cols] = m3.astype(bf16)
            loop(2 * n, 2 * n + 2, step)
        return go
    def self_back(n):
        def go():
            def step(p):
                cs = columns(p, 128)
                cv_ = pl.ds(pl.multiple_of(D + p * 128, 128), 128)
                kk = jnp.concatenate([k[:, cs], prows[:, cs]], axis=0)
                vv = jnp.concatenate([v[:, cs], prows[:, cv_]], axis=0)
                cols, m1, m2, m3 = pair_back(p, og, q, kk, vv, probs)
                dq[:, cols] = m1.astype(bf16)
                dk[:, cols] = m2[:T].astype(bf16)
                dv[:, cols] = m3[:T].astype(bf16)
                pg[:, cols] = m2[T:]
                pg[:, cv_] = m3[T:]
            loop(2 * n, 2 * n + 2, step)
        return go
    def first_grad():
        s = dcq[...]
        def step(t):
            gfirst[:, columns(t)] = gmid[:, columns(t)] + dot_right(s, ws[1, columns(t), :])
        loop(0, D // 256, step)
    def norm_one():
        norm_back_into(gfirst, n1, i1, vecs[0:1, :], gmid, nbuf.at[0], 0)
        nbuf[0, 4:6, :] = ngrad3[...]
        nbuf[0, 6:8, :] = jnp.zeros((2, D), f32)
        startl[...] = gmid[...].astype(bf16)
    def memory_part(n):
        def go():
            def step(t):
                mgrad[:, columns(t)] = (dot_right(dck[...], ws[3, columns(t), :]) + dot_right(dcv[...], ws[0, columns(t), :])).astype(bf16)
            loop(2 * n, 2 * n + 2, step)
        return go
    def input_part(n):
        def go():
            def step(t):
                s = gmid[:, columns(t)] + dot_right(dq[...], ws[1, columns(t), :]) + dot_right(dk[...], ws[2, columns(t), :]) + dot_right(dv[...], ws[3, columns(t), :])
                igrad[:, columns(t)] = s.astype(bf16)
            loop(2 * n, 2 * n + 2, step)
        return go
    norm_two()
    wait_slot(0)()
    back_project(mid, 0, 0)(); back_project(mid, 0, 1)()
    fetch(0, 6)
    adapt0()
    feed0()
    cross_back(0)(); cross_back(1)()
    adapt1()
    cross_back(2)(); cross_back(3)()
    waits[0] += offer((mid, dcq), yb.at[0, lowT], yb.at[0, highT])
    waits[1] += offer((dck, dcv), mby.at[pl.ds(0, M)], mby.at[pl.ds(M, M)])
    wait_slot(1)()
    first_grad()
    compute(0)
    fetch(1, 0)
    norm_one()
    adapt2()
    compute(1)
    wait_slot(2)()
    back_project(startl, 2, 0)(); back_project(startl, 2, 1)()
    fetch(2, 1)
    feed1()
    self_back(0)()
    one(0, 0)(); one(0, 1)()
    self_back(1)()
    one(1, 0)()
    self_back(2)()
    one(1, 1)()
    self_back(3)()
    waits[2] += offer((startl, dq), yb.at[1, lowT], yb.at[1, highT])
    waits[3] += offer((dk, dv), yb.at[2, lowT], yb.at[2, highT])
    tail0()
    compute(2)
    two(0, 0)(); two(0, 1)()
    tail_norm(1)()
    compute(3)
    tail1()
    two(1, 0)(); two(1, 1)()
    tail_norm(2)()
    feed2()
    wait_slot(3)(); wait_slot(0)()
    tail2()
    memory_part(0)()
    one(2, 0)()
    tail_norm3()
    one(2, 1)()
    tail3()
    memory_part(1)()
    fetch(3, 2)
    three(0, 0)(); three(0, 1)()
    tail_norm4()
    tail4()
    one(3, 0)()
    adapt3()
    one(3, 1)()
    tail5(1)()
    wait_slot(1)(); wait_slot(2)(); wait_slot(3)()
    two(2, 0)()
    input_part(0)()
    tail5(2)()
    two(2, 1)()
    input_part(1)()
    tail6()
    three(1, 0)(); three(1, 1)()
    tail7()
    two(3, 0)(); two(3, 1)()
    three(2, 0)(); three(2, 1)()
    three(3, 0)(); three(3, 1)()
    for e in outs: e()
    cp.close()

def back(A, r, small, fi_fo):
    gsec, memory = small[0], small[17]
    T, D = gsec.shape; M = memory.shape[0]
    fi, fo = fi_fo[1:]
    Q, H2 = fi.shape[0] // 4, fi.shape[1]
    H = H2 // 2
    half = D // 2
    v = lambda *s: pltpu.VMEM(s, bf16)
    vf = lambda *s: pltpu.VMEM(s, f32)
    any_ = pl.BlockSpec(memory_space=pl.ANY)
    vm = pl.BlockSpec(memory_space=pltpu.VMEM)
    sds = jax.ShapeDtypeStruct
    P_, N = PADDED, (8, D)
    hid = small[-2].shape[1]
    S = (P_, hid)
    return pl.pallas_call(functools.partial(back_kernel, A, r),
        out_shape=(sds((T, D), bf16), sds((M, D), bf16), sds((8, r, D), f32), sds((2, D // (2 * A), 128), f32), sds((Q, H), f32), sds((H, Q), f32),
            sds((hid, 64), f32), sds((r, hid), f32), sds((P_, r), f32), sds(N, f32)),
        in_specs=[vm] * len(small) + [any_] * 3, out_specs=(vm, vm) + (any_,) * 4 + (vm,) * 4,
        scratch_shapes=[v(4, D, D), vf(T, D), vf(T, D), v(T, D), v(T, D), v(T, D), v(M, D), v(M, D), v(T, D), v(T, D), v(T, D), v(T, D), vf(P_, 2 * D),
            v(3, 2 * T, D), v(3, 2 * T, D), v(2 * M, D), v(2 * M, D), v(2 * T, D), v(2 * T, 512),
            v(4, A, 2, 2, 2 * r, D), v(2, A, 2, D // (2 * A), 256), v(2, Q, H2), v(2, H2, Q),
            v(4, 2, A, 2, 2 * r, half), v(4, 2, A, 2 * r, half), v(4, 2, A - 1, 2 * r, half),
            v(A, 2, D // (2 * A), 256), v(A, D // (2 * A), 256), v(A - 1, D // (2 * A), 256),
            v(2, Q, H2), v(2, H2, Q), v(2, Q, H), v(2, H, Q), v(Q, H), v(H, Q),
            vf(4, 2 * r, D), vf(2, D // (2 * A), 128), vf(Q, H), vf(H, Q),
            vf(3, *S), vf(3, *S), vf(A, *S), vf(3, *N), vf(3, *N), vf(A, *N), vf(A - 1, P_, 512), vf(P_, 256), vf(P_, 128), vf(P_, 128), vf(P_, 512), vf(P_, 256), vf(P_, 128),
            pltpu.SemaphoreType.DMA((224,)), pltpu.SemaphoreType.DMA((224,))],
        compiler_params=pltpu.CompilerParams(collective_id=2, has_side_effects=True, vmem_limit_bytes=63 << 20),
        name="back")(*small, *fi_fo)

def fast_body(A, inputs, memory, cotangent, segments, memory_segments, query_self, key_self, value_self, output_self,
              query_cross, key_cross, value_cross, output_cross, self_gain, self_shift, cross_gain, cross_shift,
              final_gain, final_shift, feed_in, feed_out, adapter_down, adapter_up, prefix_embed, prefix_inner, prefix_outer):
    r = query_self.shape[0]
    w, n = lax.axis_index(WIDE), lax.axis_index(NARROW)
    norms = jnp.pad(jnp.stack([self_gain, self_shift, cross_gain, cross_shift, final_gain, final_shift]), ((0, 10), (0, 0)))
    norms = jnp.concatenate([norms] * 4, axis=1)
    outer2 = jnp.concatenate([prefix_outer, prefix_outer], axis=1)
    embed = jnp.pad(prefix_embed, ((0, PADDED - PREFIX), (0, 0)))
    (weights, fin2, fout2, down4, up4, tangent, prows, vecs, q, k, v, probs, attended, first_low, n1, i1, cq, ck, cv, cprobs, crossed, second, second_low, n2, i2) = front(
        A, r, inputs, memory, segments.reshape(-1, 1), segments.reshape(1, -1), memory_segments.reshape(1, -1), embed, prefix_inner, outer2, norms,
        [query_self, key_self, value_self, output_self, key_cross, query_cross, value_cross, output_cross], feed_in, feed_out, adapter_down, adapter_up)
    result, grad_second, fi, fo, ay, branch_low, ngrad3 = feed(A, second, cotangent, fin2, fout2, down4, up4, vecs[4:5], vecs[5:6])
    inputs_grad, memory_grad, sums, adapt, fi_sum, fo_sum, outer_grad, inner_grad, embed_grad, nsum = back(A, r,
        (grad_second, n1, i1, n2, i2, vecs, ngrad3, q, k, v, probs, cq, ck, cv, cprobs, prows, inputs, memory, attended, first_low, crossed, second_low, branch_low, ay,
         tangent, embed, prefix_inner, outer2), (weights, fi, fo))
    ng = lax.dynamic_slice_in_dim(nsum, (w * 4 + n) * r, r, 1)
    return (result, inputs_grad, memory_grad, sums[5], sums[6], sums[7], sums[4], sums[1], sums[2], sums[3], sums[0],
            ng[0], ng[1], ng[2], ng[3], ng[4], ng[5], fi_sum, fo_sum, adapt[0], adapt[1].T, embed_grad[:PREFIX], inner_grad, outer_grad)


def solution(mesh):
    wide, narrow = mesh.shape[WIDE], mesh.shape[NARROW]
    fits = narrow == 4 and wide == 8
    body = functools.partial(fast_body, wide // 2) if fits else plain_body
    return jax.shard_map(
        body,
        mesh=mesh,
        in_specs=(
            P(BOTH, None),
            P(BOTH, None),
            P(BOTH, None),
            P(BOTH),
            P(BOTH),
            P(BOTH, None),
            P(BOTH, None),
            P(BOTH, None),
            P(BOTH, None),
            P(BOTH, None),
            P(BOTH, None),
            P(BOTH, None),
            P(BOTH, None),
            P(BOTH),
            P(BOTH),
            P(BOTH),
            P(BOTH),
            P(BOTH),
            P(BOTH),
            P(None, WIDE),
            P(WIDE, None),
            P(None, NARROW),
            P(NARROW, None),
            P(None, BOTH),
            P(BOTH, None),
            P(None, BOTH),
        ),
        out_specs=(
            P(BOTH, None),
            P(BOTH, None),
            P(BOTH, None),
            P(BOTH, None),
            P(BOTH, None),
            P(BOTH, None),
            P(BOTH, None),
            P(BOTH, None),
            P(BOTH, None),
            P(BOTH, None),
            P(BOTH, None),
            P(BOTH),
            P(BOTH),
            P(BOTH),
            P(BOTH),
            P(BOTH),
            P(BOTH),
            P(NARROW, WIDE),
            P(WIDE, NARROW),
            P(WIDE, NARROW),
            P(NARROW, WIDE),
            P(None, BOTH),
            P(BOTH, None),
            P(None, BOTH),
        ),
        check_vma=False,
    )
```

```python
import functools
from functools import reduce

import jax
import jax.numpy as jnp
from jax import lax
from jax.experimental import pallas as pl
from jax.experimental.pallas import tpu as pltpu
from jax.sharding import PartitionSpec as P

MESH = pl.DeviceIdType.MESH
bf16, f32 = jnp.bfloat16, jnp.float32
WIDE, NARROW = "wide", "narrow"
BOTH = (WIDE, NARROW)


HEADS = 16
HEAD = 64
PREFIX = 30


HIGHEST = lax.Precision.HIGHEST
EPSILON = 1e-05
MASKED = -1000000000.0
ADAPT_SCALE = 4.0


def matmul(left, right):
    return jnp.dot(left, right, preferred_element_type=jnp.float32)


def left_product(left, right):
    return lax.dot_general(
        left, right, (((0,), (0,)), ((), ())), preferred_element_type=jnp.float32
    )


def right_product(left, right):
    return lax.dot_general(
        left, right, (((1,), (1,)), ((), ())), preferred_element_type=jnp.float32
    )


def exact_left(left, right):
    return lax.dot_general(
        left, right, (((0,), (0,)), ((), ())), precision=HIGHEST, preferred_element_type=jnp.float32
    )


def exact_right(left, right):
    return lax.dot_general(
        left, right, (((1,), (1,)), ((), ())), precision=HIGHEST, preferred_element_type=jnp.float32
    )


def norm_forward(values, factor, offset):
    average = jnp.mean(values, axis=-1, keepdims=True)
    center = values - average
    inverse = lax.rsqrt(jnp.mean(center * center, axis=-1, keepdims=True) + EPSILON)
    normed = center * inverse
    return (normed * factor + offset, normed, inverse)


def norm_backward(grad_out, normed, inverse, factor):
    scaled = grad_out * factor
    grad_in = inverse * (
        scaled
        - jnp.mean(scaled, axis=-1, keepdims=True)
        - normed * jnp.mean(scaled * normed, axis=-1, keepdims=True)
    )
    return (grad_in, jnp.sum(grad_out * normed, axis=0), jnp.sum(grad_out, axis=0))


def head_view(rows):
    return rows.reshape(rows.shape[0], HEADS, HEAD)


def scored(queries, key_rows, allowed):
    raw = jnp.einsum(
        "shd,khd->hsk", head_view(queries), head_view(key_rows), preferred_element_type=jnp.float32
    )
    return jnp.where(allowed[None], raw * HEAD ** (-0.5), MASKED)


def attend_forward(queries, parts):
    scores = [scored(queries, member[0], member[2]) for member in parts]
    largest = reduce(jnp.maximum, [jnp.max(matrix, axis=-1, keepdims=True) for matrix in scores])
    total = reduce(
        jnp.add, [jnp.sum(jnp.exp(matrix - largest), axis=-1, keepdims=True) for matrix in scores]
    )
    logsum = largest + jnp.log(total)
    mixed = reduce(
        jnp.add,
        [
            jnp.einsum(
                "hsk,khd->shd",
                jnp.exp(matrix - logsum).astype(jnp.bfloat16),
                head_view(member[1]),
                preferred_element_type=jnp.float32,
            )
            for matrix, member in zip(scores, parts)
        ],
    )
    return (mixed.reshape(queries.shape[0], HEADS * HEAD), logsum)


def attend_backward(queries, parts, logsum, grad_low):
    grad_heads = head_view(grad_low)
    chances = [jnp.exp(scored(queries, member[0], member[2]) - logsum) for member in parts]
    slopes = [
        jnp.einsum(
            "shd,khd->hsk", grad_heads, head_view(member[1]), preferred_element_type=jnp.float32
        )
        for member in parts
    ]
    row_dot = reduce(
        jnp.add,
        [jnp.sum(chance * slope, axis=-1, keepdims=True) for chance, slope in zip(chances, slopes)],
    )
    scale = HEAD ** (-0.5)
    grad_query = jnp.zeros((queries.shape[0], HEADS, HEAD), jnp.float32)
    results = []
    for member, chance, slope in zip(parts, chances, slopes):
        dscore = (chance * (slope - row_dot)).astype(jnp.bfloat16)
        grad_query = grad_query + jnp.einsum(
            "hsk,khd->shd", dscore, head_view(member[0]), preferred_element_type=jnp.float32
        )
        grad_key = (
            jnp.einsum(
                "hsk,shd->khd", dscore, head_view(queries), preferred_element_type=jnp.float32
            )
            * scale
        )
        grad_value = jnp.einsum(
            "hsk,shd->khd",
            chance.astype(jnp.bfloat16),
            grad_heads,
            preferred_element_type=jnp.float32,
        )
        results.append(
            (
                grad_key.reshape(grad_key.shape[0], HEADS * HEAD),
                grad_value.reshape(grad_value.shape[0], HEADS * HEAD),
            )
        )
    return ((grad_query * scale).reshape(queries.shape[0], HEADS * HEAD), results)


def gelu_back(pre_values, grad_values):
    return jax.vjp(lambda inner: jax.nn.gelu(inner, approximate=False), pre_values)[1](grad_values)[
        0
    ]


def plain_body(
    inputs,
    memory,
    cotangent,
    segments,
    memory_segments,
    query_self,
    key_self,
    value_self,
    output_self,
    query_cross,
    key_cross,
    value_cross,
    output_cross,
    self_gain,
    self_shift,
    cross_gain,
    cross_shift,
    final_gain,
    final_shift,
    feed_in,
    feed_out,
    adapter_down,
    adapter_up,
    prefix_embed,
    prefix_inner,
    prefix_outer,
):
    (
        query_one,
        key_one,
        value_one,
        output_one,
        query_two,
        key_two,
        value_two,
        output_two,
        gain_one,
        shift_one,
        gain_two,
        shift_two,
        gain_three,
        shift_three,
        embed_full,
        inner_full,
        outer_full,
    ) = (
        lax.all_gather(query_self, BOTH, axis=0, tiled=True),
        lax.all_gather(key_self, BOTH, axis=0, tiled=True),
        lax.all_gather(value_self, BOTH, axis=0, tiled=True),
        lax.all_gather(output_self, BOTH, axis=0, tiled=True),
        lax.all_gather(query_cross, BOTH, axis=0, tiled=True),
        lax.all_gather(key_cross, BOTH, axis=0, tiled=True),
        lax.all_gather(value_cross, BOTH, axis=0, tiled=True),
        lax.all_gather(output_cross, BOTH, axis=0, tiled=True),
        lax.all_gather(self_gain, BOTH, axis=0, tiled=True),
        lax.all_gather(self_shift, BOTH, axis=0, tiled=True),
        lax.all_gather(cross_gain, BOTH, axis=0, tiled=True),
        lax.all_gather(cross_shift, BOTH, axis=0, tiled=True),
        lax.all_gather(final_gain, BOTH, axis=0, tiled=True),
        lax.all_gather(final_shift, BOTH, axis=0, tiled=True),
        lax.all_gather(prefix_embed, BOTH, axis=1, tiled=True),
        lax.all_gather(prefix_inner, BOTH, axis=0, tiled=True),
        lax.all_gather(prefix_outer, BOTH, axis=1, tiled=True),
    )
    factor_one = gain_one.astype(jnp.float32)
    factor_two = gain_two.astype(jnp.float32)
    factor_three = gain_three.astype(jnp.float32)
    length = inputs.shape[0]
    width = inputs.shape[1]
    places = jnp.arange(length)
    causal = places[:, None] >= places[None, :]
    local_mask = (segments[:, None] == segments[None, :]) & causal
    prefix_mask = jnp.ones((length, PREFIX), jnp.bool_)
    cross_mask = segments[:, None] == memory_segments[None, :]
    tangent = jnp.tanh(matmul(embed_full, inner_full))
    tangent_low = tangent.astype(jnp.bfloat16)
    prefix_rows = matmul(tangent_low, outer_full).astype(jnp.bfloat16)
    prefix_keys = prefix_rows[:, :width]
    prefix_values = prefix_rows[:, width:]
    queries = matmul(inputs, query_one).astype(jnp.bfloat16)
    key_rows = matmul(inputs, key_one).astype(jnp.bfloat16)
    value_rows = matmul(inputs, value_one).astype(jnp.bfloat16)
    self_parts = ((prefix_keys, prefix_values, prefix_mask), (key_rows, value_rows, local_mask))
    attended, self_logsum = attend_forward(queries, self_parts)
    attended_low = attended.astype(jnp.bfloat16)
    first, normed_one, inverse_one = norm_forward(
        inputs.astype(jnp.float32) + matmul(attended_low, output_one),
        factor_one,
        shift_one.astype(jnp.float32),
    )
    first_low = first.astype(jnp.bfloat16)
    cross_queries = matmul(first_low, query_two).astype(jnp.bfloat16)
    cross_keys = matmul(memory, key_two).astype(jnp.bfloat16)
    cross_values = matmul(memory, value_two).astype(jnp.bfloat16)
    cross_parts = ((cross_keys, cross_values, cross_mask),)
    crossed, cross_logsum = attend_forward(cross_queries, cross_parts)
    crossed_low = crossed.astype(jnp.bfloat16)
    second, normed_two, inverse_two = norm_forward(
        first + matmul(crossed_low, output_two), factor_two, shift_two.astype(jnp.float32)
    )
    second_low = second.astype(jnp.bfloat16)
    feed_rows = lax.all_gather(second_low, WIDE, axis=0, tiled=True)
    hidden_pre = matmul(feed_rows, feed_in)
    hidden_low = jax.nn.gelu(hidden_pre, approximate=False).astype(jnp.bfloat16)
    feed_sum = lax.psum_scatter(
        matmul(hidden_low, feed_out), WIDE, scatter_dimension=0, tiled=True
    )
    adapt_rows = lax.all_gather(second_low, NARROW, axis=0, tiled=True)
    bottle_pre = matmul(adapt_rows, adapter_down)
    bottle_low = jax.nn.gelu(bottle_pre, approximate=False).astype(jnp.bfloat16)
    adapt_sum = lax.psum_scatter(
        matmul(bottle_low, adapter_up).astype(jnp.bfloat16),
        NARROW,
        scatter_dimension=0,
        tiled=True,
    ).astype(jnp.float32)
    branch = feed_sum + ADAPT_SCALE * adapt_sum
    result, normed_three, inverse_three = norm_forward(
        second + branch, factor_three, shift_three.astype(jnp.float32)
    )
    grad_branch, gain_three_grad, shift_three_grad = norm_backward(
        cotangent.astype(jnp.float32), normed_three, inverse_three, factor_three
    )
    branch_low = grad_branch.astype(jnp.bfloat16)
    branch_rows = lax.all_gather(branch_low, WIDE, axis=0, tiled=True)
    grad_hidden = right_product(branch_rows, feed_out)
    grad_pre = gelu_back(hidden_pre, grad_hidden).astype(jnp.bfloat16)
    grad_out_part = left_product(hidden_low, branch_rows)
    grad_in_part = left_product(feed_rows, grad_pre)
    grad_feed = lax.psum_scatter(
        right_product(grad_pre, feed_in), WIDE, scatter_dimension=0, tiled=True
    )
    feed_in_total, feed_out_total = (
        lax.psum_scatter(
            grad_in_part.astype(jnp.bfloat16), NARROW, scatter_dimension=0, tiled=True
        ).astype(jnp.float32),
        lax.psum_scatter(
            grad_out_part.astype(jnp.bfloat16), NARROW, scatter_dimension=1, tiled=True
        ).astype(jnp.float32),
    )
    branch_narrow = lax.all_gather(branch_low, NARROW, axis=0, tiled=True)
    grad_bottle = ADAPT_SCALE * right_product(branch_narrow, adapter_up)
    grad_bottle_pre = gelu_back(bottle_pre, grad_bottle).astype(jnp.bfloat16)
    grad_up_part = ADAPT_SCALE * left_product(bottle_low, branch_narrow)
    grad_down_part = left_product(adapt_rows, grad_bottle_pre)
    grad_adapt = lax.psum_scatter(
        right_product(grad_bottle_pre, adapter_down).astype(jnp.bfloat16),
        NARROW,
        scatter_dimension=0,
        tiled=True,
    ).astype(jnp.float32)
    down_total, up_total = (
        lax.psum_scatter(grad_down_part, WIDE, scatter_dimension=0, tiled=True),
        lax.psum_scatter(grad_up_part, WIDE, scatter_dimension=1, tiled=True),
    )
    grad_second = grad_branch + grad_feed + grad_adapt
    grad_mid, gain_two_grad, shift_two_grad = norm_backward(
        grad_second, normed_two, inverse_two, factor_two
    )
    mid_low = grad_mid.astype(jnp.bfloat16)
    output_two_grad = left_product(crossed_low, mid_low)
    crossed_grad = right_product(mid_low, output_two).astype(jnp.bfloat16)
    cross_query_grad, cross_results = attend_backward(
        cross_queries, cross_parts, cross_logsum, crossed_grad
    )
    cross_query_low = cross_query_grad.astype(jnp.bfloat16)
    cross_key_low = cross_results[0][0].astype(jnp.bfloat16)
    cross_value_low = cross_results[0][1].astype(jnp.bfloat16)
    query_two_grad = left_product(first_low, cross_query_low)
    key_two_grad = left_product(memory, cross_key_low)
    value_two_grad = left_product(memory, cross_value_low)
    memory_grad = (
        right_product(cross_key_low, key_two) + right_product(cross_value_low, value_two)
    ).astype(jnp.bfloat16)
    grad_first = grad_mid + right_product(cross_query_low, query_two)
    grad_start, gain_one_grad, shift_one_grad = norm_backward(
        grad_first, normed_one, inverse_one, factor_one
    )
    start_low = grad_start.astype(jnp.bfloat16)
    output_one_grad = left_product(attended_low, start_low)
    attended_grad = right_product(start_low, output_one).astype(jnp.bfloat16)
    self_query_grad, self_results = attend_backward(queries, self_parts, self_logsum, attended_grad)
    self_query_low = self_query_grad.astype(jnp.bfloat16)
    self_key_low = self_results[1][0].astype(jnp.bfloat16)
    self_value_low = self_results[1][1].astype(jnp.bfloat16)
    query_one_grad = left_product(inputs, self_query_low)
    key_one_grad = left_product(inputs, self_key_low)
    value_one_grad = left_product(inputs, self_value_low)
    inputs_grad = (
        grad_start
        + right_product(self_query_low, query_one)
        + right_product(self_key_low, key_one)
        + right_product(self_value_low, value_one)
    ).astype(jnp.bfloat16)
    prefix_grad = jnp.concatenate([self_results[0][0], self_results[0][1]], axis=1)
    outer_grad = exact_left(tangent_low.astype(jnp.float32), prefix_grad)
    tangent_grad = exact_right(prefix_grad, outer_full.astype(jnp.float32)) * (
        1.0 - tangent * tangent
    )
    inner_grad = exact_left(embed_full.astype(jnp.float32), tangent_grad)
    embed_grad = exact_right(tangent_grad, inner_full.astype(jnp.float32))
    (
        query_one_sum,
        key_one_sum,
        value_one_sum,
        output_one_sum,
        query_two_sum,
        key_two_sum,
        value_two_sum,
        output_two_sum,
        gain_one_sum,
        shift_one_sum,
        gain_two_sum,
        shift_two_sum,
        gain_three_sum,
        shift_three_sum,
        embed_sum,
        inner_sum,
        outer_sum,
    ) = (
        lax.psum_scatter(query_one_grad, BOTH, scatter_dimension=0, tiled=True),
        lax.psum_scatter(key_one_grad, BOTH, scatter_dimension=0, tiled=True),
        lax.psum_scatter(value_one_grad, BOTH, scatter_dimension=0, tiled=True),
        lax.psum_scatter(output_one_grad, BOTH, scatter_dimension=0, tiled=True),
        lax.psum_scatter(query_two_grad, BOTH, scatter_dimension=0, tiled=True),
        lax.psum_scatter(key_two_grad, BOTH, scatter_dimension=0, tiled=True),
        lax.psum_scatter(value_two_grad, BOTH, scatter_dimension=0, tiled=True),
        lax.psum_scatter(output_two_grad, BOTH, scatter_dimension=0, tiled=True),
        lax.psum_scatter(gain_one_grad, BOTH, scatter_dimension=0, tiled=True),
        lax.psum_scatter(shift_one_grad, BOTH, scatter_dimension=0, tiled=True),
        lax.psum_scatter(gain_two_grad, BOTH, scatter_dimension=0, tiled=True),
        lax.psum_scatter(shift_two_grad, BOTH, scatter_dimension=0, tiled=True),
        lax.psum_scatter(gain_three_grad, BOTH, scatter_dimension=0, tiled=True),
        lax.psum_scatter(shift_three_grad, BOTH, scatter_dimension=0, tiled=True),
        lax.psum_scatter(embed_grad, BOTH, scatter_dimension=1, tiled=True),
        lax.psum_scatter(inner_grad, BOTH, scatter_dimension=0, tiled=True),
        lax.psum_scatter(outer_grad, BOTH, scatter_dimension=1, tiled=True),
    )
    return (
        result.astype(jnp.bfloat16),
        inputs_grad,
        memory_grad,
        query_one_sum,
        key_one_sum,
        value_one_sum,
        output_one_sum,
        query_two_sum,
        key_two_sum,
        value_two_sum,
        output_two_sum,
        gain_one_sum,
        shift_one_sum,
        gain_two_sum,
        shift_two_sum,
        gain_three_sum,
        shift_three_sum,
        feed_in_total,
        feed_out_total,
        down_total,
        up_total,
        embed_sum,
        inner_sum,
        outer_sum,
    )


def place():
    w = lax.axis_index(WIDE); n = lax.axis_index(NARROW)
    return w // 2, w % 2, n // 2, n % 2

def device(a, b, x, c):
    return (a * 2 + b, x * 2 + c)

def greet(peers):
    barrier = pltpu.get_barrier_semaphore()
    for p in peers:
        pl.semaphore_signal(barrier, inc=1, device_id=p, device_id_type=MESH)
    pl.semaphore_wait(barrier, len(peers))

def remote(src, dst, send, recv, dev):
    return pltpu.make_async_remote_copy(src_ref=src, dst_ref=dst, send_sem=send, recv_sem=recv, device_id=dev, device_id_type=MESH)


def dot_left(l, r):
    return lax.dot_general(l, r, (((0,), (0,)), ((), ())), preferred_element_type=f32)

class Copies:
    def __init__(self, send, recv):
        self.send, self.recv, self.count, self.all = send, recv, 0, []
    def __call__(self, src, dst, dev):
        cp = remote(src, dst, self.send.at[self.count], self.recv.at[self.count], dev)
        self.count += 1
        cp.start(); self.all.append(cp)
        return cp
    def local(self, src, dst):
        cp = pltpu.make_async_copy(src, dst, self.send.at[self.count])
        self.count += 1
        cp.start()
        return cp
    def sent(self, some):
        for cp in some:
            cp.wait_send()
            self.all = [o for o in self.all if o is not cp]
    def close(self):
        for cp in self.all: cp.wait_send()


EPSILON = 1e-05
ADAPT_SCALE = 4.0

def dot(l, r):
    return jnp.dot(l, r, preferred_element_type=f32)

def dot_right(l, r):
    return lax.dot_general(l, r, (((1,), (1,)), ((), ())), preferred_element_type=f32)

def gelu_both(v):
    phi = 0.5 + 0.5 * lax.erf(v * 0.7071067811865476)
    return v * phi, phi + v * (0.3989422804014327 * jnp.exp(-0.5 * v * v))

def norm(v):
    center = v - jnp.mean(v, axis=-1, keepdims=True)
    inverse = lax.rsqrt(jnp.mean(center * center, axis=-1, keepdims=True) + EPSILON)
    return center * inverse, inverse

def norm_back(e, n, inverse, factor):
    s = e * factor
    return inverse * (s - jnp.mean(s, axis=-1, keepdims=True) - n * jnp.mean(s * n, axis=-1, keepdims=True))

def feed_kernel(A, second, cot, fin_own, fout_own, fin_two, fout_two, down_ref, up_ref, gain, shift, inputs_h, memory_h, att_h, flow_h, crossed_h,
                result, gsec, fi_out, fo_out, ay, blow, ngrad, xp0, xatt, xin, xmem, inputs, memory, att, flow, crossed, fin, fout, fi, fo, down, up, rows, brow, hid, slope, gpre, part, q1, q2, q3, bslope, acc, ssem, rsem):
    a, b, x, c = place()
    o = 1 - c
    yp = device(a, 1 - b, x, c)
    zp = device((a + A // 2) % A, b, x, c)
    core, xp, dp = device(a, b, x, o), device(a, b, 1 - x, c), device(a, b, 1 - x, o)
    cp = Copies(ssem, rsem)
    half = fin_own.shape[1]
    lo, hi = pl.ds(0, half), pl.ds(half, half)
    loads = [cp.local(fin_own, fin.at[:, lo]), cp.local(fin_two, fin.at[:, hi]), cp.local(fout_own, fout.at[lo]), cp.local(fout_two, fout.at[hi])]
    staged = [cp.local(src, dst) for src, dst in ((inputs_h, inputs), (memory_h, memory), (att_h, att), (flow_h, flow), (crossed_h, crossed))]
    greet([yp, zp, core, xp, dp])
    T, D = second.shape
    NC = 4
    R = T // NC
    HID = fin.shape[1]; TW = 256
    NT = D // TW

    def spread(buf):
        zs, ys = [], []
        for q in range(NC):
            s = pl.ds(q * R, R)
            zs.append(cp(buf.at[0, s], buf.at[2, s], zp))
            ys.append(cp(buf.at[0, s], buf.at[1, s], yp))
        passed = []
        def forward(q):
            s = pl.ds(q * R, R)
            zs[q].wait_recv()
            passed.append(cp(buf.at[2, s], buf.at[3, s], yp))
        return ys, forward, passed

    sums = {}
    def collect(level, between):
        between()
        p2 = []
        for t in range(NT):
            sums[level, 3, t].wait_recv()
            part[2, t] = part[2, t] + q3[level, t]
            p2.append(cp(part.at[2, t], q2.at[level, t], zp))
        return p2

    def send_part(level, j, t):
        sums[level, j, t] = cp(part.at[j, t], (q3 if j == 3 else q1).at[level, t], yp)

    def gather_up(level, p2):
        for t in range(NT):
            cols = pl.ds(t * TW, TW)
            sums[level, 1, t].wait_recv(); p2[t].wait_recv()
            acc[:, cols] = acc[:, cols] + q1[level, t].astype(f32) + q2[level, t].astype(f32)
        cp.sent(p2 + [sums[level, j, t] for j in (1, 3) for t in range(NT)])

    rows[0] = second[...].astype(bf16)
    ys, forward, fw = spread(rows)
    AD = down_ref.shape[1]
    n = x * 2 + c
    nd = pl.ds(pl.multiple_of(n * AD, AD), AD)
    md = pl.ds(pl.multiple_of((2 - 2 * x + c) * AD, AD), AD)
    kept, late = [cp.local(down_ref, down.at[:, nd]), cp.local(up_ref, up.at[nd])], []
    over = [cp(down_ref, down.at[:, nd], xp), cp(up_ref, up.at[nd], xp)]
    near = [cp(down_ref, down.at[:, nd], core), cp(up_ref, up.at[nd], core)]
    def rowsn(ref, m, place): return ref.at[pl.ds(pl.multiple_of(place * m, m), m)]
    def fan(srcs, dst, only=False):
        k = cp.count
        cp.count += 4
        def start(me):
            own, other = srcs[me], srcs[1 - me]
            if own is not None:
                pltpu.make_async_copy(own, rowsn(dst, T, n), ssem.at[k]).start()
                remote(own, rowsn(dst, T, n), ssem.at[k + 1], rsem.at[k + 1], xp).start()
            if other is not None:
                remote(other, rowsn(dst, T, n), ssem.at[k + 2], rsem.at[k + 2], core).start()
                remote(other, rowsn(dst, T, n), ssem.at[k + 3], rsem.at[k + 3], dp).start()
        def finish(me):
            own, other = srcs[me], srcs[1 - me]
            src = own if own is not None else other
            ways = [remote(src, rowsn(dst, T, n), ssem.at[k + i], rsem.at[k + i], d) for i, d in ((1, xp), (2, core), (3, dp))]
            if own is not None:
                pltpu.make_async_copy(own, rowsn(dst, T, n), ssem.at[k]).wait()
                ways[0].wait_send()
                for e in ways: e.wait_recv()
            if other is not None:
                ways[1].wait_send(); ways[2].wait_send()
        pl.when(c == 0)(functools.partial(start, 0))
        pl.when(c == 1)(functools.partial(start, 1))
        def done():
            pl.when(c == 0)(functools.partial(finish, 0))
            pl.when(c == 1)(functools.partial(finish, 1))
        return done
    for e in staged: e.wait()
    fans = [fan((crossed, flow), xp0), fan((att, None), xatt)]
    M = memory.shape[0]
    share = []
    for src, dst, m in ((inputs, xin, T), (memory, xmem, M)):
        kept.append(cp.local(src, rowsn(dst, m, n)))
        near.append(cp(src, rowsn(dst, m, n), core))
        share.append((cp(src, rowsn(dst, m, n), xp), rowsn(dst, m, 2 - 2 * x + c)))
    def adapter_weights():
        kept[0].wait(); kept[1].wait()
        for e, ref in zip(over, (down.at[:, md], up.at[md])):
            e.wait_recv()
            late.append(cp(ref, ref, core))
        near[0].wait_recv(); near[1].wait_recv()
        for e in late[:2]: e.wait_recv()
    def share_on():
        for e, ref in share:
            e.wait_recv()
            late.append(cp(ref, ref, core))
    def adapter_forward():
        for t in range(2):
            cols = pl.ds(t * 256, 256)
            g, s = gelu_both(dot(rows[0], down[:, cols]))
            ay[1, :, cols] = (ADAPT_SCALE * g.astype(bf16).astype(f32)).astype(bf16)
            bslope[:, cols] = s
        def tile(t, _):
            cols = pl.ds(pl.multiple_of(t * 256, 256), 256)
            acc[:, cols] = acc[:, cols] + dot(ay[1], up[:, cols])
            return 0
        lax.fori_loop(0, D // 256, tile, 0)
    def adapter_back():
        def tile(t, _):
            cols = pl.ds(pl.multiple_of(t * 256, 256), 256)
            gbot = bslope[:, cols] * (ADAPT_SCALE * dot_right(brow[0], up[cols, :]))
            ay[0, :, cols] = gbot.astype(bf16)
            return 0
        lax.fori_loop(0, down.shape[1] // 256, tile, 0)
        def tile2(t, _):
            cols = pl.ds(pl.multiple_of(t * 256, 256), 256)
            acc[:, cols] = acc[:, cols] + dot_right(ay[0], down[cols, :])
            return 0
        lax.fori_loop(0, D // 256, tile2, 0)
    def enter(j):
        def tile(t, _):
            cols = pl.ds(pl.multiple_of(t * TW, TW), TW)
            g, s = gelu_both(dot(rows[j], fin[:, cols]))
            hid[j, :, cols] = g.astype(bf16)
            slope[j, :, cols] = s
            return 0
        lax.fori_loop(0, HID // TW, tile, 0)
        for t in range(NT):
            cols = pl.ds(t * TW, TW)
            p = dot(hid[j], fout[:, cols])
            if j == 0:
                acc[:, cols] = p
            else:
                part[j, t] = p.astype(bf16)
                if j != 2: send_part(0, j, t)
    for e in loads: e.wait()
    enter(0)
    for q in ys: q.wait_recv()
    forward(0); forward(1)
    enter(1)
    forward(2); forward(3)
    enter(2)
    for q in fw: q.wait_recv()
    enter(3)
    def between():
        adapter_weights()
        adapter_forward()
    p2 = collect(0, between)
    gather_up(0, p2)
    n3, inv3 = norm(second[...] + acc[...])
    fac = gain[...].astype(f32)
    result[...] = (n3 * fac + shift[...].astype(f32)).astype(bf16)
    e = cot[...].astype(f32)
    gb = norm_back(e, n3, inv3, fac)
    gbl = gb.astype(bf16)
    brow[0] = gbl
    ys, forward, fw = spread(brow)
    blow[...] = gbl
    acc[...] = gb
    ngrad[0:1, :] = jnp.sum(e * n3, axis=0, keepdims=True)
    ngrad[1:2, :] = jnp.sum(e, axis=0, keepdims=True)
    def leave(j):
        def tile(t, _):
            cols = pl.ds(pl.multiple_of(t * TW, TW), TW)
            gh = dot_right(brow[j], fout[cols, :])
            gpre[j, :, cols] = (slope[j, :, cols] * gh).astype(bf16)
            return 0
        lax.fori_loop(0, HID // TW, tile, 0)
        for t in range(NT):
            cols = pl.ds(t * TW, TW)
            p = dot_right(gpre[j], fin[cols, :])
            if j == 0:
                acc[:, cols] = acc[:, cols] + p
            else:
                part[j, t] = p.astype(bf16)
                if j != 2: send_part(1, j, t)
    leave(0)
    for q in ys: q.wait_recv()
    forward(0); forward(1)
    leave(1)
    forward(2); forward(3)
    leave(2)
    for q in fw: q.wait_recv()
    leave(3)
    p2 = collect(1, adapter_back)
    def wtile(t, _):
        cols = pl.ds(pl.multiple_of(t * TW, TW), TW)
        fi[:, cols] = dot_left(rows[...].reshape(4 * T, D), gpre[:, :, cols].reshape(4 * T, TW)).astype(bf16)
        fo[:, cols] = dot_left(hid[...].reshape(4 * T, HID), brow[:, :, cols].reshape(4 * T, TW)).astype(bf16)
        return 0
    lax.fori_loop(0, HID // TW, wtile, 0)
    kept += [cp.local(fi, fi_out), cp.local(fo, fo_out)]
    share_on()
    gather_up(1, p2)
    gsec[...] = acc[...]
    for e in kept[2:]: e.wait()
    for e in near[2:] + late[2:]: e.wait_recv()
    for e in fans: e()
    cp.close()

def feed(A, second, cot, fin, fout, fin2, fout2, down, up, gain, shift, inputs, memory, att, flow, crossed):
    T, D = second.shape; HID = 2 * fin.shape[1]; AD = down.shape[1] * 4; M = memory.shape[0]
    v = lambda *s: pltpu.VMEM(s, bf16)
    vf = lambda *s: pltpu.VMEM(s, f32)
    vm = pl.BlockSpec(memory_space=pltpu.VMEM)
    any_ = pl.BlockSpec(memory_space=pl.ANY)
    sds = jax.ShapeDtypeStruct
    four = sds((4 * T, D), bf16)
    return pl.pallas_call(
        functools.partial(feed_kernel, A),
        out_shape=(sds((T, D), bf16), sds((T, D), f32), sds((D, HID), bf16), sds((HID, D), bf16), sds((2, T, AD), bf16), sds((T, D), bf16), sds((2, D), f32),
            four, four, four, sds((4 * M, D), bf16)),
        in_specs=[vm] * 2 + [any_] * 6 + [vm] * 2 + [any_] * 5, out_specs=(vm,) * 2 + (any_,) * 2 + (vm,) * 3 + (any_,) * 4,
        scratch_shapes=[v(T, D), v(M, D), v(T, D), v(T, D), v(T, D), v(D, HID), v(HID, D), v(D, HID), v(HID, D), v(D, AD), v(AD, D), v(4, T, D), v(4, T, D), v(4, T, HID), vf(4, T, HID), v(4, T, HID), v(4, D // 256, T, 256),
            v(2, D // 256, T, 256), v(2, D // 256, T, 256), v(2, D // 256, T, 256), vf(T, AD), vf(T, D),
            pltpu.SemaphoreType.DMA((128,)), pltpu.SemaphoreType.DMA((128,))],
        compiler_params=pltpu.CompilerParams(collective_id=3, has_side_effects=True, vmem_limit_bytes=60 << 20),
        name="feed_forward")(second, cot, fin, fout, fin2, fout2, down, up, gain, shift, inputs, memory, att, flow, crossed)


NEGATIVE = -1000000000.0
PADDED = 32

def project(x, weight, out, tile=256):
    def step(t, _):
        cols = pl.ds(pl.multiple_of(t * tile, tile), tile)
        out[:, cols] = dot(x[...], weight[:, cols]).astype(out.dtype)
        return 0
    lax.fori_loop(0, out.shape[1] // tile, step, 0)


def lane_half(rows):
    return lax.broadcasted_iota(jnp.int32, (rows, 128), 1) < 64

def split_heads(v):
    low = lane_half(v.shape[0])
    zero = jnp.zeros_like(v)
    return jnp.where(low, v, zero), jnp.where(low, zero, v)

def self_mask(seg_col, seg_row):
    T = seg_col.shape[0]
    row = lax.broadcasted_iota(jnp.int32, (T, T), 0)
    col = lax.broadcasted_iota(jnp.int32, (T, T), 1)
    own = jnp.where((row >= col) & (seg_col[...] == seg_row[...]), 0.0, NEGATIVE)
    lane = lax.broadcasted_iota(jnp.int32, (T, PADDED), 1)
    return jnp.concatenate([own, jnp.where(lane < 30, 0.0, NEGATIVE)], axis=1)

def attend(q, keys, values, penalty, probs, out, pairs=8):
    def step(p, _):
        cols = pl.ds(pl.multiple_of(p * 128, 128), 128)
        kk, vv = keys(cols), values(cols)
        qs = split_heads(q[:, cols])
        vs = split_heads(vv)
        total = None
        for s in range(2):
            score = jnp.where(penalty[...] < -1.0, NEGATIVE, dot_right(qs[s], kk) * 0.125)
            e = jnp.exp(score - jnp.max(score, axis=-1, keepdims=True))
            prob = (e * (1.0 / jnp.sum(e, axis=-1, keepdims=True))).astype(bf16)
            probs[2 * p + s] = prob
            mixed = dot(prob, vs[s])
            total = mixed if total is None else total + mixed
        out[:, cols] = total.astype(bf16)
        return 0
    lax.fori_loop(0, pairs, step, 0)


def both_keys(own, prows, offset):
    def get(cols):
        shifted = pl.ds(pl.multiple_of(cols.start + offset, 128), 128)
        return jnp.concatenate([own[:, cols], prows[:, shifted]], axis=0)
    return get

def whole(ref):
    return lambda cols: ref[:, cols]

def add_norm(base, low, weight, gain, shift, out, normed, inverse, tile=256):
    def step(t, _):
        cols = pl.ds(pl.multiple_of(t * tile, tile), tile)
        out[:, cols] = base[:, cols].astype(f32) + dot(low[...], weight[:, cols])
        return 0
    lax.fori_loop(0, out.shape[1] // tile, step, 0)
    n, i = norm(out[...])
    normed[...] = n
    inverse[...] = i
    out[...] = n * gain + shift

def forward_kernel(inputs, memory, seg_col, seg_row, mem_row, weights, prows, vecs,
                   q, k, v, probs, attended, first, n1, i1, cq, ck, cv, cprobs, crossed, second, n2, i2, pen, cpen):
    width = inputs.shape[1]
    pen[...] = self_mask(seg_col, seg_row)
    cpen[...] = jnp.where(seg_col[...] == mem_row[...], 0.0, NEGATIVE)
    project(inputs, weights.at[0], q); project(inputs, weights.at[1], k); project(inputs, weights.at[2], v)
    project(memory, weights.at[6], ck); project(memory, weights.at[7], cv)
    attend(q, both_keys(k, prows, 0), both_keys(v, prows, width), pen, probs, attended)
    add_norm(inputs, attended, weights.at[3], vecs[0:1, :], vecs[1:2, :], first, n1, i1)
    q[...] = q[...]
    def step(t, _):
        cols = pl.ds(pl.multiple_of(t * 256, 256), 256)
        cq[:, cols] = dot(first[...].astype(bf16), weights[4, :, cols]).astype(bf16)
        return 0
    lax.fori_loop(0, width // 256, step, 0)
    attend(cq, whole(ck), whole(cv), cpen, cprobs, crossed)
    add_norm(first, crossed, weights.at[5], vecs[2:3, :], vecs[3:4, :], second, n2, i2)

def forward(inputs, memory, seg_col, seg_row, mem_row, weights, prows, vecs):
    T, D = inputs.shape; M = memory.shape[0]
    vm = pl.BlockSpec(memory_space=pltpu.VMEM)
    sds = jax.ShapeDtypeStruct
    row, mrow, full, one = sds((T, D), bf16), sds((M, D), bf16), sds((T, D), f32), sds((T, 1), f32)
    return pl.pallas_call(forward_kernel,
        out_shape=(row, row, row, sds((16, T, T + PADDED), bf16), row, full, full, one, row, mrow, mrow, sds((16, T, M), bf16), row, full, full, one),
        in_specs=[vm] * 8, out_specs=(vm,) * 16,
        scratch_shapes=[pltpu.VMEM((T, T + PADDED), f32), pltpu.VMEM((T, M), f32)],
        compiler_params=pltpu.CompilerParams(vmem_limit_bytes=60 << 20), name="attention_forward")(
            inputs, memory, seg_col, seg_row, mem_row, weights, prows, vecs)

def norm_back_into(e, n, i, gain, out, ngrad, at):
    ee = e[...]
    nn = n[...]
    out[...] = norm_back(ee, nn, i[...], gain)
    ngrad[at:at + 1, :] = jnp.sum(ee * nn, axis=0, keepdims=True)
    ngrad[at + 1:at + 2, :] = jnp.sum(ee, axis=0, keepdims=True)


def repeat(n):
    row = lax.broadcasted_iota(jnp.int32, (n, 128), 0)
    col = lax.broadcasted_iota(jnp.int32, (n, 128), 1)
    return jnp.where(row == lax.rem(col, n), 1.0, 0.0).astype(bf16)

def columns(t, tile=256):
    return pl.ds(pl.multiple_of(t * tile, tile), tile)

def loop(start, stop, step):
    lax.fori_loop(start, stop, lambda t, z: (step(t), z)[1], 0)

def front_kernel(A, r, inputs, memory, seg_row, mem_row, embed, inner, outer, norms, *refs):
    ws, (fin, fout) = refs[:8], refs[8:10]
    (wout, fin2, fout2, tangent, prows_o, vecs_o, q_o, k_o, v_o, probs_o, att_o, first_o, n1_o, i1_o, cq_o, ck_o, cv_o, cprobs_o, crossed_o,
     second_o, slow_o, n2_o, i2_o) = refs[10:33]
    (g, q, k, v, probs, att, first, flow, n1, i1, cq, ck, cv, cprobs, crossed, second, slow, n2, i2, pen, cpen,
     buf, got, zbuf, r0, r1, prows, nout, vecs, tan, ssem, rsem) = refs[33:]
    a, b, x, c = place()
    core, xp, yp = device(a, b, x, 1 - c), device(a, b, 1 - x, c), device(a, 1 - b, x, c)
    zp = [device((a + j) % A, b, x, c) for j in range(A)]
    za = a + 1 - 2 * (a % 2)
    zq = device(za, b, x, c)
    greet([core, xp, yp] + zp[1:])
    cp = Copies(ssem, rsem)
    T, D = inputs.shape
    pairs = 4
    small = {}
    def pre0():
        zbuf[a] = jnp.zeros(zbuf.shape[1:], f32)
        zbuf[a, :PREFIX, :] = dot(embed[...], inner[...])
        small["s"] = [cp(zbuf.at[a], zbuf.at[a], zp[j]) for j in range(1, A)]
    pre0()
    def row(a_, b_, x_):
        return pl.multiple_of(((a_ * 2 + b_) * 2 + x_) * 2 * r, 2 * r)
    at = pl.ds(pl.multiple_of(row(a, b, x) + c * r, r), r)
    cut = (pl.ds(0, D // 2), pl.ds(D // 2, D // 2))
    def block(i, h, a_, b_, x_):
        return g.at[2 * i + c, pl.ds(row(a_, b_, x_), 2 * r), cut[h]]
    kept = []
    own, cross = [], []
    base = cp.count
    for i in range(pairs):
        s1, s2, rr = ssem.at[cp.count], ssem.at[cp.count + 1], rsem.at[cp.count]
        cp.count += 2
        def start(keep, give):
            pltpu.make_async_copy(ws[2 * i + keep], g.at[2 * i + keep, at], s2).start()
            remote(ws[2 * i + give], g.at[2 * i + give, at], s1, rr, core).start()
        pl.when(c == 0)(functools.partial(start, 0, 1))
        pl.when(c == 1)(functools.partial(start, 1, 0))
        own.append(pltpu.make_async_copy(ws[2 * i], g.at[2 * i, at], s2))
        cross.append(remote(ws[2 * i], g.at[2 * i, at], s1, rr, core))
    G = norms.shape[0]
    me = ((a * 2 + b) * 2 + x) * 2 + c
    chip = (a * 2 + b) * 2 + x
    def nrows(start, count): return nout.at[pl.ds(pl.multiple_of(start * G, G), count * G)]
    def lanes(start, count): return prows.at[:, pl.ds(pl.multiple_of(start * 128, 128), count * 128)]
    nout[pl.ds(pl.multiple_of(me * G, G), G), :] = dot(norms[...], repeat(norms.shape[1])).astype(bf16)
    peers = (core, xp, yp)
    def settle():
        for e in small["s"]: e.wait_recv()
    def pre1():
        settle()
        t = zbuf[0]
        for n in range(1, A): t = t + zbuf[n]
        buf[0] = t
        small["s"] = [cp(buf.at[0], got.at[0], core)]
    def pre2(n):
        def go():
            settle()
            buf[n] = buf[n - 1] + got[n - 1]
            small["s"] = [cp(buf.at[n], got.at[n], peers[n])]
        return go
    def pre4():
        settle()
        t = jnp.tanh(buf[2] + got[2])
        tan[...] = t
        r0[...] = dot(dot_right(t.astype(bf16), outer[...]).astype(bf16), repeat(outer.shape[0])).astype(bf16)
        small["s"] = [cp(r0, r1, core), cp(nrows(me, 1), nrows(me, 1), core)]
        kept.append(cp.local(tan, tangent))
    def pre5():
        settle()
        lane = lax.broadcasted_iota(jnp.int32, (PADDED, 128), 1)
        prows[:, pl.ds(pl.multiple_of(chip * 128, 128), 128)] = jnp.where((lane // 64) == c, r0[...].astype(f32), r1[...].astype(f32)).astype(bf16)
        small["s"] = [cp(lanes(chip, 1), lanes(chip, 1), xp), cp(nrows(me - c, 2), nrows(me - c, 2), xp)]
    def pre6():
        settle()
        small["s"] = [cp(lanes(chip - x, 2), lanes(chip - x, 2), yp), cp(nrows(me - c - 2 * x, 4), nrows(me - c - 2 * x, 4), yp)]
    def pre7():
        settle()
        small["s"] = [cp(lanes(a * 4, 4), lanes(a * 4, 4), zp[j]) for j in range(1, A)] + [cp(nrows(a * 8, 8), nrows(a * 8, 8), zp[j]) for j in range(1, A)]
    def pre8():
        settle()
        lane = lax.broadcasted_iota(jnp.int32, (G, 128), 1) // 32
        for w in range(2 * A):
            s = nout[pl.ds(w * 4 * G, G), :].astype(f32)
            for n in range(1, 4):
                s = jnp.where(lane == n, nout[pl.ds((w * 4 + n) * G, G), :].astype(f32), s)
            vecs[:, pl.ds(w * 128, 128)] = s[:8]
        kept.append(cp.local(vecs, vecs_o))
        kept.append(cp.local(prows, prows_o))
    H = fin.shape[1]
    feeds, passed = {}, []
    def feed_send(i):
        n = D // 8
        ri = pl.ds(pl.multiple_of(c * (D // 2) + i * n, n), n)
        m = H // 8
        ro = pl.ds(pl.multiple_of(c * (H // 2) + i * m, m), m)
        feeds[i] = [(cp(fin.at[ri], fin2.at[ri], zq), fin2.at[ri]),
                    (cp(fout.at[ro], fout2.at[ro], zq), fout2.at[ro])]
    def feed_pass(i):
        for e, ref in feeds[i]:
            e.wait_recv()
            passed.append(cp(ref, ref, core))
    zc, mc, lc, dc = {}, {}, {}, {}
    two, three = (yp, xp), (xp, yp)
    def first_send(i):
        own[i].wait(); cross[i].wait()
        for h in range(2):
            mc[i, h, 0] = cp(block(i, h, a, b, x), block(i, h, a, b, x), two[h])
        for h in range(2):
            lc[i, h, 0, 0] = cp(block(i, h, a, b, x), block(i, h, a, b, x), three[h])
        for j in range(1, A):
            for h in range(2):
                zc[i, h, j] = cp(block(i, h, a, b, x), block(i, h, a, b, x), zp[j])
    def mid(i, j):
        aj = (a + A - j) % A
        for h in range(2):
            zc[i, h, j].wait_recv()
            mc[i, h, j] = cp(block(i, h, aj, b, x), block(i, h, aj, b, x), two[h])
        for h in range(2):
            lc[i, h, j, 0] = cp(block(i, h, aj, b, x), block(i, h, aj, b, x), three[h])
    def third(i, j):
        aj = (a + A - j) % A
        for h in range(2):
            w = (aj, 1 - b, x) if h == 0 else (aj, b, 1 - x)
            mc[i, h, j].wait_recv()
            lc[i, h, j, 1] = cp(block(i, h, *w), block(i, h, *w), three[h])
    per = D // A
    def finish(i, j):
        aj = (a + A - j) % A
        for h in range(2):
            lc[i, h, j, 0].wait_recv(); lc[i, h, j, 1].wait_recv()
        ref = g.at[2 * i + c, pl.ds(pl.multiple_of(aj * per, per), per)]
        dc[i, j] = cp(ref, ref, core)
    def arrive(i):
        for j in range(A): dc[i, j].wait_recv()
        kept.append(cp.local(g.at[2 * i], wout.at[2 * i]))
        kept.append(cp.local(g.at[2 * i + 1], wout.at[2 * i + 1]))
    def halves(src, w, out):
        def part(n):
            def go():
                xv = src[...]
                def step(t):
                    out[:, columns(t)] = dot(xv, g[w, :, columns(t)]).astype(bf16)
                loop(2 * n, 2 * n + 2, step)
            return go
        return [part(0), part(1)]
    def keep(src, dst):
        def go(): kept.append(cp.local(src, dst))
        return go
    def masks():
        row = lax.broadcasted_iota(jnp.int32, (T, T), 0)
        col = lax.broadcasted_iota(jnp.int32, (T, T), 1)
        across = jnp.broadcast_to(seg_row[...].astype(f32), (T, T))
        down = across.T
        pen[:, :T] = jnp.where((row >= col) & (down == across), 0.0, NEGATIVE)
        lane = lax.broadcasted_iota(jnp.int32, (T, PADDED), 1)
        pen[:, T:] = jnp.where(lane < PREFIX, 0.0, NEGATIVE)
        for n in range(memory.shape[0] // T):
            span = slice(n * T, (n + 1) * T)
            cpen[:, span] = jnp.where(down == mem_row[:, span].astype(f32), 0.0, NEGATIVE)
    def softmax(qv, kk, penalty):
        score = jnp.where(penalty[...] < -1.0, NEGATIVE, dot_right(qv, kk) * 0.125)
        e = jnp.exp(score - jnp.max(score, axis=-1, keepdims=True))
        return (e * (1.0 / jnp.sum(e, axis=-1, keepdims=True))).astype(bf16)
    def own_attend(n):
        def go():
            def step(p):
                cols = columns(p, 128)
                kk = jnp.concatenate([k[:, cols], prows[:, cols]], axis=0)
                vv = jnp.concatenate([v[:, cols], prows[:, pl.ds(pl.multiple_of(D + p * 128, 128), 128)]], axis=0)
                qs, vs = split_heads(q[:, cols]), split_heads(vv)
                total = None
                for s in range(2):
                    prob = softmax(qs[s], kk, pen)
                    probs[2 * p + s] = prob
                    m = dot(prob, vs[s])
                    total = m if total is None else total + m
                att[:, cols] = total.astype(bf16)
            loop(2 * n, 2 * n + 2, step)
        return go
    def cross_scores(n):
        def go():
            def step(p):
                cols = columns(p, 128)
                qs = split_heads(cq[:, cols])
                for s in range(2):
                    cprobs[2 * p + s] = softmax(qs[s], ck[:, cols], cpen)
            loop(2 * n, 2 * n + 2, step)
        return go
    def cross_mix(n):
        def go():
            def step(p):
                cols = columns(p, 128)
                vs = split_heads(cv[:, cols])
                crossed[:, cols] = (dot(cprobs[2 * p], vs[0]) + dot(cprobs[2 * p + 1], vs[1])).astype(bf16)
            loop(4 * n, 4 * n + 4, step)
        return go
    def normed(base, low, w, at, out, nn, ii, olow):
        def part(n):
            def go():
                lv = low[...]
                def step(t):
                    out[:, columns(t)] = base[:, columns(t)].astype(f32) + dot(lv, g[w, :, columns(t)])
                loop(2 * n, 2 * n + 2, step)
            return go
        def last():
            m, inv = norm(out[...])
            nn[...] = m
            ii[...] = inv
            s = m * vecs[at:at + 1, :] + vecs[at + 1:at + 2, :]
            out[...] = s
            olow[...] = s.astype(bf16)
        return [part(0), part(1), last]
    comp = {
        0: halves(inputs, 0, q) + halves(inputs, 1, k) + [keep(q, q_o), keep(k, k_o), masks],
        1: halves(inputs, 2, v) + [keep(v, v_o)] + [own_attend(n) for n in range(4)] + [keep(probs, probs_o), keep(att, att_o)]
           + normed(inputs, att, 3, 0, first, n1, i1, flow) + [keep(flow, first_o), keep(n1, n1_o), keep(i1, i1_o)],
        2: halves(memory, 4, ck) + [keep(ck, ck_o)] + halves(flow, 5, cq) + [keep(cq, cq_o)] + [cross_scores(n) for n in range(4)] + [keep(cprobs, cprobs_o)],
        3: halves(memory, 6, cv) + [keep(cv, cv_o)] + [cross_mix(n) for n in range(2)] + [keep(crossed, crossed_o)]
           + normed(first, crossed, 7, 2, second, n2, i2, slow) + [keep(second, second_o), keep(slow, slow_o), keep(n2, n2_o), keep(i2, i2_o)],
    }
    queue = []
    def turn(count=1):
        for _ in range(count):
            if queue: queue.pop(0)()
    small_steps = [pre1, pre2(1), pre2(2), pre4, pre5, pre6, pre7]
    def tick():
        if small_steps: small_steps.pop(0)()
    first_send(0)
    tick()
    for i in range(pairs):
        if i + 1 < pairs:
            first_send(i + 1)
        feed_send(i)
        third(i, 0)
        tick()
        turn()
        if i:
            finish(i - 1, 2)
            turn()
        mid(i, 1)
        tick()
        turn()
        if i:
            finish(i - 1, 3)
            turn()
        mid(i, 2)
        tick()
        turn()
        if i: feed_pass(i - 1)
        mid(i, 3)
        tick()
        turn()
        third(i, 1)
        if i:
            arrive(i - 1)
            if i == 2: pre8()
            queue += comp[i - 1]
        turn()
        finish(i, 0)
        turn(2)
        third(i, 2)
        turn(2)
        finish(i, 1)
        turn(2)
        third(i, 3)
        turn(2)
    feed_pass(3)
    finish(3, 2)
    turn(2)
    finish(3, 3)
    turn(100)
    arrive(3)
    queue += comp[3]
    turn(100)
    for e in kept: e.wait()
    for e in passed: e.wait_recv()
    own_ids = None
    cp.close()

def front(A, r, inputs, memory, seg_row, mem_row, embed, inner, outer, norms, ws, fin, fout):
    T, D = inputs.shape; M = memory.shape[0]; H = fin.shape[1]
    vm = pl.BlockSpec(memory_space=pltpu.VMEM)
    any_ = pl.BlockSpec(memory_space=pl.ANY)
    sds = jax.ShapeDtypeStruct
    v = lambda *s: pltpu.VMEM(s, bf16)
    vf = lambda *s: pltpu.VMEM(s, f32)
    row, mrow, full, one = sds((T, D), bf16), sds((M, D), bf16), sds((T, D), f32), sds((T, 1), f32)
    S = (PADDED, inner.shape[1])
    probs, cprobs = (16, T, T + PADDED), (16, T, M)
    return pl.pallas_call(functools.partial(front_kernel, A, r),
        out_shape=(sds((8, D, D), bf16), sds((D, H), bf16), sds((H, D), bf16),
            sds(S, f32), sds((PADDED, 2 * D), bf16), sds((8, D), f32), row, row, row, sds(probs, bf16), row, row, full, one, row, mrow, mrow, sds(cprobs, bf16), row,
            full, row, full, one),
        in_specs=[vm] * 8 + [any_] * 10, out_specs=(any_,) * 23,
        scratch_shapes=[v(8, D, D), v(T, D), v(T, D), v(T, D), v(*probs), v(T, D), vf(T, D), v(T, D), vf(T, D), vf(T, 1), v(T, D), v(M, D), v(M, D), v(*cprobs), v(T, D),
            vf(T, D), v(T, D), vf(T, D), vf(T, 1), vf(T, T + PADDED), vf(T, M),
            vf(3, *S), vf(3, *S), vf(A, *S), v(PADDED, 128), v(PADDED, 128), v(PADDED, 2 * D), v(8 * A * norms.shape[0], 128), vf(8, D), vf(*S),
            pltpu.SemaphoreType.DMA((320,)), pltpu.SemaphoreType.DMA((320,))],
        compiler_params=pltpu.CompilerParams(collective_id=1, has_side_effects=True, vmem_limit_bytes=60 << 20), name="front")(
            inputs, memory, seg_row, mem_row, embed, inner, outer, norms, *ws, fin, fout)


def exact(l, r, dims):
    return lax.dot_general(l, r, (dims, ((), ())), precision=lax.Precision.HIGHEST, preferred_element_type=f32)

def back_kernel(A, r, gsec, n2, i2, vecs, ngrad3, tangent, embed, inner, outer, *refs):
    late, (slow, blow, ay, weights, fi, fo, xp0, xatt, xin, xmem) = refs[:11], refs[11:21]
    back_body(A, r, gsec, n2, i2, vecs, ngrad3, tangent, embed, inner, outer, late, slow, blow, ay, weights, fi, fo, xp0, xatt, xin, xmem, *refs[21:])

def back_body(A, r, gsec, n2, i2, vecs, ngrad3, tangent, embed, inner, outer, late, slow, blow, ay, weights, fi, fo, xp0, xatt, xin, xmem,
                igrad_o, mgrad_o, out, aout, fi_out, fo_out, outer_o, inner_o, embed_o, nsum,
                igrad, mgrad, cq, ck, cv, cprobs, n1, i1, q, k, v, probs, prows, ws, gmid, gfirst, og, mid, dcq, dck, dcv, startl, dq, dk, dv, pg,
                xb, yb, mb, mby, axb, ayb, pb, apb, fib, fob, r1, r2, r3, sb, xs, ra1, ra2, ra3, rfi, rfo, rzi, rzo, rxi, rxo, ob, aob, fib2, fob2,
                buf, got, zbuf, nbuf, ngot, nz, w0, w1, w2, w3, s0, s1, s2, ssem, rsem):
    a, b, x, c = place()
    o = 1 - c
    core, xp, yp = device(a, b, x, o), device(a, b, 1 - x, c), device(a, 1 - b, x, c)
    dp = device(a, b, 1 - x, o)
    place_n = x * 2 + c
    zp = [device((a + j) % A, b, x, c) for j in range(A)]
    za = a + 1 - 2 * (a % 2)
    zq = device(za, b, x, c)
    peers = (core, xp, yp)
    T, D = gsec.shape
    M = xmem.shape[0] // 4
    HID = fi.shape[1] // 2
    Q = fi.shape[0] // 4
    half = D // 2
    cp = Copies(ssem, rsem)
    loads = {}
    def fetch(slot, w):
        loads[slot] = cp.local(weights.at[w], ws.at[slot])
    loaded = [cp.local(src, dst) for src, dst in zip(late, (cq, ck, cv, cprobs, n1, i1, q, k, v, probs, prows))]
    def ready(start, stop):
        for e in loaded[start:stop]: e.wait()
    fetch(0, 7); fetch(1, 5); fetch(2, 3); fetch(3, 4)
    fown = []
    for xx in range(2):
        dq_ = pl.ds(pl.multiple_of((xx * 2 + c) * Q, Q), Q)
        fown += [cp.local(fi.at[dq_, :], fib.at[xx]), cp.local(fo.at[:, dq_], fob.at[xx])]
    greet([core, xp, yp, dp] + zp[1:])
    def offer(srcs, mine, theirs):
        n = cp.count
        cp.count += 2
        def start(keep, give):
            pltpu.make_async_copy(srcs[keep], mine, ssem.at[n]).start()
            remote(srcs[give], theirs, ssem.at[n + 1], rsem.at[n], core).start()
        pl.when(c == 0)(functools.partial(start, 0, 1))
        pl.when(c == 1)(functools.partial(start, 1, 0))
        e = remote(srcs[0], theirs, ssem.at[n + 1], rsem.at[n], core)
        cp.all.append(e)
        return pltpu.make_async_copy(srcs[0], mine, ssem.at[n]).wait, e.wait_recv
    lowT, highT = pl.ds(0, T), pl.ds(T, T)
    waits = {}
    aw = offer((slow, blow), axb.at[lowT], axb.at[highT]) + offer((ay.at[0], ay.at[1]), ayb.at[lowT], ayb.at[highT])
    xload = cp.count
    cp.count += 4
    def load_x(me):
        pltpu.make_async_copy(xp0, xb.at[0], ssem.at[xload]).start()
        pltpu.make_async_copy(xmem, mb, ssem.at[xload + 1]).start()
        pltpu.make_async_copy(xin if me else xatt, xb.at[1], ssem.at[xload + 2]).start()
        pltpu.make_async_copy(xin, xb.at[2], ssem.at[xload + 3]).start()
    pl.when(c == 0)(functools.partial(load_x, 0))
    pl.when(c == 1)(functools.partial(load_x, 1))
    waits[0] = (pltpu.make_async_copy(xp0, xb.at[0], ssem.at[xload]).wait,)
    waits[1] = (pltpu.make_async_copy(xmem, mb, ssem.at[xload + 1]).wait,)
    waits[2] = (pltpu.make_async_copy(xin, xb.at[1], ssem.at[xload + 2]).wait,)
    waits[3] = (pltpu.make_async_copy(xin, xb.at[2], ssem.at[xload + 3]).wait,)
    def share(srcs, dst, t):
        m = srcs[0].shape[0]
        k = cp.count
        cp.count += 4
        wide = half // 2
        here = pl.ds(pl.multiple_of(x * half + t * wide, wide), wide)
        there = pl.ds(pl.multiple_of((1 - x) * half + t * wide, wide), wide)
        spot = dst.at[pl.ds(pl.multiple_of(place_n * m, m), m), pl.ds(t * wide, wide)]
        def start(me):
            own, other = srcs[me], srcs[1 - me]
            remote(own.at[:, there], spot, ssem.at[k + 1], rsem.at[k + 1], xp).start()
            remote(other.at[:, there], spot, ssem.at[k + 3], rsem.at[k + 3], dp).start()
            remote(other.at[:, here], spot, ssem.at[k + 2], rsem.at[k + 2], core).start()
            pltpu.make_async_copy(own.at[:, here], spot, ssem.at[k]).start()
        pl.when(c == 0)(functools.partial(start, 0))
        pl.when(c == 1)(functools.partial(start, 1))
        ways = [remote(srcs[0].at[:, here], spot, ssem.at[k + i], rsem.at[k + i], d) for i, d in ((1, xp), (2, core), (3, dp))]
        cp.all.extend(ways)
        return (pltpu.make_async_copy(srcs[0].at[:, here], spot, ssem.at[k]).wait,) + tuple(e.wait_recv for e in ways)
    fcopies = []
    for xx in range(2):
        dq_ = pl.ds(pl.multiple_of((xx * 2 + o) * Q, Q), Q)
        fcopies += [cp(fi.at[dq_, :], rfi.at[xx], core), cp(fo.at[:, dq_], rfo.at[xx], core)]

    zf, xf, outs = [], [], []
    def feed0():
        for e in fown: e.wait()
        for e in fcopies: e.wait_recv()
        for xx in range(2):
            def rows_fi(t):
                s = pl.ds(t * 32, 32)
                fib[xx, s, :] = fib[xx, s, :] + rfi[xx, s, :]
            loop(0, Q // 32, rows_fi)
            def rows_fo(t):
                s = pl.ds(t * 64, 64)
                fob[xx, s, :] = fob[xx, s, :] + rfo[xx, s, :]
            loop(0, 2 * HID // 64, rows_fo)
        zf.extend([cp(fib.at[:, :, pl.ds(HID, HID)], rzi, zq), cp(fob.at[:, pl.ds(HID, HID), :], rzo, zq)])
    def feed1():
        for e in zf: e.wait_recv()
        for xx in range(2):
            def rows_fi(t):
                s = pl.ds(t * 32, 32)
                fib[xx, s, pl.ds(0, HID)] = fib[xx, s, pl.ds(0, HID)] + rzi[xx, s, :]
            loop(0, Q // 32, rows_fi)
            def rows_fo(t):
                s = pl.ds(t * 64, 64)
                fob[xx, s, :] = fob[xx, s, :] + rzo[xx, s, :]
            loop(0, HID // 64, rows_fo)
        xf.extend([cp(fib.at[1 - x, :, pl.ds(0, HID)], rxi, xp), cp(fob.at[1 - x, pl.ds(0, HID), :], rxo, xp)])
    def feed2():
        for e in xf: e.wait_recv()
        def rows_fi(t):
            s = pl.ds(t * 32, 32)
            fib2[s, :] = fib[x, s, pl.ds(0, HID)].astype(f32) + rxi[s, :].astype(f32)
        loop(0, Q // 32, rows_fi)
        def rows_fo(t):
            s = pl.ds(t * 64, 64)
            fob2[s, :] = fob[x, s, :].astype(f32) + rxo[s, :].astype(f32)
        loop(0, HID // 64, rows_fo)
        outs.extend([cp.local(fib2, fi_out).wait, cp.local(fob2, fo_out).wait])

    first, second, third, fourth = {}, {}, {}, {}
    wide = half // 2
    numbers = {}
    for i in range(4):
        for t in range(2):
            numbers[i, t] = cp.count
            cp.count += 1
    def level1(i, t):
        n = numbers[i, t]
        return remote(pb.at[i, t, :, 1 - b], r1.at[i, t], ssem.at[n], rsem.at[n], yp)
    for i in range(4):
        for t in range(2):
            first[i, t] = level1(i, t)
            cp.all.append(first[i, t])
    def compute(i, t):
        if t == 0:
            for e in waits[i]: e()
        for e in shared[i, t]: e()
        cols = pl.ds(t * wide, wide)
        n = (0, None, 1, 2)[i]
        def rows(u):
            d = columns(u)
            p = dot_left(mb[:, d], mby[:, cols]) if i == 1 else dot_left(xb[n, :, d], yb[n, :, cols])
            pb[i, t, u] = p.astype(bf16).reshape(2, 2, 2 * r, wide)
        loop(0, A, rows)
        level1(i, t).start()
    def one(i, t):
        def go():
            first[i, t].wait_recv()
            for j in range(1, A):
                aj = (a + j) % A
                pb[i, t, aj, b] = pb[i, t, aj, b] + r1[i, t, aj]
                third[i, t, j] = cp(pb.at[i, t, aj, b], r2.at[i, t, j - 1], zp[j])
            pb[i, t, a, b] = pb[i, t, a, b] + r1[i, t, a]
        return go
    def two(i, t):
        def go():
            for j in range(1, A): third[i, t, j].wait_recv()
            for s in (1 - x, x):
                e = pb[i, t, a, b, s].astype(f32)
                for j in range(1, A): e = e + r2[i, t, j - 1, s].astype(f32)
                sb[i, t, s] = e
            xs[i, t] = sb[i, t, 1 - x].astype(bf16)
            fourth[i, t] = cp(xs.at[i, t], r3.at[i, t], xp)
        return go
    def three(i, t):
        def go():
            fourth[i, t].wait_recv()
            ob[i, :, pl.ds(pl.multiple_of(x * half + t * wide, wide), wide)] = sb[i, t, x]
            ob[i, :, pl.ds(pl.multiple_of((1 - x) * half + t * wide, wide), wide)] = r3[i, t].astype(f32)
            if t == 1:
                outs.append(cp.local(ob.at[i, pl.ds(pl.multiple_of(c * r, r), r)], out.at[2 * i + c]).wait)
                outs.append(cp(ob.at[i, pl.ds(pl.multiple_of(o * r, r), r)], out.at[2 * i + c], core).wait_recv)
        return go
    def adapt0():
        for e in aw: e()
        for t in range(2):
            apb[t] = dot_left(axb[...], ayb[:, pl.ds(t * 256, 256)]).astype(bf16).reshape(A, 2, D // (2 * A), 256)
        first["a"] = cp(apb.at[1 - x], ra1, xp)
    def adapt1():
        first["a"].wait_recv()
        def row(z):
            for s in range(2):
                apb[x, z, s] = apb[x, z, s] + ra1[z, s]
        loop(0, A, row)
        second["a"] = cp(apb.at[x, :, 1 - b], ra2, yp)
    def adapt2():
        second["a"].wait_recv()
        for j in range(1, A):
            aj = (a + j) % A
            apb[x, aj, b] = apb[x, aj, b] + ra2[aj]
            third["a", j] = cp(apb.at[x, aj, b], ra3.at[j - 1], zp[j])
        apb[x, a, b] = apb[x, a, b] + ra2[a]
    def adapt3():
        for j in range(1, A): third["a", j].wait_recv()
        t = apb[x, a, b].astype(f32)
        for j in range(1, A): t = t + ra3[j - 1].astype(f32)
        aob[0] = t[:, :128]
        aob[1] = t[:, 128:]
        outs.append(cp.local(aob.at[c], aout.at[c]).wait)
        outs.append(cp(aob.at[o], aout.at[c], core).wait_recv)
    small = {}
    def lanes(start, count): return pl.ds(pl.multiple_of(start * 128, 128), count * 128)
    def tail_norm0():
        small["n"] = [cp(nbuf.at[0], ngot.at[0], core)]
    def tail0():
        small["w"] = [cp(pg.at[:, lanes((a + j) % A * 4, 4)], w0.at[j - 1], zp[j]) for j in range(1, A)]
    def tail_norm(n):
        def go():
            for e in small["n"]: e.wait_recv()
            nbuf[n] = nbuf[n - 1] + ngot[n - 1]
            small["n"] = [cp(nbuf.at[n], ngot.at[n], peers[n])]
        return go
    def tail_norm3():
        for e in small["n"]: e.wait_recv()
        nz[a] = nbuf[2] + ngot[2]
        small["n"] = [cp(nz.at[a], nz.at[a], zp[j]) for j in range(1, A)]
    def tail_norm4():
        for e in small["n"]: e.wait_recv()
        t = nz[0]
        for n in range(1, A): t = t + nz[n]
        nsum[...] = t
    def tail1():
        t = pg[:, lanes(a * 4, 4)]
        for j, e in enumerate(small["w"]):
            e.wait_recv()
            t = t + w0[j]
        s0[...] = t
        small["w"] = [cp(s0.at[:, lanes((1 - b) * 2, 2)], w1, yp)]
    def tail2():
        small["w"][0].wait_recv()
        s1[...] = s0[:, lanes(b * 2, 2)] + w1[...]
        small["w"] = [cp(s1.at[:, lanes(1 - x, 1)], w2, xp)]
    def tail3():
        small["w"][0].wait_recv()
        s2[...] = s1[:, lanes(x, 1)] + w2[...]
        small["w"] = [cp(s2, w3, core)]
    def tail4():
        small["w"][0].wait_recv()
        t = s2[...] + w3[...]
        mine = jnp.where(c == 0, t[:, :64], t[:, 64:])
        buf[0] = exact(mine, outer[...].astype(f32), ((1,), (0,)))
        small["w"] = [cp(buf.at[0], got.at[0], core)]
        outer_o[...] = exact(mine, tangent[...].astype(bf16).astype(f32), ((0,), (0,)))
    def tail5(n):
        def go():
            small["w"][0].wait_recv()
            buf[n] = buf[n - 1] + got[n - 1]
            small["w"] = [cp(buf.at[n], got.at[n], peers[n])]
        return go
    def tail6():
        small["w"][0].wait_recv()
        zbuf[a] = buf[2] + got[2]
        small["w"] = [cp(zbuf.at[a], zbuf.at[a], zp[j]) for j in range(1, A)]
    def tail7():
        for e in small["w"]: e.wait_recv()
        t = zbuf[0]
        for n in range(1, A): t = t + zbuf[n]
        tan = tangent[...]
        t = t * (1.0 - tan * tan)
        inner_o[...] = exact(embed[...].astype(f32), t[:PREFIX], ((0,), (0,)))
        embed_o[...] = exact(t[:PREFIX], inner[...].astype(f32), ((1,), (1,)))
    def norm_two():
        norm_back_into(gsec, n2, i2, vecs[2:3, :], gmid, nbuf.at[0], 2)
        mid[...] = gmid[...].astype(bf16)
    def back_project(src, slot, n):
        def go():
            s = src[...]
            loop(2 * n, 2 * n + 2, lambda t: og.__setitem__((slice(None), columns(t)), dot_right(s, ws[slot, columns(t), :]).astype(bf16)))
        return go
    def wait_slot(slot):
        def go(): loads[slot].wait()
        return go
    def pair_back(p, grad, qr, kk, vv, pr):
        cols = columns(p, 128)
        qs, ks, gs = split_heads(qr[:, cols]), split_heads(kk), split_heads(grad[:, cols])
        res = None
        for s in range(2):
            low = pr[2 * p + s]
            prob = low.astype(f32)
            t = prob * dot_right(gs[s], vv)
            ds = (t - prob * jnp.sum(t, axis=-1, keepdims=True)).astype(bf16)
            m = (dot(ds, ks[s]), dot_left(ds, qs[s]), dot_left(low, gs[s]))
            res = m if res is None else tuple(e + f for e, f in zip(res, m))
        return cols, res[0] * 0.125, res[1] * 0.125, res[2]
    def cross_back(n):
        def go():
            def step(p):
                cs = columns(p, 128)
                cols, m1, m2, m3 = pair_back(p, og, cq, ck[:, cs], cv[:, cs], cprobs)
                dcq[:, cols] = m1.astype(bf16)
                dck[:, cols] = m2.astype(bf16)
                dcv[:, cols] = m3.astype(bf16)
            for p in range(2 * n, 2 * n + 2): step(p)
        return go
    def self_back(n):
        def go():
            def step(p):
                cs = columns(p, 128)
                cv_ = pl.ds(pl.multiple_of(D + p * 128, 128), 128)
                kk = jnp.concatenate([k[:, cs], prows[:, cs]], axis=0)
                vv = jnp.concatenate([v[:, cs], prows[:, cv_]], axis=0)
                cols, m1, m2, m3 = pair_back(p, og, q, kk, vv, probs)
                dq[:, cols] = m1.astype(bf16)
                dk[:, cols] = m2[:T].astype(bf16)
                dv[:, cols] = m3[:T].astype(bf16)
                pg[:, cols] = m2[T:]
                pg[:, cv_] = m3[T:]
            for p in range(2 * n, 2 * n + 2): step(p)
        return go
    def first_grad():
        s = dcq[...]
        def step(t):
            gfirst[:, columns(t)] = gmid[:, columns(t)] + dot_right(s, ws[1, columns(t), :])
        loop(0, D // 256, step)
    def norm_one():
        norm_back_into(gfirst, n1, i1, vecs[0:1, :], gmid, nbuf.at[0], 0)
        nbuf[0, 4:6, :] = ngrad3[...]
        nbuf[0, 6:8, :] = jnp.zeros((2, D), f32)
        startl[...] = gmid[...].astype(bf16)
    def memory_part(n):
        def go():
            def step(t):
                mgrad[:, columns(t)] = (dot_right(dck[...], ws[3, columns(t), :]) + dot_right(dcv[...], ws[0, columns(t), :])).astype(bf16)
            loop(2 * n, 2 * n + 2, step)
        return go
    def input_part(n):
        def go():
            def step(t):
                s = gmid[:, columns(t)] + dot_right(dq[...], ws[1, columns(t), :]) + dot_right(dk[...], ws[2, columns(t), :]) + dot_right(dv[...], ws[3, columns(t), :])
                igrad[:, columns(t)] = s.astype(bf16)
            loop(2 * n, 2 * n + 2, step)
        return go
    shared = {}
    def spread(i, srcs, dst):
        for t in range(2): shared[i, t] = share(srcs, dst, t)
    norm_two()
    wait_slot(0)()
    back_project(mid, 0, 0)(); back_project(mid, 0, 1)()
    fetch(0, 6)
    adapt0()
    ready(0, 4)
    cross_back(0)()
    feed0()
    cross_back(1)(); cross_back(2)(); cross_back(3)()
    spread(0, (mid, dcq), yb.at[0])
    spread(1, (dck, dcv), mby)
    wait_slot(1)()
    first_grad()
    fetch(1, 0)
    ready(4, 6)
    norm_one()
    tail_norm0()
    wait_slot(2)()
    back_project(startl, 2, 0)(); back_project(startl, 2, 1)()
    fetch(2, 1)
    ready(6, 11)
    self_back(0)()
    compute(0, 0)
    tail_norm(1)()
    self_back(1)()
    compute(0, 1)
    adapt1()
    self_back(2)()
    compute(1, 0)
    tail_norm(2)()
    self_back(3)()
    tail0()
    spread(2, (startl, dq), yb.at[1])
    spread(3, (dk, dv), yb.at[2])
    compute(1, 1)
    one(0, 0)(); one(0, 1)()
    tail_norm3()
    compute(2, 0); compute(2, 1)
    tail1()
    one(1, 0)()
    compute(3, 0); compute(3, 1)
    adapt2()
    one(1, 1)()
    tail2()
    tail_norm4()
    two(0, 0)(); two(0, 1)()
    wait_slot(3)(); wait_slot(0)()
    memory_part(0)()
    feed1()
    tail3()
    memory_part(1)()
    outs.append(cp.local(mgrad, mgrad_o).wait)
    fetch(3, 2)
    one(2, 0)()
    two(1, 0)()
    tail4()
    one(2, 1)()
    two(1, 1)()
    tail5(1)()
    three(0, 0)(); three(0, 1)()
    wait_slot(1)(); wait_slot(2)(); wait_slot(3)()
    input_part(0)()
    tail5(2)()
    one(3, 0)()
    input_part(1)()
    outs.append(cp.local(igrad, igrad_o).wait)
    tail6()
    two(2, 0)()
    one(3, 1)()
    feed2()
    adapt3()
    three(1, 0)(); three(1, 1)()
    two(2, 1)(); two(3, 0)()
    tail7()
    three(2, 0)(); three(2, 1)()
    two(3, 1)()
    three(3, 0)(); three(3, 1)()
    for e in outs: e()
    cp.close()

def back(A, r, first, late, rest):
    gsec = first[0]
    T, D = gsec.shape; M = rest[-1].shape[0] // 4
    fi, fo = rest[4:6]
    Q, H2 = fi.shape[0] // 4, fi.shape[1]
    H = H2 // 2
    half = D // 2
    v = lambda *s: pltpu.VMEM(s, bf16)
    vf = lambda *s: pltpu.VMEM(s, f32)
    any_ = pl.BlockSpec(memory_space=pl.ANY)
    vm = pl.BlockSpec(memory_space=pltpu.VMEM)
    sds = jax.ShapeDtypeStruct
    P_, N = PADDED, (8, D)
    hid = first[-2].shape[1]
    S = (P_, hid)
    return pl.pallas_call(functools.partial(back_kernel, A, r),
        out_shape=(sds((T, D), bf16), sds((M, D), bf16), sds((8, r, D), f32), sds((2, D // (2 * A), 128), f32), sds((Q, H), f32), sds((H, Q), f32),
            sds((64, hid), f32), sds((r, hid), f32), sds((PREFIX, r), f32), sds(N, f32)),
        in_specs=[vm] * len(first) + [any_] * (len(late) + len(rest)), out_specs=(any_,) * 6 + (vm,) * 4,
        scratch_shapes=[v(T, D), v(M, D)] + [pltpu.VMEM(e.shape, e.dtype) for e in late] + [v(4, D, D), vf(T, D), vf(T, D), v(T, D), v(T, D), v(T, D), v(M, D), v(M, D), v(T, D), v(T, D), v(T, D), v(T, D), vf(P_, 2 * D),
            v(3, 4 * T, D), v(3, 4 * T, half), v(4 * M, D), v(4 * M, half), v(2 * T, D), v(2 * T, 512),
            v(4, 2, A, 2, 2, 2 * r, half // 2), v(2, A, 2, D // (2 * A), 256), v(2, Q, H2), v(2, H2, Q),
            v(4, 2, A, 2, 2 * r, half // 2), v(4, 2, A - 1, 2, 2 * r, half // 2), v(4, 2, 2 * r, half // 2), vf(4, 2, 2, 2 * r, half // 2), v(4, 2, 2 * r, half // 2),
            v(A, 2, D // (2 * A), 256), v(A, D // (2 * A), 256), v(A - 1, D // (2 * A), 256),
            v(2, Q, H2), v(2, H2, Q), v(2, Q, H), v(2, H, Q), v(Q, H), v(H, Q),
            vf(4, 2 * r, D), vf(2, D // (2 * A), 128), vf(Q, H), vf(H, Q),
            vf(3, *S), vf(3, *S), vf(A, *S), vf(3, *N), vf(3, *N), vf(A, *N), vf(A - 1, P_, 512), vf(P_, 256), vf(P_, 128), vf(P_, 128), vf(P_, 512), vf(P_, 256), vf(P_, 128),
            pltpu.SemaphoreType.DMA((224,)), pltpu.SemaphoreType.DMA((224,))],
        compiler_params=pltpu.CompilerParams(collective_id=2, has_side_effects=True, vmem_limit_bytes=63 << 20),
        name="back")(*first, *late, *rest)

def fast_body(A, inputs, memory, cotangent, segments, memory_segments, query_self, key_self, value_self, output_self,
              query_cross, key_cross, value_cross, output_cross, self_gain, self_shift, cross_gain, cross_shift,
              final_gain, final_shift, feed_in, feed_out, adapter_down, adapter_up, prefix_embed, prefix_inner, prefix_outer):
    r = query_self.shape[0]
    w, n = lax.axis_index(WIDE), lax.axis_index(NARROW)
    blank = jnp.zeros_like(self_gain)
    norms = jnp.stack([self_gain, self_shift, cross_gain, cross_shift, final_gain, final_shift] + [blank] * 10)
    (weights, fin2, fout2, tangent, prows, vecs, q, k, v, probs, attended, first_low, n1, i1, cq, ck, cv, cprobs, crossed, second, second_low, n2, i2) = front(
        A, r, inputs, memory, segments.reshape(1, -1), memory_segments.reshape(1, -1), prefix_embed, prefix_inner, prefix_outer.T, norms,
        [query_self, key_self, value_self, output_self, key_cross, query_cross, value_cross, output_cross], feed_in, feed_out)
    result, grad_second, fi, fo, ay, branch_low, ngrad3, xp0, xatt, xin, xmem = feed(
        A, second, cotangent, feed_in, feed_out, fin2, fout2, adapter_down, adapter_up, vecs[4:5], vecs[5:6], inputs, memory, attended, first_low, crossed)
    igrad, mgrad, sums, adapt, fi_sum, fo_sum, outer_grad, inner_grad, embed_grad, nsum = back(A, r,
        (grad_second, n2, i2, vecs, ngrad3, tangent, prefix_embed, prefix_inner, prefix_outer.T), (cq, ck, cv, cprobs, n1, i1, q, k, v, probs, prows),
        (second_low, branch_low, ay, weights, fi, fo, xp0, xatt, xin, xmem))
    ng = lax.dynamic_slice_in_dim(nsum, (w * 4 + n) * r, r, 1)
    whole = deliver(result, igrad, mgrad, sums, fi_sum, fo_sum, outer_grad, inner_grad, embed_grad, adapt)
    return whole[:11] + tuple(ng[k] for k in range(6)) + whole[11:17] + (whole[17].T,)


def deliver_kernel(result, igrad, mgrad, sums, fi, fo, outer, inner, embed, adapt, *outs):
    order = (5, 6, 7, 4, 1, 2, 3, 0)
    for dst, src in zip(outs[:3], (result, igrad, mgrad)): dst[...] = src[...]
    for dst, k in zip(outs[3:11], order): dst[...] = sums[k]
    for dst, src in zip(outs[11:13] + outs[15:], (fi, fo, embed, inner, outer)): dst[...] = src[...]
    outs[13][...] = adapt[0]
    outs[14][...] = adapt[1].T


def deliver(result, igrad, mgrad, sums, fi, fo, outer, inner, embed, adapt):
    like = lambda e: jax.ShapeDtypeStruct(e.shape, e.dtype)
    row = jax.ShapeDtypeStruct(sums.shape[1:], f32)
    square = jax.ShapeDtypeStruct(adapt.shape[1:], f32)
    vm = pl.BlockSpec(memory_space=pltpu.VMEM)
    return pl.pallas_call(deliver_kernel,
        out_shape=(like(result), like(igrad), like(mgrad)) + (row,) * 8 + (like(fi), like(fo), square, square, like(embed), like(inner), like(outer)),
        in_specs=[vm] * 10, out_specs=(vm,) * 18, compiler_params=pltpu.CompilerParams(vmem_limit_bytes=60 << 20),
        name="deliver")(result, igrad, mgrad, sums, fi, fo, outer, inner, embed, adapt)


def solution(mesh):
    wide, narrow = mesh.shape[WIDE], mesh.shape[NARROW]
    fits = narrow == 4 and wide == 8
    body = functools.partial(fast_body, wide // 2) if fits else plain_body
    return jax.shard_map(
        body,
        mesh=mesh,
        in_specs=(
            P(BOTH, None),
            P(BOTH, None),
            P(BOTH, None),
            P(BOTH),
            P(BOTH),
            P(BOTH, None),
            P(BOTH, None),
            P(BOTH, None),
            P(BOTH, None),
            P(BOTH, None),
            P(BOTH, None),
            P(BOTH, None),
            P(BOTH, None),
            P(BOTH),
            P(BOTH),
            P(BOTH),
            P(BOTH),
            P(BOTH),
            P(BOTH),
            P(None, WIDE),
            P(WIDE, None),
            P(None, NARROW),
            P(NARROW, None),
            P(None, BOTH),
            P(BOTH, None),
            P(None, BOTH),
        ),
        out_specs=(
            P(BOTH, None),
            P(BOTH, None),
            P(BOTH, None),
            P(BOTH, None),
            P(BOTH, None),
            P(BOTH, None),
            P(BOTH, None),
            P(BOTH, None),
            P(BOTH, None),
            P(BOTH, None),
            P(BOTH, None),
            P(BOTH),
            P(BOTH),
            P(BOTH),
            P(BOTH),
            P(BOTH),
            P(BOTH),
            P(NARROW, WIDE),
            P(WIDE, NARROW),
            P(WIDE, NARROW),
            P(NARROW, WIDE),
            P(None, BOTH),
            P(BOTH, None),
            P(None, BOTH),
        ),
        check_vma=False,
    )
```

```python
import functools
from functools import reduce

import jax
import jax.numpy as jnp
from jax import lax
from jax.experimental import pallas as pl
from jax.experimental.pallas import tpu as pltpu
from jax.sharding import PartitionSpec as P

MESH = pl.DeviceIdType.MESH
bf16, f32 = jnp.bfloat16, jnp.float32
WIDE, NARROW = "wide", "narrow"
BOTH = (WIDE, NARROW)


HEADS = 16
HEAD = 64
PREFIX = 30


HIGHEST = lax.Precision.HIGHEST
EPSILON = 1e-05
MASKED = -1000000000.0
ADAPT_SCALE = 4.0


def matmul(left, right):
    return jnp.dot(left, right, preferred_element_type=jnp.float32)


def left_product(left, right):
    return lax.dot_general(
        left, right, (((0,), (0,)), ((), ())), preferred_element_type=jnp.float32
    )


def right_product(left, right):
    return lax.dot_general(
        left, right, (((1,), (1,)), ((), ())), preferred_element_type=jnp.float32
    )


def exact_left(left, right):
    return lax.dot_general(
        left, right, (((0,), (0,)), ((), ())), precision=HIGHEST, preferred_element_type=jnp.float32
    )


def exact_right(left, right):
    return lax.dot_general(
        left, right, (((1,), (1,)), ((), ())), precision=HIGHEST, preferred_element_type=jnp.float32
    )


def norm_forward(values, factor, offset):
    average = jnp.mean(values, axis=-1, keepdims=True)
    center = values - average
    inverse = lax.rsqrt(jnp.mean(center * center, axis=-1, keepdims=True) + EPSILON)
    normed = center * inverse
    return (normed * factor + offset, normed, inverse)


def norm_backward(grad_out, normed, inverse, factor):
    scaled = grad_out * factor
    grad_in = inverse * (
        scaled
        - jnp.mean(scaled, axis=-1, keepdims=True)
        - normed * jnp.mean(scaled * normed, axis=-1, keepdims=True)
    )
    return (grad_in, jnp.sum(grad_out * normed, axis=0), jnp.sum(grad_out, axis=0))


def head_view(rows):
    return rows.reshape(rows.shape[0], HEADS, HEAD)


def scored(queries, key_rows, allowed):
    raw = jnp.einsum(
        "shd,khd->hsk", head_view(queries), head_view(key_rows), preferred_element_type=jnp.float32
    )
    return jnp.where(allowed[None], raw * HEAD ** (-0.5), MASKED)


def attend_forward(queries, parts):
    scores = [scored(queries, member[0], member[2]) for member in parts]
    largest = reduce(jnp.maximum, [jnp.max(matrix, axis=-1, keepdims=True) for matrix in scores])
    total = reduce(
        jnp.add, [jnp.sum(jnp.exp(matrix - largest), axis=-1, keepdims=True) for matrix in scores]
    )
    logsum = largest + jnp.log(total)
    mixed = reduce(
        jnp.add,
        [
            jnp.einsum(
                "hsk,khd->shd",
                jnp.exp(matrix - logsum).astype(jnp.bfloat16),
                head_view(member[1]),
                preferred_element_type=jnp.float32,
            )
            for matrix, member in zip(scores, parts)
        ],
    )
    return (mixed.reshape(queries.shape[0], HEADS * HEAD), logsum)


def attend_backward(queries, parts, logsum, grad_low):
    grad_heads = head_view(grad_low)
    chances = [jnp.exp(scored(queries, member[0], member[2]) - logsum) for member in parts]
    slopes = [
        jnp.einsum(
            "shd,khd->hsk", grad_heads, head_view(member[1]), preferred_element_type=jnp.float32
        )
        for member in parts
    ]
    row_dot = reduce(
        jnp.add,
        [jnp.sum(chance * slope, axis=-1, keepdims=True) for chance, slope in zip(chances, slopes)],
    )
    scale = HEAD ** (-0.5)
    grad_query = jnp.zeros((queries.shape[0], HEADS, HEAD), jnp.float32)
    results = []
    for member, chance, slope in zip(parts, chances, slopes):
        dscore = (chance * (slope - row_dot)).astype(jnp.bfloat16)
        grad_query = grad_query + jnp.einsum(
            "hsk,khd->shd", dscore, head_view(member[0]), preferred_element_type=jnp.float32
        )
        grad_key = (
            jnp.einsum(
                "hsk,shd->khd", dscore, head_view(queries), preferred_element_type=jnp.float32
            )
            * scale
        )
        grad_value = jnp.einsum(
            "hsk,shd->khd",
            chance.astype(jnp.bfloat16),
            grad_heads,
            preferred_element_type=jnp.float32,
        )
        results.append(
            (
                grad_key.reshape(grad_key.shape[0], HEADS * HEAD),
                grad_value.reshape(grad_value.shape[0], HEADS * HEAD),
            )
        )
    return ((grad_query * scale).reshape(queries.shape[0], HEADS * HEAD), results)


def gelu_back(pre_values, grad_values):
    return jax.vjp(lambda inner: jax.nn.gelu(inner, approximate=False), pre_values)[1](grad_values)[
        0
    ]


def plain_body(
    inputs,
    memory,
    cotangent,
    segments,
    memory_segments,
    query_self,
    key_self,
    value_self,
    output_self,
    query_cross,
    key_cross,
    value_cross,
    output_cross,
    self_gain,
    self_shift,
    cross_gain,
    cross_shift,
    final_gain,
    final_shift,
    feed_in,
    feed_out,
    adapter_down,
    adapter_up,
    prefix_embed,
    prefix_inner,
    prefix_outer,
):
    (
        query_one,
        key_one,
        value_one,
        output_one,
        query_two,
        key_two,
        value_two,
        output_two,
        gain_one,
        shift_one,
        gain_two,
        shift_two,
        gain_three,
        shift_three,
        embed_full,
        inner_full,
        outer_full,
    ) = (
        lax.all_gather(query_self, BOTH, axis=0, tiled=True),
        lax.all_gather(key_self, BOTH, axis=0, tiled=True),
        lax.all_gather(value_self, BOTH, axis=0, tiled=True),
        lax.all_gather(output_self, BOTH, axis=0, tiled=True),
        lax.all_gather(query_cross, BOTH, axis=0, tiled=True),
        lax.all_gather(key_cross, BOTH, axis=0, tiled=True),
        lax.all_gather(value_cross, BOTH, axis=0, tiled=True),
        lax.all_gather(output_cross, BOTH, axis=0, tiled=True),
        lax.all_gather(self_gain, BOTH, axis=0, tiled=True),
        lax.all_gather(self_shift, BOTH, axis=0, tiled=True),
        lax.all_gather(cross_gain, BOTH, axis=0, tiled=True),
        lax.all_gather(cross_shift, BOTH, axis=0, tiled=True),
        lax.all_gather(final_gain, BOTH, axis=0, tiled=True),
        lax.all_gather(final_shift, BOTH, axis=0, tiled=True),
        lax.all_gather(prefix_embed, BOTH, axis=1, tiled=True),
        lax.all_gather(prefix_inner, BOTH, axis=0, tiled=True),
        lax.all_gather(prefix_outer, BOTH, axis=1, tiled=True),
    )
    factor_one = gain_one.astype(jnp.float32)
    factor_two = gain_two.astype(jnp.float32)
    factor_three = gain_three.astype(jnp.float32)
    length = inputs.shape[0]
    width = inputs.shape[1]
    places = jnp.arange(length)
    causal = places[:, None] >= places[None, :]
    local_mask = (segments[:, None] == segments[None, :]) & causal
    prefix_mask = jnp.ones((length, PREFIX), jnp.bool_)
    cross_mask = segments[:, None] == memory_segments[None, :]
    tangent = jnp.tanh(matmul(embed_full, inner_full))
    tangent_low = tangent.astype(jnp.bfloat16)
    prefix_rows = matmul(tangent_low, outer_full).astype(jnp.bfloat16)
    prefix_keys = prefix_rows[:, :width]
    prefix_values = prefix_rows[:, width:]
    queries = matmul(inputs, query_one).astype(jnp.bfloat16)
    key_rows = matmul(inputs, key_one).astype(jnp.bfloat16)
    value_rows = matmul(inputs, value_one).astype(jnp.bfloat16)
    self_parts = ((prefix_keys, prefix_values, prefix_mask), (key_rows, value_rows, local_mask))
    attended, self_logsum = attend_forward(queries, self_parts)
    attended_low = attended.astype(jnp.bfloat16)
    first, normed_one, inverse_one = norm_forward(
        inputs.astype(jnp.float32) + matmul(attended_low, output_one),
        factor_one,
        shift_one.astype(jnp.float32),
    )
    first_low = first.astype(jnp.bfloat16)
    cross_queries = matmul(first_low, query_two).astype(jnp.bfloat16)
    cross_keys = matmul(memory, key_two).astype(jnp.bfloat16)
    cross_values = matmul(memory, value_two).astype(jnp.bfloat16)
    cross_parts = ((cross_keys, cross_values, cross_mask),)
    crossed, cross_logsum = attend_forward(cross_queries, cross_parts)
    crossed_low = crossed.astype(jnp.bfloat16)
    second, normed_two, inverse_two = norm_forward(
        first + matmul(crossed_low, output_two), factor_two, shift_two.astype(jnp.float32)
    )
    second_low = second.astype(jnp.bfloat16)
    feed_rows = lax.all_gather(second_low, WIDE, axis=0, tiled=True)
    hidden_pre = matmul(feed_rows, feed_in)
    hidden_low = jax.nn.gelu(hidden_pre, approximate=False).astype(jnp.bfloat16)
    feed_sum = lax.psum_scatter(
        matmul(hidden_low, feed_out), WIDE, scatter_dimension=0, tiled=True
    )
    adapt_rows = lax.all_gather(second_low, NARROW, axis=0, tiled=True)
    bottle_pre = matmul(adapt_rows, adapter_down)
    bottle_low = jax.nn.gelu(bottle_pre, approximate=False).astype(jnp.bfloat16)
    adapt_sum = lax.psum_scatter(
        matmul(bottle_low, adapter_up).astype(jnp.bfloat16),
        NARROW,
        scatter_dimension=0,
        tiled=True,
    ).astype(jnp.float32)
    branch = feed_sum + ADAPT_SCALE * adapt_sum
    result, normed_three, inverse_three = norm_forward(
        second + branch, factor_three, shift_three.astype(jnp.float32)
    )
    grad_branch, gain_three_grad, shift_three_grad = norm_backward(
        cotangent.astype(jnp.float32), normed_three, inverse_three, factor_three
    )
    branch_low = grad_branch.astype(jnp.bfloat16)
    branch_rows = lax.all_gather(branch_low, WIDE, axis=0, tiled=True)
    grad_hidden = right_product(branch_rows, feed_out)
    grad_pre = gelu_back(hidden_pre, grad_hidden).astype(jnp.bfloat16)
    grad_out_part = left_product(hidden_low, branch_rows)
    grad_in_part = left_product(feed_rows, grad_pre)
    grad_feed = lax.psum_scatter(
        right_product(grad_pre, feed_in), WIDE, scatter_dimension=0, tiled=True
    )
    feed_in_total, feed_out_total = (
        lax.psum_scatter(
            grad_in_part.astype(jnp.bfloat16), NARROW, scatter_dimension=0, tiled=True
        ).astype(jnp.float32),
        lax.psum_scatter(
            grad_out_part.astype(jnp.bfloat16), NARROW, scatter_dimension=1, tiled=True
        ).astype(jnp.float32),
    )
    branch_narrow = lax.all_gather(branch_low, NARROW, axis=0, tiled=True)
    grad_bottle = ADAPT_SCALE * right_product(branch_narrow, adapter_up)
    grad_bottle_pre = gelu_back(bottle_pre, grad_bottle).astype(jnp.bfloat16)
    grad_up_part = ADAPT_SCALE * left_product(bottle_low, branch_narrow)
    grad_down_part = left_product(adapt_rows, grad_bottle_pre)
    grad_adapt = lax.psum_scatter(
        right_product(grad_bottle_pre, adapter_down).astype(jnp.bfloat16),
        NARROW,
        scatter_dimension=0,
        tiled=True,
    ).astype(jnp.float32)
    down_total, up_total = (
        lax.psum_scatter(grad_down_part, WIDE, scatter_dimension=0, tiled=True),
        lax.psum_scatter(grad_up_part, WIDE, scatter_dimension=1, tiled=True),
    )
    grad_second = grad_branch + grad_feed + grad_adapt
    grad_mid, gain_two_grad, shift_two_grad = norm_backward(
        grad_second, normed_two, inverse_two, factor_two
    )
    mid_low = grad_mid.astype(jnp.bfloat16)
    output_two_grad = left_product(crossed_low, mid_low)
    crossed_grad = right_product(mid_low, output_two).astype(jnp.bfloat16)
    cross_query_grad, cross_results = attend_backward(
        cross_queries, cross_parts, cross_logsum, crossed_grad
    )
    cross_query_low = cross_query_grad.astype(jnp.bfloat16)
    cross_key_low = cross_results[0][0].astype(jnp.bfloat16)
    cross_value_low = cross_results[0][1].astype(jnp.bfloat16)
    query_two_grad = left_product(first_low, cross_query_low)
    key_two_grad = left_product(memory, cross_key_low)
    value_two_grad = left_product(memory, cross_value_low)
    memory_grad = (
        right_product(cross_key_low, key_two) + right_product(cross_value_low, value_two)
    ).astype(jnp.bfloat16)
    grad_first = grad_mid + right_product(cross_query_low, query_two)
    grad_start, gain_one_grad, shift_one_grad = norm_backward(
        grad_first, normed_one, inverse_one, factor_one
    )
    start_low = grad_start.astype(jnp.bfloat16)
    output_one_grad = left_product(attended_low, start_low)
    attended_grad = right_product(start_low, output_one).astype(jnp.bfloat16)
    self_query_grad, self_results = attend_backward(queries, self_parts, self_logsum, attended_grad)
    self_query_low = self_query_grad.astype(jnp.bfloat16)
    self_key_low = self_results[1][0].astype(jnp.bfloat16)
    self_value_low = self_results[1][1].astype(jnp.bfloat16)
    query_one_grad = left_product(inputs, self_query_low)
    key_one_grad = left_product(inputs, self_key_low)
    value_one_grad = left_product(inputs, self_value_low)
    inputs_grad = (
        grad_start
        + right_product(self_query_low, query_one)
        + right_product(self_key_low, key_one)
        + right_product(self_value_low, value_one)
    ).astype(jnp.bfloat16)
    prefix_grad = jnp.concatenate([self_results[0][0], self_results[0][1]], axis=1)
    outer_grad = exact_left(tangent_low.astype(jnp.float32), prefix_grad)
    tangent_grad = exact_right(prefix_grad, outer_full.astype(jnp.float32)) * (
        1.0 - tangent * tangent
    )
    inner_grad = exact_left(embed_full.astype(jnp.float32), tangent_grad)
    embed_grad = exact_right(tangent_grad, inner_full.astype(jnp.float32))
    (
        query_one_sum,
        key_one_sum,
        value_one_sum,
        output_one_sum,
        query_two_sum,
        key_two_sum,
        value_two_sum,
        output_two_sum,
        gain_one_sum,
        shift_one_sum,
        gain_two_sum,
        shift_two_sum,
        gain_three_sum,
        shift_three_sum,
        embed_sum,
        inner_sum,
        outer_sum,
    ) = (
        lax.psum_scatter(query_one_grad, BOTH, scatter_dimension=0, tiled=True),
        lax.psum_scatter(key_one_grad, BOTH, scatter_dimension=0, tiled=True),
        lax.psum_scatter(value_one_grad, BOTH, scatter_dimension=0, tiled=True),
        lax.psum_scatter(output_one_grad, BOTH, scatter_dimension=0, tiled=True),
        lax.psum_scatter(query_two_grad, BOTH, scatter_dimension=0, tiled=True),
        lax.psum_scatter(key_two_grad, BOTH, scatter_dimension=0, tiled=True),
        lax.psum_scatter(value_two_grad, BOTH, scatter_dimension=0, tiled=True),
        lax.psum_scatter(output_two_grad, BOTH, scatter_dimension=0, tiled=True),
        lax.psum_scatter(gain_one_grad, BOTH, scatter_dimension=0, tiled=True),
        lax.psum_scatter(shift_one_grad, BOTH, scatter_dimension=0, tiled=True),
        lax.psum_scatter(gain_two_grad, BOTH, scatter_dimension=0, tiled=True),
        lax.psum_scatter(shift_two_grad, BOTH, scatter_dimension=0, tiled=True),
        lax.psum_scatter(gain_three_grad, BOTH, scatter_dimension=0, tiled=True),
        lax.psum_scatter(shift_three_grad, BOTH, scatter_dimension=0, tiled=True),
        lax.psum_scatter(embed_grad, BOTH, scatter_dimension=1, tiled=True),
        lax.psum_scatter(inner_grad, BOTH, scatter_dimension=0, tiled=True),
        lax.psum_scatter(outer_grad, BOTH, scatter_dimension=1, tiled=True),
    )
    return (
        result.astype(jnp.bfloat16),
        inputs_grad,
        memory_grad,
        query_one_sum,
        key_one_sum,
        value_one_sum,
        output_one_sum,
        query_two_sum,
        key_two_sum,
        value_two_sum,
        output_two_sum,
        gain_one_sum,
        shift_one_sum,
        gain_two_sum,
        shift_two_sum,
        gain_three_sum,
        shift_three_sum,
        feed_in_total,
        feed_out_total,
        down_total,
        up_total,
        embed_sum,
        inner_sum,
        outer_sum,
    )


def place():
    w = lax.axis_index(WIDE); n = lax.axis_index(NARROW)
    return w // 2, w % 2, n // 2, n % 2

def device(a, b, x, c):
    return (a * 2 + b, x * 2 + c)

def greet(peers):
    barrier = pltpu.get_barrier_semaphore()
    for p in peers:
        pl.semaphore_signal(barrier, inc=1, device_id=p, device_id_type=MESH)
    pl.semaphore_wait(barrier, len(peers))

def remote(src, dst, send, recv, dev):
    return pltpu.make_async_remote_copy(src_ref=src, dst_ref=dst, send_sem=send, recv_sem=recv, device_id=dev, device_id_type=MESH)


def dot_left(l, r):
    return lax.dot_general(l, r, (((0,), (0,)), ((), ())), preferred_element_type=f32)

class Copies:
    def __init__(self, send, recv):
        self.send, self.recv, self.count, self.all = send, recv, 0, []
    def __call__(self, src, dst, dev):
        cp = remote(src, dst, self.send.at[self.count], self.recv.at[self.count], dev)
        self.count += 1
        cp.start(); self.all.append(cp)
        return cp
    def local(self, src, dst):
        cp = pltpu.make_async_copy(src, dst, self.send.at[self.count])
        self.count += 1
        cp.start()
        return cp
    def sent(self, some):
        for cp in some:
            cp.wait_send()
            self.all = [o for o in self.all if o is not cp]
    def close(self):
        for cp in self.all: cp.wait_send()


EPSILON = 1e-05
ADAPT_SCALE = 4.0

def dot(l, r):
    return jnp.dot(l, r, preferred_element_type=f32)

def dot_right(l, r):
    return lax.dot_general(l, r, (((1,), (1,)), ((), ())), preferred_element_type=f32)

def gelu_both(v):
    phi = 0.5 + 0.5 * lax.erf(v * 0.7071067811865476)
    return v * phi, phi + v * (0.3989422804014327 * jnp.exp(-0.5 * v * v))

def norm(v):
    center = v - jnp.mean(v, axis=-1, keepdims=True)
    inverse = lax.rsqrt(jnp.mean(center * center, axis=-1, keepdims=True) + EPSILON)
    return center * inverse, inverse

def norm_back(e, n, inverse, factor):
    s = e * factor
    return inverse * (s - jnp.mean(s, axis=-1, keepdims=True) - n * jnp.mean(s * n, axis=-1, keepdims=True))

def feed_kernel(A, second, cot, fin_own, fout_own, fin_two, fout_two, down_ref, up_ref, gain, shift, inputs_h, memory_h, att_h, flow_h, crossed_h,
                result, gsec, fi_out, fo_out, ay, blow, ngrad, xp0, xatt, xin, xmem, inputs, memory, att, flow, crossed, fin, fout, fi, fo, down, up, rows, brow, hid, slope, gpre, part, q1, q2, q3, bslope, acc, ssem, rsem):
    a, b, x, c = place()
    o = 1 - c
    yp = device(a, 1 - b, x, c)
    zp = device((a + A // 2) % A, b, x, c)
    core, xp, dp = device(a, b, x, o), device(a, b, 1 - x, c), device(a, b, 1 - x, o)
    cp = Copies(ssem, rsem)
    half = fin_own.shape[1]
    lo, hi = pl.ds(0, half), pl.ds(half, half)
    loads = [cp.local(fin_own, fin.at[:, lo]), cp.local(fin_two, fin.at[:, hi]), cp.local(fout_own, fout.at[lo]), cp.local(fout_two, fout.at[hi])]
    staged = [cp.local(src, dst) for src, dst in ((inputs_h, inputs), (memory_h, memory), (att_h, att), (flow_h, flow), (crossed_h, crossed))]
    greet([yp, zp, core, xp, dp])
    T, D = second.shape
    NC, R = 2, T // 2
    C = R // NC
    HID = fin.shape[1]; TW = 256
    NT = D // TW
    def span(h): return pl.ds(h * R, R)

    def spread(buf, h):
        zs, ys, passed = [], [], []
        for u in range(NC):
            s = pl.ds(u * C, C)
            zs.append(cp(buf.at[h, 0, s], buf.at[h, 2, s], zp))
        for u in range(NC):
            s = pl.ds(u * C, C)
            ys.append(cp(buf.at[h, 0, s], buf.at[h, 1, s], yp))
        def beside():
            for e in ys: e.wait_recv()
        def forward():
            for u in range(NC):
                s = pl.ds(u * C, C)
                zs[u].wait_recv()
                passed.append(cp(buf.at[h, 2, s], buf.at[h, 3, s], yp))
        def across():
            for e in passed: e.wait_recv()
        return beside, forward, across

    sums, onward = {}, {}
    def send_part(level, h, j, t):
        sums[level, h, j, t] = cp(part.at[h, j, t], (q3 if j == 3 else q1).at[level, h, t], yp)
    def collect(level, h):
        for t in range(NT):
            sums[level, h, 3, t].wait_recv()
            part[h, 2, t] = part[h, 2, t] + q3[level, h, t]
            onward[level, h, t] = cp(part.at[h, 2, t], q2.at[level, h, t], zp)
    def gather_up(level, h):
        for t in range(NT):
            cols = pl.ds(t * TW, TW)
            sums[level, h, 1, t].wait_recv(); onward[level, h, t].wait_recv()
            acc[h, :, cols] = acc[h, :, cols] + q1[level, h, t].astype(f32) + q2[level, h, t].astype(f32)
        cp.sent([onward[level, h, t] for t in range(NT)] + [sums[level, h, j, t] for j in (1, 3) for t in range(NT)])

    for h in range(2): rows[h, 0] = second[span(h), :].astype(bf16)
    ways = [spread(rows, h) for h in range(2)]
    AD = down_ref.shape[1]
    n = x * 2 + c
    nd = pl.ds(pl.multiple_of(n * AD, AD), AD)
    md = pl.ds(pl.multiple_of((2 - 2 * x + c) * AD, AD), AD)
    kept, late = [cp.local(down_ref, down.at[:, nd]), cp.local(up_ref, up.at[nd])], []
    over = [cp(down_ref, down.at[:, nd], xp), cp(up_ref, up.at[nd], xp)]
    near = [cp(down_ref, down.at[:, nd], core), cp(up_ref, up.at[nd], core)]
    def rowsn(ref, m, place): return ref.at[pl.ds(pl.multiple_of(place * m, m), m)]
    def fan(srcs, dst, only=False):
        k = cp.count
        cp.count += 4
        def start(me):
            own, other = srcs[me], srcs[1 - me]
            if own is not None:
                pltpu.make_async_copy(own, rowsn(dst, T, n), ssem.at[k]).start()
                remote(own, rowsn(dst, T, n), ssem.at[k + 1], rsem.at[k + 1], xp).start()
            if other is not None:
                remote(other, rowsn(dst, T, n), ssem.at[k + 2], rsem.at[k + 2], core).start()
                remote(other, rowsn(dst, T, n), ssem.at[k + 3], rsem.at[k + 3], dp).start()
        def finish(me):
            own, other = srcs[me], srcs[1 - me]
            src = own if own is not None else other
            ways = [remote(src, rowsn(dst, T, n), ssem.at[k + i], rsem.at[k + i], d) for i, d in ((1, xp), (2, core), (3, dp))]
            if own is not None:
                pltpu.make_async_copy(own, rowsn(dst, T, n), ssem.at[k]).wait()
                ways[0].wait_send()
                for e in ways: e.wait_recv()
            if other is not None:
                ways[1].wait_send(); ways[2].wait_send()
        pl.when(c == 0)(functools.partial(start, 0))
        pl.when(c == 1)(functools.partial(start, 1))
        def done():
            pl.when(c == 0)(functools.partial(finish, 0))
            pl.when(c == 1)(functools.partial(finish, 1))
        return done
    for e in staged: e.wait()
    fans = [fan((crossed, flow), xp0), fan((att, None), xatt)]
    M = memory.shape[0]
    share = []
    for src, dst, m in ((inputs, xin, T), (memory, xmem, M)):
        kept.append(cp.local(src, rowsn(dst, m, n)))
        near.append(cp(src, rowsn(dst, m, n), core))
        share.append((cp(src, rowsn(dst, m, n), xp), rowsn(dst, m, 2 - 2 * x + c)))
    def adapter_weights():
        kept[0].wait(); kept[1].wait()
        for e, ref in zip(over, (down.at[:, md], up.at[md])):
            e.wait_recv()
            late.append(cp(ref, ref, core))
        near[0].wait_recv(); near[1].wait_recv()
        for e in late[:2]: e.wait_recv()
    def share_on():
        for e, ref in share:
            e.wait_recv()
            late.append(cp(ref, ref, core))
    def adapter_forward():
        own = rows[:, 0].reshape(T, D)
        for t in range(2):
            cols = pl.ds(t * 256, 256)
            g, s = gelu_both(dot(own, down[:, cols]))
            ay[1, :, cols] = (ADAPT_SCALE * g.astype(bf16).astype(f32)).astype(bf16)
            bslope[:, cols] = s
        def tile(t, _):
            cols = pl.ds(pl.multiple_of(t * 256, 256), 256)
            acc[:, :, cols] = acc[:, :, cols] + dot(ay[1], up[:, cols]).reshape(2, R, 256)
            return 0
        lax.fori_loop(0, D // 256, tile, 0)
    def adapter_back():
        def tile(t, _):
            cols = pl.ds(pl.multiple_of(t * 256, 256), 256)
            gbot = bslope[:, cols] * (ADAPT_SCALE * dot_right(brow[:, 0].reshape(T, D), up[cols, :]))
            ay[0, :, cols] = gbot.astype(bf16)
            return 0
        lax.fori_loop(0, down.shape[1] // 256, tile, 0)
        def tile2(t, _):
            cols = pl.ds(pl.multiple_of(t * 256, 256), 256)
            acc[:, :, cols] = acc[:, :, cols] + dot_right(ay[0], down[cols, :]).reshape(2, R, 256)
            return 0
        lax.fori_loop(0, D // 256, tile2, 0)
    def both(buf, h, g): return buf[h, 2 * g:2 * g + 2].reshape(2 * R, buf.shape[3])
    def put_out(level, h, g, t, p):
        cols = pl.ds(t * TW, TW)
        if g == 0:
            acc[h, :, cols] = p[:R] if level == 0 else acc[h, :, cols] + p[:R]
            part[h, 1, t] = p[R:].astype(bf16)
            send_part(level, h, 1, t)
        else:
            part[h, 3, t] = p[R:].astype(bf16)
            send_part(level, h, 3, t)
            part[h, 2, t] = p[:R].astype(bf16)
    def enter(h, g):
        xv = both(rows, h, g)
        def tile(t, _):
            cols = pl.ds(pl.multiple_of(t * TW, TW), TW)
            e, s = gelu_both(dot(xv, fin[:, cols]))
            hid[h, 2 * g:2 * g + 2, :, cols] = e.astype(bf16).reshape(2, R, TW)
            slope[h, 2 * g:2 * g + 2, :, cols] = s.reshape(2, R, TW)
            return 0
        lax.fori_loop(0, HID // TW, tile, 0)
        hv = both(hid, h, g)
        for t in range(NT):
            put_out(0, h, g, t, dot(hv, fout[:, pl.ds(t * TW, TW)]))
    def leave(h, g):
        xv = both(brow, h, g)
        def tile(t, _):
            cols = pl.ds(pl.multiple_of(t * TW, TW), TW)
            gh = dot_right(xv, fout[cols, :])
            gpre[h, 2 * g:2 * g + 2, :, cols] = (slope[h, 2 * g:2 * g + 2, :, cols].reshape(2 * R, TW) * gh).astype(bf16).reshape(2, R, TW)
            return 0
        lax.fori_loop(0, HID // TW, tile, 0)
        hv = both(gpre, h, g)
        for t in range(NT):
            put_out(1, h, g, t, dot_right(hv, fin[pl.ds(t * TW, TW), :]))
    fac = gain[...].astype(f32)
    off = shift[...].astype(f32)
    back = []
    def turn(h):
        n3, inv3 = norm(second[span(h), :] + acc[h])
        result[span(h), :] = (n3 * fac + off).astype(bf16)
        e = cot[span(h), :].astype(f32)
        gb = norm_back(e, n3, inv3, fac)
        gbl = gb.astype(bf16)
        brow[h, 0] = gbl
        back.append(spread(brow, h))
        blow[span(h), :] = gbl
        acc[h] = gb
        gg, gs = jnp.sum(e * n3, axis=0, keepdims=True), jnp.sum(e, axis=0, keepdims=True)
        ngrad[0:1, :] = gg if h == 0 else ngrad[0:1, :] + gg
        ngrad[1:2, :] = gs if h == 0 else ngrad[1:2, :] + gs
    (beside0, forward0, across0), (beside1, forward1, across1) = ways
    for e in loads: e.wait()
    beside0()
    enter(0, 0)
    forward0()
    across0()
    enter(0, 1)
    forward1()
    beside1()
    enter(1, 0)
    collect(0, 0)
    across1()
    enter(1, 1)
    adapter_weights()
    adapter_forward()
    collect(0, 1)
    gather_up(0, 0)
    turn(0)
    gather_up(0, 1)
    turn(1)
    (beside0, forward0, across0), (beside1, forward1, across1) = back
    beside0()
    leave(0, 0)
    forward0()
    adapter_back()
    across0()
    leave(0, 1)
    forward1()
    beside1()
    leave(1, 0)
    collect(1, 0)
    across1()
    leave(1, 1)
    def wtile(t, _):
        cols = pl.ds(pl.multiple_of(t * TW, TW), TW)
        fi[:, cols] = dot_left(rows[...].reshape(4 * T, D), gpre[:, :, :, cols].reshape(4 * T, TW)).astype(bf16)
        fo[:, cols] = dot_left(hid[...].reshape(4 * T, HID), brow[:, :, :, cols].reshape(4 * T, TW)).astype(bf16)
        return 0
    lax.fori_loop(0, 1, wtile, 0)
    collect(1, 1)
    lax.fori_loop(1, HID // TW, wtile, 0)
    kept += [cp.local(fi, fi_out), cp.local(fo, fo_out)]
    share_on()
    for h in range(2):
        gather_up(1, h)
        gsec[span(h), :] = acc[h]
    for e in kept[2:]: e.wait()
    for e in near[2:] + late[2:]: e.wait_recv()
    for e in fans: e()
    cp.close()

def feed(A, second, cot, fin, fout, fin2, fout2, down, up, gain, shift, inputs, memory, att, flow, crossed):
    T, D = second.shape; HID = 2 * fin.shape[1]; AD = down.shape[1] * 4; M = memory.shape[0]
    v = lambda *s: pltpu.VMEM(s, bf16)
    vf = lambda *s: pltpu.VMEM(s, f32)
    vm = pl.BlockSpec(memory_space=pltpu.VMEM)
    any_ = pl.BlockSpec(memory_space=pl.ANY)
    sds = jax.ShapeDtypeStruct
    four = sds((4 * T, D), bf16)
    return pl.pallas_call(
        functools.partial(feed_kernel, A),
        out_shape=(sds((T, D), bf16), sds((T, D), f32), sds((D, HID), bf16), sds((HID, D), bf16), sds((2, T, AD), bf16), sds((T, D), bf16), sds((2, D), f32),
            four, four, four, sds((4 * M, D), bf16)),
        in_specs=[vm] * 2 + [any_] * 6 + [vm] * 2 + [any_] * 5, out_specs=(vm,) * 2 + (any_,) * 2 + (vm,) * 3 + (any_,) * 4,
        scratch_shapes=[v(T, D), v(M, D), v(T, D), v(T, D), v(T, D), v(D, HID), v(HID, D), v(D, HID), v(HID, D), v(D, AD), v(AD, D), v(2, 4, T // 2, D), v(2, 4, T // 2, D), v(2, 4, T // 2, HID), vf(2, 4, T // 2, HID), v(2, 4, T // 2, HID), v(2, 4, D // 256, T // 2, 256),
            v(2, 2, D // 256, T // 2, 256), v(2, 2, D // 256, T // 2, 256), v(2, 2, D // 256, T // 2, 256), vf(T, AD), vf(2, T // 2, D),
            pltpu.SemaphoreType.DMA((128,)), pltpu.SemaphoreType.DMA((128,))],
        compiler_params=pltpu.CompilerParams(collective_id=3, has_side_effects=True, vmem_limit_bytes=60 << 20),
        name="feed_forward")(second, cot, fin, fout, fin2, fout2, down, up, gain, shift, inputs, memory, att, flow, crossed)


NEGATIVE = -1000000000.0
PADDED = 32
PREFIX = 30

def project(x, weight, out, tile=256):
    def step(t, _):
        cols = pl.ds(pl.multiple_of(t * tile, tile), tile)
        out[:, cols] = dot(x[...], weight[:, cols]).astype(out.dtype)
        return 0
    lax.fori_loop(0, out.shape[1] // tile, step, 0)


def lane_half(rows):
    return lax.broadcasted_iota(jnp.int32, (rows, 128), 1) < 64

def split_heads(v):
    low = lane_half(v.shape[0])
    zero = jnp.zeros_like(v)
    return jnp.where(low, v, zero), jnp.where(low, zero, v)

def self_mask(seg_col, seg_row):
    T = seg_col.shape[0]
    row = lax.broadcasted_iota(jnp.int32, (T, T), 0)
    col = lax.broadcasted_iota(jnp.int32, (T, T), 1)
    own = jnp.where((row >= col) & (seg_col[...] == seg_row[...]), 0.0, NEGATIVE)
    lane = lax.broadcasted_iota(jnp.int32, (T, PADDED), 1)
    return jnp.concatenate([own, jnp.where(lane < 30, 0.0, NEGATIVE)], axis=1)

def attend(q, keys, values, penalty, probs, out, pairs=8):
    def step(p, _):
        cols = pl.ds(pl.multiple_of(p * 128, 128), 128)
        kk, vv = keys(cols), values(cols)
        qs = split_heads(q[:, cols])
        vs = split_heads(vv)
        total = None
        for s in range(2):
            score = jnp.where(penalty[...] < -1.0, NEGATIVE, dot_right(qs[s], kk) * 0.125)
            e = jnp.exp(score - jnp.max(score, axis=-1, keepdims=True))
            prob = (e * (1.0 / jnp.sum(e, axis=-1, keepdims=True))).astype(bf16)
            probs[2 * p + s] = prob
            mixed = dot(prob, vs[s])
            total = mixed if total is None else total + mixed
        out[:, cols] = total.astype(bf16)
        return 0
    lax.fori_loop(0, pairs, step, 0)


def both_keys(own, prows, offset):
    def get(cols):
        shifted = pl.ds(pl.multiple_of(cols.start + offset, 128), 128)
        return jnp.concatenate([own[:, cols], prows[:, shifted]], axis=0)
    return get

def whole(ref):
    return lambda cols: ref[:, cols]

def add_norm(base, low, weight, gain, shift, out, normed, inverse, tile=256):
    def step(t, _):
        cols = pl.ds(pl.multiple_of(t * tile, tile), tile)
        out[:, cols] = base[:, cols].astype(f32) + dot(low[...], weight[:, cols])
        return 0
    lax.fori_loop(0, out.shape[1] // tile, step, 0)
    n, i = norm(out[...])
    normed[...] = n
    inverse[...] = i
    out[...] = n * gain + shift

def forward_kernel(inputs, memory, seg_col, seg_row, mem_row, weights, prows, vecs,
                   q, k, v, probs, attended, first, n1, i1, cq, ck, cv, cprobs, crossed, second, n2, i2, pen, cpen):
    width = inputs.shape[1]
    pen[...] = self_mask(seg_col, seg_row)
    cpen[...] = jnp.where(seg_col[...] == mem_row[...], 0.0, NEGATIVE)
    project(inputs, weights.at[0], q); project(inputs, weights.at[1], k); project(inputs, weights.at[2], v)
    project(memory, weights.at[6], ck); project(memory, weights.at[7], cv)
    attend(q, both_keys(k, prows, 0), both_keys(v, prows, width), pen, probs, attended)
    add_norm(inputs, attended, weights.at[3], vecs[0:1, :], vecs[1:2, :], first, n1, i1)
    q[...] = q[...]
    def step(t, _):
        cols = pl.ds(pl.multiple_of(t * 256, 256), 256)
        cq[:, cols] = dot(first[...].astype(bf16), weights[4, :, cols]).astype(bf16)
        return 0
    lax.fori_loop(0, width // 256, step, 0)
    attend(cq, whole(ck), whole(cv), cpen, cprobs, crossed)
    add_norm(first, crossed, weights.at[5], vecs[2:3, :], vecs[3:4, :], second, n2, i2)

def forward(inputs, memory, seg_col, seg_row, mem_row, weights, prows, vecs):
    T, D = inputs.shape; M = memory.shape[0]
    vm = pl.BlockSpec(memory_space=pltpu.VMEM)
    sds = jax.ShapeDtypeStruct
    row, mrow, full, one = sds((T, D), bf16), sds((M, D), bf16), sds((T, D), f32), sds((T, 1), f32)
    return pl.pallas_call(forward_kernel,
        out_shape=(row, row, row, sds((16, T, T + PADDED), bf16), row, full, full, one, row, mrow, mrow, sds((16, T, M), bf16), row, full, full, one),
        in_specs=[vm] * 8, out_specs=(vm,) * 16,
        scratch_shapes=[pltpu.VMEM((T, T + PADDED), f32), pltpu.VMEM((T, M), f32)],
        compiler_params=pltpu.CompilerParams(vmem_limit_bytes=60 << 20), name="attention_forward")(
            inputs, memory, seg_col, seg_row, mem_row, weights, prows, vecs)

def norm_back_into(e, n, i, gain, out, ngrad, at):
    ee = e[...]
    nn = n[...]
    out[...] = norm_back(ee, nn, i[...], gain)
    ngrad[at:at + 1, :] = jnp.sum(ee * nn, axis=0, keepdims=True)
    ngrad[at + 1:at + 2, :] = jnp.sum(ee, axis=0, keepdims=True)


def repeat(n):
    row = lax.broadcasted_iota(jnp.int32, (n, 128), 0)
    col = lax.broadcasted_iota(jnp.int32, (n, 128), 1)
    return jnp.where(row == lax.rem(col, n), 1.0, 0.0).astype(bf16)

def columns(t, tile=256):
    return pl.ds(pl.multiple_of(t * tile, tile), tile)

def loop(start, stop, step):
    lax.fori_loop(start, stop, lambda t, z: (step(t), z)[1], 0)

def front_kernel(A, r, inputs, memory, seg_row, mem_row, embed, inner, outer, norms, *refs):
    ws, (fin, fout) = refs[:8], refs[8:10]
    (wout, fin2, fout2, tangent, prows_o, vecs_o, q_o, k_o, v_o, probs_o, att_o, first_o, n1_o, i1_o, cq_o, ck_o, cv_o, cprobs_o, crossed_o,
     second_o, slow_o, n2_o, i2_o) = refs[10:33]
    (g, q, k, v, probs, att, first, flow, n1, i1, cq, ck, cv, cprobs, crossed, second, slow, n2, i2, pen, cpen,
     buf, got, zbuf, r0, r1, prows, nout, vecs, tan, ssem, rsem) = refs[33:]
    a, b, x, c = place()
    core, xp, yp = device(a, b, x, 1 - c), device(a, b, 1 - x, c), device(a, 1 - b, x, c)
    zp = [device((a + j) % A, b, x, c) for j in range(A)]
    za = a + 1 - 2 * (a % 2)
    zq = device(za, b, x, c)
    greet([core, xp, yp] + zp[1:])
    cp = Copies(ssem, rsem)
    T, D = inputs.shape
    pairs = 4
    small = {}
    def pre0():
        zbuf[a] = jnp.zeros(zbuf.shape[1:], f32)
        zbuf[a, :PREFIX, :] = dot(embed[...], inner[...])
        small["s"] = [cp(zbuf.at[a], zbuf.at[a], zp[j]) for j in range(1, A)]
    pre0()
    def row(a_, b_, x_):
        return pl.multiple_of(((a_ * 2 + b_) * 2 + x_) * 2 * r, 2 * r)
    at = pl.ds(pl.multiple_of(row(a, b, x) + c * r, r), r)
    cut = (pl.ds(0, D // 2), pl.ds(D // 2, D // 2))
    def block(i, h, a_, b_, x_):
        return g.at[2 * i + c, pl.ds(row(a_, b_, x_), 2 * r), cut[h]]
    kept = []
    own, cross = [], []
    base = cp.count
    for i in range(pairs):
        s1, s2, rr = ssem.at[cp.count], ssem.at[cp.count + 1], rsem.at[cp.count]
        cp.count += 2
        def start(keep, give):
            pltpu.make_async_copy(ws[2 * i + keep], g.at[2 * i + keep, at], s2).start()
            remote(ws[2 * i + give], g.at[2 * i + give, at], s1, rr, core).start()
        pl.when(c == 0)(functools.partial(start, 0, 1))
        pl.when(c == 1)(functools.partial(start, 1, 0))
        own.append(pltpu.make_async_copy(ws[2 * i], g.at[2 * i, at], s2))
        cross.append(remote(ws[2 * i], g.at[2 * i, at], s1, rr, core))
    G = norms.shape[0]
    me = ((a * 2 + b) * 2 + x) * 2 + c
    chip = (a * 2 + b) * 2 + x
    def nrows(start, count): return nout.at[pl.ds(pl.multiple_of(start * G, G), count * G)]
    def lanes(start, count): return prows.at[:, pl.ds(pl.multiple_of(start * 128, 128), count * 128)]
    nout[pl.ds(pl.multiple_of(me * G, G), G), :] = dot(norms[...], repeat(norms.shape[1])).astype(bf16)
    peers = (core, xp, yp)
    def settle():
        for e in small["s"]: e.wait_recv()
    def pre1():
        settle()
        t = zbuf[0]
        for n in range(1, A): t = t + zbuf[n]
        buf[0] = t
        small["s"] = [cp(buf.at[0], got.at[0], core)]
    def pre2(n):
        def go():
            settle()
            buf[n] = buf[n - 1] + got[n - 1]
            small["s"] = [cp(buf.at[n], got.at[n], peers[n])]
        return go
    def pre4():
        settle()
        t = jnp.tanh(buf[2] + got[2])
        tan[...] = t
        r0[...] = dot(dot_right(t.astype(bf16), outer[...]).astype(bf16), repeat(outer.shape[0])).astype(bf16)
        small["s"] = [cp(r0, r1, core), cp(nrows(me, 1), nrows(me, 1), core)]
        kept.append(cp.local(tan, tangent))
    def pre5():
        settle()
        lane = lax.broadcasted_iota(jnp.int32, (PADDED, 128), 1)
        prows[:, pl.ds(pl.multiple_of(chip * 128, 128), 128)] = jnp.where((lane // 64) == c, r0[...].astype(f32), r1[...].astype(f32)).astype(bf16)
        small["s"] = [cp(lanes(chip, 1), lanes(chip, 1), xp), cp(nrows(me - c, 2), nrows(me - c, 2), xp)]
    def pre6():
        settle()
        small["s"] = [cp(lanes(chip - x, 2), lanes(chip - x, 2), yp), cp(nrows(me - c - 2 * x, 4), nrows(me - c - 2 * x, 4), yp)]
    def pre7():
        settle()
        small["s"] = [cp(lanes(a * 4, 4), lanes(a * 4, 4), zp[j]) for j in range(1, A)] + [cp(nrows(a * 8, 8), nrows(a * 8, 8), zp[j]) for j in range(1, A)]
    def pre8():
        settle()
        lane = lax.broadcasted_iota(jnp.int32, (G, 128), 1) // 32
        for w in range(2 * A):
            s = nout[pl.ds(w * 4 * G, G), :].astype(f32)
            for n in range(1, 4):
                s = jnp.where(lane == n, nout[pl.ds((w * 4 + n) * G, G), :].astype(f32), s)
            vecs[:, pl.ds(w * 128, 128)] = s[:8]
        kept.append(cp.local(vecs, vecs_o))
        kept.append(cp.local(prows, prows_o))
    H = fin.shape[1]
    feeds, passed = {}, []
    def feed_send(i):
        n = D // 8
        ri = pl.ds(pl.multiple_of(c * (D // 2) + i * n, n), n)
        m = H // 8
        ro = pl.ds(pl.multiple_of(c * (H // 2) + i * m, m), m)
        feeds[i] = [(cp(fin.at[ri], fin2.at[ri], zq), fin2.at[ri]),
                    (cp(fout.at[ro], fout2.at[ro], zq), fout2.at[ro])]
    def feed_pass(i):
        for e, ref in feeds[i]:
            e.wait_recv()
            passed.append(cp(ref, ref, core))
    zc, mc, lc, dc = {}, {}, {}, {}
    two, three = (yp, xp), (xp, yp)
    def first_send(i):
        own[i].wait(); cross[i].wait()
        for h in range(2):
            mc[i, h, 0] = cp(block(i, h, a, b, x), block(i, h, a, b, x), two[h])
        for h in range(2):
            lc[i, h, 0, 0] = cp(block(i, h, a, b, x), block(i, h, a, b, x), three[h])
        for j in range(1, A):
            for h in range(2):
                zc[i, h, j] = cp(block(i, h, a, b, x), block(i, h, a, b, x), zp[j])
    def mid(i, j):
        aj = (a + A - j) % A
        for h in range(2):
            zc[i, h, j].wait_recv()
            mc[i, h, j] = cp(block(i, h, aj, b, x), block(i, h, aj, b, x), two[h])
        for h in range(2):
            lc[i, h, j, 0] = cp(block(i, h, aj, b, x), block(i, h, aj, b, x), three[h])
    def third(i, j):
        aj = (a + A - j) % A
        for h in range(2):
            w = (aj, 1 - b, x) if h == 0 else (aj, b, 1 - x)
            mc[i, h, j].wait_recv()
            lc[i, h, j, 1] = cp(block(i, h, *w), block(i, h, *w), three[h])
    per = D // A
    def finish(i, j):
        aj = (a + A - j) % A
        for h in range(2):
            lc[i, h, j, 0].wait_recv(); lc[i, h, j, 1].wait_recv()
        ref = g.at[2 * i + c, pl.ds(pl.multiple_of(aj * per, per), per)]
        dc[i, j] = cp(ref, ref, core)
    def arrive(i):
        for j in range(A): dc[i, j].wait_recv()
        kept.append(cp.local(g.at[2 * i], wout.at[2 * i]))
        kept.append(cp.local(g.at[2 * i + 1], wout.at[2 * i + 1]))
    def halves(src, w, out):
        def part(n):
            def go():
                xv = src[...]
                def step(t):
                    out[:, columns(t)] = dot(xv, g[w, :, columns(t)]).astype(bf16)
                loop(2 * n, 2 * n + 2, step)
            return go
        return [part(0), part(1)]
    def keep(src, dst):
        def go(): kept.append(cp.local(src, dst))
        return go
    def masks():
        row = lax.broadcasted_iota(jnp.int32, (T, T), 0)
        col = lax.broadcasted_iota(jnp.int32, (T, T), 1)
        across = jnp.broadcast_to(seg_row[...].astype(f32), (T, T))
        down = across.T
        pen[:, :T] = jnp.where((row >= col) & (down == across), 0.0, NEGATIVE)
        lane = lax.broadcasted_iota(jnp.int32, (T, PADDED), 1)
        pen[:, T:] = jnp.where(lane < PREFIX, 0.0, NEGATIVE)
        for n in range(memory.shape[0] // T):
            span = slice(n * T, (n + 1) * T)
            cpen[:, span] = jnp.where(down == mem_row[:, span].astype(f32), 0.0, NEGATIVE)
    def softmax(qv, kk, penalty):
        score = jnp.where(penalty[...] < -1.0, NEGATIVE, dot_right(qv, kk) * 0.125)
        e = jnp.exp(score - jnp.max(score, axis=-1, keepdims=True))
        return (e * (1.0 / jnp.sum(e, axis=-1, keepdims=True))).astype(bf16)
    def own_attend(n):
        def go():
            def step(p):
                cols = columns(p, 128)
                kk = jnp.concatenate([k[:, cols], prows[:, cols]], axis=0)
                vv = jnp.concatenate([v[:, cols], prows[:, pl.ds(pl.multiple_of(D + p * 128, 128), 128)]], axis=0)
                qs, vs = split_heads(q[:, cols]), split_heads(vv)
                total = None
                for s in range(2):
                    prob = softmax(qs[s], kk, pen)
                    probs[2 * p + s] = prob
                    m = dot(prob, vs[s])
                    total = m if total is None else total + m
                att[:, cols] = total.astype(bf16)
            loop(2 * n, 2 * n + 2, step)
        return go
    def cross_scores(n):
        def go():
            def step(p):
                cols = columns(p, 128)
                qs = split_heads(cq[:, cols])
                for s in range(2):
                    cprobs[2 * p + s] = softmax(qs[s], ck[:, cols], cpen)
            loop(2 * n, 2 * n + 2, step)
        return go
    def cross_mix(n):
        def go():
            def step(p):
                cols = columns(p, 128)
                vs = split_heads(cv[:, cols])
                crossed[:, cols] = (dot(cprobs[2 * p], vs[0]) + dot(cprobs[2 * p + 1], vs[1])).astype(bf16)
            loop(4 * n, 4 * n + 4, step)
        return go
    def normed(base, low, w, at, out, nn, ii, olow):
        def part(n):
            def go():
                lv = low[...]
                def step(t):
                    out[:, columns(t)] = base[:, columns(t)].astype(f32) + dot(lv, g[w, :, columns(t)])
                loop(2 * n, 2 * n + 2, step)
            return go
        def last():
            m, inv = norm(out[...])
            nn[...] = m
            ii[...] = inv
            s = m * vecs[at:at + 1, :] + vecs[at + 1:at + 2, :]
            out[...] = s
            olow[...] = s.astype(bf16)
        return [part(0), part(1), last]
    comp = {
        0: halves(inputs, 0, q) + halves(inputs, 1, k) + [keep(q, q_o), keep(k, k_o), masks],
        1: halves(inputs, 2, v) + [keep(v, v_o)] + [own_attend(n) for n in range(4)] + [keep(probs, probs_o), keep(att, att_o)]
           + normed(inputs, att, 3, 0, first, n1, i1, flow) + [keep(flow, first_o), keep(n1, n1_o), keep(i1, i1_o)],
        2: halves(memory, 4, ck) + [keep(ck, ck_o)] + halves(flow, 5, cq) + [keep(cq, cq_o)] + [cross_scores(n) for n in range(4)] + [keep(cprobs, cprobs_o)],
        3: halves(memory, 6, cv) + [keep(cv, cv_o)] + [cross_mix(n) for n in range(2)] + [keep(crossed, crossed_o)]
           + normed(first, crossed, 7, 2, second, n2, i2, slow) + [keep(second, second_o), keep(slow, slow_o), keep(n2, n2_o), keep(i2, i2_o)],
    }
    queue = []
    def turn(count=1):
        for _ in range(count):
            if queue: queue.pop(0)()
    small_steps = [pre1, pre2(1), pre2(2), pre4, pre5, pre6, pre7]
    def tick():
        if small_steps: small_steps.pop(0)()
    first_send(0)
    tick()
    for i in range(pairs):
        if i + 1 < pairs:
            first_send(i + 1)
        feed_send(i)
        third(i, 0)
        tick()
        turn()
        if i:
            finish(i - 1, 2)
            turn()
        mid(i, 1)
        tick()
        turn()
        if i:
            finish(i - 1, 3)
            turn()
        mid(i, 2)
        tick()
        turn()
        if i: feed_pass(i - 1)
        mid(i, 3)
        tick()
        turn()
        third(i, 1)
        if i:
            arrive(i - 1)
            if i == 2: pre8()
            queue += comp[i - 1]
        turn()
        finish(i, 0)
        turn(2)
        third(i, 2)
        turn(2)
        finish(i, 1)
        turn(2)
        third(i, 3)
        turn(2)
    feed_pass(3)
    finish(3, 2)
    turn(2)
    finish(3, 3)
    turn(100)
    arrive(3)
    queue += comp[3]
    turn(100)
    for e in kept: e.wait()
    for e in passed: e.wait_recv()
    own_ids = None
    cp.close()

def front(A, r, inputs, memory, seg_row, mem_row, embed, inner, outer, norms, ws, fin, fout):
    T, D = inputs.shape; M = memory.shape[0]; H = fin.shape[1]
    vm = pl.BlockSpec(memory_space=pltpu.VMEM)
    any_ = pl.BlockSpec(memory_space=pl.ANY)
    sds = jax.ShapeDtypeStruct
    v = lambda *s: pltpu.VMEM(s, bf16)
    vf = lambda *s: pltpu.VMEM(s, f32)
    row, mrow, full, one = sds((T, D), bf16), sds((M, D), bf16), sds((T, D), f32), sds((T, 1), f32)
    S = (PADDED, inner.shape[1])
    probs, cprobs = (16, T, T + PADDED), (16, T, M)
    return pl.pallas_call(functools.partial(front_kernel, A, r),
        out_shape=(sds((8, D, D), bf16), sds((D, H), bf16), sds((H, D), bf16),
            sds(S, f32), sds((PADDED, 2 * D), bf16), sds((8, D), f32), row, row, row, sds(probs, bf16), row, row, full, one, row, mrow, mrow, sds(cprobs, bf16), row,
            full, row, full, one),
        in_specs=[vm] * 8 + [any_] * 10, out_specs=(any_,) * 23,
        scratch_shapes=[v(8, D, D), v(T, D), v(T, D), v(T, D), v(*probs), v(T, D), vf(T, D), v(T, D), vf(T, D), vf(T, 1), v(T, D), v(M, D), v(M, D), v(*cprobs), v(T, D),
            vf(T, D), v(T, D), vf(T, D), vf(T, 1), vf(T, T + PADDED), vf(T, M),
            vf(3, *S), vf(3, *S), vf(A, *S), v(PADDED, 128), v(PADDED, 128), v(PADDED, 2 * D), v(8 * A * norms.shape[0], 128), vf(8, D), vf(*S),
            pltpu.SemaphoreType.DMA((320,)), pltpu.SemaphoreType.DMA((320,))],
        compiler_params=pltpu.CompilerParams(collective_id=1, has_side_effects=True, vmem_limit_bytes=60 << 20), name="front")(
            inputs, memory, seg_row, mem_row, embed, inner, outer, norms, *ws, fin, fout)


def exact(l, r, dims):
    return lax.dot_general(l, r, (dims, ((), ())), precision=lax.Precision.HIGHEST, preferred_element_type=f32)

def back_kernel(A, r, gsec, n2, i2, vecs, ngrad3, tangent, embed, inner, outer, *refs):
    late, (slow, blow, ay, weights, fi, fo, xp0, xatt, xin, xmem) = refs[:11], refs[11:21]
    back_body(A, r, gsec, n2, i2, vecs, ngrad3, tangent, embed, inner, outer, late, slow, blow, ay, weights, fi, fo, xp0, xatt, xin, xmem, *refs[21:])

def back_body(A, r, gsec, n2, i2, vecs, ngrad3, tangent, embed, inner, outer, late, slow, blow, ay, weights, fi, fo, xp0, xatt, xin, xmem,
                igrad_o, mgrad_o, out, aout, fi_out, fo_out, outer_o, inner_o, embed_o, nsum,
                igrad, mgrad, cq, ck, cv, cprobs, n1, i1, q, k, v, probs, prows, ws, gmid, gfirst, og, mid, dcq, dck, dcv, startl, dq, dk, dv, pg,
                xb, yb, mb, mby, axb, ayb, pb, apb, fib, fob, r1, r2, r3, sb, xs, ra1, ra2, ra3, rfi, rfo, rzi, rzo, rxi, rxo, ob, aob, fib2, fob2,
                buf, got, zbuf, nbuf, ngot, nz, w0, w1, w2, w3, s0, s1, s2, ssem, rsem):
    a, b, x, c = place()
    o = 1 - c
    core, xp, yp = device(a, b, x, o), device(a, b, 1 - x, c), device(a, 1 - b, x, c)
    dp = device(a, b, 1 - x, o)
    place_n = x * 2 + c
    zp = [device((a + j) % A, b, x, c) for j in range(A)]
    za = a + 1 - 2 * (a % 2)
    zq = device(za, b, x, c)
    peers = (core, xp, yp)
    T, D = gsec.shape
    M = xmem.shape[0] // 4
    HID = fi.shape[1] // 2
    Q = fi.shape[0] // 4
    half = D // 2
    cp = Copies(ssem, rsem)
    loads = {}
    def fetch(slot, w):
        loads[slot] = cp.local(weights.at[w], ws.at[slot])
    loaded = [cp.local(src, dst) for src, dst in zip(late, (cq, ck, cv, cprobs, n1, i1, q, k, v, probs, prows))]
    def ready(start, stop):
        for e in loaded[start:stop]: e.wait()
    fetch(0, 7); fetch(1, 5); fetch(2, 3); fetch(3, 4)
    fown = []
    for xx in range(2):
        dq_ = pl.ds(pl.multiple_of((xx * 2 + c) * Q, Q), Q)
        fown += [cp.local(fi.at[dq_, :], fib.at[xx]), cp.local(fo.at[:, dq_], fob.at[xx])]
    greet([core, xp, yp, dp] + zp[1:])
    def offer(srcs, mine, theirs):
        n = cp.count
        cp.count += 2
        def start(keep, give):
            pltpu.make_async_copy(srcs[keep], mine, ssem.at[n]).start()
            remote(srcs[give], theirs, ssem.at[n + 1], rsem.at[n], core).start()
        pl.when(c == 0)(functools.partial(start, 0, 1))
        pl.when(c == 1)(functools.partial(start, 1, 0))
        e = remote(srcs[0], theirs, ssem.at[n + 1], rsem.at[n], core)
        cp.all.append(e)
        return pltpu.make_async_copy(srcs[0], mine, ssem.at[n]).wait, e.wait_recv
    lowT, highT = pl.ds(0, T), pl.ds(T, T)
    waits = {}
    aw = offer((slow, blow), axb.at[lowT], axb.at[highT]) + offer((ay.at[0], ay.at[1]), ayb.at[lowT], ayb.at[highT])
    xload = cp.count
    cp.count += 4
    def load_x(me):
        pltpu.make_async_copy(xp0, xb.at[0], ssem.at[xload]).start()
        pltpu.make_async_copy(xmem, mb, ssem.at[xload + 1]).start()
        pltpu.make_async_copy(xin if me else xatt, xb.at[1], ssem.at[xload + 2]).start()
        pltpu.make_async_copy(xin, xb.at[2], ssem.at[xload + 3]).start()
    pl.when(c == 0)(functools.partial(load_x, 0))
    pl.when(c == 1)(functools.partial(load_x, 1))
    waits[0] = (pltpu.make_async_copy(xp0, xb.at[0], ssem.at[xload]).wait,)
    waits[1] = (pltpu.make_async_copy(xmem, mb, ssem.at[xload + 1]).wait,)
    waits[2] = (pltpu.make_async_copy(xin, xb.at[1], ssem.at[xload + 2]).wait,)
    waits[3] = (pltpu.make_async_copy(xin, xb.at[2], ssem.at[xload + 3]).wait,)
    def share(srcs, dst, t):
        m = srcs[0].shape[0]
        k = cp.count
        cp.count += 4
        wide = half // 2
        here = pl.ds(pl.multiple_of(x * half + t * wide, wide), wide)
        there = pl.ds(pl.multiple_of((1 - x) * half + t * wide, wide), wide)
        spot = dst.at[pl.ds(pl.multiple_of(place_n * m, m), m), pl.ds(t * wide, wide)]
        def start(me):
            own, other = srcs[me], srcs[1 - me]
            remote(own.at[:, there], spot, ssem.at[k + 1], rsem.at[k + 1], xp).start()
            remote(other.at[:, there], spot, ssem.at[k + 3], rsem.at[k + 3], dp).start()
            remote(other.at[:, here], spot, ssem.at[k + 2], rsem.at[k + 2], core).start()
            pltpu.make_async_copy(own.at[:, here], spot, ssem.at[k]).start()
        pl.when(c == 0)(functools.partial(start, 0))
        pl.when(c == 1)(functools.partial(start, 1))
        ways = [remote(srcs[0].at[:, here], spot, ssem.at[k + i], rsem.at[k + i], d) for i, d in ((1, xp), (2, core), (3, dp))]
        cp.all.extend(ways)
        return (pltpu.make_async_copy(srcs[0].at[:, here], spot, ssem.at[k]).wait,) + tuple(e.wait_recv for e in ways)
    fcopies = []
    for xx in range(2):
        dq_ = pl.ds(pl.multiple_of((xx * 2 + o) * Q, Q), Q)
        fcopies += [cp(fi.at[dq_, :], rfi.at[xx], core), cp(fo.at[:, dq_], rfo.at[xx], core)]

    zf, xf, outs = [], [], []
    def feed0():
        for e in fown: e.wait()
        for e in fcopies: e.wait_recv()
        for xx in range(2):
            def rows_fi(t):
                s = pl.ds(t * 32, 32)
                fib[xx, s, :] = fib[xx, s, :] + rfi[xx, s, :]
            loop(0, Q // 32, rows_fi)
            def rows_fo(t):
                s = pl.ds(t * 64, 64)
                fob[xx, s, :] = fob[xx, s, :] + rfo[xx, s, :]
            loop(0, 2 * HID // 64, rows_fo)
        zf.extend([cp(fib.at[:, :, pl.ds(HID, HID)], rzi, zq), cp(fob.at[:, pl.ds(HID, HID), :], rzo, zq)])
    def feed1():
        for e in zf: e.wait_recv()
        for xx in range(2):
            def rows_fi(t):
                s = pl.ds(t * 32, 32)
                fib[xx, s, pl.ds(0, HID)] = fib[xx, s, pl.ds(0, HID)] + rzi[xx, s, :]
            loop(0, Q // 32, rows_fi)
            def rows_fo(t):
                s = pl.ds(t * 64, 64)
                fob[xx, s, :] = fob[xx, s, :] + rzo[xx, s, :]
            loop(0, HID // 64, rows_fo)
        xf.extend([cp(fib.at[1 - x, :, pl.ds(0, HID)], rxi, xp), cp(fob.at[1 - x, pl.ds(0, HID), :], rxo, xp)])
    def feed2():
        for e in xf: e.wait_recv()
        def rows_fi(t):
            s = pl.ds(t * 32, 32)
            fib2[s, :] = fib[x, s, pl.ds(0, HID)].astype(f32) + rxi[s, :].astype(f32)
        loop(0, Q // 32, rows_fi)
        def rows_fo(t):
            s = pl.ds(t * 64, 64)
            fob2[s, :] = fob[x, s, :].astype(f32) + rxo[s, :].astype(f32)
        loop(0, HID // 64, rows_fo)
        outs.extend([cp.local(fib2, fi_out).wait, cp.local(fob2, fo_out).wait])

    first, second, third, fourth = {}, {}, {}, {}
    wide = half // 2
    numbers = {}
    for i in range(4):
        for t in range(2):
            numbers[i, t] = cp.count
            cp.count += 1
    def level1(i, t):
        n = numbers[i, t]
        return remote(pb.at[i, t, :, 1 - b], r1.at[i, t], ssem.at[n], rsem.at[n], yp)
    for i in range(4):
        for t in range(2):
            first[i, t] = level1(i, t)
            cp.all.append(first[i, t])
    def share_one(src, dst, t, owner):
        m = src.shape[0]
        k = cp.count
        cp.count += 4
        wide = half // 2
        here = pl.ds(pl.multiple_of(x * half + t * wide, wide), wide)
        there = pl.ds(pl.multiple_of((1 - x) * half + t * wide, wide), wide)
        spot = dst.at[pl.ds(pl.multiple_of(place_n * m, m), m), pl.ds(t * wide, wide)]
        kept = pltpu.make_async_copy(src.at[:, here], spot, ssem.at[k])
        ways = [remote(src.at[:, there], spot, ssem.at[k + 1], rsem.at[k + 1], xp), remote(src.at[:, here], spot, ssem.at[k + 2], rsem.at[k + 2], core),
                remote(src.at[:, there], spot, ssem.at[k + 3], rsem.at[k + 3], dp)]
        def mine():
            ways[0].start()
            kept.start()
        def other():
            ways[2].start()
            ways[1].start()
        pl.when(c == owner)(mine)
        pl.when(c != owner)(other)
        def arrived():
            kept.wait()
            for e in ways: e.wait_recv()
        def sent():
            pl.when(c == owner)(ways[0].wait_send)
            def both():
                ways[1].wait_send()
                ways[2].wait_send()
            pl.when(c != owner)(both)
        ending.append(sent)
        return (arrived,)
    ending = []
    used, filled = set(), set()
    def compute(i, t, owner=None):
        def go():
            if (i, owner) not in used:
                used.add((i, owner))
                for e in waits[i]: e()
            for e in shared[(i, t) if owner is None else (i, t, owner)]: e()
            cols = pl.ds(t * wide, wide)
            n = (0, None, 1, 2)[i]
            def rows(u):
                d = columns(u)
                p = dot_left(mb[:, d], mby[:, cols]) if i == 1 else dot_left(xb[n, :, d], yb[n, :, cols])
                pb[i, t, u] = p.astype(bf16).reshape(2, 2, 2 * r, wide)
            loop(0, A, rows)
            level1(i, t).start()
        if owner is None: go()
        else: pl.when(c == owner)(go)
    def one(i, t):
        def go():
            first[i, t].wait_recv()
            for j in range(1, A):
                aj = (a + j) % A
                pb[i, t, aj, b] = pb[i, t, aj, b] + r1[i, t, aj]
                third[i, t, j] = cp(pb.at[i, t, aj, b], r2.at[i, t, j - 1], zp[j])
            pb[i, t, a, b] = pb[i, t, a, b] + r1[i, t, a]
        return go
    def two(i, t):
        def go():
            for j in range(1, A): third[i, t, j].wait_recv()
            for s in (1 - x, x):
                e = pb[i, t, a, b, s].astype(f32)
                for j in range(1, A): e = e + r2[i, t, j - 1, s].astype(f32)
                sb[i, t, s] = e
            xs[i, t] = sb[i, t, 1 - x].astype(bf16)
            fourth[i, t] = cp(xs.at[i, t], r3.at[i, t], xp)
        return go
    def three(i, t):
        def go():
            fourth[i, t].wait_recv()
            ob[i, :, pl.ds(pl.multiple_of(x * half + t * wide, wide), wide)] = sb[i, t, x]
            ob[i, :, pl.ds(pl.multiple_of((1 - x) * half + t * wide, wide), wide)] = r3[i, t].astype(f32)
            filled.add((i, t))
            if (i, 1 - t) in filled:
                outs.append(cp.local(ob.at[i, pl.ds(pl.multiple_of(c * r, r), r)], out.at[2 * i + c]).wait)
                outs.append(cp(ob.at[i, pl.ds(pl.multiple_of(o * r, r), r)], out.at[2 * i + c], core).wait_recv)
        return go
    def adapt0():
        for e in aw: e()
        for t in range(2):
            apb[t] = dot_left(axb[...], ayb[:, pl.ds(t * 256, 256)]).astype(bf16).reshape(A, 2, D // (2 * A), 256)
        first["a"] = cp(apb.at[1 - x], ra1, xp)
    def adapt1():
        first["a"].wait_recv()
        def row(z):
            for s in range(2):
                apb[x, z, s] = apb[x, z, s] + ra1[z, s]
        loop(0, A, row)
        second["a"] = cp(apb.at[x, :, 1 - b], ra2, yp)
    def adapt2():
        second["a"].wait_recv()
        for j in range(1, A):
            aj = (a + j) % A
            apb[x, aj, b] = apb[x, aj, b] + ra2[aj]
            third["a", j] = cp(apb.at[x, aj, b], ra3.at[j - 1], zp[j])
        apb[x, a, b] = apb[x, a, b] + ra2[a]
    def adapt3():
        for j in range(1, A): third["a", j].wait_recv()
        t = apb[x, a, b].astype(f32)
        for j in range(1, A): t = t + ra3[j - 1].astype(f32)
        aob[0] = t[:, :128]
        aob[1] = t[:, 128:]
        outs.append(cp.local(aob.at[c], aout.at[c]).wait)
        outs.append(cp(aob.at[o], aout.at[c], core).wait_recv)
    small = {}
    def lanes(start, count): return pl.ds(pl.multiple_of(start * 128, 128), count * 128)
    def tail_norm0():
        small["n"] = [cp(nbuf.at[0], ngot.at[0], core)]
    def tail0():
        small["w"] = [cp(pg.at[:, lanes((a + j) % A * 4, 4)], w0.at[j - 1], zp[j]) for j in range(1, A)]
    def tail_norm(n):
        def go():
            for e in small["n"]: e.wait_recv()
            nbuf[n] = nbuf[n - 1] + ngot[n - 1]
            small["n"] = [cp(nbuf.at[n], ngot.at[n], peers[n])]
        return go
    def tail_norm3():
        for e in small["n"]: e.wait_recv()
        nz[a] = nbuf[2] + ngot[2]
        small["n"] = [cp(nz.at[a], nz.at[a], zp[j]) for j in range(1, A)]
    def tail_norm4():
        for e in small["n"]: e.wait_recv()
        t = nz[0]
        for n in range(1, A): t = t + nz[n]
        nsum[...] = t
    def tail1():
        t = pg[:, lanes(a * 4, 4)]
        for j, e in enumerate(small["w"]):
            e.wait_recv()
            t = t + w0[j]
        s0[...] = t
        small["w"] = [cp(s0.at[:, lanes((1 - b) * 2, 2)], w1, yp)]
    def tail2():
        small["w"][0].wait_recv()
        s1[...] = s0[:, lanes(b * 2, 2)] + w1[...]
        small["w"] = [cp(s1.at[:, lanes(1 - x, 1)], w2, xp)]
    def tail3():
        small["w"][0].wait_recv()
        s2[...] = s1[:, lanes(x, 1)] + w2[...]
        small["w"] = [cp(s2, w3, core)]
    def tail4():
        small["w"][0].wait_recv()
        t = s2[...] + w3[...]
        mine = jnp.where(c == 0, t[:, :64], t[:, 64:])
        buf[0] = exact(mine, outer[...].astype(f32), ((1,), (0,)))
        small["w"] = [cp(buf.at[0], got.at[0], core)]
        outer_o[...] = exact(mine, tangent[...].astype(bf16).astype(f32), ((0,), (0,)))
    def tail5(n):
        def go():
            small["w"][0].wait_recv()
            buf[n] = buf[n - 1] + got[n - 1]
            small["w"] = [cp(buf.at[n], got.at[n], peers[n])]
        return go
    def tail6():
        small["w"][0].wait_recv()
        zbuf[a] = buf[2] + got[2]
        small["w"] = [cp(zbuf.at[a], zbuf.at[a], zp[j]) for j in range(1, A)]
    def tail7():
        for e in small["w"]: e.wait_recv()
        t = zbuf[0]
        for n in range(1, A): t = t + zbuf[n]
        tan = tangent[...]
        t = t * (1.0 - tan * tan)
        inner_o[...] = exact(embed[...].astype(f32), t[:PREFIX], ((0,), (0,)))
        embed_o[...] = exact(t[:PREFIX], inner[...].astype(f32), ((1,), (1,)))
    def norm_two():
        norm_back_into(gsec, n2, i2, vecs[2:3, :], gmid, nbuf.at[0], 2)
        mid[...] = gmid[...].astype(bf16)
    def back_project(src, slot, n):
        def go():
            s = src[...]
            loop(2 * n, 2 * n + 2, lambda t: og.__setitem__((slice(None), columns(t)), dot_right(s, ws[slot, columns(t), :]).astype(bf16)))
        return go
    def wait_slot(slot):
        def go(): loads[slot].wait()
        return go
    def pair_back(p, grad, qr, kk, vv, pr):
        cols = columns(p, 128)
        qs, ks, gs = split_heads(qr[:, cols]), split_heads(kk), split_heads(grad[:, cols])
        res = None
        for s in range(2):
            low = pr[2 * p + s]
            prob = low.astype(f32)
            t = prob * dot_right(gs[s], vv)
            ds = (t - prob * jnp.sum(t, axis=-1, keepdims=True)).astype(bf16)
            m = (dot(ds, ks[s]), dot_left(ds, qs[s]), dot_left(low, gs[s]))
            res = m if res is None else tuple(e + f for e, f in zip(res, m))
        return cols, res[0] * 0.125, res[1] * 0.125, res[2]
    def cross_back(n):
        def go():
            def step(p):
                cs = columns(p, 128)
                cols, m1, m2, m3 = pair_back(p, og, cq, ck[:, cs], cv[:, cs], cprobs)
                dcq[:, cols] = m1.astype(bf16)
                dck[:, cols] = m2.astype(bf16)
                dcv[:, cols] = m3.astype(bf16)
            for p in range(2 * n, 2 * n + 2): step(p)
        return go
    def self_back(n):
        def go():
            def step(p):
                cs = columns(p, 128)
                cv_ = pl.ds(pl.multiple_of(D + p * 128, 128), 128)
                kk = jnp.concatenate([k[:, cs], prows[:, cs]], axis=0)
                vv = jnp.concatenate([v[:, cs], prows[:, cv_]], axis=0)
                cols, m1, m2, m3 = pair_back(p, og, q, kk, vv, probs)
                dq[:, cols] = m1.astype(bf16)
                dk[:, cols] = m2[:T].astype(bf16)
                dv[:, cols] = m3[:T].astype(bf16)
                pg[:, cols] = m2[T:]
                pg[:, cv_] = m3[T:]
            for p in range(2 * n, 2 * n + 2): step(p)
        return go
    def first_grad():
        s = dcq[...]
        def step(t):
            gfirst[:, columns(t)] = gmid[:, columns(t)] + dot_right(s, ws[1, columns(t), :])
        loop(0, D // 256, step)
    def norm_one():
        norm_back_into(gfirst, n1, i1, vecs[0:1, :], gmid, nbuf.at[0], 0)
        nbuf[0, 4:6, :] = ngrad3[...]
        nbuf[0, 6:8, :] = jnp.zeros((2, D), f32)
        startl[...] = gmid[...].astype(bf16)
    def memory_part(n):
        def go():
            def step(t):
                mgrad[:, columns(t)] = (dot_right(dck[...], ws[3, columns(t), :]) + dot_right(dcv[...], ws[0, columns(t), :])).astype(bf16)
            loop(2 * n, 2 * n + 2, step)
        return go
    def input_part(n):
        def go():
            def step(t):
                s = gmid[:, columns(t)] + dot_right(dq[...], ws[1, columns(t), :]) + dot_right(dk[...], ws[2, columns(t), :]) + dot_right(dv[...], ws[3, columns(t), :])
                igrad[:, columns(t)] = s.astype(bf16)
            loop(2 * n, 2 * n + 2, step)
        return go
    shared = {}
    def spread(i, srcs, dst):
        for t in range(2): shared[i, t] = share(srcs, dst, t)
    def spread_one(i, src, dst, owner):
        for t in range(2): shared[i, t, owner] = share_one(src, dst, t, owner)
    norm_two()
    spread_one(0, mid, yb.at[0], 0)
    wait_slot(0)()
    back_project(mid, 0, 0)()
    back_project(mid, 0, 1)()
    fetch(0, 6)
    ready(0, 4)
    cross_back(0)()
    cross_back(1)()
    cross_back(2)()
    cross_back(3)()
    compute(0, 1, 0)
    spread_one(0, dcq, yb.at[0], 1)
    feed0()
    wait_slot(1)()
    first_grad()
    fetch(1, 0)
    ready(4, 6)
    norm_one()
    spread(1, (dck, dcv), mby)
    compute(0, 1, 1)
    compute(0, 0, 0)
    wait_slot(2)()
    back_project(startl, 2, 0)()
    back_project(startl, 2, 1)()
    fetch(2, 1)
    ready(6, 11)
    self_back(0)()
    wait_slot(3)()
    wait_slot(0)()
    memory_part(0)()
    one(0, 1)()
    compute(0, 0, 1)
    self_back(1)()
    compute(1, 0)
    self_back(2)()
    tail_norm0()
    spread_one(2, startl, yb.at[1], 0)
    one(0, 0)()
    tail_norm(1)()
    self_back(3)()
    compute(1, 1)
    tail0()
    spread_one(2, dq, yb.at[1], 1)
    spread(3, (dk, dv), yb.at[2])
    compute(2, 0, 0)
    compute(2, 1, 0)
    compute(2, 0, 1)
    one(1, 0)()
    adapt0()
    compute(3, 1)
    feed1()
    one(1, 1)()
    one(2, 0)()
    tail1()
    compute(2, 1, 1)
    one(3, 1)()
    tail2()
    compute(3, 0)
    one(2, 1)()
    adapt1()
    one(3, 0)()
    two(0, 1)()
    tail3()
    tail4()
    two(1, 1)()
    adapt2()
    tail5(1)()
    two(0, 0)()
    two(1, 0)()
    tail5(2)()
    three(1, 1)()
    memory_part(1)()
    outs.append(cp.local(mgrad, mgrad_o).wait)
    fetch(3, 2)
    wait_slot(1)()
    wait_slot(2)()
    wait_slot(3)()
    input_part(0)()
    two(3, 1)()
    three(1, 0)()
    tail6()
    three(0, 0)()
    two(3, 0)()
    tail_norm(2)()
    three(0, 1)()
    three(3, 1)()
    input_part(1)()
    outs.append(cp.local(igrad, igrad_o).wait)
    adapt3()
    three(3, 0)()
    two(2, 0)()
    tail_norm3()
    feed2()
    two(2, 1)()
    three(2, 1)()
    three(2, 0)()
    tail7()
    tail_norm4()
    for e in ending: e()
    for e in outs: e()
    cp.close()

def back(A, r, first, late, rest):
    gsec = first[0]
    T, D = gsec.shape; M = rest[-1].shape[0] // 4
    fi, fo = rest[4:6]
    Q, H2 = fi.shape[0] // 4, fi.shape[1]
    H = H2 // 2
    half = D // 2
    v = lambda *s: pltpu.VMEM(s, bf16)
    vf = lambda *s: pltpu.VMEM(s, f32)
    any_ = pl.BlockSpec(memory_space=pl.ANY)
    vm = pl.BlockSpec(memory_space=pltpu.VMEM)
    sds = jax.ShapeDtypeStruct
    P_, N = PADDED, (8, D)
    hid = first[-2].shape[1]
    S = (P_, hid)
    return pl.pallas_call(functools.partial(back_kernel, A, r),
        out_shape=(sds((T, D), bf16), sds((M, D), bf16), sds((8, r, D), f32), sds((2, D // (2 * A), 128), f32), sds((Q, H), f32), sds((H, Q), f32),
            sds((64, hid), f32), sds((r, hid), f32), sds((PREFIX, r), f32), sds(N, f32)),
        in_specs=[vm] * len(first) + [any_] * (len(late) + len(rest)), out_specs=(any_,) * 6 + (vm,) * 4,
        scratch_shapes=[v(T, D), v(M, D)] + [pltpu.VMEM(e.shape, e.dtype) for e in late] + [v(4, D, D), vf(T, D), vf(T, D), v(T, D), v(T, D), v(T, D), v(M, D), v(M, D), v(T, D), v(T, D), v(T, D), v(T, D), vf(P_, 2 * D),
            v(3, 4 * T, D), v(3, 4 * T, half), v(4 * M, D), v(4 * M, half), v(2 * T, D), v(2 * T, 512),
            v(4, 2, A, 2, 2, 2 * r, half // 2), v(2, A, 2, D // (2 * A), 256), v(2, Q, H2), v(2, H2, Q),
            v(4, 2, A, 2, 2 * r, half // 2), v(4, 2, A - 1, 2, 2 * r, half // 2), v(4, 2, 2 * r, half // 2), vf(4, 2, 2, 2 * r, half // 2), v(4, 2, 2 * r, half // 2),
            v(A, 2, D // (2 * A), 256), v(A, D // (2 * A), 256), v(A - 1, D // (2 * A), 256),
            v(2, Q, H2), v(2, H2, Q), v(2, Q, H), v(2, H, Q), v(Q, H), v(H, Q),
            vf(4, 2 * r, D), vf(2, D // (2 * A), 128), vf(Q, H), vf(H, Q),
            vf(3, *S), vf(3, *S), vf(A, *S), vf(3, *N), vf(3, *N), vf(A, *N), vf(A - 1, P_, 512), vf(P_, 256), vf(P_, 128), vf(P_, 128), vf(P_, 512), vf(P_, 256), vf(P_, 128),
            pltpu.SemaphoreType.DMA((224,)), pltpu.SemaphoreType.DMA((224,))],
        compiler_params=pltpu.CompilerParams(collective_id=2, has_side_effects=True, vmem_limit_bytes=63 << 20),
        name="back")(*first, *late, *rest)

def fast_body(A, inputs, memory, cotangent, segments, memory_segments, query_self, key_self, value_self, output_self,
              query_cross, key_cross, value_cross, output_cross, self_gain, self_shift, cross_gain, cross_shift,
              final_gain, final_shift, feed_in, feed_out, adapter_down, adapter_up, prefix_embed, prefix_inner, prefix_outer):
    r = query_self.shape[0]
    w, n = lax.axis_index(WIDE), lax.axis_index(NARROW)
    blank = jnp.zeros_like(self_gain)
    norms = jnp.stack([self_gain, self_shift, cross_gain, cross_shift, final_gain, final_shift] + [blank] * 10)
    (weights, fin2, fout2, tangent, prows, vecs, q, k, v, probs, attended, first_low, n1, i1, cq, ck, cv, cprobs, crossed, second, second_low, n2, i2) = front(
        A, r, inputs, memory, segments.reshape(1, -1), memory_segments.reshape(1, -1), prefix_embed, prefix_inner, prefix_outer.T, norms,
        [query_self, key_self, value_self, output_self, key_cross, query_cross, value_cross, output_cross], feed_in, feed_out)
    result, grad_second, fi, fo, ay, branch_low, ngrad3, xp0, xatt, xin, xmem = feed(
        A, second, cotangent, feed_in, feed_out, fin2, fout2, adapter_down, adapter_up, vecs[4:5], vecs[5:6], inputs, memory, attended, first_low, crossed)
    igrad, mgrad, sums, adapt, fi_sum, fo_sum, outer_grad, inner_grad, embed_grad, nsum = back(A, r,
        (grad_second, n2, i2, vecs, ngrad3, tangent, prefix_embed, prefix_inner, prefix_outer.T), (cq, ck, cv, cprobs, n1, i1, q, k, v, probs, prows),
        (second_low, branch_low, ay, weights, fi, fo, xp0, xatt, xin, xmem))
    ng = lax.dynamic_slice_in_dim(nsum, (w * 4 + n) * r, r, 1)
    whole = deliver(result, igrad, mgrad, sums, fi_sum, fo_sum, outer_grad, inner_grad, embed_grad, adapt)
    return whole[:11] + tuple(ng[k] for k in range(6)) + whole[11:17] + (whole[17].T,)


def deliver_kernel(result, igrad, mgrad, sums, fi, fo, outer, inner, embed, adapt, *outs):
    order = (5, 6, 7, 4, 1, 2, 3, 0)
    for dst, src in zip(outs[:3], (result, igrad, mgrad)): dst[...] = src[...]
    for dst, k in zip(outs[3:11], order): dst[...] = sums[k]
    for dst, src in zip(outs[11:13] + outs[15:], (fi, fo, embed, inner, outer)): dst[...] = src[...]
    outs[13][...] = adapt[0]
    outs[14][...] = adapt[1].T


def deliver(result, igrad, mgrad, sums, fi, fo, outer, inner, embed, adapt):
    like = lambda e: jax.ShapeDtypeStruct(e.shape, e.dtype)
    row = jax.ShapeDtypeStruct(sums.shape[1:], f32)
    square = jax.ShapeDtypeStruct(adapt.shape[1:], f32)
    vm = pl.BlockSpec(memory_space=pltpu.VMEM)
    return pl.pallas_call(deliver_kernel,
        out_shape=(like(result), like(igrad), like(mgrad)) + (row,) * 8 + (like(fi), like(fo), square, square, like(embed), like(inner), like(outer)),
        in_specs=[vm] * 10, out_specs=(vm,) * 18, compiler_params=pltpu.CompilerParams(vmem_limit_bytes=60 << 20),
        name="deliver")(result, igrad, mgrad, sums, fi, fo, outer, inner, embed, adapt)


def solution(mesh):
    wide, narrow = mesh.shape[WIDE], mesh.shape[NARROW]
    fits = narrow == 4 and wide == 8
    body = functools.partial(fast_body, wide // 2) if fits else plain_body
    return jax.shard_map(
        body,
        mesh=mesh,
        in_specs=(
            P(BOTH, None),
            P(BOTH, None),
            P(BOTH, None),
            P(BOTH),
            P(BOTH),
            P(BOTH, None),
            P(BOTH, None),
            P(BOTH, None),
            P(BOTH, None),
            P(BOTH, None),
            P(BOTH, None),
            P(BOTH, None),
            P(BOTH, None),
            P(BOTH),
            P(BOTH),
            P(BOTH),
            P(BOTH),
            P(BOTH),
            P(BOTH),
            P(None, WIDE),
            P(WIDE, None),
            P(None, NARROW),
            P(NARROW, None),
            P(None, BOTH),
            P(BOTH, None),
            P(None, BOTH),
        ),
        out_specs=(
            P(BOTH, None),
            P(BOTH, None),
            P(BOTH, None),
            P(BOTH, None),
            P(BOTH, None),
            P(BOTH, None),
            P(BOTH, None),
            P(BOTH, None),
            P(BOTH, None),
            P(BOTH, None),
            P(BOTH, None),
            P(BOTH),
            P(BOTH),
            P(BOTH),
            P(BOTH),
            P(BOTH),
            P(BOTH),
            P(NARROW, WIDE),
            P(WIDE, NARROW),
            P(WIDE, NARROW),
            P(NARROW, WIDE),
            P(None, BOTH),
            P(BOTH, None),
            P(None, BOTH),
        ),
        check_vma=False,
    )
```

```python
import functools
from functools import reduce

import jax
import jax.numpy as jnp
from jax import lax
from jax.experimental import pallas as pl
from jax.experimental.pallas import tpu as pltpu
from jax.sharding import PartitionSpec as P

MESH = pl.DeviceIdType.MESH
bf16, f32 = jnp.bfloat16, jnp.float32
WIDE, NARROW = "wide", "narrow"
BOTH = (WIDE, NARROW)


HEADS = 16
HEAD = 64
PREFIX = 30


HIGHEST = lax.Precision.HIGHEST
EPSILON = 1e-05
MASKED = -1000000000.0
ADAPT_SCALE = 4.0


def matmul(left, right):
    return jnp.dot(left, right, preferred_element_type=jnp.float32)


def left_product(left, right):
    return lax.dot_general(
        left, right, (((0,), (0,)), ((), ())), preferred_element_type=jnp.float32
    )


def right_product(left, right):
    return lax.dot_general(
        left, right, (((1,), (1,)), ((), ())), preferred_element_type=jnp.float32
    )


def exact_left(left, right):
    return lax.dot_general(
        left, right, (((0,), (0,)), ((), ())), precision=HIGHEST, preferred_element_type=jnp.float32
    )


def exact_right(left, right):
    return lax.dot_general(
        left, right, (((1,), (1,)), ((), ())), precision=HIGHEST, preferred_element_type=jnp.float32
    )


def norm_forward(values, factor, offset):
    average = jnp.mean(values, axis=-1, keepdims=True)
    center = values - average
    inverse = lax.rsqrt(jnp.mean(center * center, axis=-1, keepdims=True) + EPSILON)
    normed = center * inverse
    return (normed * factor + offset, normed, inverse)


def norm_backward(grad_out, normed, inverse, factor):
    scaled = grad_out * factor
    grad_in = inverse * (
        scaled
        - jnp.mean(scaled, axis=-1, keepdims=True)
        - normed * jnp.mean(scaled * normed, axis=-1, keepdims=True)
    )
    return (grad_in, jnp.sum(grad_out * normed, axis=0), jnp.sum(grad_out, axis=0))


def head_view(rows):
    return rows.reshape(rows.shape[0], HEADS, HEAD)


def scored(queries, key_rows, allowed):
    raw = jnp.einsum(
        "shd,khd->hsk", head_view(queries), head_view(key_rows), preferred_element_type=jnp.float32
    )
    return jnp.where(allowed[None], raw * HEAD ** (-0.5), MASKED)


def attend_forward(queries, parts):
    scores = [scored(queries, member[0], member[2]) for member in parts]
    largest = reduce(jnp.maximum, [jnp.max(matrix, axis=-1, keepdims=True) for matrix in scores])
    total = reduce(
        jnp.add, [jnp.sum(jnp.exp(matrix - largest), axis=-1, keepdims=True) for matrix in scores]
    )
    logsum = largest + jnp.log(total)
    mixed = reduce(
        jnp.add,
        [
            jnp.einsum(
                "hsk,khd->shd",
                jnp.exp(matrix - logsum).astype(jnp.bfloat16),
                head_view(member[1]),
                preferred_element_type=jnp.float32,
            )
            for matrix, member in zip(scores, parts)
        ],
    )
    return (mixed.reshape(queries.shape[0], HEADS * HEAD), logsum)


def attend_backward(queries, parts, logsum, grad_low):
    grad_heads = head_view(grad_low)
    chances = [jnp.exp(scored(queries, member[0], member[2]) - logsum) for member in parts]
    slopes = [
        jnp.einsum(
            "shd,khd->hsk", grad_heads, head_view(member[1]), preferred_element_type=jnp.float32
        )
        for member in parts
    ]
    row_dot = reduce(
        jnp.add,
        [jnp.sum(chance * slope, axis=-1, keepdims=True) for chance, slope in zip(chances, slopes)],
    )
    scale = HEAD ** (-0.5)
    grad_query = jnp.zeros((queries.shape[0], HEADS, HEAD), jnp.float32)
    results = []
    for member, chance, slope in zip(parts, chances, slopes):
        dscore = (chance * (slope - row_dot)).astype(jnp.bfloat16)
        grad_query = grad_query + jnp.einsum(
            "hsk,khd->shd", dscore, head_view(member[0]), preferred_element_type=jnp.float32
        )
        grad_key = (
            jnp.einsum(
                "hsk,shd->khd", dscore, head_view(queries), preferred_element_type=jnp.float32
            )
            * scale
        )
        grad_value = jnp.einsum(
            "hsk,shd->khd",
            chance.astype(jnp.bfloat16),
            grad_heads,
            preferred_element_type=jnp.float32,
        )
        results.append(
            (
                grad_key.reshape(grad_key.shape[0], HEADS * HEAD),
                grad_value.reshape(grad_value.shape[0], HEADS * HEAD),
            )
        )
    return ((grad_query * scale).reshape(queries.shape[0], HEADS * HEAD), results)


def gelu_back(pre_values, grad_values):
    return jax.vjp(lambda inner: jax.nn.gelu(inner, approximate=False), pre_values)[1](grad_values)[
        0
    ]


def plain_body(
    inputs,
    memory,
    cotangent,
    segments,
    memory_segments,
    query_self,
    key_self,
    value_self,
    output_self,
    query_cross,
    key_cross,
    value_cross,
    output_cross,
    self_gain,
    self_shift,
    cross_gain,
    cross_shift,
    final_gain,
    final_shift,
    feed_in,
    feed_out,
    adapter_down,
    adapter_up,
    prefix_embed,
    prefix_inner,
    prefix_outer,
):
    (
        query_one,
        key_one,
        value_one,
        output_one,
        query_two,
        key_two,
        value_two,
        output_two,
        gain_one,
        shift_one,
        gain_two,
        shift_two,
        gain_three,
        shift_three,
        embed_full,
        inner_full,
        outer_full,
    ) = (
        lax.all_gather(query_self, BOTH, axis=0, tiled=True),
        lax.all_gather(key_self, BOTH, axis=0, tiled=True),
        lax.all_gather(value_self, BOTH, axis=0, tiled=True),
        lax.all_gather(output_self, BOTH, axis=0, tiled=True),
        lax.all_gather(query_cross, BOTH, axis=0, tiled=True),
        lax.all_gather(key_cross, BOTH, axis=0, tiled=True),
        lax.all_gather(value_cross, BOTH, axis=0, tiled=True),
        lax.all_gather(output_cross, BOTH, axis=0, tiled=True),
        lax.all_gather(self_gain, BOTH, axis=0, tiled=True),
        lax.all_gather(self_shift, BOTH, axis=0, tiled=True),
        lax.all_gather(cross_gain, BOTH, axis=0, tiled=True),
        lax.all_gather(cross_shift, BOTH, axis=0, tiled=True),
        lax.all_gather(final_gain, BOTH, axis=0, tiled=True),
        lax.all_gather(final_shift, BOTH, axis=0, tiled=True),
        lax.all_gather(prefix_embed, BOTH, axis=1, tiled=True),
        lax.all_gather(prefix_inner, BOTH, axis=0, tiled=True),
        lax.all_gather(prefix_outer, BOTH, axis=1, tiled=True),
    )
    factor_one = gain_one.astype(jnp.float32)
    factor_two = gain_two.astype(jnp.float32)
    factor_three = gain_three.astype(jnp.float32)
    length = inputs.shape[0]
    width = inputs.shape[1]
    places = jnp.arange(length)
    causal = places[:, None] >= places[None, :]
    local_mask = (segments[:, None] == segments[None, :]) & causal
    prefix_mask = jnp.ones((length, PREFIX), jnp.bool_)
    cross_mask = segments[:, None] == memory_segments[None, :]
    tangent = jnp.tanh(matmul(embed_full, inner_full))
    tangent_low = tangent.astype(jnp.bfloat16)
    prefix_rows = matmul(tangent_low, outer_full).astype(jnp.bfloat16)
    prefix_keys = prefix_rows[:, :width]
    prefix_values = prefix_rows[:, width:]
    queries = matmul(inputs, query_one).astype(jnp.bfloat16)
    key_rows = matmul(inputs, key_one).astype(jnp.bfloat16)
    value_rows = matmul(inputs, value_one).astype(jnp.bfloat16)
    self_parts = ((prefix_keys, prefix_values, prefix_mask), (key_rows, value_rows, local_mask))
    attended, self_logsum = attend_forward(queries, self_parts)
    attended_low = attended.astype(jnp.bfloat16)
    first, normed_one, inverse_one = norm_forward(
        inputs.astype(jnp.float32) + matmul(attended_low, output_one),
        factor_one,
        shift_one.astype(jnp.float32),
    )
    first_low = first.astype(jnp.bfloat16)
    cross_queries = matmul(first_low, query_two).astype(jnp.bfloat16)
    cross_keys = matmul(memory, key_two).astype(jnp.bfloat16)
    cross_values = matmul(memory, value_two).astype(jnp.bfloat16)
    cross_parts = ((cross_keys, cross_values, cross_mask),)
    crossed, cross_logsum = attend_forward(cross_queries, cross_parts)
    crossed_low = crossed.astype(jnp.bfloat16)
    second, normed_two, inverse_two = norm_forward(
        first + matmul(crossed_low, output_two), factor_two, shift_two.astype(jnp.float32)
    )
    second_low = second.astype(jnp.bfloat16)
    feed_rows = lax.all_gather(second_low, WIDE, axis=0, tiled=True)
    hidden_pre = matmul(feed_rows, feed_in)
    hidden_low = jax.nn.gelu(hidden_pre, approximate=False).astype(jnp.bfloat16)
    feed_sum = lax.psum_scatter(
        matmul(hidden_low, feed_out), WIDE, scatter_dimension=0, tiled=True
    )
    adapt_rows = lax.all_gather(second_low, NARROW, axis=0, tiled=True)
    bottle_pre = matmul(adapt_rows, adapter_down)
    bottle_low = jax.nn.gelu(bottle_pre, approximate=False).astype(jnp.bfloat16)
    adapt_sum = lax.psum_scatter(
        matmul(bottle_low, adapter_up).astype(jnp.bfloat16),
        NARROW,
        scatter_dimension=0,
        tiled=True,
    ).astype(jnp.float32)
    branch = feed_sum + ADAPT_SCALE * adapt_sum
    result, normed_three, inverse_three = norm_forward(
        second + branch, factor_three, shift_three.astype(jnp.float32)
    )
    grad_branch, gain_three_grad, shift_three_grad = norm_backward(
        cotangent.astype(jnp.float32), normed_three, inverse_three, factor_three
    )
    branch_low = grad_branch.astype(jnp.bfloat16)
    branch_rows = lax.all_gather(branch_low, WIDE, axis=0, tiled=True)
    grad_hidden = right_product(branch_rows, feed_out)
    grad_pre = gelu_back(hidden_pre, grad_hidden).astype(jnp.bfloat16)
    grad_out_part = left_product(hidden_low, branch_rows)
    grad_in_part = left_product(feed_rows, grad_pre)
    grad_feed = lax.psum_scatter(
        right_product(grad_pre, feed_in), WIDE, scatter_dimension=0, tiled=True
    )
    feed_in_total, feed_out_total = (
        lax.psum_scatter(
            grad_in_part.astype(jnp.bfloat16), NARROW, scatter_dimension=0, tiled=True
        ).astype(jnp.float32),
        lax.psum_scatter(
            grad_out_part.astype(jnp.bfloat16), NARROW, scatter_dimension=1, tiled=True
        ).astype(jnp.float32),
    )
    branch_narrow = lax.all_gather(branch_low, NARROW, axis=0, tiled=True)
    grad_bottle = ADAPT_SCALE * right_product(branch_narrow, adapter_up)
    grad_bottle_pre = gelu_back(bottle_pre, grad_bottle).astype(jnp.bfloat16)
    grad_up_part = ADAPT_SCALE * left_product(bottle_low, branch_narrow)
    grad_down_part = left_product(adapt_rows, grad_bottle_pre)
    grad_adapt = lax.psum_scatter(
        right_product(grad_bottle_pre, adapter_down).astype(jnp.bfloat16),
        NARROW,
        scatter_dimension=0,
        tiled=True,
    ).astype(jnp.float32)
    down_total, up_total = (
        lax.psum_scatter(grad_down_part, WIDE, scatter_dimension=0, tiled=True),
        lax.psum_scatter(grad_up_part, WIDE, scatter_dimension=1, tiled=True),
    )
    grad_second = grad_branch + grad_feed + grad_adapt
    grad_mid, gain_two_grad, shift_two_grad = norm_backward(
        grad_second, normed_two, inverse_two, factor_two
    )
    mid_low = grad_mid.astype(jnp.bfloat16)
    output_two_grad = left_product(crossed_low, mid_low)
    crossed_grad = right_product(mid_low, output_two).astype(jnp.bfloat16)
    cross_query_grad, cross_results = attend_backward(
        cross_queries, cross_parts, cross_logsum, crossed_grad
    )
    cross_query_low = cross_query_grad.astype(jnp.bfloat16)
    cross_key_low = cross_results[0][0].astype(jnp.bfloat16)
    cross_value_low = cross_results[0][1].astype(jnp.bfloat16)
    query_two_grad = left_product(first_low, cross_query_low)
    key_two_grad = left_product(memory, cross_key_low)
    value_two_grad = left_product(memory, cross_value_low)
    memory_grad = (
        right_product(cross_key_low, key_two) + right_product(cross_value_low, value_two)
    ).astype(jnp.bfloat16)
    grad_first = grad_mid + right_product(cross_query_low, query_two)
    grad_start, gain_one_grad, shift_one_grad = norm_backward(
        grad_first, normed_one, inverse_one, factor_one
    )
    start_low = grad_start.astype(jnp.bfloat16)
    output_one_grad = left_product(attended_low, start_low)
    attended_grad = right_product(start_low, output_one).astype(jnp.bfloat16)
    self_query_grad, self_results = attend_backward(queries, self_parts, self_logsum, attended_grad)
    self_query_low = self_query_grad.astype(jnp.bfloat16)
    self_key_low = self_results[1][0].astype(jnp.bfloat16)
    self_value_low = self_results[1][1].astype(jnp.bfloat16)
    query_one_grad = left_product(inputs, self_query_low)
    key_one_grad = left_product(inputs, self_key_low)
    value_one_grad = left_product(inputs, self_value_low)
    inputs_grad = (
        grad_start
        + right_product(self_query_low, query_one)
        + right_product(self_key_low, key_one)
        + right_product(self_value_low, value_one)
    ).astype(jnp.bfloat16)
    prefix_grad = jnp.concatenate([self_results[0][0], self_results[0][1]], axis=1)
    outer_grad = exact_left(tangent_low.astype(jnp.float32), prefix_grad)
    tangent_grad = exact_right(prefix_grad, outer_full.astype(jnp.float32)) * (
        1.0 - tangent * tangent
    )
    inner_grad = exact_left(embed_full.astype(jnp.float32), tangent_grad)
    embed_grad = exact_right(tangent_grad, inner_full.astype(jnp.float32))
    (
        query_one_sum,
        key_one_sum,
        value_one_sum,
        output_one_sum,
        query_two_sum,
        key_two_sum,
        value_two_sum,
        output_two_sum,
        gain_one_sum,
        shift_one_sum,
        gain_two_sum,
        shift_two_sum,
        gain_three_sum,
        shift_three_sum,
        embed_sum,
        inner_sum,
        outer_sum,
    ) = (
        lax.psum_scatter(query_one_grad, BOTH, scatter_dimension=0, tiled=True),
        lax.psum_scatter(key_one_grad, BOTH, scatter_dimension=0, tiled=True),
        lax.psum_scatter(value_one_grad, BOTH, scatter_dimension=0, tiled=True),
        lax.psum_scatter(output_one_grad, BOTH, scatter_dimension=0, tiled=True),
        lax.psum_scatter(query_two_grad, BOTH, scatter_dimension=0, tiled=True),
        lax.psum_scatter(key_two_grad, BOTH, scatter_dimension=0, tiled=True),
        lax.psum_scatter(value_two_grad, BOTH, scatter_dimension=0, tiled=True),
        lax.psum_scatter(output_two_grad, BOTH, scatter_dimension=0, tiled=True),
        lax.psum_scatter(gain_one_grad, BOTH, scatter_dimension=0, tiled=True),
        lax.psum_scatter(shift_one_grad, BOTH, scatter_dimension=0, tiled=True),
        lax.psum_scatter(gain_two_grad, BOTH, scatter_dimension=0, tiled=True),
        lax.psum_scatter(shift_two_grad, BOTH, scatter_dimension=0, tiled=True),
        lax.psum_scatter(gain_three_grad, BOTH, scatter_dimension=0, tiled=True),
        lax.psum_scatter(shift_three_grad, BOTH, scatter_dimension=0, tiled=True),
        lax.psum_scatter(embed_grad, BOTH, scatter_dimension=1, tiled=True),
        lax.psum_scatter(inner_grad, BOTH, scatter_dimension=0, tiled=True),
        lax.psum_scatter(outer_grad, BOTH, scatter_dimension=1, tiled=True),
    )
    return (
        result.astype(jnp.bfloat16),
        inputs_grad,
        memory_grad,
        query_one_sum,
        key_one_sum,
        value_one_sum,
        output_one_sum,
        query_two_sum,
        key_two_sum,
        value_two_sum,
        output_two_sum,
        gain_one_sum,
        shift_one_sum,
        gain_two_sum,
        shift_two_sum,
        gain_three_sum,
        shift_three_sum,
        feed_in_total,
        feed_out_total,
        down_total,
        up_total,
        embed_sum,
        inner_sum,
        outer_sum,
    )


def place():
    w = lax.axis_index(WIDE); n = lax.axis_index(NARROW)
    return w // 2, w % 2, n // 2, n % 2

def device(a, b, x, c):
    return (a * 2 + b, x * 2 + c)

def greet(peers):
    barrier = pltpu.get_barrier_semaphore()
    for p in peers:
        pl.semaphore_signal(barrier, inc=1, device_id=p, device_id_type=MESH)
    pl.semaphore_wait(barrier, len(peers))

def remote(src, dst, send, recv, dev):
    return pltpu.make_async_remote_copy(src_ref=src, dst_ref=dst, send_sem=send, recv_sem=recv, device_id=dev, device_id_type=MESH)


def dot_left(l, r):
    return lax.dot_general(l, r, (((0,), (0,)), ((), ())), preferred_element_type=f32)

class Copies:
    def __init__(self, send, recv):
        self.send, self.recv, self.count, self.all = send, recv, 0, []
    def __call__(self, src, dst, dev):
        cp = remote(src, dst, self.send.at[self.count], self.recv.at[self.count], dev)
        self.count += 1
        cp.start(); self.all.append(cp)
        return cp
    def local(self, src, dst):
        cp = pltpu.make_async_copy(src, dst, self.send.at[self.count])
        self.count += 1
        cp.start()
        return cp
    def sent(self, some):
        for cp in some:
            cp.wait_send()
            self.all = [o for o in self.all if o is not cp]
    def close(self):
        for cp in self.all: cp.wait_send()


EPSILON = 1e-05
ADAPT_SCALE = 4.0

def dot(l, r):
    return jnp.dot(l, r, preferred_element_type=f32)

def dot_right(l, r):
    return lax.dot_general(l, r, (((1,), (1,)), ((), ())), preferred_element_type=f32)

def gelu_both(v):
    phi = 0.5 + 0.5 * lax.erf(v * 0.7071067811865476)
    return v * phi, phi + v * (0.3989422804014327 * jnp.exp(-0.5 * v * v))

def norm(v):
    center = v - jnp.mean(v, axis=-1, keepdims=True)
    inverse = lax.rsqrt(jnp.mean(center * center, axis=-1, keepdims=True) + EPSILON)
    return center * inverse, inverse

def norm_back(e, n, inverse, factor):
    s = e * factor
    return inverse * (s - jnp.mean(s, axis=-1, keepdims=True) - n * jnp.mean(s * n, axis=-1, keepdims=True))

def feed_part(A, second, vecs, cot, fin_own, fout_own, down_ref, up_ref, inputs, memory, att, flow, crossed, partner, outs, scratch):
    result, gsec, fi_out, fo_out, ay, blow, ngrad, xp0, xatt, xin, xmem = outs
    fin, fout, fi, fo, down, up, rows, brow, hid, slope, gpre, part, q1, q2, q3, bslope, acc, ssem, rsem = scratch
    a, b, x, c = place()
    o = 1 - c
    yp = device(a, 1 - b, x, c)
    zp = device((a + A // 2) % A, b, x, c)
    core, xp, dp = device(a, b, x, o), device(a, b, 1 - x, c), device(a, b, 1 - x, o)
    cp = Copies(ssem, rsem)
    half = fin_own.shape[1]
    loads = [cp.local(fin_own, fin.at[:, pl.ds(0, half)]), cp.local(fout_own, fout.at[pl.ds(0, half)])]
    T, D = second.shape
    NC, R = 2, T // 2
    C = R // NC
    HID = fin.shape[1]; TW = 256
    NT = D // TW
    def span(h): return pl.ds(h * R, R)

    def spread(buf, h):
        zs, ys, passed = [], [], []
        for u in range(NC):
            s = pl.ds(u * C, C)
            zs.append(cp(buf.at[h, 0, s], buf.at[h, 2, s], zp))
        for u in range(NC):
            s = pl.ds(u * C, C)
            ys.append(cp(buf.at[h, 0, s], buf.at[h, 1, s], yp))
        def beside():
            for e in ys: e.wait_recv()
        def forward():
            for u in range(NC):
                s = pl.ds(u * C, C)
                zs[u].wait_recv()
                passed.append(cp(buf.at[h, 2, s], buf.at[h, 3, s], yp))
        def across():
            for e in passed: e.wait_recv()
        return beside, forward, across

    sums, onward = {}, {}
    def send_part(level, h, j, t):
        sums[level, h, j, t] = cp(part.at[h, j, t], (q3 if j == 3 else q1).at[level, h, t], yp)
    def collect(level, h):
        for t in range(NT):
            sums[level, h, 3, t].wait_recv()
            part[h, 2, t] = part[h, 2, t] + q3[level, h, t]
            onward[level, h, t] = cp(part.at[h, 2, t], q2.at[level, h, t], zp)
    def gather_up(level, h):
        for t in range(NT):
            cols = pl.ds(t * TW, TW)
            sums[level, h, 1, t].wait_recv(); onward[level, h, t].wait_recv()
            acc[h, :, cols] = acc[h, :, cols] + q1[level, h, t].astype(f32) + q2[level, h, t].astype(f32)
        cp.sent([onward[level, h, t] for t in range(NT)] + [sums[level, h, j, t] for j in (1, 3) for t in range(NT)])

    for h in range(2): rows[h, 0] = second[span(h), :].astype(bf16)
    ways = [spread(rows, h) for h in range(2)]
    AD = down_ref.shape[1]
    n = x * 2 + c
    nd = pl.ds(pl.multiple_of(n * AD, AD), AD)
    md = pl.ds(pl.multiple_of((2 - 2 * x + c) * AD, AD), AD)
    kept, late = [cp.local(down_ref, down.at[:, nd]), cp.local(up_ref, up.at[nd])], []
    over = [cp(down_ref, down.at[:, nd], xp), cp(up_ref, up.at[nd], xp)]
    near = [cp(down_ref, down.at[:, nd], core), cp(up_ref, up.at[nd], core)]
    def rowsn(ref, m, place): return ref.at[pl.ds(pl.multiple_of(place * m, m), m)]
    def fan(srcs, dst, only=False):
        k = cp.count
        cp.count += 4
        def start(me):
            own, other = srcs[me], srcs[1 - me]
            if own is not None:
                pltpu.make_async_copy(own, rowsn(dst, T, n), ssem.at[k]).start()
                remote(own, rowsn(dst, T, n), ssem.at[k + 1], rsem.at[k + 1], xp).start()
            if other is not None:
                remote(other, rowsn(dst, T, n), ssem.at[k + 2], rsem.at[k + 2], core).start()
                remote(other, rowsn(dst, T, n), ssem.at[k + 3], rsem.at[k + 3], dp).start()
        def finish(me):
            own, other = srcs[me], srcs[1 - me]
            src = own if own is not None else other
            ways = [remote(src, rowsn(dst, T, n), ssem.at[k + i], rsem.at[k + i], d) for i, d in ((1, xp), (2, core), (3, dp))]
            if own is not None:
                pltpu.make_async_copy(own, rowsn(dst, T, n), ssem.at[k]).wait()
                ways[0].wait_send()
                for e in ways: e.wait_recv()
            if other is not None:
                ways[1].wait_send(); ways[2].wait_send()
        pl.when(c == 0)(functools.partial(start, 0))
        pl.when(c == 1)(functools.partial(start, 1))
        def done():
            pl.when(c == 0)(functools.partial(finish, 0))
            pl.when(c == 1)(functools.partial(finish, 1))
        return done
    fans = [fan((crossed, flow), xp0), fan((att, None), xatt)]
    M = memory.shape[0]
    share = []
    for src, dst, m in ((inputs, xin, T), (memory, xmem, M)):
        kept.append(cp.local(src, rowsn(dst, m, n)))
        near.append(cp(src, rowsn(dst, m, n), core))
        share.append((cp(src, rowsn(dst, m, n), xp), rowsn(dst, m, 2 - 2 * x + c)))
    def adapter_weights():
        kept[0].wait(); kept[1].wait()
        for e, ref in zip(over, (down.at[:, md], up.at[md])):
            e.wait_recv()
            late.append(cp(ref, ref, core))
        near[0].wait_recv(); near[1].wait_recv()
        for e in late[:2]: e.wait_recv()
    def share_on():
        for e, ref in share:
            e.wait_recv()
            late.append(cp(ref, ref, core))
    def adapter_forward():
        own = rows[:, 0].reshape(T, D)
        for t in range(2):
            cols = pl.ds(t * 256, 256)
            g, s = gelu_both(dot(own, down[:, cols]))
            ay[1, :, cols] = (ADAPT_SCALE * g.astype(bf16).astype(f32)).astype(bf16)
            bslope[:, cols] = s
        def tile(t, _):
            cols = pl.ds(pl.multiple_of(t * 256, 256), 256)
            acc[:, :, cols] = acc[:, :, cols] + dot(ay[1], up[:, cols]).reshape(2, R, 256)
            return 0
        lax.fori_loop(0, D // 256, tile, 0)
    def adapter_back():
        def tile(t, _):
            cols = pl.ds(pl.multiple_of(t * 256, 256), 256)
            gbot = bslope[:, cols] * (ADAPT_SCALE * dot_right(brow[:, 0].reshape(T, D), up[cols, :]))
            ay[0, :, cols] = gbot.astype(bf16)
            return 0
        lax.fori_loop(0, down.shape[1] // 256, tile, 0)
        def tile2(t, _):
            cols = pl.ds(pl.multiple_of(t * 256, 256), 256)
            acc[:, :, cols] = acc[:, :, cols] + dot_right(ay[0], down[cols, :]).reshape(2, R, 256)
            return 0
        lax.fori_loop(0, D // 256, tile2, 0)
    def both(buf, h, g): return buf[h, 2 * g:2 * g + 2].reshape(2 * R, buf.shape[3])
    def put_out(level, h, g, t, p):
        cols = pl.ds(t * TW, TW)
        if g == 0:
            acc[h, :, cols] = p[:R] if level == 0 else acc[h, :, cols] + p[:R]
            part[h, 1, t] = p[R:].astype(bf16)
            send_part(level, h, 1, t)
        else:
            part[h, 3, t] = p[R:].astype(bf16)
            send_part(level, h, 3, t)
            part[h, 2, t] = p[:R].astype(bf16)
    def enter(h, g):
        xv = both(rows, h, g)
        def tile(t, _):
            cols = pl.ds(pl.multiple_of(t * TW, TW), TW)
            e, s = gelu_both(dot(xv, fin[:, cols]))
            hid[h, 2 * g:2 * g + 2, :, cols] = e.astype(bf16).reshape(2, R, TW)
            slope[h, 2 * g:2 * g + 2, :, cols] = s.reshape(2, R, TW)
            return 0
        lax.fori_loop(0, HID // TW, tile, 0)
        hv = both(hid, h, g)
        for t in range(NT):
            put_out(0, h, g, t, dot(hv, fout[:, pl.ds(t * TW, TW)]))
    def leave(h, g):
        xv = both(brow, h, g)
        def tile(t, _):
            cols = pl.ds(pl.multiple_of(t * TW, TW), TW)
            gh = dot_right(xv, fout[cols, :])
            gpre[h, 2 * g:2 * g + 2, :, cols] = (slope[h, 2 * g:2 * g + 2, :, cols].reshape(2 * R, TW) * gh).astype(bf16).reshape(2, R, TW)
            return 0
        lax.fori_loop(0, HID // TW, tile, 0)
        hv = both(gpre, h, g)
        for t in range(NT):
            put_out(1, h, g, t, dot_right(hv, fin[pl.ds(t * TW, TW), :]))
    fac, off = vecs[4:5, :], vecs[5:6, :]
    back = []
    def turn(h):
        n3, inv3 = norm(second[span(h), :] + acc[h])
        result[span(h), :] = (n3 * fac + off).astype(bf16)
        e = cot[span(h), :].astype(f32)
        gb = norm_back(e, n3, inv3, fac)
        gbl = gb.astype(bf16)
        brow[h, 0] = gbl
        back.append(spread(brow, h))
        blow[span(h), :] = gbl
        acc[h] = gb
        gg, gs = jnp.sum(e * n3, axis=0, keepdims=True), jnp.sum(e, axis=0, keepdims=True)
        ngrad[0:1, :] = gg if h == 0 else ngrad[0:1, :] + gg
        ngrad[1:2, :] = gs if h == 0 else ngrad[1:2, :] + gs
    (beside0, forward0, across0), (beside1, forward1, across1) = ways
    for e in loads: e.wait()
    partner()
    beside0()
    enter(0, 0)
    forward0()
    across0()
    enter(0, 1)
    forward1()
    beside1()
    enter(1, 0)
    collect(0, 0)
    across1()
    enter(1, 1)
    adapter_weights()
    adapter_forward()
    collect(0, 1)
    gather_up(0, 0)
    turn(0)
    gather_up(0, 1)
    turn(1)
    (beside0, forward0, across0), (beside1, forward1, across1) = back
    beside0()
    leave(0, 0)
    forward0()
    adapter_back()
    across0()
    leave(0, 1)
    forward1()
    beside1()
    leave(1, 0)
    collect(1, 0)
    across1()
    leave(1, 1)
    def wtile(t, _):
        cols = pl.ds(pl.multiple_of(t * TW, TW), TW)
        fi[:, cols] = dot_left(rows[...].reshape(4 * T, D), gpre[:, :, :, cols].reshape(4 * T, TW)).astype(bf16)
        fo[:, cols] = dot_left(hid[...].reshape(4 * T, HID), brow[:, :, :, cols].reshape(4 * T, TW)).astype(bf16)
        return 0
    lax.fori_loop(0, 1, wtile, 0)
    collect(1, 1)
    lax.fori_loop(1, HID // TW, wtile, 0)
    kept += [cp.local(fi, fi_out), cp.local(fo, fo_out)]
    share_on()
    for h in range(2):
        gather_up(1, h)
        gsec[span(h), :] = acc[h]
    for e in kept[2:]: e.wait()
    for e in near[2:] + late[2:]: e.wait_recv()
    for e in fans: e()
    cp.close()


NEGATIVE = -1000000000.0
PADDED = 32
PREFIX = 30


def lane_half(rows):
    return lax.broadcasted_iota(jnp.int32, (rows, 128), 1) < 64

def split_heads(v):
    low = lane_half(v.shape[0])
    zero = jnp.zeros_like(v)
    return jnp.where(low, v, zero), jnp.where(low, zero, v)


def whole(ref):
    return lambda cols: ref[:, cols]


def norm_back_into(e, n, i, gain, out, ngrad, at):
    ee = e[...]
    nn = n[...]
    out[...] = norm_back(ee, nn, i[...], gain)
    ngrad[at:at + 1, :] = jnp.sum(ee * nn, axis=0, keepdims=True)
    ngrad[at + 1:at + 2, :] = jnp.sum(ee, axis=0, keepdims=True)


def repeat(n):
    row = lax.broadcasted_iota(jnp.int32, (n, 128), 0)
    col = lax.broadcasted_iota(jnp.int32, (n, 128), 1)
    return jnp.where(row == lax.rem(col, n), 1.0, 0.0).astype(bf16)

def columns(t, tile=256):
    return pl.ds(pl.multiple_of(t * tile, tile), tile)

def loop(start, stop, step):
    lax.fori_loop(start, stop, lambda t, z: (step(t), z)[1], 0)

def front_part(A, r, inputs, memory, seg_row, mem_row, embed, inner, outer, norms, ws, fin, fout, fin2, fout2, outs, scratch):
    (wout, tangent, prows_o, vecs_o, q_o, k_o, v_o, probs_o, att_o, first_o, n1_o, i1_o, cq_o, ck_o, cv_o, cprobs_o, crossed_o, slow_o, n2_o, i2_o) = outs
    (g, q, k, v, probs, att, first, flow, n1, i1, cq, ck, cv, cprobs, crossed, second, slow, n2, i2, pen, cpen,
     buf, got, zbuf, r0, r1, prows, nout, vecs, tan, ssem, rsem) = scratch
    a, b, x, c = place()
    core, xp, yp = device(a, b, x, 1 - c), device(a, b, 1 - x, c), device(a, 1 - b, x, c)
    zp = [device((a + j) % A, b, x, c) for j in range(A)]
    za = a + 1 - 2 * (a % 2)
    zq = device(za, b, x, c)
    greet([core, xp, yp, device(a, b, 1 - x, 1 - c)] + zp[1:])
    cp = Copies(ssem, rsem)
    T, D = inputs.shape
    pairs = 4
    small = {}
    def pre0():
        zbuf[a] = jnp.zeros(zbuf.shape[1:], f32)
        zbuf[a, :PREFIX, :] = dot(embed[...], inner[...])
        small["s"] = [cp(zbuf.at[a], zbuf.at[a], zp[j]) for j in range(1, A)]
    pre0()
    def row(a_, b_, x_):
        return pl.multiple_of(((a_ * 2 + b_) * 2 + x_) * 2 * r, 2 * r)
    at = pl.ds(pl.multiple_of(row(a, b, x) + c * r, r), r)
    cut = (pl.ds(0, D // 2), pl.ds(D // 2, D // 2))
    def block(i, h, a_, b_, x_):
        return g.at[2 * i + c, pl.ds(row(a_, b_, x_), 2 * r), cut[h]]
    kept = []
    own, cross = [], []
    base = cp.count
    for i in range(pairs):
        s1, s2, rr = ssem.at[cp.count], ssem.at[cp.count + 1], rsem.at[cp.count]
        cp.count += 2
        def start(keep, give):
            pltpu.make_async_copy(ws[2 * i + keep], g.at[2 * i + keep, at], s2).start()
            remote(ws[2 * i + give], g.at[2 * i + give, at], s1, rr, core).start()
        pl.when(c == 0)(functools.partial(start, 0, 1))
        pl.when(c == 1)(functools.partial(start, 1, 0))
        own.append(pltpu.make_async_copy(ws[2 * i], g.at[2 * i, at], s2))
        cross.append(remote(ws[2 * i], g.at[2 * i, at], s1, rr, core))
    G = norms.shape[0]
    me = ((a * 2 + b) * 2 + x) * 2 + c
    chip = (a * 2 + b) * 2 + x
    def nrows(start, count): return nout.at[pl.ds(pl.multiple_of(start * G, G), count * G)]
    def lanes(start, count): return prows.at[:, pl.ds(pl.multiple_of(start * 128, 128), count * 128)]
    nout[pl.ds(pl.multiple_of(me * G, G), G), :] = dot(norms[...], repeat(norms.shape[1])).astype(bf16)
    peers = (core, xp, yp)
    def settle():
        for e in small["s"]: e.wait_recv()
    def pre1():
        settle()
        t = zbuf[0]
        for n in range(1, A): t = t + zbuf[n]
        buf[0] = t
        small["s"] = [cp(buf.at[0], got.at[0], core)]
    def pre2(n):
        def go():
            settle()
            buf[n] = buf[n - 1] + got[n - 1]
            small["s"] = [cp(buf.at[n], got.at[n], peers[n])]
        return go
    def pre4():
        settle()
        t = jnp.tanh(buf[2] + got[2])
        tan[...] = t
        r0[...] = dot(dot_right(t.astype(bf16), outer[...]).astype(bf16), repeat(outer.shape[0])).astype(bf16)
        small["s"] = [cp(r0, r1, core), cp(nrows(me, 1), nrows(me, 1), core)]
        kept.append(cp.local(tan, tangent))
    def pre5():
        settle()
        lane = lax.broadcasted_iota(jnp.int32, (PADDED, 128), 1)
        prows[:, pl.ds(pl.multiple_of(chip * 128, 128), 128)] = jnp.where((lane // 64) == c, r0[...].astype(f32), r1[...].astype(f32)).astype(bf16)
        small["s"] = [cp(lanes(chip, 1), lanes(chip, 1), xp), cp(nrows(me - c, 2), nrows(me - c, 2), xp)]
    def pre6():
        settle()
        small["s"] = [cp(lanes(chip - x, 2), lanes(chip - x, 2), yp), cp(nrows(me - c - 2 * x, 4), nrows(me - c - 2 * x, 4), yp)]
    def pre7():
        settle()
        small["s"] = [cp(lanes(a * 4, 4), lanes(a * 4, 4), zp[j]) for j in range(1, A)] + [cp(nrows(a * 8, 8), nrows(a * 8, 8), zp[j]) for j in range(1, A)]
    def pre8():
        settle()
        lane = lax.broadcasted_iota(jnp.int32, (G, 128), 1) // 32
        for w in range(2 * A):
            s = nout[pl.ds(w * 4 * G, G), :].astype(f32)
            for n in range(1, 4):
                s = jnp.where(lane == n, nout[pl.ds((w * 4 + n) * G, G), :].astype(f32), s)
            vecs[:, pl.ds(w * 128, 128)] = s[:8]
        kept.append(cp.local(vecs, vecs_o))
        kept.append(cp.local(prows, prows_o))
    H = fin.shape[1]
    feeds, passed = {}, []
    def feed_send(i):
        n = D // 8
        ri = pl.ds(pl.multiple_of(c * (D // 2) + i * n, n), n)
        m = H // 8
        ro = pl.ds(pl.multiple_of(c * (H // 2) + i * m, m), m)
        ro2 = pl.ds(pl.multiple_of(H + c * (H // 2) + i * m, m), m)
        feeds[i] = [(cp(fin.at[ri], fin2.at[ri, pl.ds(H, H)], zq), fin2.at[ri, pl.ds(H, H)]),
                    (cp(fout.at[ro], fout2.at[ro2], zq), fout2.at[ro2])]
    def feed_pass(i):
        for e, ref in feeds[i]:
            e.wait_recv()
            passed.append(cp(ref, ref, core))
    zc, mc, lc, dc = {}, {}, {}, {}
    two, three = (yp, xp), (xp, yp)
    begun = set()
    def fs(i, h):
        if i not in begun:
            begun.add(i)
            own[i].wait(); cross[i].wait()
        mc[i, h, 0] = cp(block(i, h, a, b, x), block(i, h, a, b, x), two[h])
        lc[i, h, 0, 0] = cp(block(i, h, a, b, x), block(i, h, a, b, x), three[h])
    def fz(i, h):
        for j in range(1, A):
            zc[i, h, j] = cp(block(i, h, a, b, x), block(i, h, a, b, x), zp[j])
    def mid(i, h, j):
        aj = (a + A - j) % A
        zc[i, h, j].wait_recv()
        mc[i, h, j] = cp(block(i, h, aj, b, x), block(i, h, aj, b, x), two[h])
        lc[i, h, j, 0] = cp(block(i, h, aj, b, x), block(i, h, aj, b, x), three[h])
    def third(i, h, j):
        aj = (a + A - j) % A
        w = (aj, 1 - b, x) if h == 0 else (aj, b, 1 - x)
        mc[i, h, j].wait_recv()
        lc[i, h, j, 1] = cp(block(i, h, *w), block(i, h, *w), three[h])
    per = D // A
    def finish(i, j):
        aj = (a + A - j) % A
        for h in range(2):
            lc[i, h, j, 0].wait_recv(); lc[i, h, j, 1].wait_recv()
        ref = g.at[2 * i + c, pl.ds(pl.multiple_of(aj * per, per), per)]
        dc[i, j] = cp(ref, ref, core)
    def arrive(i):
        for j in range(A): dc[i, j].wait_recv()
        kept.append(cp.local(g.at[2 * i], wout.at[2 * i]))
        kept.append(cp.local(g.at[2 * i + 1], wout.at[2 * i + 1]))
    def halves(src, w, out):
        def part(n):
            def go():
                xv = src[...]
                def step(t):
                    out[:, columns(t)] = dot(xv, g[w, :, columns(t)]).astype(bf16)
                loop(2 * n, 2 * n + 2, step)
            return go
        return [part(0), part(1)]
    def masks():
        row = lax.broadcasted_iota(jnp.int32, (T, T), 0)
        col = lax.broadcasted_iota(jnp.int32, (T, T), 1)
        across = jnp.broadcast_to(seg_row[...].astype(f32), (T, T))
        down = across.T
        pen[:, :T] = jnp.where((row >= col) & (down == across), 0.0, NEGATIVE)
        lane = lax.broadcasted_iota(jnp.int32, (T, PADDED), 1)
        pen[:, T:] = jnp.where(lane < PREFIX, 0.0, NEGATIVE)
        for n in range(memory.shape[0] // T):
            span = slice(n * T, (n + 1) * T)
            cpen[:, span] = jnp.where(down == mem_row[:, span].astype(f32), 0.0, NEGATIVE)
    def softmax(qv, kk, penalty):
        score = jnp.where(penalty[...] < -1.0, NEGATIVE, dot_right(qv, kk) * 0.125)
        e = jnp.exp(score - jnp.max(score, axis=-1, keepdims=True))
        return (e * (1.0 / jnp.sum(e, axis=-1, keepdims=True))).astype(bf16)
    def own_attend(n):
        def go():
            def step(p):
                cols = columns(p, 128)
                kk = jnp.concatenate([k[:, cols], prows[:, cols]], axis=0)
                vv = jnp.concatenate([v[:, cols], prows[:, pl.ds(pl.multiple_of(D + p * 128, 128), 128)]], axis=0)
                qs, vs = split_heads(q[:, cols]), split_heads(vv)
                total = None
                for s in range(2):
                    prob = softmax(qs[s], kk, pen)
                    probs[2 * p + s] = prob
                    m = dot(prob, vs[s])
                    total = m if total is None else total + m
                att[:, cols] = total.astype(bf16)
            loop(2 * n, 2 * n + 2, step)
        return go
    def cross_scores(n):
        def go():
            def step(p):
                cols = columns(p, 128)
                qs = split_heads(cq[:, cols])
                for s in range(2):
                    cprobs[2 * p + s] = softmax(qs[s], ck[:, cols], cpen)
            loop(2 * n, 2 * n + 2, step)
        return go
    def cross_mix(n):
        def go():
            def step(p):
                cols = columns(p, 128)
                vs = split_heads(cv[:, cols])
                crossed[:, cols] = (dot(cprobs[2 * p], vs[0]) + dot(cprobs[2 * p + 1], vs[1])).astype(bf16)
            loop(4 * n, 4 * n + 4, step)
        return go
    def normed(base, low, w, at, out, nn, ii, olow):
        def part(n):
            def go():
                lv = low[...]
                def step(t):
                    out[:, columns(t)] = base[:, columns(t)].astype(f32) + dot(lv, g[w, :, columns(t)])
                loop(2 * n, 2 * n + 2, step)
            return go
        def last():
            m, inv = norm(out[...])
            nn[...] = m
            ii[...] = inv
            s = m * vecs[at:at + 1, :] + vecs[at + 1:at + 2, :]
            out[...] = s
            olow[...] = s.astype(bf16)
        return [part(0), part(1), last]
    make_q, make_k, make_v = halves(inputs, 0, q), halves(inputs, 1, k), halves(inputs, 2, v)
    make_ck, make_cq, make_cv = halves(memory, 4, ck), halves(flow, 5, cq), halves(memory, 6, cv)
    norm_one, norm_two = normed(inputs, att, 3, 0, first, n1, i1, flow), normed(first, crossed, 7, 2, second, n2, i2, slow)
    fs(0, 0)
    fs(0, 1)
    fz(0, 0)
    fs(1, 1)
    fs(1, 0)
    fz(0, 1)
    fs(3, 0)
    fs(2, 0)
    fz(1, 0)
    fs(2, 1)
    third(0, 1, 0)
    third(1, 1, 0)
    pre1()
    fs(3, 1)
    pre2(1)()
    mid(0, 0, 3)
    mid(0, 1, 1)
    third(0, 0, 0)
    mid(0, 0, 2)
    pre2(2)()
    fz(1, 1)
    mid(0, 1, 3)
    mid(0, 0, 1)
    mid(1, 0, 2)
    finish(0, 0)
    third(0, 0, 2)
    mid(1, 0, 1)
    fz(2, 0)
    pre4()
    pre5()
    third(0, 0, 1)
    mid(1, 1, 1)
    mid(0, 1, 2)
    feed_send(2)
    third(1, 0, 0)
    mid(1, 1, 2)
    third(0, 1, 1)
    mid(1, 1, 3)
    third(0, 1, 2)
    pre6()
    fz(2, 1)
    third(0, 1, 3)
    third(2, 0, 0)
    third(0, 0, 3)
    mid(1, 0, 3)
    mid(2, 1, 1)
    finish(0, 2)
    pre7()
    finish(0, 1)
    fz(3, 0)
    third(1, 0, 1)
    third(1, 1, 2)
    third(1, 0, 2)
    mid(2, 1, 2)
    third(1, 0, 3)
    mid(2, 0, 2)
    fz(3, 1)
    third(1, 1, 1)
    third(1, 1, 3)
    mid(2, 1, 3)
    finish(0, 3)
    finish(1, 0)
    finish(1, 1)
    feed_send(3)
    arrive(0)
    third(2, 1, 0)
    make_q[0]()
    finish(1, 3)
    mid(2, 0, 1)
    mid(2, 0, 3)
    finish(1, 2)
    pre8()
    third(2, 1, 2)
    feed_send(0)
    feed_send(1)
    make_q[1]()
    kept.append(cp.local(q, q_o))
    mid(3, 0, 2)
    third(2, 1, 3)
    arrive(1)
    make_k[0]()
    make_k[1]()
    kept.append(cp.local(k, k_o))
    third(2, 0, 2)
    third(2, 1, 1)
    masks()
    make_v[0]()
    mid(3, 1, 1)
    mid(3, 0, 1)
    third(2, 0, 3)
    third(2, 0, 1)
    feed_pass(2)
    mid(3, 0, 3)
    make_v[1]()
    kept.append(cp.local(v, v_o))
    own_attend(0)()
    mid(3, 1, 2)
    finish(2, 2)
    finish(2, 0)
    own_attend(1)()
    mid(3, 1, 3)
    feed_pass(3)
    own_attend(2)()
    own_attend(3)()
    kept.append(cp.local(probs, probs_o))
    kept.append(cp.local(att, att_o))
    third(3, 1, 1)
    finish(2, 3)
    norm_one[0]()
    finish(2, 1)
    third(3, 0, 1)
    third(3, 0, 0)
    third(3, 1, 0)
    norm_one[1]()
    norm_one[2]()
    kept.append(cp.local(flow, first_o))
    kept.append(cp.local(n1, n1_o))
    kept.append(cp.local(i1, i1_o))
    feed_pass(0)
    arrive(2)
    make_ck[0]()
    third(3, 0, 2)
    third(3, 1, 2)
    make_cq[0]()
    make_cq[1]()
    kept.append(cp.local(cq, cq_o))
    make_ck[1]()
    kept.append(cp.local(ck, ck_o))
    third(3, 1, 3)
    third(3, 0, 3)
    cross_scores(0)()
    finish(3, 1)
    finish(3, 0)
    cross_scores(1)()
    finish(3, 2)
    cross_scores(2)()
    finish(3, 3)
    cross_scores(3)()
    kept.append(cp.local(cprobs, cprobs_o))
    feed_pass(1)
    arrive(3)
    make_cv[0]()
    make_cv[1]()
    kept.append(cp.local(cv, cv_o))
    cross_mix(0)()
    cross_mix(1)()
    kept.append(cp.local(crossed, crossed_o))
    norm_two[0]()
    norm_two[1]()
    norm_two[2]()
    kept.append(cp.local(slow, slow_o))
    kept.append(cp.local(n2, n2_o))
    kept.append(cp.local(i2, i2_o))
    def partner():
        for e in passed: e.wait_recv()
    def finish():
        for e in kept: e.wait()
        cp.close()
    return (second, vecs, att, flow, crossed), partner, finish

def forward_kernel(A, r, inputs, memory, seg_row, mem_row, embed, inner, outer, norms, cot, *refs):
    ws, (fin, fout, down, up), outs, scratch = refs[:8], refs[8:12], refs[12:43], refs[43:]
    fin2, fout2 = scratch[32:34]
    (second, vecs, att, flow, crossed), partner, finish = front_part(A, r, inputs, memory, seg_row, mem_row, embed, inner, outer, norms, ws, fin, fout, fin2, fout2, outs[:20], scratch[:32])
    feed_part(A, second, vecs, cot, fin, fout, down, up, inputs, memory, att, flow, crossed, partner, outs[20:], scratch[32:])
    finish()

def forward(A, r, inputs, memory, seg_row, mem_row, embed, inner, outer, norms, cot, ws, fin, fout, down, up):
    T, D = inputs.shape; M = memory.shape[0]; H = fin.shape[1]; AD = down.shape[1] * 4
    HID = 2 * H
    vm = pl.BlockSpec(memory_space=pltpu.VMEM)
    any_ = pl.BlockSpec(memory_space=pl.ANY)
    sds = jax.ShapeDtypeStruct
    v = lambda *s: pltpu.VMEM(s, bf16)
    vf = lambda *s: pltpu.VMEM(s, f32)
    row, mrow, full, one = sds((T, D), bf16), sds((M, D), bf16), sds((T, D), f32), sds((T, 1), f32)
    S = (PADDED, inner.shape[1])
    probs, cprobs = (16, T, T + PADDED), (16, T, M)
    R = T // 2
    sums = (2, 2, D // 256, R, 256)
    four = sds((4 * T, D), bf16)
    sem = pltpu.SemaphoreType.DMA
    return pl.pallas_call(functools.partial(forward_kernel, A, r),
        out_shape=(sds((8, D, D), bf16), sds(S, f32), sds((PADDED, 2 * D), bf16), sds((8, D), f32), row, row, row, sds(probs, bf16), row, row, full, one, row, mrow, mrow,
            sds(cprobs, bf16), row, row, full, one,
            row, full, sds((D, HID), bf16), sds((HID, D), bf16), sds((2, T, AD), bf16), row, sds((2, D), f32), four, four, four, sds((4 * M, D), bf16)),
        in_specs=[vm] * 9 + [any_] * 12, out_specs=(any_,) * 20 + (vm,) * 2 + (any_,) * 2 + (vm,) * 3 + (any_,) * 4,
        scratch_shapes=[v(8, D, D), v(T, D), v(T, D), v(T, D), v(*probs), v(T, D), vf(T, D), v(T, D), vf(T, D), vf(T, 1), v(T, D), v(M, D), v(M, D), v(*cprobs), v(T, D),
            vf(T, D), v(T, D), vf(T, D), vf(T, 1), vf(T, T + PADDED), vf(T, M),
            vf(3, *S), vf(3, *S), vf(A, *S), v(PADDED, 128), v(PADDED, 128), v(PADDED, 2 * D), v(8 * A * norms.shape[0], 128), vf(8, D), vf(*S), sem((320,)), sem((320,)),
            v(D, HID), v(HID, D), v(D, HID), v(HID, D), v(D, AD), v(AD, D), v(2, 4, R, D), v(2, 4, R, D), v(2, 4, R, HID), vf(2, 4, R, HID), v(2, 4, R, HID), v(2, 4, D // 256, R, 256),
            v(*sums), v(*sums), v(*sums), vf(T, AD), vf(2, R, D), sem((128,)), sem((128,))],
        compiler_params=pltpu.CompilerParams(collective_id=1, has_side_effects=True, vmem_limit_bytes=60 << 20), name="forward")(
            inputs, memory, seg_row, mem_row, embed, inner, outer, norms, cot, *ws, fin, fout, down, up)


def exact(l, r, dims):
    return lax.dot_general(l, r, (dims, ((), ())), precision=lax.Precision.HIGHEST, preferred_element_type=f32)

def back_kernel(A, r, gsec, n2, i2, vecs, ngrad3, tangent, embed, inner, outer, *refs):
    late, (slow, blow, ay, weights, fi, fo, xp0, xatt, xin, xmem) = refs[:11], refs[11:21]
    back_body(A, r, gsec, n2, i2, vecs, ngrad3, tangent, embed, inner, outer, late, slow, blow, ay, weights, fi, fo, xp0, xatt, xin, xmem, *refs[21:])

def back_body(A, r, gsec, n2, i2, vecs, ngrad3, tangent, embed, inner, outer, late, slow, blow, ay, weights, fi, fo, xp0, xatt, xin, xmem,
                igrad_o, mgrad_o, out, aout, fi_out, fo_out, outer_o, inner_o, embed_o, nsum,
                igrad, mgrad, cq, ck, cv, cprobs, n1, i1, q, k, v, probs, prows, ws, gmid, gfirst, og, mid, dcq, dck, dcv, startl, dq, dk, dv, pg,
                xb, yb, mb, mby, axb, ayb, pb, apb, fib, fob, r1, r2, r3, sb, xs, ra1, ra2, ra3, rfi, rfo, rzi, rzo, rxi, rxo, ob, aob, fib2, fob2,
                buf, got, zbuf, nbuf, ngot, nz, w0, w1, w2, w3, s0, s1, s2, ssem, rsem):
    a, b, x, c = place()
    o = 1 - c
    core, xp, yp = device(a, b, x, o), device(a, b, 1 - x, c), device(a, 1 - b, x, c)
    dp = device(a, b, 1 - x, o)
    place_n = x * 2 + c
    zp = [device((a + j) % A, b, x, c) for j in range(A)]
    za = a + 1 - 2 * (a % 2)
    zq = device(za, b, x, c)
    peers = (core, xp, yp)
    T, D = gsec.shape
    M = xmem.shape[0] // 4
    HID = fi.shape[1] // 2
    Q = fi.shape[0] // 4
    half = D // 2
    cp = Copies(ssem, rsem)
    loads = {}
    def fetch(slot, w):
        loads[slot] = cp.local(weights.at[w], ws.at[slot])
    loaded = [cp.local(src, dst) for src, dst in zip(late, (cq, ck, cv, cprobs, n1, i1, q, k, v, probs, prows))]
    def ready(start, stop):
        for e in loaded[start:stop]: e.wait()
    fetch(0, 7); fetch(1, 5); fetch(2, 3); fetch(3, 4)
    fown = []
    for xx in range(2):
        dq_ = pl.ds(pl.multiple_of((xx * 2 + c) * Q, Q), Q)
        fown += [cp.local(fi.at[dq_, :], fib.at[xx]), cp.local(fo.at[:, dq_], fob.at[xx])]
    greet([core, xp, yp, dp] + zp[1:])
    def offer(srcs, mine, theirs):
        n = cp.count
        cp.count += 2
        def start(keep, give):
            pltpu.make_async_copy(srcs[keep], mine, ssem.at[n]).start()
            remote(srcs[give], theirs, ssem.at[n + 1], rsem.at[n], core).start()
        pl.when(c == 0)(functools.partial(start, 0, 1))
        pl.when(c == 1)(functools.partial(start, 1, 0))
        e = remote(srcs[0], theirs, ssem.at[n + 1], rsem.at[n], core)
        cp.all.append(e)
        return pltpu.make_async_copy(srcs[0], mine, ssem.at[n]).wait, e.wait_recv
    lowT, highT = pl.ds(0, T), pl.ds(T, T)
    waits = {}
    aw = offer((slow, blow), axb.at[lowT], axb.at[highT]) + offer((ay.at[0], ay.at[1]), ayb.at[lowT], ayb.at[highT])
    xload = cp.count
    cp.count += 4
    def load_x(me):
        pltpu.make_async_copy(xp0, xb.at[0], ssem.at[xload]).start()
        pltpu.make_async_copy(xmem, mb, ssem.at[xload + 1]).start()
        pltpu.make_async_copy(xin if me else xatt, xb.at[1], ssem.at[xload + 2]).start()
        pltpu.make_async_copy(xin, xb.at[2], ssem.at[xload + 3]).start()
    pl.when(c == 0)(functools.partial(load_x, 0))
    pl.when(c == 1)(functools.partial(load_x, 1))
    waits[0] = (pltpu.make_async_copy(xp0, xb.at[0], ssem.at[xload]).wait,)
    waits[1] = (pltpu.make_async_copy(xmem, mb, ssem.at[xload + 1]).wait,)
    waits[2] = (pltpu.make_async_copy(xin, xb.at[1], ssem.at[xload + 2]).wait,)
    waits[3] = (pltpu.make_async_copy(xin, xb.at[2], ssem.at[xload + 3]).wait,)
    def share(srcs, dst, t):
        m = srcs[0].shape[0]
        k = cp.count
        cp.count += 4
        wide = half // 2
        here = pl.ds(pl.multiple_of(x * half + t * wide, wide), wide)
        there = pl.ds(pl.multiple_of((1 - x) * half + t * wide, wide), wide)
        spot = dst.at[pl.ds(pl.multiple_of(place_n * m, m), m), pl.ds(t * wide, wide)]
        def start(me):
            own, other = srcs[me], srcs[1 - me]
            remote(own.at[:, there], spot, ssem.at[k + 1], rsem.at[k + 1], xp).start()
            remote(other.at[:, there], spot, ssem.at[k + 3], rsem.at[k + 3], dp).start()
            remote(other.at[:, here], spot, ssem.at[k + 2], rsem.at[k + 2], core).start()
            pltpu.make_async_copy(own.at[:, here], spot, ssem.at[k]).start()
        pl.when(c == 0)(functools.partial(start, 0))
        pl.when(c == 1)(functools.partial(start, 1))
        ways = [remote(srcs[0].at[:, here], spot, ssem.at[k + i], rsem.at[k + i], d) for i, d in ((1, xp), (2, core), (3, dp))]
        cp.all.extend(ways)
        return (pltpu.make_async_copy(srcs[0].at[:, here], spot, ssem.at[k]).wait,) + tuple(e.wait_recv for e in ways)
    fcopies = []
    for xx in range(2):
        dq_ = pl.ds(pl.multiple_of((xx * 2 + o) * Q, Q), Q)
        fcopies += [cp(fi.at[dq_, :], rfi.at[xx], core), cp(fo.at[:, dq_], rfo.at[xx], core)]

    zf, xf, outs = [], [], []
    def feed0():
        for e in fown: e.wait()
        for e in fcopies: e.wait_recv()
        for xx in range(2):
            def rows_fi(t):
                s = pl.ds(t * 32, 32)
                fib[xx, s, :] = fib[xx, s, :] + rfi[xx, s, :]
            loop(0, Q // 32, rows_fi)
            def rows_fo(t):
                s = pl.ds(t * 64, 64)
                fob[xx, s, :] = fob[xx, s, :] + rfo[xx, s, :]
            loop(0, 2 * HID // 64, rows_fo)
        zf.extend([cp(fib.at[:, :, pl.ds(HID, HID)], rzi, zq), cp(fob.at[:, pl.ds(HID, HID), :], rzo, zq)])
    def feed1():
        for e in zf: e.wait_recv()
        for xx in range(2):
            def rows_fi(t):
                s = pl.ds(t * 32, 32)
                fib[xx, s, pl.ds(0, HID)] = fib[xx, s, pl.ds(0, HID)] + rzi[xx, s, :]
            loop(0, Q // 32, rows_fi)
            def rows_fo(t):
                s = pl.ds(t * 64, 64)
                fob[xx, s, :] = fob[xx, s, :] + rzo[xx, s, :]
            loop(0, HID // 64, rows_fo)
        xf.extend([cp(fib.at[1 - x, :, pl.ds(0, HID)], rxi, xp), cp(fob.at[1 - x, pl.ds(0, HID), :], rxo, xp)])
    def feed2():
        for e in xf: e.wait_recv()
        def rows_fi(t):
            s = pl.ds(t * 32, 32)
            fib2[s, :] = fib[x, s, pl.ds(0, HID)].astype(f32) + rxi[s, :].astype(f32)
        loop(0, Q // 32, rows_fi)
        def rows_fo(t):
            s = pl.ds(t * 64, 64)
            fob2[s, :] = fob[x, s, :].astype(f32) + rxo[s, :].astype(f32)
        loop(0, HID // 64, rows_fo)
        outs.extend([cp.local(fib2, fi_out).wait, cp.local(fob2, fo_out).wait])

    first, second, third, fourth = {}, {}, {}, {}
    wide = half // 2
    numbers = {}
    for i in range(4):
        for t in range(2):
            numbers[i, t] = cp.count
            cp.count += 1
    def level1(i, t):
        n = numbers[i, t]
        return remote(pb.at[i, t, :, 1 - b], r1.at[i, t], ssem.at[n], rsem.at[n], yp)
    for i in range(4):
        for t in range(2):
            first[i, t] = level1(i, t)
            cp.all.append(first[i, t])
    def share_one(src, dst, t, owner):
        m = src.shape[0]
        k = cp.count
        cp.count += 4
        wide = half // 2
        here = pl.ds(pl.multiple_of(x * half + t * wide, wide), wide)
        there = pl.ds(pl.multiple_of((1 - x) * half + t * wide, wide), wide)
        spot = dst.at[pl.ds(pl.multiple_of(place_n * m, m), m), pl.ds(t * wide, wide)]
        kept = pltpu.make_async_copy(src.at[:, here], spot, ssem.at[k])
        ways = [remote(src.at[:, there], spot, ssem.at[k + 1], rsem.at[k + 1], xp), remote(src.at[:, here], spot, ssem.at[k + 2], rsem.at[k + 2], core),
                remote(src.at[:, there], spot, ssem.at[k + 3], rsem.at[k + 3], dp)]
        def mine():
            ways[0].start()
            kept.start()
        def other():
            ways[2].start()
            ways[1].start()
        pl.when(c == owner)(mine)
        pl.when(c != owner)(other)
        def arrived():
            kept.wait()
            for e in ways: e.wait_recv()
        def sent():
            pl.when(c == owner)(ways[0].wait_send)
            def both():
                ways[1].wait_send()
                ways[2].wait_send()
            pl.when(c != owner)(both)
        ending.append(sent)
        return (arrived,)
    ending = []
    used, filled = set(), set()
    def compute(i, t, owner=None):
        def go():
            if (i, owner) not in used:
                used.add((i, owner))
                for e in waits[i]: e()
            for e in shared[(i, t) if owner is None else (i, t, owner)]: e()
            cols = pl.ds(t * wide, wide)
            n = (0, None, 1, 2)[i]
            def rows(u):
                d = columns(u)
                p = dot_left(mb[:, d], mby[:, cols]) if i == 1 else dot_left(xb[n, :, d], yb[n, :, cols])
                pb[i, t, u] = p.astype(bf16).reshape(2, 2, 2 * r, wide)
            loop(0, A, rows)
            level1(i, t).start()
        if owner is None: go()
        else: pl.when(c == owner)(go)
    def one(i, t):
        def go():
            first[i, t].wait_recv()
            for j in range(1, A):
                aj = (a + j) % A
                pb[i, t, aj, b] = pb[i, t, aj, b] + r1[i, t, aj]
                third[i, t, j] = cp(pb.at[i, t, aj, b], r2.at[i, t, j - 1], zp[j])
            pb[i, t, a, b] = pb[i, t, a, b] + r1[i, t, a]
        return go
    def two(i, t):
        def go():
            for j in range(1, A): third[i, t, j].wait_recv()
            for s in (1 - x, x):
                e = pb[i, t, a, b, s].astype(f32)
                for j in range(1, A): e = e + r2[i, t, j - 1, s].astype(f32)
                sb[i, t, s] = e
            xs[i, t] = sb[i, t, 1 - x].astype(bf16)
            fourth[i, t] = cp(xs.at[i, t], r3.at[i, t], xp)
        return go
    def three(i, t):
        def go():
            fourth[i, t].wait_recv()
            ob[i, :, pl.ds(pl.multiple_of(x * half + t * wide, wide), wide)] = sb[i, t, x]
            ob[i, :, pl.ds(pl.multiple_of((1 - x) * half + t * wide, wide), wide)] = r3[i, t].astype(f32)
            filled.add((i, t))
            if (i, 1 - t) in filled:
                outs.append(cp.local(ob.at[i, pl.ds(pl.multiple_of(c * r, r), r)], out.at[2 * i + c]).wait)
                outs.append(cp(ob.at[i, pl.ds(pl.multiple_of(o * r, r), r)], out.at[2 * i + c], core).wait_recv)
        return go
    def adapt0():
        for e in aw: e()
        for t in range(2):
            apb[t] = dot_left(axb[...], ayb[:, pl.ds(t * 256, 256)]).astype(bf16).reshape(A, 2, D // (2 * A), 256)
        first["a"] = cp(apb.at[1 - x], ra1, xp)
    def adapt1():
        first["a"].wait_recv()
        def row(z):
            for s in range(2):
                apb[x, z, s] = apb[x, z, s] + ra1[z, s]
        loop(0, A, row)
        second["a"] = cp(apb.at[x, :, 1 - b], ra2, yp)
    def adapt2():
        second["a"].wait_recv()
        for j in range(1, A):
            aj = (a + j) % A
            apb[x, aj, b] = apb[x, aj, b] + ra2[aj]
            third["a", j] = cp(apb.at[x, aj, b], ra3.at[j - 1], zp[j])
        apb[x, a, b] = apb[x, a, b] + ra2[a]
    def adapt3():
        for j in range(1, A): third["a", j].wait_recv()
        t = apb[x, a, b].astype(f32)
        for j in range(1, A): t = t + ra3[j - 1].astype(f32)
        aob[0] = t[:, :128]
        aob[1] = t[:, 128:]
        outs.append(cp.local(aob.at[c], aout.at[c]).wait)
        outs.append(cp(aob.at[o], aout.at[c], core).wait_recv)
    small = {}
    def lanes(start, count): return pl.ds(pl.multiple_of(start * 128, 128), count * 128)
    def tail_norm0():
        small["n"] = [cp(nbuf.at[0], ngot.at[0], core)]
    def tail0():
        small["w"] = [cp(pg.at[:, lanes((a + j) % A * 4, 4)], w0.at[j - 1], zp[j]) for j in range(1, A)]
    def tail_norm(n):
        def go():
            for e in small["n"]: e.wait_recv()
            nbuf[n] = nbuf[n - 1] + ngot[n - 1]
            small["n"] = [cp(nbuf.at[n], ngot.at[n], peers[n])]
        return go
    def tail_norm3():
        for e in small["n"]: e.wait_recv()
        nz[a] = nbuf[2] + ngot[2]
        small["n"] = [cp(nz.at[a], nz.at[a], zp[j]) for j in range(1, A)]
    def tail_norm4():
        for e in small["n"]: e.wait_recv()
        t = nz[0]
        for n in range(1, A): t = t + nz[n]
        nsum[...] = t
    def tail1():
        t = pg[:, lanes(a * 4, 4)]
        for j, e in enumerate(small["w"]):
            e.wait_recv()
            t = t + w0[j]
        s0[...] = t
        small["w"] = [cp(s0.at[:, lanes((1 - b) * 2, 2)], w1, yp)]
    def tail2():
        small["w"][0].wait_recv()
        s1[...] = s0[:, lanes(b * 2, 2)] + w1[...]
        small["w"] = [cp(s1.at[:, lanes(1 - x, 1)], w2, xp)]
    def tail3():
        small["w"][0].wait_recv()
        s2[...] = s1[:, lanes(x, 1)] + w2[...]
        small["w"] = [cp(s2, w3, core)]
    def tail4():
        small["w"][0].wait_recv()
        t = s2[...] + w3[...]
        mine = jnp.where(c == 0, t[:, :64], t[:, 64:])
        buf[0] = exact(mine, outer[...].astype(f32), ((1,), (0,)))
        small["w"] = [cp(buf.at[0], got.at[0], core)]
        outer_o[...] = exact(mine, tangent[...].astype(bf16).astype(f32), ((0,), (0,)))
    def tail5(n):
        def go():
            small["w"][0].wait_recv()
            buf[n] = buf[n - 1] + got[n - 1]
            small["w"] = [cp(buf.at[n], got.at[n], peers[n])]
        return go
    def tail6():
        small["w"][0].wait_recv()
        zbuf[a] = buf[2] + got[2]
        small["w"] = [cp(zbuf.at[a], zbuf.at[a], zp[j]) for j in range(1, A)]
    def tail7():
        for e in small["w"]: e.wait_recv()
        t = zbuf[0]
        for n in range(1, A): t = t + zbuf[n]
        tan = tangent[...]
        t = t * (1.0 - tan * tan)
        inner_o[...] = exact(embed[...].astype(f32), t[:PREFIX], ((0,), (0,)))
        embed_o[...] = exact(t[:PREFIX], inner[...].astype(f32), ((1,), (1,)))
    def norm_two():
        norm_back_into(gsec, n2, i2, vecs[2:3, :], gmid, nbuf.at[0], 2)
        mid[...] = gmid[...].astype(bf16)
    def back_project(src, slot, n):
        def go():
            s = src[...]
            loop(2 * n, 2 * n + 2, lambda t: og.__setitem__((slice(None), columns(t)), dot_right(s, ws[slot, columns(t), :]).astype(bf16)))
        return go
    def wait_slot(slot):
        def go(): loads[slot].wait()
        return go
    def pair_back(p, grad, qr, kk, vv, pr):
        cols = columns(p, 128)
        qs, ks, gs = split_heads(qr[:, cols]), split_heads(kk), split_heads(grad[:, cols])
        res = None
        for s in range(2):
            low = pr[2 * p + s]
            prob = low.astype(f32)
            t = prob * dot_right(gs[s], vv)
            ds = (t - prob * jnp.sum(t, axis=-1, keepdims=True)).astype(bf16)
            m = (dot(ds, ks[s]), dot_left(ds, qs[s]), dot_left(low, gs[s]))
            res = m if res is None else tuple(e + f for e, f in zip(res, m))
        return cols, res[0] * 0.125, res[1] * 0.125, res[2]
    def cross_back(n):
        def go():
            def step(p):
                cs = columns(p, 128)
                cols, m1, m2, m3 = pair_back(p, og, cq, ck[:, cs], cv[:, cs], cprobs)
                dcq[:, cols] = m1.astype(bf16)
                dck[:, cols] = m2.astype(bf16)
                dcv[:, cols] = m3.astype(bf16)
            for p in range(2 * n, 2 * n + 2): step(p)
        return go
    def self_back(n):
        def go():
            def step(p):
                cs = columns(p, 128)
                cv_ = pl.ds(pl.multiple_of(D + p * 128, 128), 128)
                kk = jnp.concatenate([k[:, cs], prows[:, cs]], axis=0)
                vv = jnp.concatenate([v[:, cs], prows[:, cv_]], axis=0)
                cols, m1, m2, m3 = pair_back(p, og, q, kk, vv, probs)
                dq[:, cols] = m1.astype(bf16)
                dk[:, cols] = m2[:T].astype(bf16)
                dv[:, cols] = m3[:T].astype(bf16)
                pg[:, cols] = m2[T:]
                pg[:, cv_] = m3[T:]
            for p in range(2 * n, 2 * n + 2): step(p)
        return go
    def first_grad():
        s = dcq[...]
        def step(t):
            gfirst[:, columns(t)] = gmid[:, columns(t)] + dot_right(s, ws[1, columns(t), :])
        loop(0, D // 256, step)
    def norm_one():
        norm_back_into(gfirst, n1, i1, vecs[0:1, :], gmid, nbuf.at[0], 0)
        nbuf[0, 4:6, :] = ngrad3[...]
        nbuf[0, 6:8, :] = jnp.zeros((2, D), f32)
        startl[...] = gmid[...].astype(bf16)
    def memory_part(n):
        def go():
            def step(t):
                mgrad[:, columns(t)] = (dot_right(dck[...], ws[3, columns(t), :]) + dot_right(dcv[...], ws[0, columns(t), :])).astype(bf16)
            loop(2 * n, 2 * n + 2, step)
        return go
    def input_part(n):
        def go():
            def step(t):
                s = gmid[:, columns(t)] + dot_right(dq[...], ws[1, columns(t), :]) + dot_right(dk[...], ws[2, columns(t), :]) + dot_right(dv[...], ws[3, columns(t), :])
                igrad[:, columns(t)] = s.astype(bf16)
            loop(2 * n, 2 * n + 2, step)
        return go
    shared = {}
    def spread(i, srcs, dst):
        for t in range(2): shared[i, t] = share(srcs, dst, t)
    def spread_one(i, src, dst, owner):
        for t in range(2): shared[i, t, owner] = share_one(src, dst, t, owner)
    norm_two()
    spread_one(0, mid, yb.at[0], 0)
    wait_slot(0)()
    back_project(mid, 0, 0)()
    back_project(mid, 0, 1)()
    fetch(0, 6)
    ready(0, 4)
    cross_back(0)()
    cross_back(1)()
    cross_back(2)()
    cross_back(3)()
    compute(0, 1, 0)
    spread_one(0, dcq, yb.at[0], 1)
    feed0()
    wait_slot(1)()
    first_grad()
    fetch(1, 0)
    ready(4, 6)
    norm_one()
    spread(1, (dck, dcv), mby)
    compute(0, 1, 1)
    compute(0, 0, 0)
    wait_slot(2)()
    back_project(startl, 2, 0)()
    back_project(startl, 2, 1)()
    fetch(2, 1)
    ready(6, 11)
    self_back(0)()
    wait_slot(3)()
    wait_slot(0)()
    memory_part(0)()
    one(0, 1)()
    compute(0, 0, 1)
    self_back(1)()
    compute(1, 0)
    self_back(2)()
    tail_norm0()
    spread_one(2, startl, yb.at[1], 0)
    one(0, 0)()
    tail_norm(1)()
    self_back(3)()
    compute(1, 1)
    tail0()
    spread_one(2, dq, yb.at[1], 1)
    spread(3, (dk, dv), yb.at[2])
    compute(2, 0, 0)
    compute(2, 1, 0)
    compute(2, 0, 1)
    one(1, 0)()
    adapt0()
    compute(3, 1)
    feed1()
    one(1, 1)()
    one(2, 0)()
    tail1()
    compute(2, 1, 1)
    one(3, 1)()
    tail2()
    compute(3, 0)
    one(2, 1)()
    adapt1()
    one(3, 0)()
    two(0, 1)()
    tail3()
    tail4()
    two(1, 1)()
    adapt2()
    tail5(1)()
    two(0, 0)()
    two(1, 0)()
    tail5(2)()
    three(1, 1)()
    memory_part(1)()
    outs.append(cp.local(mgrad, mgrad_o).wait)
    fetch(3, 2)
    wait_slot(1)()
    wait_slot(2)()
    wait_slot(3)()
    input_part(0)()
    two(3, 1)()
    three(1, 0)()
    tail6()
    three(0, 0)()
    two(3, 0)()
    tail_norm(2)()
    three(0, 1)()
    three(3, 1)()
    input_part(1)()
    outs.append(cp.local(igrad, igrad_o).wait)
    adapt3()
    three(3, 0)()
    two(2, 0)()
    tail_norm3()
    feed2()
    two(2, 1)()
    three(2, 1)()
    three(2, 0)()
    tail7()
    tail_norm4()
    for e in ending: e()
    for e in outs: e()
    cp.close()

def back(A, r, first, late, rest):
    gsec = first[0]
    T, D = gsec.shape; M = rest[-1].shape[0] // 4
    fi, fo = rest[4:6]
    Q, H2 = fi.shape[0] // 4, fi.shape[1]
    H = H2 // 2
    half = D // 2
    v = lambda *s: pltpu.VMEM(s, bf16)
    vf = lambda *s: pltpu.VMEM(s, f32)
    any_ = pl.BlockSpec(memory_space=pl.ANY)
    vm = pl.BlockSpec(memory_space=pltpu.VMEM)
    sds = jax.ShapeDtypeStruct
    P_, N = PADDED, (8, D)
    hid = first[-2].shape[1]
    S = (P_, hid)
    return pl.pallas_call(functools.partial(back_kernel, A, r),
        out_shape=(sds((T, D), bf16), sds((M, D), bf16), sds((8, r, D), f32), sds((2, D // (2 * A), 128), f32), sds((Q, H), f32), sds((H, Q), f32),
            sds((64, hid), f32), sds((r, hid), f32), sds((PREFIX, r), f32), sds(N, f32)),
        in_specs=[vm] * len(first) + [any_] * (len(late) + len(rest)), out_specs=(any_,) * 6 + (vm,) * 4,
        scratch_shapes=[v(T, D), v(M, D)] + [pltpu.VMEM(e.shape, e.dtype) for e in late] + [v(4, D, D), vf(T, D), vf(T, D), v(T, D), v(T, D), v(T, D), v(M, D), v(M, D), v(T, D), v(T, D), v(T, D), v(T, D), vf(P_, 2 * D),
            v(3, 4 * T, D), v(3, 4 * T, half), v(4 * M, D), v(4 * M, half), v(2 * T, D), v(2 * T, 512),
            v(4, 2, A, 2, 2, 2 * r, half // 2), v(2, A, 2, D // (2 * A), 256), v(2, Q, H2), v(2, H2, Q),
            v(4, 2, A, 2, 2 * r, half // 2), v(4, 2, A - 1, 2, 2 * r, half // 2), v(4, 2, 2 * r, half // 2), vf(4, 2, 2, 2 * r, half // 2), v(4, 2, 2 * r, half // 2),
            v(A, 2, D // (2 * A), 256), v(A, D // (2 * A), 256), v(A - 1, D // (2 * A), 256),
            v(2, Q, H2), v(2, H2, Q), v(2, Q, H), v(2, H, Q), v(Q, H), v(H, Q),
            vf(4, 2 * r, D), vf(2, D // (2 * A), 128), vf(Q, H), vf(H, Q),
            vf(3, *S), vf(3, *S), vf(A, *S), vf(3, *N), vf(3, *N), vf(A, *N), vf(A - 1, P_, 512), vf(P_, 256), vf(P_, 128), vf(P_, 128), vf(P_, 512), vf(P_, 256), vf(P_, 128),
            pltpu.SemaphoreType.DMA((224,)), pltpu.SemaphoreType.DMA((224,))],
        compiler_params=pltpu.CompilerParams(collective_id=2, has_side_effects=True, vmem_limit_bytes=63 << 20),
        name="back")(*first, *late, *rest)

def fast_body(A, inputs, memory, cotangent, segments, memory_segments, query_self, key_self, value_self, output_self,
              query_cross, key_cross, value_cross, output_cross, self_gain, self_shift, cross_gain, cross_shift,
              final_gain, final_shift, feed_in, feed_out, adapter_down, adapter_up, prefix_embed, prefix_inner, prefix_outer):
    r = query_self.shape[0]
    w, n = lax.axis_index(WIDE), lax.axis_index(NARROW)
    blank = jnp.zeros_like(self_gain)
    norms = jnp.stack([self_gain, self_shift, cross_gain, cross_shift, final_gain, final_shift] + [blank] * 10)
    (weights, tangent, prows, vecs, q, k, v, probs, attended, first_low, n1, i1, cq, ck, cv, cprobs, crossed, second_low, n2, i2,
     result, grad_second, fi, fo, ay, branch_low, ngrad3, xp0, xatt, xin, xmem) = forward(
        A, r, inputs, memory, segments.reshape(1, -1), memory_segments.reshape(1, -1), prefix_embed, prefix_inner, prefix_outer.T, norms, cotangent,
        [query_self, key_self, value_self, output_self, key_cross, query_cross, value_cross, output_cross], feed_in, feed_out, adapter_down, adapter_up)
    igrad, mgrad, sums, adapt, fi_sum, fo_sum, outer_grad, inner_grad, embed_grad, nsum = back(A, r,
        (grad_second, n2, i2, vecs, ngrad3, tangent, prefix_embed, prefix_inner, prefix_outer.T), (cq, ck, cv, cprobs, n1, i1, q, k, v, probs, prows),
        (second_low, branch_low, ay, weights, fi, fo, xp0, xatt, xin, xmem))
    ng = lax.dynamic_slice_in_dim(nsum, (w * 4 + n) * r, r, 1)
    whole = deliver(result, igrad, mgrad, sums, fi_sum, fo_sum, outer_grad, inner_grad, embed_grad, adapt)
    return whole[:11] + tuple(ng[k] for k in range(6)) + whole[11:17] + (whole[17].T,)


def deliver_kernel(result, igrad, mgrad, sums, fi, fo, outer, inner, embed, adapt, *outs):
    order = (5, 6, 7, 4, 1, 2, 3, 0)
    for dst, src in zip(outs[:3], (result, igrad, mgrad)): dst[...] = src[...]
    for dst, k in zip(outs[3:11], order): dst[...] = sums[k]
    for dst, src in zip(outs[11:13] + outs[15:], (fi, fo, embed, inner, outer)): dst[...] = src[...]
    outs[13][...] = adapt[0]
    outs[14][...] = adapt[1].T


def deliver(result, igrad, mgrad, sums, fi, fo, outer, inner, embed, adapt):
    like = lambda e: jax.ShapeDtypeStruct(e.shape, e.dtype)
    row = jax.ShapeDtypeStruct(sums.shape[1:], f32)
    square = jax.ShapeDtypeStruct(adapt.shape[1:], f32)
    vm = pl.BlockSpec(memory_space=pltpu.VMEM)
    return pl.pallas_call(deliver_kernel,
        out_shape=(like(result), like(igrad), like(mgrad)) + (row,) * 8 + (like(fi), like(fo), square, square, like(embed), like(inner), like(outer)),
        in_specs=[vm] * 10, out_specs=(vm,) * 18, compiler_params=pltpu.CompilerParams(vmem_limit_bytes=60 << 20),
        name="deliver")(result, igrad, mgrad, sums, fi, fo, outer, inner, embed, adapt)


def solution(mesh):
    wide, narrow = mesh.shape[WIDE], mesh.shape[NARROW]
    fits = narrow == 4 and wide == 8
    body = functools.partial(fast_body, wide // 2) if fits else plain_body
    return jax.shard_map(
        body,
        mesh=mesh,
        in_specs=(
            P(BOTH, None),
            P(BOTH, None),
            P(BOTH, None),
            P(BOTH),
            P(BOTH),
            P(BOTH, None),
            P(BOTH, None),
            P(BOTH, None),
            P(BOTH, None),
            P(BOTH, None),
            P(BOTH, None),
            P(BOTH, None),
            P(BOTH, None),
            P(BOTH),
            P(BOTH),
            P(BOTH),
            P(BOTH),
            P(BOTH),
            P(BOTH),
            P(None, WIDE),
            P(WIDE, None),
            P(None, NARROW),
            P(NARROW, None),
            P(None, BOTH),
            P(BOTH, None),
            P(None, BOTH),
        ),
        out_specs=(
            P(BOTH, None),
            P(BOTH, None),
            P(BOTH, None),
            P(BOTH, None),
            P(BOTH, None),
            P(BOTH, None),
            P(BOTH, None),
            P(BOTH, None),
            P(BOTH, None),
            P(BOTH, None),
            P(BOTH, None),
            P(BOTH),
            P(BOTH),
            P(BOTH),
            P(BOTH),
            P(BOTH),
            P(BOTH),
            P(NARROW, WIDE),
            P(WIDE, NARROW),
            P(WIDE, NARROW),
            P(NARROW, WIDE),
            P(None, BOTH),
            P(BOTH, None),
            P(None, BOTH),
        ),
        check_vma=False,
    )
```

```python
import functools
from functools import reduce

import jax
import jax.numpy as jnp
from jax import lax
from jax.experimental import pallas as pl
from jax.experimental.pallas import tpu as pltpu
from jax.sharding import PartitionSpec as P

MESH = pl.DeviceIdType.MESH
bf16, f32 = jnp.bfloat16, jnp.float32
WIDE, NARROW = "wide", "narrow"
BOTH = (WIDE, NARROW)


HEADS = 16
HEAD = 64
PREFIX = 30


HIGHEST = lax.Precision.HIGHEST
EPSILON = 1e-05
MASKED = -1000000000.0
ADAPT_SCALE = 4.0


def matmul(left, right):
    return jnp.dot(left, right, preferred_element_type=jnp.float32)


def left_product(left, right):
    return lax.dot_general(
        left, right, (((0,), (0,)), ((), ())), preferred_element_type=jnp.float32
    )


def right_product(left, right):
    return lax.dot_general(
        left, right, (((1,), (1,)), ((), ())), preferred_element_type=jnp.float32
    )


def exact_left(left, right):
    return lax.dot_general(
        left, right, (((0,), (0,)), ((), ())), precision=HIGHEST, preferred_element_type=jnp.float32
    )


def exact_right(left, right):
    return lax.dot_general(
        left, right, (((1,), (1,)), ((), ())), precision=HIGHEST, preferred_element_type=jnp.float32
    )


def norm_forward(values, factor, offset):
    average = jnp.mean(values, axis=-1, keepdims=True)
    center = values - average
    inverse = lax.rsqrt(jnp.mean(center * center, axis=-1, keepdims=True) + EPSILON)
    normed = center * inverse
    return (normed * factor + offset, normed, inverse)


def norm_backward(grad_out, normed, inverse, factor):
    scaled = grad_out * factor
    grad_in = inverse * (
        scaled
        - jnp.mean(scaled, axis=-1, keepdims=True)
        - normed * jnp.mean(scaled * normed, axis=-1, keepdims=True)
    )
    return (grad_in, jnp.sum(grad_out * normed, axis=0), jnp.sum(grad_out, axis=0))


def head_view(rows):
    return rows.reshape(rows.shape[0], HEADS, HEAD)


def scored(queries, key_rows, allowed):
    raw = jnp.einsum(
        "shd,khd->hsk", head_view(queries), head_view(key_rows), preferred_element_type=jnp.float32
    )
    return jnp.where(allowed[None], raw * HEAD ** (-0.5), MASKED)


def attend_forward(queries, parts):
    scores = [scored(queries, member[0], member[2]) for member in parts]
    largest = reduce(jnp.maximum, [jnp.max(matrix, axis=-1, keepdims=True) for matrix in scores])
    total = reduce(
        jnp.add, [jnp.sum(jnp.exp(matrix - largest), axis=-1, keepdims=True) for matrix in scores]
    )
    logsum = largest + jnp.log(total)
    mixed = reduce(
        jnp.add,
        [
            jnp.einsum(
                "hsk,khd->shd",
                jnp.exp(matrix - logsum).astype(jnp.bfloat16),
                head_view(member[1]),
                preferred_element_type=jnp.float32,
            )
            for matrix, member in zip(scores, parts)
        ],
    )
    return (mixed.reshape(queries.shape[0], HEADS * HEAD), logsum)


def attend_backward(queries, parts, logsum, grad_low):
    grad_heads = head_view(grad_low)
    chances = [jnp.exp(scored(queries, member[0], member[2]) - logsum) for member in parts]
    slopes = [
        jnp.einsum(
            "shd,khd->hsk", grad_heads, head_view(member[1]), preferred_element_type=jnp.float32
        )
        for member in parts
    ]
    row_dot = reduce(
        jnp.add,
        [jnp.sum(chance * slope, axis=-1, keepdims=True) for chance, slope in zip(chances, slopes)],
    )
    scale = HEAD ** (-0.5)
    grad_query = jnp.zeros((queries.shape[0], HEADS, HEAD), jnp.float32)
    results = []
    for member, chance, slope in zip(parts, chances, slopes):
        dscore = (chance * (slope - row_dot)).astype(jnp.bfloat16)
        grad_query = grad_query + jnp.einsum(
            "hsk,khd->shd", dscore, head_view(member[0]), preferred_element_type=jnp.float32
        )
        grad_key = (
            jnp.einsum(
                "hsk,shd->khd", dscore, head_view(queries), preferred_element_type=jnp.float32
            )
            * scale
        )
        grad_value = jnp.einsum(
            "hsk,shd->khd",
            chance.astype(jnp.bfloat16),
            grad_heads,
            preferred_element_type=jnp.float32,
        )
        results.append(
            (
                grad_key.reshape(grad_key.shape[0], HEADS * HEAD),
                grad_value.reshape(grad_value.shape[0], HEADS * HEAD),
            )
        )
    return ((grad_query * scale).reshape(queries.shape[0], HEADS * HEAD), results)


def gelu_back(pre_values, grad_values):
    return jax.vjp(lambda inner: jax.nn.gelu(inner, approximate=False), pre_values)[1](grad_values)[
        0
    ]


def plain_body(
    inputs,
    memory,
    cotangent,
    segments,
    memory_segments,
    query_self,
    key_self,
    value_self,
    output_self,
    query_cross,
    key_cross,
    value_cross,
    output_cross,
    self_gain,
    self_shift,
    cross_gain,
    cross_shift,
    final_gain,
    final_shift,
    feed_in,
    feed_out,
    adapter_down,
    adapter_up,
    prefix_embed,
    prefix_inner,
    prefix_outer,
):
    (
        query_one,
        key_one,
        value_one,
        output_one,
        query_two,
        key_two,
        value_two,
        output_two,
        gain_one,
        shift_one,
        gain_two,
        shift_two,
        gain_three,
        shift_three,
        embed_full,
        inner_full,
        outer_full,
    ) = (
        lax.all_gather(query_self, BOTH, axis=0, tiled=True),
        lax.all_gather(key_self, BOTH, axis=0, tiled=True),
        lax.all_gather(value_self, BOTH, axis=0, tiled=True),
        lax.all_gather(output_self, BOTH, axis=0, tiled=True),
        lax.all_gather(query_cross, BOTH, axis=0, tiled=True),
        lax.all_gather(key_cross, BOTH, axis=0, tiled=True),
        lax.all_gather(value_cross, BOTH, axis=0, tiled=True),
        lax.all_gather(output_cross, BOTH, axis=0, tiled=True),
        lax.all_gather(self_gain, BOTH, axis=0, tiled=True),
        lax.all_gather(self_shift, BOTH, axis=0, tiled=True),
        lax.all_gather(cross_gain, BOTH, axis=0, tiled=True),
        lax.all_gather(cross_shift, BOTH, axis=0, tiled=True),
        lax.all_gather(final_gain, BOTH, axis=0, tiled=True),
        lax.all_gather(final_shift, BOTH, axis=0, tiled=True),
        lax.all_gather(prefix_embed, BOTH, axis=1, tiled=True),
        lax.all_gather(prefix_inner, BOTH, axis=0, tiled=True),
        lax.all_gather(prefix_outer, BOTH, axis=1, tiled=True),
    )
    factor_one = gain_one.astype(jnp.float32)
    factor_two = gain_two.astype(jnp.float32)
    factor_three = gain_three.astype(jnp.float32)
    length = inputs.shape[0]
    width = inputs.shape[1]
    places = jnp.arange(length)
    causal = places[:, None] >= places[None, :]
    local_mask = (segments[:, None] == segments[None, :]) & causal
    prefix_mask = jnp.ones((length, PREFIX), jnp.bool_)
    cross_mask = segments[:, None] == memory_segments[None, :]
    tangent = jnp.tanh(matmul(embed_full, inner_full))
    tangent_low = tangent.astype(jnp.bfloat16)
    prefix_rows = matmul(tangent_low, outer_full).astype(jnp.bfloat16)
    prefix_keys = prefix_rows[:, :width]
    prefix_values = prefix_rows[:, width:]
    queries = matmul(inputs, query_one).astype(jnp.bfloat16)
    key_rows = matmul(inputs, key_one).astype(jnp.bfloat16)
    value_rows = matmul(inputs, value_one).astype(jnp.bfloat16)
    self_parts = ((prefix_keys, prefix_values, prefix_mask), (key_rows, value_rows, local_mask))
    attended, self_logsum = attend_forward(queries, self_parts)
    attended_low = attended.astype(jnp.bfloat16)
    first, normed_one, inverse_one = norm_forward(
        inputs.astype(jnp.float32) + matmul(attended_low, output_one),
        factor_one,
        shift_one.astype(jnp.float32),
    )
    first_low = first.astype(jnp.bfloat16)
    cross_queries = matmul(first_low, query_two).astype(jnp.bfloat16)
    cross_keys = matmul(memory, key_two).astype(jnp.bfloat16)
    cross_values = matmul(memory, value_two).astype(jnp.bfloat16)
    cross_parts = ((cross_keys, cross_values, cross_mask),)
    crossed, cross_logsum = attend_forward(cross_queries, cross_parts)
    crossed_low = crossed.astype(jnp.bfloat16)
    second, normed_two, inverse_two = norm_forward(
        first + matmul(crossed_low, output_two), factor_two, shift_two.astype(jnp.float32)
    )
    second_low = second.astype(jnp.bfloat16)
    feed_rows = lax.all_gather(second_low, WIDE, axis=0, tiled=True)
    hidden_pre = matmul(feed_rows, feed_in)
    hidden_low = jax.nn.gelu(hidden_pre, approximate=False).astype(jnp.bfloat16)
    feed_sum = lax.psum_scatter(
        matmul(hidden_low, feed_out), WIDE, scatter_dimension=0, tiled=True
    )
    adapt_rows = lax.all_gather(second_low, NARROW, axis=0, tiled=True)
    bottle_pre = matmul(adapt_rows, adapter_down)
    bottle_low = jax.nn.gelu(bottle_pre, approximate=False).astype(jnp.bfloat16)
    adapt_sum = lax.psum_scatter(
        matmul(bottle_low, adapter_up).astype(jnp.bfloat16),
        NARROW,
        scatter_dimension=0,
        tiled=True,
    ).astype(jnp.float32)
    branch = feed_sum + ADAPT_SCALE * adapt_sum
    result, normed_three, inverse_three = norm_forward(
        second + branch, factor_three, shift_three.astype(jnp.float32)
    )
    grad_branch, gain_three_grad, shift_three_grad = norm_backward(
        cotangent.astype(jnp.float32), normed_three, inverse_three, factor_three
    )
    branch_low = grad_branch.astype(jnp.bfloat16)
    branch_rows = lax.all_gather(branch_low, WIDE, axis=0, tiled=True)
    grad_hidden = right_product(branch_rows, feed_out)
    grad_pre = gelu_back(hidden_pre, grad_hidden).astype(jnp.bfloat16)
    grad_out_part = left_product(hidden_low, branch_rows)
    grad_in_part = left_product(feed_rows, grad_pre)
    grad_feed = lax.psum_scatter(
        right_product(grad_pre, feed_in), WIDE, scatter_dimension=0, tiled=True
    )
    feed_in_total, feed_out_total = (
        lax.psum_scatter(
            grad_in_part.astype(jnp.bfloat16), NARROW, scatter_dimension=0, tiled=True
        ).astype(jnp.float32),
        lax.psum_scatter(
            grad_out_part.astype(jnp.bfloat16), NARROW, scatter_dimension=1, tiled=True
        ).astype(jnp.float32),
    )
    branch_narrow = lax.all_gather(branch_low, NARROW, axis=0, tiled=True)
    grad_bottle = ADAPT_SCALE * right_product(branch_narrow, adapter_up)
    grad_bottle_pre = gelu_back(bottle_pre, grad_bottle).astype(jnp.bfloat16)
    grad_up_part = ADAPT_SCALE * left_product(bottle_low, branch_narrow)
    grad_down_part = left_product(adapt_rows, grad_bottle_pre)
    grad_adapt = lax.psum_scatter(
        right_product(grad_bottle_pre, adapter_down).astype(jnp.bfloat16),
        NARROW,
        scatter_dimension=0,
        tiled=True,
    ).astype(jnp.float32)
    down_total, up_total = (
        lax.psum_scatter(grad_down_part, WIDE, scatter_dimension=0, tiled=True),
        lax.psum_scatter(grad_up_part, WIDE, scatter_dimension=1, tiled=True),
    )
    grad_second = grad_branch + grad_feed + grad_adapt
    grad_mid, gain_two_grad, shift_two_grad = norm_backward(
        grad_second, normed_two, inverse_two, factor_two
    )
    mid_low = grad_mid.astype(jnp.bfloat16)
    output_two_grad = left_product(crossed_low, mid_low)
    crossed_grad = right_product(mid_low, output_two).astype(jnp.bfloat16)
    cross_query_grad, cross_results = attend_backward(
        cross_queries, cross_parts, cross_logsum, crossed_grad
    )
    cross_query_low = cross_query_grad.astype(jnp.bfloat16)
    cross_key_low = cross_results[0][0].astype(jnp.bfloat16)
    cross_value_low = cross_results[0][1].astype(jnp.bfloat16)
    query_two_grad = left_product(first_low, cross_query_low)
    key_two_grad = left_product(memory, cross_key_low)
    value_two_grad = left_product(memory, cross_value_low)
    memory_grad = (
        right_product(cross_key_low, key_two) + right_product(cross_value_low, value_two)
    ).astype(jnp.bfloat16)
    grad_first = grad_mid + right_product(cross_query_low, query_two)
    grad_start, gain_one_grad, shift_one_grad = norm_backward(
        grad_first, normed_one, inverse_one, factor_one
    )
    start_low = grad_start.astype(jnp.bfloat16)
    output_one_grad = left_product(attended_low, start_low)
    attended_grad = right_product(start_low, output_one).astype(jnp.bfloat16)
    self_query_grad, self_results = attend_backward(queries, self_parts, self_logsum, attended_grad)
    self_query_low = self_query_grad.astype(jnp.bfloat16)
    self_key_low = self_results[1][0].astype(jnp.bfloat16)
    self_value_low = self_results[1][1].astype(jnp.bfloat16)
    query_one_grad = left_product(inputs, self_query_low)
    key_one_grad = left_product(inputs, self_key_low)
    value_one_grad = left_product(inputs, self_value_low)
    inputs_grad = (
        grad_start
        + right_product(self_query_low, query_one)
        + right_product(self_key_low, key_one)
        + right_product(self_value_low, value_one)
    ).astype(jnp.bfloat16)
    prefix_grad = jnp.concatenate([self_results[0][0], self_results[0][1]], axis=1)
    outer_grad = exact_left(tangent_low.astype(jnp.float32), prefix_grad)
    tangent_grad = exact_right(prefix_grad, outer_full.astype(jnp.float32)) * (
        1.0 - tangent * tangent
    )
    inner_grad = exact_left(embed_full.astype(jnp.float32), tangent_grad)
    embed_grad = exact_right(tangent_grad, inner_full.astype(jnp.float32))
    (
        query_one_sum,
        key_one_sum,
        value_one_sum,
        output_one_sum,
        query_two_sum,
        key_two_sum,
        value_two_sum,
        output_two_sum,
        gain_one_sum,
        shift_one_sum,
        gain_two_sum,
        shift_two_sum,
        gain_three_sum,
        shift_three_sum,
        embed_sum,
        inner_sum,
        outer_sum,
    ) = (
        lax.psum_scatter(query_one_grad, BOTH, scatter_dimension=0, tiled=True),
        lax.psum_scatter(key_one_grad, BOTH, scatter_dimension=0, tiled=True),
        lax.psum_scatter(value_one_grad, BOTH, scatter_dimension=0, tiled=True),
        lax.psum_scatter(output_one_grad, BOTH, scatter_dimension=0, tiled=True),
        lax.psum_scatter(query_two_grad, BOTH, scatter_dimension=0, tiled=True),
        lax.psum_scatter(key_two_grad, BOTH, scatter_dimension=0, tiled=True),
        lax.psum_scatter(value_two_grad, BOTH, scatter_dimension=0, tiled=True),
        lax.psum_scatter(output_two_grad, BOTH, scatter_dimension=0, tiled=True),
        lax.psum_scatter(gain_one_grad, BOTH, scatter_dimension=0, tiled=True),
        lax.psum_scatter(shift_one_grad, BOTH, scatter_dimension=0, tiled=True),
        lax.psum_scatter(gain_two_grad, BOTH, scatter_dimension=0, tiled=True),
        lax.psum_scatter(shift_two_grad, BOTH, scatter_dimension=0, tiled=True),
        lax.psum_scatter(gain_three_grad, BOTH, scatter_dimension=0, tiled=True),
        lax.psum_scatter(shift_three_grad, BOTH, scatter_dimension=0, tiled=True),
        lax.psum_scatter(embed_grad, BOTH, scatter_dimension=1, tiled=True),
        lax.psum_scatter(inner_grad, BOTH, scatter_dimension=0, tiled=True),
        lax.psum_scatter(outer_grad, BOTH, scatter_dimension=1, tiled=True),
    )
    return (
        result.astype(jnp.bfloat16),
        inputs_grad,
        memory_grad,
        query_one_sum,
        key_one_sum,
        value_one_sum,
        output_one_sum,
        query_two_sum,
        key_two_sum,
        value_two_sum,
        output_two_sum,
        gain_one_sum,
        shift_one_sum,
        gain_two_sum,
        shift_two_sum,
        gain_three_sum,
        shift_three_sum,
        feed_in_total,
        feed_out_total,
        down_total,
        up_total,
        embed_sum,
        inner_sum,
        outer_sum,
    )


def place():
    w = lax.axis_index(WIDE); n = lax.axis_index(NARROW)
    return w // 2, w % 2, n // 2, n % 2

def device(a, b, x, c):
    return (a * 2 + b, x * 2 + c)

def greet(peers):
    barrier = pltpu.get_barrier_semaphore()
    for p in peers:
        pl.semaphore_signal(barrier, inc=1, device_id=p, device_id_type=MESH)
    pl.semaphore_wait(barrier, len(peers))

def remote(src, dst, send, recv, dev):
    return pltpu.make_async_remote_copy(src_ref=src, dst_ref=dst, send_sem=send, recv_sem=recv, device_id=dev, device_id_type=MESH)


def dot_left(l, r):
    return lax.dot_general(l, r, (((0,), (0,)), ((), ())), preferred_element_type=f32)

class Copies:
    def __init__(self, send, recv):
        self.send, self.recv, self.count, self.all = send, recv, 0, []
    def __call__(self, src, dst, dev):
        cp = remote(src, dst, self.send.at[self.count], self.recv.at[self.count], dev)
        self.count += 1
        cp.start(); self.all.append(cp)
        return cp
    def local(self, src, dst):
        cp = pltpu.make_async_copy(src, dst, self.send.at[self.count])
        self.count += 1
        cp.start()
        return cp
    def sent(self, some):
        for cp in some:
            cp.wait_send()
            self.all = [o for o in self.all if o is not cp]
    def close(self):
        for cp in self.all: cp.wait_send()


EPSILON = 1e-05
ADAPT_SCALE = 4.0

def dot(l, r):
    return jnp.dot(l, r, preferred_element_type=f32)

def dot_right(l, r):
    return lax.dot_general(l, r, (((1,), (1,)), ((), ())), preferred_element_type=f32)

def gelu_both(v):
    phi = 0.5 + 0.5 * lax.erf(v * 0.7071067811865476)
    return v * phi, phi + v * (0.3989422804014327 * jnp.exp(-0.5 * v * v))

def norm(v):
    center = v - jnp.mean(v, axis=-1, keepdims=True)
    inverse = lax.rsqrt(jnp.mean(center * center, axis=-1, keepdims=True) + EPSILON)
    return center * inverse, inverse

def norm_back(e, n, inverse, factor):
    s = e * factor
    return inverse * (s - jnp.mean(s, axis=-1, keepdims=True) - n * jnp.mean(s * n, axis=-1, keepdims=True))

def feed_part(A, second, vecs, cot, fin_own, fout_own, down_ref, up_ref, inputs, memory, att, flow, crossed, partner, outs, scratch):
    result, gsec, fi_out, fo_out, ay, blow, ngrad, xp0, xatt, xin, xmem = outs
    fin, fout, fi, fo, down, up, rows, brow, hid, slope, gpre, part, q1, q2, q3, bslope, acc, ssem, rsem = scratch
    a, b, x, c = place()
    o = 1 - c
    yp = device(a, 1 - b, x, c)
    zp = device((a + A // 2) % A, b, x, c)
    core, xp, dp = device(a, b, x, o), device(a, b, 1 - x, c), device(a, b, 1 - x, o)
    cp = Copies(ssem, rsem)
    half = fin_own.shape[1]
    loads = [cp.local(fin_own, fin.at[:, pl.ds(0, half)]), cp.local(fout_own, fout.at[pl.ds(0, half)])]
    T, D = second.shape
    NC, R = 2, T // 2
    C = R // NC
    HID = fin.shape[1]; TW = 256
    NT = D // TW
    def span(h): return pl.ds(h * R, R)

    def spread(buf, h):
        zs, ys, passed = [], [], []
        for u in range(NC):
            s = pl.ds(u * C, C)
            zs.append(cp(buf.at[h, 0, s], buf.at[h, 2, s], zp))
        for u in range(NC):
            s = pl.ds(u * C, C)
            ys.append(cp(buf.at[h, 0, s], buf.at[h, 1, s], yp))
        def beside():
            for e in ys: e.wait_recv()
        def forward():
            for u in range(NC):
                s = pl.ds(u * C, C)
                zs[u].wait_recv()
                passed.append(cp(buf.at[h, 2, s], buf.at[h, 3, s], yp))
        def across():
            for e in passed: e.wait_recv()
        return beside, forward, across

    sums, onward = {}, {}
    def send_part(level, h, j, t):
        sums[level, h, j, t] = cp(part.at[h, j, t], (q3 if j == 3 else q1).at[level, h, t], yp)
    def collect(level, h, t):
        sums[level, h, 3, t].wait_recv()
        part[h, 2, t] = part[h, 2, t] + q3[level, h, t]
        onward[level, h, t] = cp(part.at[h, 2, t], q2.at[level, h, t], zp)
    def gather_up(level, h):
        for t in range(NT):
            cols = pl.ds(t * TW, TW)
            sums[level, h, 1, t].wait_recv(); onward[level, h, t].wait_recv()
            acc[h, :, cols] = acc[h, :, cols] + q1[level, h, t].astype(f32) + q2[level, h, t].astype(f32)
        cp.sent([onward[level, h, t] for t in range(NT)] + [sums[level, h, j, t] for j in (1, 3) for t in range(NT)])

    for h in range(2): rows[h, 0] = second[span(h), :].astype(bf16)
    moves = {(0, h): spread(rows, h) for h in range(2)}
    AD = down_ref.shape[1]
    n = x * 2 + c
    nd = pl.ds(pl.multiple_of(n * AD, AD), AD)
    md = pl.ds(pl.multiple_of((2 - 2 * x + c) * AD, AD), AD)
    kept, late = [cp.local(down_ref, down.at[:, nd]), cp.local(up_ref, up.at[nd])], []
    over = [cp(down_ref, down.at[:, nd], xp), cp(up_ref, up.at[nd], xp)]
    near = [cp(down_ref, down.at[:, nd], core), cp(up_ref, up.at[nd], core)]
    def rowsn(ref, m, place): return ref.at[pl.ds(pl.multiple_of(place * m, m), m)]
    def fan(srcs, dst, only=False):
        k = cp.count
        cp.count += 4
        def start(me):
            own, other = srcs[me], srcs[1 - me]
            if own is not None:
                pltpu.make_async_copy(own, rowsn(dst, T, n), ssem.at[k]).start()
                remote(own, rowsn(dst, T, n), ssem.at[k + 1], rsem.at[k + 1], xp).start()
            if other is not None:
                remote(other, rowsn(dst, T, n), ssem.at[k + 2], rsem.at[k + 2], core).start()
                remote(other, rowsn(dst, T, n), ssem.at[k + 3], rsem.at[k + 3], dp).start()
        def finish(me):
            own, other = srcs[me], srcs[1 - me]
            src = own if own is not None else other
            ways = [remote(src, rowsn(dst, T, n), ssem.at[k + i], rsem.at[k + i], d) for i, d in ((1, xp), (2, core), (3, dp))]
            if own is not None:
                pltpu.make_async_copy(own, rowsn(dst, T, n), ssem.at[k]).wait()
                ways[0].wait_send()
                for e in ways: e.wait_recv()
            if other is not None:
                ways[1].wait_send(); ways[2].wait_send()
        pl.when(c == 0)(functools.partial(start, 0))
        pl.when(c == 1)(functools.partial(start, 1))
        def done():
            pl.when(c == 0)(functools.partial(finish, 0))
            pl.when(c == 1)(functools.partial(finish, 1))
        return done
    fans = [fan((crossed, flow), xp0), fan((att, None), xatt)]
    M = memory.shape[0]
    share = []
    for src, dst, m in ((inputs, xin, T), (memory, xmem, M)):
        kept.append(cp.local(src, rowsn(dst, m, n)))
        near.append(cp(src, rowsn(dst, m, n), core))
        share.append((cp(src, rowsn(dst, m, n), xp), rowsn(dst, m, 2 - 2 * x + c)))
    def adapter_weights():
        kept[0].wait(); kept[1].wait()
        for e, ref in zip(over, (down.at[:, md], up.at[md])):
            e.wait_recv()
            late.append(cp(ref, ref, core))
        ready.extend(late[:2])
    ready = []
    def adapter_ready():
        near[0].wait_recv(); near[1].wait_recv()
        for e in ready: e.wait_recv()
    def share_on():
        for e, ref in share:
            e.wait_recv()
            late.append(cp(ref, ref, core))
    def adapter_forward():
        own = rows[:, 0].reshape(T, D)
        for t in range(2):
            cols = pl.ds(t * 256, 256)
            g, s = gelu_both(dot(own, down[:, cols]))
            ay[1, :, cols] = (ADAPT_SCALE * g.astype(bf16).astype(f32)).astype(bf16)
            bslope[:, cols] = s
        def tile(t, _):
            cols = pl.ds(pl.multiple_of(t * 256, 256), 256)
            acc[:, :, cols] = acc[:, :, cols] + dot(ay[1], up[:, cols]).reshape(2, R, 256)
            return 0
        lax.fori_loop(0, D // 256, tile, 0)
    def adapter_back():
        def tile(t, _):
            cols = pl.ds(pl.multiple_of(t * 256, 256), 256)
            gbot = bslope[:, cols] * (ADAPT_SCALE * dot_right(brow[:, 0].reshape(T, D), up[cols, :]))
            ay[0, :, cols] = gbot.astype(bf16)
            return 0
        lax.fori_loop(0, down.shape[1] // 256, tile, 0)
        def tile2(t, _):
            cols = pl.ds(pl.multiple_of(t * 256, 256), 256)
            acc[:, :, cols] = acc[:, :, cols] + dot_right(ay[0], down[cols, :]).reshape(2, R, 256)
            return 0
        lax.fori_loop(0, D // 256, tile2, 0)
    def both(buf, h, g): return buf[h, 2 * g:2 * g + 2].reshape(2 * R, buf.shape[3])
    def put_out(level, h, g, t, p):
        cols = pl.ds(t * TW, TW)
        if g == 0:
            acc[h, :, cols] = p[:R] if level == 0 else acc[h, :, cols] + p[:R]
            part[h, 1, t] = p[R:].astype(bf16)
            send_part(level, h, 1, t)
        else:
            part[h, 3, t] = p[R:].astype(bf16)
            send_part(level, h, 3, t)
            part[h, 2, t] = p[:R].astype(bf16)
    def enter(h, g):
        moves[0, h][2 * g]()
        xv = both(rows, h, g)
        def tile(t, _):
            cols = pl.ds(pl.multiple_of(t * TW, TW), TW)
            e, s = gelu_both(dot(xv, fin[:, cols]))
            hid[h, 2 * g:2 * g + 2, :, cols] = e.astype(bf16).reshape(2, R, TW)
            slope[h, 2 * g:2 * g + 2, :, cols] = s.reshape(2, R, TW)
            return 0
        lax.fori_loop(0, HID // TW, tile, 0)
    def leave(h, g):
        moves[1, h][2 * g]()
        xv = both(brow, h, g)
        def tile(t, _):
            cols = pl.ds(pl.multiple_of(t * TW, TW), TW)
            gh = dot_right(xv, fout[cols, :])
            gpre[h, 2 * g:2 * g + 2, :, cols] = (slope[h, 2 * g:2 * g + 2, :, cols].reshape(2 * R, TW) * gh).astype(bf16).reshape(2, R, TW)
            return 0
        lax.fori_loop(0, HID // TW, tile, 0)
    def out_tile(level, h, g, t):
        cols = pl.ds(t * TW, TW)
        put_out(level, h, g, t, dot_right(both(gpre, h, g), fin[cols, :]) if level else dot(both(hid, h, g), fout[:, cols]))
    fac, off = vecs[4:5, :], vecs[5:6, :]
    def turn(h):
        n3, inv3 = norm(second[span(h), :] + acc[h])
        result[span(h), :] = (n3 * fac + off).astype(bf16)
        e = cot[span(h), :].astype(f32)
        gb = norm_back(e, n3, inv3, fac)
        gbl = gb.astype(bf16)
        brow[h, 0] = gbl
        moves[1, h] = spread(brow, h)
        blow[span(h), :] = gbl
        acc[h] = gb
        gg, gs = jnp.sum(e * n3, axis=0, keepdims=True), jnp.sum(e, axis=0, keepdims=True)
        ngrad[0:1, :] = gg if h == 0 else ngrad[0:1, :] + gg
        ngrad[1:2, :] = gs if h == 0 else ngrad[1:2, :] + gs
    def wtile(t):
        cols = pl.ds(t * TW, TW)
        fi[:, cols] = dot_left(rows[...].reshape(4 * T, D), gpre[:, :, :, cols].reshape(4 * T, TW)).astype(bf16)
        fo[:, cols] = dot_left(hid[...].reshape(4 * T, HID), brow[:, :, :, cols].reshape(4 * T, TW)).astype(bf16)
    for e in loads: e.wait()
    partner()
    enter(1, 0)
    moves[0, 0][1]()
    enter(0, 0)
    moves[0, 1][1]()
    enter(0, 1)
    out_tile(0, 0, 1, 0)
    out_tile(0, 0, 1, 1)
    out_tile(0, 0, 0, 0)
    out_tile(0, 0, 1, 2)
    out_tile(0, 0, 0, 1)
    out_tile(0, 1, 0, 0)
    out_tile(0, 0, 1, 3)
    out_tile(0, 0, 0, 2)
    adapter_weights()
    collect(0, 0, 0)
    collect(0, 0, 1)
    enter(1, 1)
    collect(0, 0, 2)
    adapter_ready()
    out_tile(0, 1, 1, 0)
    out_tile(0, 1, 1, 1)
    out_tile(0, 1, 1, 2)
    collect(0, 0, 3)
    out_tile(0, 1, 0, 1)
    out_tile(0, 0, 0, 3)
    collect(0, 1, 0)
    out_tile(0, 1, 1, 3)
    out_tile(0, 1, 0, 2)
    out_tile(0, 1, 0, 3)
    collect(0, 1, 1)
    adapter_forward()
    collect(0, 1, 2)
    gather_up(0, 0)
    collect(0, 1, 3)
    turn(0)
    gather_up(0, 1)
    turn(1)
    moves[1, 0][1]()
    leave(0, 0)
    leave(1, 0)
    out_tile(1, 0, 0, 0)
    out_tile(1, 0, 0, 1)
    moves[1, 1][1]()
    leave(0, 1)
    out_tile(1, 0, 1, 0)
    share_on()
    out_tile(1, 0, 1, 1)
    out_tile(1, 0, 1, 2)
    out_tile(1, 0, 1, 3)
    out_tile(1, 1, 0, 0)
    out_tile(1, 1, 0, 1)
    out_tile(1, 1, 0, 2)
    collect(1, 0, 0)
    leave(1, 1)
    collect(1, 0, 2)
    out_tile(1, 1, 1, 0)
    collect(1, 0, 1)
    out_tile(1, 1, 1, 1)
    collect(1, 0, 3)
    out_tile(1, 1, 1, 2)
    out_tile(1, 1, 1, 3)
    wtile(0)
    collect(1, 1, 0)
    out_tile(1, 0, 0, 2)
    out_tile(1, 0, 0, 3)
    collect(1, 1, 1)
    collect(1, 1, 2)
    wtile(1)
    out_tile(1, 1, 0, 3)
    collect(1, 1, 3)
    adapter_back()
    gather_up(1, 0)
    gsec[span(0), :] = acc[0]
    wtile(2)
    wtile(3)
    kept += [cp.local(fi, fi_out), cp.local(fo, fo_out)]
    gather_up(1, 1)
    gsec[span(1), :] = acc[1]
    for e in kept[2:]: e.wait()
    for e in near[2:]: e.wait_recv()
    for e in late:
        if not any(e is o for o in ready): e.wait_recv()
    for e in fans: e()
    cp.close()


NEGATIVE = -1000000000.0
PADDED = 32
PREFIX = 30


def lane_half(rows):
    return lax.broadcasted_iota(jnp.int32, (rows, 128), 1) < 64

def split_heads(v):
    low = lane_half(v.shape[0])
    zero = jnp.zeros_like(v)
    return jnp.where(low, v, zero), jnp.where(low, zero, v)


def whole(ref):
    return lambda cols: ref[:, cols]


def norm_back_into(e, n, i, gain, out, ngrad, at):
    ee = e[...]
    nn = n[...]
    out[...] = norm_back(ee, nn, i[...], gain)
    ngrad[at:at + 1, :] = jnp.sum(ee * nn, axis=0, keepdims=True)
    ngrad[at + 1:at + 2, :] = jnp.sum(ee, axis=0, keepdims=True)


def repeat(n):
    row = lax.broadcasted_iota(jnp.int32, (n, 128), 0)
    col = lax.broadcasted_iota(jnp.int32, (n, 128), 1)
    return jnp.where(row == lax.rem(col, n), 1.0, 0.0).astype(bf16)

def columns(t, tile=256):
    return pl.ds(pl.multiple_of(t * tile, tile), tile)

def loop(start, stop, step):
    lax.fori_loop(start, stop, lambda t, z: (step(t), z)[1], 0)

def front_part(A, r, inputs, memory, seg_row, mem_row, embed, inner, outer, norms, ws, fin, fout, fin2, fout2, outs, scratch):
    (wout, tangent, prows_o, vecs_o, q_o, k_o, v_o, probs_o, att_o, first_o, n1_o, i1_o, cq_o, ck_o, cv_o, cprobs_o, crossed_o, slow_o, n2_o, i2_o) = outs
    (g, q, k, v, probs, att, first, flow, n1, i1, cq, ck, cv, cprobs, crossed, second, slow, n2, i2, pen, cpen,
     buf, got, zbuf, r0, r1, prows, nout, vecs, tan, ssem, rsem) = scratch
    a, b, x, c = place()
    core, xp, yp = device(a, b, x, 1 - c), device(a, b, 1 - x, c), device(a, 1 - b, x, c)
    zp = [device((a + j) % A, b, x, c) for j in range(A)]
    za = a + 1 - 2 * (a % 2)
    zq = device(za, b, x, c)
    greet([core, xp, yp, device(a, b, 1 - x, 1 - c)] + zp[1:])
    cp = Copies(ssem, rsem)
    T, D = inputs.shape
    pairs = 4
    small = {}
    def pre0():
        zbuf[a] = jnp.zeros(zbuf.shape[1:], f32)
        zbuf[a, :PREFIX, :] = dot(embed[...], inner[...])
        small["s"] = [cp(zbuf.at[a], zbuf.at[a], zp[j]) for j in range(1, A)]
    pre0()
    def row(a_, b_, x_):
        return pl.multiple_of(((a_ * 2 + b_) * 2 + x_) * 2 * r, 2 * r)
    at = pl.ds(pl.multiple_of(row(a, b, x) + c * r, r), r)
    cut = (pl.ds(0, D // 2), pl.ds(D // 2, D // 2))
    def block(i, h, a_, b_, x_):
        return g.at[2 * i + c, pl.ds(row(a_, b_, x_), 2 * r), cut[h]]
    kept = []
    own, cross = [], []
    base = cp.count
    for i in range(pairs):
        s1, s2, rr = ssem.at[cp.count], ssem.at[cp.count + 1], rsem.at[cp.count]
        cp.count += 2
        def start(keep, give):
            pltpu.make_async_copy(ws[2 * i + keep], g.at[2 * i + keep, at], s2).start()
            remote(ws[2 * i + give], g.at[2 * i + give, at], s1, rr, core).start()
        pl.when(c == 0)(functools.partial(start, 0, 1))
        pl.when(c == 1)(functools.partial(start, 1, 0))
        own.append(pltpu.make_async_copy(ws[2 * i], g.at[2 * i, at], s2))
        cross.append(remote(ws[2 * i], g.at[2 * i, at], s1, rr, core))
    G = norms.shape[0]
    me = ((a * 2 + b) * 2 + x) * 2 + c
    chip = (a * 2 + b) * 2 + x
    def nrows(start, count): return nout.at[pl.ds(pl.multiple_of(start * G, G), count * G)]
    def lanes(start, count): return prows.at[:, pl.ds(pl.multiple_of(start * 128, 128), count * 128)]
    nout[pl.ds(pl.multiple_of(me * G, G), G), :] = dot(norms[...], repeat(norms.shape[1])).astype(bf16)
    peers = (core, xp, yp)
    def settle():
        for e in small["s"]: e.wait_recv()
    def pre1():
        settle()
        t = zbuf[0]
        for n in range(1, A): t = t + zbuf[n]
        buf[0] = t
        small["s"] = [cp(buf.at[0], got.at[0], core)]
    def pre2(n):
        def go():
            settle()
            buf[n] = buf[n - 1] + got[n - 1]
            small["s"] = [cp(buf.at[n], got.at[n], peers[n])]
        return go
    def pre4():
        settle()
        t = jnp.tanh(buf[2] + got[2])
        tan[...] = t
        r0[...] = dot(dot_right(t.astype(bf16), outer[...]).astype(bf16), repeat(outer.shape[0])).astype(bf16)
        small["s"] = [cp(r0, r1, core), cp(nrows(me, 1), nrows(me, 1), core)]
        kept.append(cp.local(tan, tangent))
    def pre5():
        settle()
        lane = lax.broadcasted_iota(jnp.int32, (PADDED, 128), 1)
        prows[:, pl.ds(pl.multiple_of(chip * 128, 128), 128)] = jnp.where((lane // 64) == c, r0[...].astype(f32), r1[...].astype(f32)).astype(bf16)
        small["s"] = [cp(lanes(chip, 1), lanes(chip, 1), xp), cp(nrows(me - c, 2), nrows(me - c, 2), xp)]
    def pre6():
        settle()
        small["s"] = [cp(lanes(chip - x, 2), lanes(chip - x, 2), yp), cp(nrows(me - c - 2 * x, 4), nrows(me - c - 2 * x, 4), yp)]
    def pre7():
        settle()
        small["s"] = [cp(lanes(a * 4, 4), lanes(a * 4, 4), zp[j]) for j in range(1, A)] + [cp(nrows(a * 8, 8), nrows(a * 8, 8), zp[j]) for j in range(1, A)]
    def pre8():
        settle()
        lane = lax.broadcasted_iota(jnp.int32, (G, 128), 1) // 32
        for w in range(2 * A):
            s = nout[pl.ds(w * 4 * G, G), :].astype(f32)
            for n in range(1, 4):
                s = jnp.where(lane == n, nout[pl.ds((w * 4 + n) * G, G), :].astype(f32), s)
            vecs[:, pl.ds(w * 128, 128)] = s[:8]
        kept.append(cp.local(vecs, vecs_o))
        kept.append(cp.local(prows, prows_o))
    H = fin.shape[1]
    feeds, passed = {}, []
    def feed_send(i):
        n = D // 8
        ri = pl.ds(pl.multiple_of(c * (D // 2) + i * n, n), n)
        m = H // 8
        ro = pl.ds(pl.multiple_of(c * (H // 2) + i * m, m), m)
        ro2 = pl.ds(pl.multiple_of(H + c * (H // 2) + i * m, m), m)
        feeds[i] = [(cp(fin.at[ri], fin2.at[ri, pl.ds(H, H)], zq), fin2.at[ri, pl.ds(H, H)]),
                    (cp(fout.at[ro], fout2.at[ro2], zq), fout2.at[ro2])]
    def feed_pass(i):
        for e, ref in feeds[i]:
            e.wait_recv()
            passed.append(cp(ref, ref, core))
    zc, mc, lc, dc = {}, {}, {}, {}
    two, three = (yp, xp), (xp, yp)
    begun = set()
    def fs(i, h):
        if i not in begun:
            begun.add(i)
            own[i].wait(); cross[i].wait()
        mc[i, h, 0] = cp(block(i, h, a, b, x), block(i, h, a, b, x), two[h])
        lc[i, h, 0, 0] = cp(block(i, h, a, b, x), block(i, h, a, b, x), three[h])
    def fz(i, h):
        for j in range(1, A):
            zc[i, h, j] = cp(block(i, h, a, b, x), block(i, h, a, b, x), zp[j])
    def mid(i, h, j):
        aj = (a + A - j) % A
        zc[i, h, j].wait_recv()
        mc[i, h, j] = cp(block(i, h, aj, b, x), block(i, h, aj, b, x), two[h])
        lc[i, h, j, 0] = cp(block(i, h, aj, b, x), block(i, h, aj, b, x), three[h])
    def third(i, h, j):
        aj = (a + A - j) % A
        w = (aj, 1 - b, x) if h == 0 else (aj, b, 1 - x)
        mc[i, h, j].wait_recv()
        lc[i, h, j, 1] = cp(block(i, h, *w), block(i, h, *w), three[h])
    per = D // A
    def finish(i, j):
        aj = (a + A - j) % A
        for h in range(2):
            lc[i, h, j, 0].wait_recv(); lc[i, h, j, 1].wait_recv()
        ref = g.at[2 * i + c, pl.ds(pl.multiple_of(aj * per, per), per)]
        dc[i, j] = cp(ref, ref, core)
    def arrive(i):
        for j in range(A): dc[i, j].wait_recv()
        kept.append(cp.local(g.at[2 * i], wout.at[2 * i]))
        kept.append(cp.local(g.at[2 * i + 1], wout.at[2 * i + 1]))
    def halves(src, w, out):
        def part(n):
            def go():
                xv = src[...]
                def step(t):
                    out[:, columns(t)] = dot(xv, g[w, :, columns(t)]).astype(bf16)
                loop(2 * n, 2 * n + 2, step)
            return go
        return [part(0), part(1)]
    def masks():
        row = lax.broadcasted_iota(jnp.int32, (T, T), 0)
        col = lax.broadcasted_iota(jnp.int32, (T, T), 1)
        across = jnp.broadcast_to(seg_row[...].astype(f32), (T, T))
        down = across.T
        pen[:, :T] = jnp.where((row >= col) & (down == across), 0.0, NEGATIVE)
        lane = lax.broadcasted_iota(jnp.int32, (T, PADDED), 1)
        pen[:, T:] = jnp.where(lane < PREFIX, 0.0, NEGATIVE)
        for n in range(memory.shape[0] // T):
            span = slice(n * T, (n + 1) * T)
            cpen[:, span] = jnp.where(down == mem_row[:, span].astype(f32), 0.0, NEGATIVE)
    def softmax(qv, kk, penalty):
        score = jnp.where(penalty[...] < -1.0, NEGATIVE, dot_right(qv, kk) * 0.125)
        e = jnp.exp(score - jnp.max(score, axis=-1, keepdims=True))
        return (e * (1.0 / jnp.sum(e, axis=-1, keepdims=True))).astype(bf16)
    def own_attend(n):
        def go():
            def step(p):
                cols = columns(p, 128)
                kk = jnp.concatenate([k[:, cols], prows[:, cols]], axis=0)
                vv = jnp.concatenate([v[:, cols], prows[:, pl.ds(pl.multiple_of(D + p * 128, 128), 128)]], axis=0)
                qs, vs = split_heads(q[:, cols]), split_heads(vv)
                total = None
                for s in range(2):
                    prob = softmax(qs[s], kk, pen)
                    probs[2 * p + s] = prob
                    m = dot(prob, vs[s])
                    total = m if total is None else total + m
                att[:, cols] = total.astype(bf16)
            loop(2 * n, 2 * n + 2, step)
        return go
    def cross_scores(n):
        def go():
            def step(p):
                cols = columns(p, 128)
                qs = split_heads(cq[:, cols])
                for s in range(2):
                    cprobs[2 * p + s] = softmax(qs[s], ck[:, cols], cpen)
            loop(2 * n, 2 * n + 2, step)
        return go
    def cross_mix(n):
        def go():
            def step(p):
                cols = columns(p, 128)
                vs = split_heads(cv[:, cols])
                crossed[:, cols] = (dot(cprobs[2 * p], vs[0]) + dot(cprobs[2 * p + 1], vs[1])).astype(bf16)
            loop(4 * n, 4 * n + 4, step)
        return go
    def normed(base, low, w, at, out, nn, ii, olow):
        def part(n):
            def go():
                lv = low[...]
                def step(t):
                    out[:, columns(t)] = base[:, columns(t)].astype(f32) + dot(lv, g[w, :, columns(t)])
                loop(2 * n, 2 * n + 2, step)
            return go
        def last():
            m, inv = norm(out[...])
            nn[...] = m
            ii[...] = inv
            s = m * vecs[at:at + 1, :] + vecs[at + 1:at + 2, :]
            out[...] = s
            olow[...] = s.astype(bf16)
        return [part(0), part(1), last]
    make_q, make_k, make_v = halves(inputs, 0, q), halves(inputs, 1, k), halves(inputs, 2, v)
    make_ck, make_cq, make_cv = halves(memory, 4, ck), halves(flow, 5, cq), halves(memory, 6, cv)
    norm_one, norm_two = normed(inputs, att, 3, 0, first, n1, i1, flow), normed(first, crossed, 7, 2, second, n2, i2, slow)
    fs(0, 0)
    fs(0, 1)
    fz(0, 0)
    fs(1, 1)
    fs(1, 0)
    fz(0, 1)
    fs(3, 0)
    fs(2, 0)
    fz(1, 0)
    fs(2, 1)
    third(0, 1, 0)
    third(1, 1, 0)
    pre1()
    fs(3, 1)
    pre2(1)()
    mid(0, 0, 3)
    mid(0, 1, 1)
    third(0, 0, 0)
    mid(0, 0, 2)
    pre2(2)()
    fz(1, 1)
    mid(0, 1, 3)
    mid(0, 0, 1)
    mid(1, 0, 2)
    finish(0, 0)
    third(0, 0, 2)
    mid(1, 0, 1)
    fz(2, 0)
    pre4()
    pre5()
    third(0, 0, 1)
    mid(1, 1, 1)
    mid(0, 1, 2)
    feed_send(2)
    third(1, 0, 0)
    mid(1, 1, 2)
    third(0, 1, 1)
    mid(1, 1, 3)
    third(0, 1, 2)
    pre6()
    fz(2, 1)
    third(0, 1, 3)
    third(2, 0, 0)
    third(0, 0, 3)
    mid(1, 0, 3)
    mid(2, 1, 1)
    finish(0, 2)
    pre7()
    finish(0, 1)
    fz(3, 0)
    third(1, 0, 1)
    third(1, 1, 2)
    third(1, 0, 2)
    mid(2, 1, 2)
    third(1, 0, 3)
    mid(2, 0, 2)
    fz(3, 1)
    third(1, 1, 1)
    third(1, 1, 3)
    mid(2, 1, 3)
    finish(0, 3)
    finish(1, 0)
    finish(1, 1)
    feed_send(3)
    arrive(0)
    third(2, 1, 0)
    make_q[0]()
    finish(1, 3)
    mid(2, 0, 1)
    mid(2, 0, 3)
    finish(1, 2)
    pre8()
    third(2, 1, 2)
    feed_send(0)
    feed_send(1)
    make_q[1]()
    kept.append(cp.local(q, q_o))
    mid(3, 0, 2)
    third(2, 1, 3)
    arrive(1)
    make_k[0]()
    make_k[1]()
    kept.append(cp.local(k, k_o))
    third(2, 0, 2)
    third(2, 1, 1)
    masks()
    make_v[0]()
    mid(3, 1, 1)
    mid(3, 0, 1)
    third(2, 0, 3)
    third(2, 0, 1)
    feed_pass(2)
    mid(3, 0, 3)
    make_v[1]()
    kept.append(cp.local(v, v_o))
    own_attend(0)()
    mid(3, 1, 2)
    finish(2, 2)
    finish(2, 0)
    own_attend(1)()
    mid(3, 1, 3)
    feed_pass(3)
    own_attend(2)()
    own_attend(3)()
    kept.append(cp.local(probs, probs_o))
    kept.append(cp.local(att, att_o))
    third(3, 1, 1)
    finish(2, 3)
    norm_one[0]()
    finish(2, 1)
    third(3, 0, 1)
    third(3, 0, 0)
    third(3, 1, 0)
    norm_one[1]()
    norm_one[2]()
    kept.append(cp.local(flow, first_o))
    kept.append(cp.local(n1, n1_o))
    kept.append(cp.local(i1, i1_o))
    feed_pass(0)
    arrive(2)
    make_ck[0]()
    third(3, 0, 2)
    third(3, 1, 2)
    make_cq[0]()
    make_cq[1]()
    kept.append(cp.local(cq, cq_o))
    make_ck[1]()
    kept.append(cp.local(ck, ck_o))
    third(3, 1, 3)
    third(3, 0, 3)
    cross_scores(0)()
    finish(3, 1)
    finish(3, 0)
    cross_scores(1)()
    finish(3, 2)
    cross_scores(2)()
    finish(3, 3)
    cross_scores(3)()
    kept.append(cp.local(cprobs, cprobs_o))
    feed_pass(1)
    arrive(3)
    make_cv[0]()
    make_cv[1]()
    kept.append(cp.local(cv, cv_o))
    cross_mix(0)()
    cross_mix(1)()
    kept.append(cp.local(crossed, crossed_o))
    norm_two[0]()
    norm_two[1]()
    norm_two[2]()
    kept.append(cp.local(slow, slow_o))
    kept.append(cp.local(n2, n2_o))
    kept.append(cp.local(i2, i2_o))
    def partner():
        for e in passed: e.wait_recv()
    def finish():
        for e in kept: e.wait()
        cp.close()
    return (second, vecs, att, flow, crossed), partner, finish

def forward_kernel(A, r, inputs, memory, seg_row, mem_row, embed, inner, outer, norms, cot, *refs):
    ws, (fin, fout, down, up), outs, scratch = refs[:8], refs[8:12], refs[12:43], refs[43:]
    fin2, fout2 = scratch[32:34]
    (second, vecs, att, flow, crossed), partner, finish = front_part(A, r, inputs, memory, seg_row, mem_row, embed, inner, outer, norms, ws, fin, fout, fin2, fout2, outs[:20], scratch[:32])
    feed_part(A, second, vecs, cot, fin, fout, down, up, inputs, memory, att, flow, crossed, partner, outs[20:], scratch[32:])
    finish()

def forward(A, r, inputs, memory, seg_row, mem_row, embed, inner, outer, norms, cot, ws, fin, fout, down, up):
    T, D = inputs.shape; M = memory.shape[0]; H = fin.shape[1]; AD = down.shape[1] * 4
    HID = 2 * H
    vm = pl.BlockSpec(memory_space=pltpu.VMEM)
    any_ = pl.BlockSpec(memory_space=pl.ANY)
    sds = jax.ShapeDtypeStruct
    v = lambda *s: pltpu.VMEM(s, bf16)
    vf = lambda *s: pltpu.VMEM(s, f32)
    row, mrow, full, one = sds((T, D), bf16), sds((M, D), bf16), sds((T, D), f32), sds((T, 1), f32)
    S = (PADDED, inner.shape[1])
    probs, cprobs = (16, T, T + PADDED), (16, T, M)
    R = T // 2
    sums = (2, 2, D // 256, R, 256)
    four = sds((4 * T, D), bf16)
    sem = pltpu.SemaphoreType.DMA
    return pl.pallas_call(functools.partial(forward_kernel, A, r),
        out_shape=(sds((8, D, D), bf16), sds(S, f32), sds((PADDED, 2 * D), bf16), sds((8, D), f32), row, row, row, sds(probs, bf16), row, row, full, one, row, mrow, mrow,
            sds(cprobs, bf16), row, row, full, one,
            row, full, sds((D, HID), bf16), sds((HID, D), bf16), sds((2, T, AD), bf16), row, sds((2, D), f32), four, four, four, sds((4 * M, D), bf16)),
        in_specs=[vm] * 9 + [any_] * 12, out_specs=(any_,) * 20 + (vm,) * 2 + (any_,) * 2 + (vm,) * 3 + (any_,) * 4,
        scratch_shapes=[v(8, D, D), v(T, D), v(T, D), v(T, D), v(*probs), v(T, D), vf(T, D), v(T, D), vf(T, D), vf(T, 1), v(T, D), v(M, D), v(M, D), v(*cprobs), v(T, D),
            vf(T, D), v(T, D), vf(T, D), vf(T, 1), vf(T, T + PADDED), vf(T, M),
            vf(3, *S), vf(3, *S), vf(A, *S), v(PADDED, 128), v(PADDED, 128), v(PADDED, 2 * D), v(8 * A * norms.shape[0], 128), vf(8, D), vf(*S), sem((320,)), sem((320,)),
            v(D, HID), v(HID, D), v(D, HID), v(HID, D), v(D, AD), v(AD, D), v(2, 4, R, D), v(2, 4, R, D), v(2, 4, R, HID), vf(2, 4, R, HID), v(2, 4, R, HID), v(2, 4, D // 256, R, 256),
            v(*sums), v(*sums), v(*sums), vf(T, AD), vf(2, R, D), sem((128,)), sem((128,))],
        compiler_params=pltpu.CompilerParams(collective_id=1, has_side_effects=True, vmem_limit_bytes=60 << 20), name="forward")(
            inputs, memory, seg_row, mem_row, embed, inner, outer, norms, cot, *ws, fin, fout, down, up)


def exact(l, r, dims):
    return lax.dot_general(l, r, (dims, ((), ())), precision=lax.Precision.HIGHEST, preferred_element_type=f32)

def back_kernel(A, r, gsec, n2, i2, vecs, ngrad3, tangent, embed, inner, outer, *refs):
    late, (slow, blow, ay, weights, fi, fo, xp0, xatt, xin, xmem) = refs[:11], refs[11:21]
    back_body(A, r, gsec, n2, i2, vecs, ngrad3, tangent, embed, inner, outer, late, slow, blow, ay, weights, fi, fo, xp0, xatt, xin, xmem, *refs[21:])

def back_body(A, r, gsec, n2, i2, vecs, ngrad3, tangent, embed, inner, outer, late, slow, blow, ay, weights, fi, fo, xp0, xatt, xin, xmem,
                igrad_o, mgrad_o, out, aout, fi_out, fo_out, outer_o, inner_o, embed_o, nsum,
                igrad, mgrad, cq, ck, cv, cprobs, n1, i1, q, k, v, probs, prows, ws, gmid, gfirst, og, mid, dcq, dck, dcv, startl, dq, dk, dv, pg,
                xb, yb, mb, mby, axb, ayb, pb, apb, fib, fob, r1, r2, r3, sb, xs, ra1, ra2, ra3, rfi, rfo, rzi, rzo, rxi, rxo, ob, aob, fib2, fob2,
                buf, got, zbuf, nbuf, ngot, nz, w0, w1, w2, w3, s0, s1, s2, nfull, ssem, rsem):
    a, b, x, c = place()
    o = 1 - c
    core, xp, yp = device(a, b, x, o), device(a, b, 1 - x, c), device(a, 1 - b, x, c)
    dp = device(a, b, 1 - x, o)
    place_n = x * 2 + c
    zp = [device((a + j) % A, b, x, c) for j in range(A)]
    za = a + 1 - 2 * (a % 2)
    zq = device(za, b, x, c)
    peers = (core, xp, yp)
    T, D = gsec.shape
    M = xmem.shape[0] // 4
    HID = fi.shape[1] // 2
    Q = fi.shape[0] // 4
    half = D // 2
    cp = Copies(ssem, rsem)
    loads = {}
    def fetch(slot, w):
        loads[slot] = cp.local(weights.at[w], ws.at[slot])
    loaded = [cp.local(src, dst) for src, dst in zip(late, (cq, ck, cv, cprobs, n1, i1, q, k, v, probs, prows))]
    def ready(start, stop):
        for e in loaded[start:stop]: e.wait()
    fetch(0, 7); fetch(1, 5); fetch(2, 3); fetch(3, 4)
    fown = []
    for xx in range(2):
        dq_ = pl.ds(pl.multiple_of((xx * 2 + c) * Q, Q), Q)
        fown += [cp.local(fi.at[dq_, :], fib.at[xx]), cp.local(fo.at[:, dq_], fob.at[xx])]
    greet([core, xp, yp, dp] + zp[1:])
    def offer(srcs, mine, theirs):
        n = cp.count
        cp.count += 2
        def start(keep, give):
            pltpu.make_async_copy(srcs[keep], mine, ssem.at[n]).start()
            remote(srcs[give], theirs, ssem.at[n + 1], rsem.at[n], core).start()
        pl.when(c == 0)(functools.partial(start, 0, 1))
        pl.when(c == 1)(functools.partial(start, 1, 0))
        e = remote(srcs[0], theirs, ssem.at[n + 1], rsem.at[n], core)
        cp.all.append(e)
        return pltpu.make_async_copy(srcs[0], mine, ssem.at[n]).wait, e.wait_recv
    lowT, highT = pl.ds(0, T), pl.ds(T, T)
    waits = {}
    aw = offer((slow, blow), axb.at[lowT], axb.at[highT]) + offer((ay.at[0], ay.at[1]), ayb.at[lowT], ayb.at[highT])
    xload = cp.count
    cp.count += 4
    def load_x(me):
        pltpu.make_async_copy(xp0, xb.at[0], ssem.at[xload]).start()
        pltpu.make_async_copy(xmem, mb, ssem.at[xload + 1]).start()
        pltpu.make_async_copy(xin if me else xatt, xb.at[1], ssem.at[xload + 2]).start()
        pltpu.make_async_copy(xin, xb.at[2], ssem.at[xload + 3]).start()
    pl.when(c == 0)(functools.partial(load_x, 0))
    pl.when(c == 1)(functools.partial(load_x, 1))
    waits[0] = (pltpu.make_async_copy(xp0, xb.at[0], ssem.at[xload]).wait,)
    waits[1] = (pltpu.make_async_copy(xmem, mb, ssem.at[xload + 1]).wait,)
    waits[2] = (pltpu.make_async_copy(xin, xb.at[1], ssem.at[xload + 2]).wait,)
    waits[3] = (pltpu.make_async_copy(xin, xb.at[2], ssem.at[xload + 3]).wait,)
    def share(srcs, dst, t):
        m = srcs[0].shape[0]
        k = cp.count
        cp.count += 4
        wide = half // 2
        here = pl.ds(pl.multiple_of(x * half + t * wide, wide), wide)
        there = pl.ds(pl.multiple_of((1 - x) * half + t * wide, wide), wide)
        spot = dst.at[pl.ds(pl.multiple_of(place_n * m, m), m), pl.ds(t * wide, wide)]
        def start(me):
            own, other = srcs[me], srcs[1 - me]
            remote(own.at[:, there], spot, ssem.at[k + 1], rsem.at[k + 1], xp).start()
            remote(other.at[:, there], spot, ssem.at[k + 3], rsem.at[k + 3], dp).start()
            remote(other.at[:, here], spot, ssem.at[k + 2], rsem.at[k + 2], core).start()
            pltpu.make_async_copy(own.at[:, here], spot, ssem.at[k]).start()
        pl.when(c == 0)(functools.partial(start, 0))
        pl.when(c == 1)(functools.partial(start, 1))
        ways = [remote(srcs[0].at[:, here], spot, ssem.at[k + i], rsem.at[k + i], d) for i, d in ((1, xp), (2, core), (3, dp))]
        cp.all.extend(ways)
        return (pltpu.make_async_copy(srcs[0].at[:, here], spot, ssem.at[k]).wait,) + tuple(e.wait_recv for e in ways)
    fcopies = []
    for xx in range(2):
        dq_ = pl.ds(pl.multiple_of((xx * 2 + o) * Q, Q), Q)
        fcopies += [cp(fi.at[dq_, :], rfi.at[xx], core), cp(fo.at[:, dq_], rfo.at[xx], core)]

    zf, xf, outs = [], [], []
    def feed0():
        for e in fown: e.wait()
        for e in fcopies: e.wait_recv()
        for xx in range(2):
            def rows_fi(t):
                s = pl.ds(t * 32, 32)
                fib[xx, s, :] = fib[xx, s, :] + rfi[xx, s, :]
            loop(0, Q // 32, rows_fi)
            def rows_fo(t):
                s = pl.ds(t * 64, 64)
                fob[xx, s, :] = fob[xx, s, :] + rfo[xx, s, :]
            loop(0, 2 * HID // 64, rows_fo)
        zf.extend([cp(fib.at[:, :, pl.ds(HID, HID)], rzi, zq), cp(fob.at[:, pl.ds(HID, HID), :], rzo, zq)])
    def feed1():
        for e in zf: e.wait_recv()
        for xx in range(2):
            def rows_fi(t):
                s = pl.ds(t * 32, 32)
                fib[xx, s, pl.ds(0, HID)] = fib[xx, s, pl.ds(0, HID)] + rzi[xx, s, :]
            loop(0, Q // 32, rows_fi)
            def rows_fo(t):
                s = pl.ds(t * 64, 64)
                fob[xx, s, :] = fob[xx, s, :] + rzo[xx, s, :]
            loop(0, HID // 64, rows_fo)
        xf.extend([cp(fib.at[1 - x, :, pl.ds(0, HID)], rxi, xp), cp(fob.at[1 - x, pl.ds(0, HID), :], rxo, xp)])
    def feed2():
        for e in xf: e.wait_recv()
        def rows_fi(t):
            s = pl.ds(t * 32, 32)
            fib2[s, :] = fib[x, s, pl.ds(0, HID)].astype(f32) + rxi[s, :].astype(f32)
        loop(0, Q // 32, rows_fi)
        def rows_fo(t):
            s = pl.ds(t * 64, 64)
            fob2[s, :] = fob[x, s, :].astype(f32) + rxo[s, :].astype(f32)
        loop(0, HID // 64, rows_fo)
        outs.extend([cp.local(fib2, fi_out).wait, cp.local(fob2, fo_out).wait])

    first, second, third, fourth = {}, {}, {}, {}
    wide = half // 2
    numbers = {}
    for i in range(4):
        for t in range(2):
            numbers[i, t] = cp.count
            cp.count += 1
    def level1(i, t):
        n = numbers[i, t]
        return remote(pb.at[i, t, :, 1 - b], r1.at[i, t], ssem.at[n], rsem.at[n], yp)
    for i in range(4):
        for t in range(2):
            first[i, t] = level1(i, t)
            cp.all.append(first[i, t])
    def share_one(src, dst, t, owner):
        m = src.shape[0]
        k = cp.count
        cp.count += 4
        wide = half // 2
        here = pl.ds(pl.multiple_of(x * half + t * wide, wide), wide)
        there = pl.ds(pl.multiple_of((1 - x) * half + t * wide, wide), wide)
        spot = dst.at[pl.ds(pl.multiple_of(place_n * m, m), m), pl.ds(t * wide, wide)]
        kept = pltpu.make_async_copy(src.at[:, here], spot, ssem.at[k])
        ways = [remote(src.at[:, there], spot, ssem.at[k + 1], rsem.at[k + 1], xp), remote(src.at[:, here], spot, ssem.at[k + 2], rsem.at[k + 2], core),
                remote(src.at[:, there], spot, ssem.at[k + 3], rsem.at[k + 3], dp)]
        def mine():
            ways[0].start()
            kept.start()
        def other():
            ways[2].start()
            ways[1].start()
        pl.when(c == owner)(mine)
        pl.when(c != owner)(other)
        def arrived():
            kept.wait()
            for e in ways: e.wait_recv()
        def sent():
            pl.when(c == owner)(ways[0].wait_send)
            def both():
                ways[1].wait_send()
                ways[2].wait_send()
            pl.when(c != owner)(both)
        ending.append(sent)
        return (arrived,)
    ending = []
    used, filled = set(), set()
    def compute(i, t, owner=None):
        def go():
            if (i, owner) not in used:
                used.add((i, owner))
                for e in waits[i]: e()
            for e in shared[(i, t) if owner is None else (i, t, owner)]: e()
            cols = pl.ds(t * wide, wide)
            n = (0, None, 1, 2)[i]
            def rows(u):
                d = columns(u)
                p = dot_left(mb[:, d], mby[:, cols]) if i == 1 else dot_left(xb[n, :, d], yb[n, :, cols])
                pb[i, t, u] = p.astype(bf16).reshape(2, 2, 2 * r, wide)
            loop(0, A, rows)
            level1(i, t).start()
        if owner is None: go()
        else: pl.when(c == owner)(go)
    def one(i, t):
        def go():
            first[i, t].wait_recv()
            for j in range(1, A):
                aj = (a + j) % A
                pb[i, t, aj, b] = pb[i, t, aj, b] + r1[i, t, aj]
                third[i, t, j] = cp(pb.at[i, t, aj, b], r2.at[i, t, j - 1], zp[j])
            pb[i, t, a, b] = pb[i, t, a, b] + r1[i, t, a]
        return go
    def two(i, t):
        def go():
            for j in range(1, A): third[i, t, j].wait_recv()
            for s in (1 - x, x):
                e = pb[i, t, a, b, s].astype(f32)
                for j in range(1, A): e = e + r2[i, t, j - 1, s].astype(f32)
                sb[i, t, s] = e
            xs[i, t] = sb[i, t, 1 - x].astype(bf16)
            fourth[i, t] = cp(xs.at[i, t], r3.at[i, t], xp)
        return go
    def three(i, t):
        def go():
            fourth[i, t].wait_recv()
            ob[i, :, pl.ds(pl.multiple_of(x * half + t * wide, wide), wide)] = sb[i, t, x]
            ob[i, :, pl.ds(pl.multiple_of((1 - x) * half + t * wide, wide), wide)] = r3[i, t].astype(f32)
            filled.add((i, t))
            if (i, 1 - t) in filled:
                outs.append(cp.local(ob.at[i, pl.ds(pl.multiple_of(c * r, r), r)], out.at[2 * i + c]).wait)
                outs.append(cp(ob.at[i, pl.ds(pl.multiple_of(o * r, r), r)], out.at[2 * i + c], core).wait_recv)
        return go
    def adapt0():
        for e in aw: e()
        for t in range(2):
            apb[t] = dot_left(axb[...], ayb[:, pl.ds(t * 256, 256)]).astype(bf16).reshape(A, 2, D // (2 * A), 256)
        first["a"] = cp(apb.at[1 - x], ra1, xp)
    def adapt1():
        first["a"].wait_recv()
        def row(z):
            for s in range(2):
                apb[x, z, s] = apb[x, z, s] + ra1[z, s]
        loop(0, A, row)
        second["a"] = cp(apb.at[x, :, 1 - b], ra2, yp)
    def adapt2():
        second["a"].wait_recv()
        for j in range(1, A):
            aj = (a + j) % A
            apb[x, aj, b] = apb[x, aj, b] + ra2[aj]
            third["a", j] = cp(apb.at[x, aj, b], ra3.at[j - 1], zp[j])
        apb[x, a, b] = apb[x, a, b] + ra2[a]
    def adapt3():
        for j in range(1, A): third["a", j].wait_recv()
        t = apb[x, a, b].astype(f32)
        for j in range(1, A): t = t + ra3[j - 1].astype(f32)
        aob[0] = t[:, :128]
        aob[1] = t[:, 128:]
        outs.append(cp.local(aob.at[c], aout.at[c]).wait)
        outs.append(cp(aob.at[o], aout.at[c], core).wait_recv)
    small = {}
    def lanes(start, count): return pl.ds(pl.multiple_of(start * 128, 128), count * 128)
    def tail_norm0():
        small["n"] = [cp(nbuf.at[0], ngot.at[0], core)]
    def tail0():
        small["w"] = [cp(pg.at[:, lanes((a + j) % A * 4, 4)], w0.at[j - 1], zp[j]) for j in range(1, A)]
    def tail_norm(n):
        def go():
            for e in small["n"]: e.wait_recv()
            nbuf[n] = nbuf[n - 1] + ngot[n - 1]
            small["n"] = [cp(nbuf.at[n], ngot.at[n], peers[n])]
        return go
    def tail_norm3():
        for e in small["n"]: e.wait_recv()
        nz[a] = nbuf[2] + ngot[2]
        small["n"] = [cp(nz.at[a], nz.at[a], zp[j]) for j in range(1, A)]
    def tail_norm4():
        for e in small["n"]: e.wait_recv()
        t = nz[0]
        for n in range(1, A): t = t + nz[n]
        nfull[...] = t
        quad = nfull[:, pl.ds(pl.multiple_of((a * 2 + b) * 128, 128), 128)]
        piece = quad[:, :r]
        for e in range(1, 4): piece = jnp.where(place_n == e, quad[:, e * r:(e + 1) * r], piece)
        nsum[...] = piece
    def tail1():
        t = pg[:, lanes(a * 4, 4)]
        for j, e in enumerate(small["w"]):
            e.wait_recv()
            t = t + w0[j]
        s0[...] = t
        small["w"] = [cp(s0.at[:, lanes((1 - b) * 2, 2)], w1, yp)]
    def tail2():
        small["w"][0].wait_recv()
        s1[...] = s0[:, lanes(b * 2, 2)] + w1[...]
        small["w"] = [cp(s1.at[:, lanes(1 - x, 1)], w2, xp)]
    def tail3():
        small["w"][0].wait_recv()
        s2[...] = s1[:, lanes(x, 1)] + w2[...]
        small["w"] = [cp(s2, w3, core)]
    def tail4():
        small["w"][0].wait_recv()
        t = s2[...] + w3[...]
        mine = jnp.where(c == 0, t[:, :64], t[:, 64:])
        buf[0] = exact(mine, outer[...].astype(f32), ((1,), (0,)))
        small["w"] = [cp(buf.at[0], got.at[0], core)]
        outer_o[...] = exact(mine, tangent[...].astype(bf16).astype(f32), ((0,), (0,)))
    def tail5(n):
        def go():
            small["w"][0].wait_recv()
            buf[n] = buf[n - 1] + got[n - 1]
            small["w"] = [cp(buf.at[n], got.at[n], peers[n])]
        return go
    def tail6():
        small["w"][0].wait_recv()
        zbuf[a] = buf[2] + got[2]
        small["w"] = [cp(zbuf.at[a], zbuf.at[a], zp[j]) for j in range(1, A)]
    def tail7():
        for e in small["w"]: e.wait_recv()
        t = zbuf[0]
        for n in range(1, A): t = t + zbuf[n]
        tan = tangent[...]
        t = t * (1.0 - tan * tan)
        inner_o[...] = exact(embed[...].astype(f32), t[:PREFIX], ((0,), (0,)))
        embed_o[...] = exact(t[:PREFIX], inner[...].astype(f32), ((1,), (1,)))
    def norm_two():
        norm_back_into(gsec, n2, i2, vecs[2:3, :], gmid, nbuf.at[0], 2)
        mid[...] = gmid[...].astype(bf16)
    def back_project(src, slot, n):
        def go():
            s = src[...]
            loop(2 * n, 2 * n + 2, lambda t: og.__setitem__((slice(None), columns(t)), dot_right(s, ws[slot, columns(t), :]).astype(bf16)))
        return go
    def wait_slot(slot):
        def go(): loads[slot].wait()
        return go
    def pair_back(p, grad, qr, kk, vv, pr):
        cols = columns(p, 128)
        qs, ks, gs = split_heads(qr[:, cols]), split_heads(kk), split_heads(grad[:, cols])
        res = None
        for s in range(2):
            low = pr[2 * p + s]
            prob = low.astype(f32)
            t = prob * dot_right(gs[s], vv)
            ds = (t - prob * jnp.sum(t, axis=-1, keepdims=True)).astype(bf16)
            m = (dot(ds, ks[s]), dot_left(ds, qs[s]), dot_left(low, gs[s]))
            res = m if res is None else tuple(e + f for e, f in zip(res, m))
        return cols, res[0] * 0.125, res[1] * 0.125, res[2]
    def cross_back(n):
        def go():
            def step(p):
                cs = columns(p, 128)
                cols, m1, m2, m3 = pair_back(p, og, cq, ck[:, cs], cv[:, cs], cprobs)
                dcq[:, cols] = m1.astype(bf16)
                dck[:, cols] = m2.astype(bf16)
                dcv[:, cols] = m3.astype(bf16)
            for p in range(2 * n, 2 * n + 2): step(p)
        return go
    def self_back(n):
        def go():
            def step(p):
                cs = columns(p, 128)
                cv_ = pl.ds(pl.multiple_of(D + p * 128, 128), 128)
                kk = jnp.concatenate([k[:, cs], prows[:, cs]], axis=0)
                vv = jnp.concatenate([v[:, cs], prows[:, cv_]], axis=0)
                cols, m1, m2, m3 = pair_back(p, og, q, kk, vv, probs)
                dq[:, cols] = m1.astype(bf16)
                dk[:, cols] = m2[:T].astype(bf16)
                dv[:, cols] = m3[:T].astype(bf16)
                pg[:, cols] = m2[T:]
                pg[:, cv_] = m3[T:]
            for p in range(2 * n, 2 * n + 2): step(p)
        return go
    def first_grad():
        s = dcq[...]
        def step(t):
            gfirst[:, columns(t)] = gmid[:, columns(t)] + dot_right(s, ws[1, columns(t), :])
        loop(0, D // 256, step)
    def norm_one():
        norm_back_into(gfirst, n1, i1, vecs[0:1, :], gmid, nbuf.at[0], 0)
        nbuf[0, 4:6, :] = ngrad3[...]
        nbuf[0, 6:8, :] = jnp.zeros((2, D), f32)
        startl[...] = gmid[...].astype(bf16)
    def memory_part(n):
        def go():
            def step(t):
                mgrad[:, columns(t)] = (dot_right(dck[...], ws[3, columns(t), :]) + dot_right(dcv[...], ws[0, columns(t), :])).astype(bf16)
            loop(2 * n, 2 * n + 2, step)
        return go
    def input_part(n):
        def go():
            def step(t):
                s = gmid[:, columns(t)] + dot_right(dq[...], ws[1, columns(t), :]) + dot_right(dk[...], ws[2, columns(t), :]) + dot_right(dv[...], ws[3, columns(t), :])
                igrad[:, columns(t)] = s.astype(bf16)
            loop(2 * n, 2 * n + 2, step)
        return go
    shared = {}
    def spread(i, srcs, dst):
        for t in range(2): shared[i, t] = share(srcs, dst, t)
    def spread_one(i, src, dst, owner):
        for t in range(2): shared[i, t, owner] = share_one(src, dst, t, owner)
    norm_two()
    spread_one(0, mid, yb.at[0], 0)
    wait_slot(0)()
    back_project(mid, 0, 0)()
    back_project(mid, 0, 1)()
    fetch(0, 6)
    ready(0, 4)
    cross_back(0)()
    cross_back(1)()
    cross_back(2)()
    cross_back(3)()
    spread_one(0, dcq, yb.at[0], 1)
    compute(0, 0, 0)
    feed0()
    spread(1, (dck, dcv), mby)
    compute(0, 0, 1)
    wait_slot(1)()
    first_grad()
    fetch(1, 0)
    ready(4, 6)
    norm_one()
    wait_slot(2)()
    back_project(startl, 2, 0)()
    back_project(startl, 2, 1)()
    fetch(2, 1)
    ready(6, 11)
    self_back(0)()
    one(0, 0)()
    compute(0, 1, 0)
    self_back(1)()
    compute(0, 1, 1)
    self_back(2)()
    spread_one(2, startl, yb.at[1], 0)
    self_back(3)()
    tail0()
    compute(1, 0)
    spread_one(2, dq, yb.at[1], 1)
    compute(1, 1)
    adapt0()
    compute(2, 1, 0)
    one(0, 1)()
    spread(3, (dk, dv), yb.at[2])
    tail_norm0()
    one(1, 0)()
    compute(2, 1, 1)
    one(1, 1)()
    adapt1()
    tail_norm(1)()
    tail1()
    one(2, 1)()
    compute(3, 0)
    wait_slot(3)()
    wait_slot(0)()
    memory_part(0)()
    compute(3, 1)
    adapt2()
    tail2()
    two(0, 0)()
    memory_part(1)()
    outs.append(cp.local(mgrad, mgrad_o).wait)
    fetch(3, 2)
    compute(2, 0, 0)
    tail3()
    tail4()
    one(3, 0)()
    compute(2, 0, 1)
    tail5(1)()
    two(1, 1)()
    one(3, 1)()
    three(0, 0)()
    wait_slot(1)()
    wait_slot(2)()
    wait_slot(3)()
    input_part(0)()
    three(1, 1)()
    two(0, 1)()
    two(2, 1)()
    tail5(2)()
    two(1, 0)()
    feed1()
    one(2, 0)()
    three(0, 1)()
    input_part(1)()
    outs.append(cp.local(igrad, igrad_o).wait)
    two(3, 0)()
    tail_norm(2)()
    three(1, 0)()
    tail6()
    two(3, 1)()
    adapt3()
    tail_norm3()
    three(2, 1)()
    two(2, 0)()
    three(3, 1)()
    three(2, 0)()
    three(3, 0)()
    tail7()
    feed2()
    tail_norm4()
    for e in ending: e()
    for e in outs: e()
    cp.close()

def back(A, r, first, late, rest):
    gsec = first[0]
    T, D = gsec.shape; M = rest[-1].shape[0] // 4
    fi, fo = rest[4:6]
    Q, H2 = fi.shape[0] // 4, fi.shape[1]
    H = H2 // 2
    half = D // 2
    v = lambda *s: pltpu.VMEM(s, bf16)
    vf = lambda *s: pltpu.VMEM(s, f32)
    any_ = pl.BlockSpec(memory_space=pl.ANY)
    vm = pl.BlockSpec(memory_space=pltpu.VMEM)
    sds = jax.ShapeDtypeStruct
    P_, N = PADDED, (8, D)
    hid = first[-2].shape[1]
    S = (P_, hid)
    return pl.pallas_call(functools.partial(back_kernel, A, r),
        out_shape=(sds((T, D), bf16), sds((M, D), bf16), sds((8, r, D), f32), sds((2, D // (2 * A), 128), f32), sds((Q, H), f32), sds((H, Q), f32),
            sds((64, hid), f32), sds((r, hid), f32), sds((PREFIX, r), f32), sds((8, r), f32)),
        in_specs=[vm] * len(first) + [any_] * (len(late) + len(rest)), out_specs=(any_,) * 6 + (vm,) * 4,
        scratch_shapes=[v(T, D), v(M, D)] + [pltpu.VMEM(e.shape, e.dtype) for e in late] + [v(4, D, D), vf(T, D), vf(T, D), v(T, D), v(T, D), v(T, D), v(M, D), v(M, D), v(T, D), v(T, D), v(T, D), v(T, D), vf(P_, 2 * D),
            v(3, 4 * T, D), v(3, 4 * T, half), v(4 * M, D), v(4 * M, half), v(2 * T, D), v(2 * T, 512),
            v(4, 2, A, 2, 2, 2 * r, half // 2), v(2, A, 2, D // (2 * A), 256), v(2, Q, H2), v(2, H2, Q),
            v(4, 2, A, 2, 2 * r, half // 2), v(4, 2, A - 1, 2, 2 * r, half // 2), v(4, 2, 2 * r, half // 2), vf(4, 2, 2, 2 * r, half // 2), v(4, 2, 2 * r, half // 2),
            v(A, 2, D // (2 * A), 256), v(A, D // (2 * A), 256), v(A - 1, D // (2 * A), 256),
            v(2, Q, H2), v(2, H2, Q), v(2, Q, H), v(2, H, Q), v(Q, H), v(H, Q),
            vf(4, 2 * r, D), vf(2, D // (2 * A), 128), vf(Q, H), vf(H, Q),
            vf(3, *S), vf(3, *S), vf(A, *S), vf(3, *N), vf(3, *N), vf(A, *N), vf(A - 1, P_, 512), vf(P_, 256), vf(P_, 128), vf(P_, 128), vf(P_, 512), vf(P_, 256), vf(P_, 128), vf(8, D),
            pltpu.SemaphoreType.DMA((224,)), pltpu.SemaphoreType.DMA((224,))],
        compiler_params=pltpu.CompilerParams(collective_id=2, has_side_effects=True, vmem_limit_bytes=63 << 20),
        name="back")(*first, *late, *rest)

def fast_body(A, inputs, memory, cotangent, segments, memory_segments, query_self, key_self, value_self, output_self,
              query_cross, key_cross, value_cross, output_cross, self_gain, self_shift, cross_gain, cross_shift,
              final_gain, final_shift, feed_in, feed_out, adapter_down, adapter_up, prefix_embed, prefix_inner, prefix_outer):
    r = query_self.shape[0]
    blank = jnp.zeros_like(self_gain)
    norms = jnp.stack([self_gain, self_shift, cross_gain, cross_shift, final_gain, final_shift] + [blank] * 10)
    (weights, tangent, prows, vecs, q, k, v, probs, attended, first_low, n1, i1, cq, ck, cv, cprobs, crossed, second_low, n2, i2,
     result, grad_second, fi, fo, ay, branch_low, ngrad3, xp0, xatt, xin, xmem) = forward(
        A, r, inputs, memory, segments.reshape(1, -1), memory_segments.reshape(1, -1), prefix_embed, prefix_inner, prefix_outer.T, norms, cotangent,
        [query_self, key_self, value_self, output_self, key_cross, query_cross, value_cross, output_cross], feed_in, feed_out, adapter_down, adapter_up)
    igrad, mgrad, sums, adapt, fi_sum, fo_sum, outer_grad, inner_grad, embed_grad, ng = back(A, r,
        (grad_second, n2, i2, vecs, ngrad3, tangent, prefix_embed, prefix_inner, prefix_outer.T), (cq, ck, cv, cprobs, n1, i1, q, k, v, probs, prows),
        (second_low, branch_low, ay, weights, fi, fo, xp0, xatt, xin, xmem))
    whole = deliver(result, igrad, mgrad, sums, fi_sum, fo_sum, outer_grad, inner_grad, embed_grad, adapt)
    return whole[:11] + tuple(ng[k] for k in range(6)) + whole[11:17] + (whole[17].T,)


def deliver_kernel(*refs):
    ins, outs, held, (turned, into, out_of) = refs[:10], refs[10:28], refs[28:38], refs[38:]
    loads = [pltpu.make_async_copy(src, dst, into.at[i]) for i, (src, dst) in enumerate(zip(ins, held))]
    for e in loads: e.start()
    order = (5, 6, 7, 4, 1, 2, 3, 0)
    moves = [(3, held[3].at[k], outs[3 + i]) for i, k in enumerate(order)]
    moves += [(i, held[i], outs[i]) for i in range(3)] + [(4, held[4], outs[11]), (5, held[5], outs[12]), (9, held[9].at[0], outs[13]), (9, turned, outs[14])]
    moves += [(8, held[8], outs[15]), (7, held[7], outs[16]), (6, held[6], outs[17])]
    stores, ready = [], set()
    for n, (i, src, dst) in enumerate(moves):
        if i not in ready:
            ready.add(i)
            loads[i].wait()
        if src is turned: turned[...] = held[9][1].T
        stores.append(pltpu.make_async_copy(src, dst, out_of.at[n]))
        stores[-1].start()
    for e in stores: e.wait()


def deliver(result, igrad, mgrad, sums, fi, fo, outer, inner, embed, adapt):
    ins = (result, igrad, mgrad, sums, fi, fo, outer, inner, embed, adapt)
    like = lambda e: jax.ShapeDtypeStruct(e.shape, e.dtype)
    row = jax.ShapeDtypeStruct(sums.shape[1:], f32)
    square = jax.ShapeDtypeStruct(adapt.shape[1:], f32)
    any_ = pl.BlockSpec(memory_space=pl.ANY)
    return pl.pallas_call(deliver_kernel,
        out_shape=(like(result), like(igrad), like(mgrad)) + (row,) * 8 + (like(fi), like(fo), square, square, like(embed), like(inner), like(outer)),
        in_specs=[any_] * 10, out_specs=(any_,) * 18,
        scratch_shapes=[pltpu.VMEM(e.shape, e.dtype) for e in ins] + [pltpu.VMEM(adapt.shape[1:], f32), pltpu.SemaphoreType.DMA((10,)), pltpu.SemaphoreType.DMA((18,))],
        compiler_params=pltpu.CompilerParams(vmem_limit_bytes=60 << 20), name="deliver")(*ins)


def solution(mesh):
    wide, narrow = mesh.shape[WIDE], mesh.shape[NARROW]
    fits = narrow == 4 and wide == 8
    body = functools.partial(fast_body, wide // 2) if fits else plain_body
    return jax.shard_map(
        body,
        mesh=mesh,
        in_specs=(
            P(BOTH, None),
            P(BOTH, None),
            P(BOTH, None),
            P(BOTH),
            P(BOTH),
            P(BOTH, None),
            P(BOTH, None),
            P(BOTH, None),
            P(BOTH, None),
            P(BOTH, None),
            P(BOTH, None),
            P(BOTH, None),
            P(BOTH, None),
            P(BOTH),
            P(BOTH),
            P(BOTH),
            P(BOTH),
            P(BOTH),
            P(BOTH),
            P(None, WIDE),
            P(WIDE, None),
            P(None, NARROW),
            P(NARROW, None),
            P(None, BOTH),
            P(BOTH, None),
            P(None, BOTH),
        ),
        out_specs=(
            P(BOTH, None),
            P(BOTH, None),
            P(BOTH, None),
            P(BOTH, None),
            P(BOTH, None),
            P(BOTH, None),
            P(BOTH, None),
            P(BOTH, None),
            P(BOTH, None),
            P(BOTH, None),
            P(BOTH, None),
            P(BOTH),
            P(BOTH),
            P(BOTH),
            P(BOTH),
            P(BOTH),
            P(BOTH),
            P(NARROW, WIDE),
            P(WIDE, NARROW),
            P(WIDE, NARROW),
            P(NARROW, WIDE),
            P(None, BOTH),
            P(BOTH, None),
            P(None, BOTH),
        ),
        check_vma=False,
    )
```

```python
import functools
from functools import reduce

import jax
import jax.numpy as jnp
from jax import lax
from jax.experimental import pallas as pl
from jax.experimental.pallas import tpu as pltpu
from jax.sharding import PartitionSpec as P

MESH = pl.DeviceIdType.MESH
bf16, f32 = jnp.bfloat16, jnp.float32
WIDE, NARROW = "wide", "narrow"
BOTH = (WIDE, NARROW)


HEADS = 16
HEAD = 64
PREFIX = 30


HIGHEST = lax.Precision.HIGHEST
EPSILON = 1e-05
MASKED = -1000000000.0
ADAPT_SCALE = 4.0


def matmul(left, right):
    return jnp.dot(left, right, preferred_element_type=jnp.float32)


def left_product(left, right):
    return lax.dot_general(
        left, right, (((0,), (0,)), ((), ())), preferred_element_type=jnp.float32
    )


def right_product(left, right):
    return lax.dot_general(
        left, right, (((1,), (1,)), ((), ())), preferred_element_type=jnp.float32
    )


def exact_left(left, right):
    return lax.dot_general(
        left, right, (((0,), (0,)), ((), ())), precision=HIGHEST, preferred_element_type=jnp.float32
    )


def exact_right(left, right):
    return lax.dot_general(
        left, right, (((1,), (1,)), ((), ())), precision=HIGHEST, preferred_element_type=jnp.float32
    )


def norm_forward(values, factor, offset):
    average = jnp.mean(values, axis=-1, keepdims=True)
    center = values - average
    inverse = lax.rsqrt(jnp.mean(center * center, axis=-1, keepdims=True) + EPSILON)
    normed = center * inverse
    return (normed * factor + offset, normed, inverse)


def norm_backward(grad_out, normed, inverse, factor):
    scaled = grad_out * factor
    grad_in = inverse * (
        scaled
        - jnp.mean(scaled, axis=-1, keepdims=True)
        - normed * jnp.mean(scaled * normed, axis=-1, keepdims=True)
    )
    return (grad_in, jnp.sum(grad_out * normed, axis=0), jnp.sum(grad_out, axis=0))


def head_view(rows):
    return rows.reshape(rows.shape[0], HEADS, HEAD)


def scored(queries, key_rows, allowed):
    raw = jnp.einsum(
        "shd,khd->hsk", head_view(queries), head_view(key_rows), preferred_element_type=jnp.float32
    )
    return jnp.where(allowed[None], raw * HEAD ** (-0.5), MASKED)


def attend_forward(queries, parts):
    scores = [scored(queries, member[0], member[2]) for member in parts]
    largest = reduce(jnp.maximum, [jnp.max(matrix, axis=-1, keepdims=True) for matrix in scores])
    total = reduce(
        jnp.add, [jnp.sum(jnp.exp(matrix - largest), axis=-1, keepdims=True) for matrix in scores]
    )
    logsum = largest + jnp.log(total)
    mixed = reduce(
        jnp.add,
        [
            jnp.einsum(
                "hsk,khd->shd",
                jnp.exp(matrix - logsum).astype(jnp.bfloat16),
                head_view(member[1]),
                preferred_element_type=jnp.float32,
            )
            for matrix, member in zip(scores, parts)
        ],
    )
    return (mixed.reshape(queries.shape[0], HEADS * HEAD), logsum)


def attend_backward(queries, parts, logsum, grad_low):
    grad_heads = head_view(grad_low)
    chances = [jnp.exp(scored(queries, member[0], member[2]) - logsum) for member in parts]
    slopes = [
        jnp.einsum(
            "shd,khd->hsk", grad_heads, head_view(member[1]), preferred_element_type=jnp.float32
        )
        for member in parts
    ]
    row_dot = reduce(
        jnp.add,
        [jnp.sum(chance * slope, axis=-1, keepdims=True) for chance, slope in zip(chances, slopes)],
    )
    scale = HEAD ** (-0.5)
    grad_query = jnp.zeros((queries.shape[0], HEADS, HEAD), jnp.float32)
    results = []
    for member, chance, slope in zip(parts, chances, slopes):
        dscore = (chance * (slope - row_dot)).astype(jnp.bfloat16)
        grad_query = grad_query + jnp.einsum(
            "hsk,khd->shd", dscore, head_view(member[0]), preferred_element_type=jnp.float32
        )
        grad_key = (
            jnp.einsum(
                "hsk,shd->khd", dscore, head_view(queries), preferred_element_type=jnp.float32
            )
            * scale
        )
        grad_value = jnp.einsum(
            "hsk,shd->khd",
            chance.astype(jnp.bfloat16),
            grad_heads,
            preferred_element_type=jnp.float32,
        )
        results.append(
            (
                grad_key.reshape(grad_key.shape[0], HEADS * HEAD),
                grad_value.reshape(grad_value.shape[0], HEADS * HEAD),
            )
        )
    return ((grad_query * scale).reshape(queries.shape[0], HEADS * HEAD), results)


def gelu_back(pre_values, grad_values):
    return jax.vjp(lambda inner: jax.nn.gelu(inner, approximate=False), pre_values)[1](grad_values)[
        0
    ]


def plain_body(
    inputs,
    memory,
    cotangent,
    segments,
    memory_segments,
    query_self,
    key_self,
    value_self,
    output_self,
    query_cross,
    key_cross,
    value_cross,
    output_cross,
    self_gain,
    self_shift,
    cross_gain,
    cross_shift,
    final_gain,
    final_shift,
    feed_in,
    feed_out,
    adapter_down,
    adapter_up,
    prefix_embed,
    prefix_inner,
    prefix_outer,
):
    (
        query_one,
        key_one,
        value_one,
        output_one,
        query_two,
        key_two,
        value_two,
        output_two,
        gain_one,
        shift_one,
        gain_two,
        shift_two,
        gain_three,
        shift_three,
        embed_full,
        inner_full,
        outer_full,
    ) = (
        lax.all_gather(query_self, BOTH, axis=0, tiled=True),
        lax.all_gather(key_self, BOTH, axis=0, tiled=True),
        lax.all_gather(value_self, BOTH, axis=0, tiled=True),
        lax.all_gather(output_self, BOTH, axis=0, tiled=True),
        lax.all_gather(query_cross, BOTH, axis=0, tiled=True),
        lax.all_gather(key_cross, BOTH, axis=0, tiled=True),
        lax.all_gather(value_cross, BOTH, axis=0, tiled=True),
        lax.all_gather(output_cross, BOTH, axis=0, tiled=True),
        lax.all_gather(self_gain, BOTH, axis=0, tiled=True),
        lax.all_gather(self_shift, BOTH, axis=0, tiled=True),
        lax.all_gather(cross_gain, BOTH, axis=0, tiled=True),
        lax.all_gather(cross_shift, BOTH, axis=0, tiled=True),
        lax.all_gather(final_gain, BOTH, axis=0, tiled=True),
        lax.all_gather(final_shift, BOTH, axis=0, tiled=True),
        lax.all_gather(prefix_embed, BOTH, axis=1, tiled=True),
        lax.all_gather(prefix_inner, BOTH, axis=0, tiled=True),
        lax.all_gather(prefix_outer, BOTH, axis=1, tiled=True),
    )
    factor_one = gain_one.astype(jnp.float32)
    factor_two = gain_two.astype(jnp.float32)
    factor_three = gain_three.astype(jnp.float32)
    length = inputs.shape[0]
    width = inputs.shape[1]
    places = jnp.arange(length)
    causal = places[:, None] >= places[None, :]
    local_mask = (segments[:, None] == segments[None, :]) & causal
    prefix_mask = jnp.ones((length, PREFIX), jnp.bool_)
    cross_mask = segments[:, None] == memory_segments[None, :]
    tangent = jnp.tanh(matmul(embed_full, inner_full))
    tangent_low = tangent.astype(jnp.bfloat16)
    prefix_rows = matmul(tangent_low, outer_full).astype(jnp.bfloat16)
    prefix_keys = prefix_rows[:, :width]
    prefix_values = prefix_rows[:, width:]
    queries = matmul(inputs, query_one).astype(jnp.bfloat16)
    key_rows = matmul(inputs, key_one).astype(jnp.bfloat16)
    value_rows = matmul(inputs, value_one).astype(jnp.bfloat16)
    self_parts = ((prefix_keys, prefix_values, prefix_mask), (key_rows, value_rows, local_mask))
    attended, self_logsum = attend_forward(queries, self_parts)
    attended_low = attended.astype(jnp.bfloat16)
    first, normed_one, inverse_one = norm_forward(
        inputs.astype(jnp.float32) + matmul(attended_low, output_one),
        factor_one,
        shift_one.astype(jnp.float32),
    )
    first_low = first.astype(jnp.bfloat16)
    cross_queries = matmul(first_low, query_two).astype(jnp.bfloat16)
    cross_keys = matmul(memory, key_two).astype(jnp.bfloat16)
    cross_values = matmul(memory, value_two).astype(jnp.bfloat16)
    cross_parts = ((cross_keys, cross_values, cross_mask),)
    crossed, cross_logsum = attend_forward(cross_queries, cross_parts)
    crossed_low = crossed.astype(jnp.bfloat16)
    second, normed_two, inverse_two = norm_forward(
        first + matmul(crossed_low, output_two), factor_two, shift_two.astype(jnp.float32)
    )
    second_low = second.astype(jnp.bfloat16)
    feed_rows = lax.all_gather(second_low, WIDE, axis=0, tiled=True)
    hidden_pre = matmul(feed_rows, feed_in)
    hidden_low = jax.nn.gelu(hidden_pre, approximate=False).astype(jnp.bfloat16)
    feed_sum = lax.psum_scatter(
        matmul(hidden_low, feed_out), WIDE, scatter_dimension=0, tiled=True
    )
    adapt_rows = lax.all_gather(second_low, NARROW, axis=0, tiled=True)
    bottle_pre = matmul(adapt_rows, adapter_down)
    bottle_low = jax.nn.gelu(bottle_pre, approximate=False).astype(jnp.bfloat16)
    adapt_sum = lax.psum_scatter(
        matmul(bottle_low, adapter_up).astype(jnp.bfloat16),
        NARROW,
        scatter_dimension=0,
        tiled=True,
    ).astype(jnp.float32)
    branch = feed_sum + ADAPT_SCALE * adapt_sum
    result, normed_three, inverse_three = norm_forward(
        second + branch, factor_three, shift_three.astype(jnp.float32)
    )
    grad_branch, gain_three_grad, shift_three_grad = norm_backward(
        cotangent.astype(jnp.float32), normed_three, inverse_three, factor_three
    )
    branch_low = grad_branch.astype(jnp.bfloat16)
    branch_rows = lax.all_gather(branch_low, WIDE, axis=0, tiled=True)
    grad_hidden = right_product(branch_rows, feed_out)
    grad_pre = gelu_back(hidden_pre, grad_hidden).astype(jnp.bfloat16)
    grad_out_part = left_product(hidden_low, branch_rows)
    grad_in_part = left_product(feed_rows, grad_pre)
    grad_feed = lax.psum_scatter(
        right_product(grad_pre, feed_in), WIDE, scatter_dimension=0, tiled=True
    )
    feed_in_total, feed_out_total = (
        lax.psum_scatter(
            grad_in_part.astype(jnp.bfloat16), NARROW, scatter_dimension=0, tiled=True
        ).astype(jnp.float32),
        lax.psum_scatter(
            grad_out_part.astype(jnp.bfloat16), NARROW, scatter_dimension=1, tiled=True
        ).astype(jnp.float32),
    )
    branch_narrow = lax.all_gather(branch_low, NARROW, axis=0, tiled=True)
    grad_bottle = ADAPT_SCALE * right_product(branch_narrow, adapter_up)
    grad_bottle_pre = gelu_back(bottle_pre, grad_bottle).astype(jnp.bfloat16)
    grad_up_part = ADAPT_SCALE * left_product(bottle_low, branch_narrow)
    grad_down_part = left_product(adapt_rows, grad_bottle_pre)
    grad_adapt = lax.psum_scatter(
        right_product(grad_bottle_pre, adapter_down).astype(jnp.bfloat16),
        NARROW,
        scatter_dimension=0,
        tiled=True,
    ).astype(jnp.float32)
    down_total, up_total = (
        lax.psum_scatter(grad_down_part, WIDE, scatter_dimension=0, tiled=True),
        lax.psum_scatter(grad_up_part, WIDE, scatter_dimension=1, tiled=True),
    )
    grad_second = grad_branch + grad_feed + grad_adapt
    grad_mid, gain_two_grad, shift_two_grad = norm_backward(
        grad_second, normed_two, inverse_two, factor_two
    )
    mid_low = grad_mid.astype(jnp.bfloat16)
    output_two_grad = left_product(crossed_low, mid_low)
    crossed_grad = right_product(mid_low, output_two).astype(jnp.bfloat16)
    cross_query_grad, cross_results = attend_backward(
        cross_queries, cross_parts, cross_logsum, crossed_grad
    )
    cross_query_low = cross_query_grad.astype(jnp.bfloat16)
    cross_key_low = cross_results[0][0].astype(jnp.bfloat16)
    cross_value_low = cross_results[0][1].astype(jnp.bfloat16)
    query_two_grad = left_product(first_low, cross_query_low)
    key_two_grad = left_product(memory, cross_key_low)
    value_two_grad = left_product(memory, cross_value_low)
    memory_grad = (
        right_product(cross_key_low, key_two) + right_product(cross_value_low, value_two)
    ).astype(jnp.bfloat16)
    grad_first = grad_mid + right_product(cross_query_low, query_two)
    grad_start, gain_one_grad, shift_one_grad = norm_backward(
        grad_first, normed_one, inverse_one, factor_one
    )
    start_low = grad_start.astype(jnp.bfloat16)
    output_one_grad = left_product(attended_low, start_low)
    attended_grad = right_product(start_low, output_one).astype(jnp.bfloat16)
    self_query_grad, self_results = attend_backward(queries, self_parts, self_logsum, attended_grad)
    self_query_low = self_query_grad.astype(jnp.bfloat16)
    self_key_low = self_results[1][0].astype(jnp.bfloat16)
    self_value_low = self_results[1][1].astype(jnp.bfloat16)
    query_one_grad = left_product(inputs, self_query_low)
    key_one_grad = left_product(inputs, self_key_low)
    value_one_grad = left_product(inputs, self_value_low)
    inputs_grad = (
        grad_start
        + right_product(self_query_low, query_one)
        + right_product(self_key_low, key_one)
        + right_product(self_value_low, value_one)
    ).astype(jnp.bfloat16)
    prefix_grad = jnp.concatenate([self_results[0][0], self_results[0][1]], axis=1)
    outer_grad = exact_left(tangent_low.astype(jnp.float32), prefix_grad)
    tangent_grad = exact_right(prefix_grad, outer_full.astype(jnp.float32)) * (
        1.0 - tangent * tangent
    )
    inner_grad = exact_left(embed_full.astype(jnp.float32), tangent_grad)
    embed_grad = exact_right(tangent_grad, inner_full.astype(jnp.float32))
    (
        query_one_sum,
        key_one_sum,
        value_one_sum,
        output_one_sum,
        query_two_sum,
        key_two_sum,
        value_two_sum,
        output_two_sum,
        gain_one_sum,
        shift_one_sum,
        gain_two_sum,
        shift_two_sum,
        gain_three_sum,
        shift_three_sum,
        embed_sum,
        inner_sum,
        outer_sum,
    ) = (
        lax.psum_scatter(query_one_grad, BOTH, scatter_dimension=0, tiled=True),
        lax.psum_scatter(key_one_grad, BOTH, scatter_dimension=0, tiled=True),
        lax.psum_scatter(value_one_grad, BOTH, scatter_dimension=0, tiled=True),
        lax.psum_scatter(output_one_grad, BOTH, scatter_dimension=0, tiled=True),
        lax.psum_scatter(query_two_grad, BOTH, scatter_dimension=0, tiled=True),
        lax.psum_scatter(key_two_grad, BOTH, scatter_dimension=0, tiled=True),
        lax.psum_scatter(value_two_grad, BOTH, scatter_dimension=0, tiled=True),
        lax.psum_scatter(output_two_grad, BOTH, scatter_dimension=0, tiled=True),
        lax.psum_scatter(gain_one_grad, BOTH, scatter_dimension=0, tiled=True),
        lax.psum_scatter(shift_one_grad, BOTH, scatter_dimension=0, tiled=True),
        lax.psum_scatter(gain_two_grad, BOTH, scatter_dimension=0, tiled=True),
        lax.psum_scatter(shift_two_grad, BOTH, scatter_dimension=0, tiled=True),
        lax.psum_scatter(gain_three_grad, BOTH, scatter_dimension=0, tiled=True),
        lax.psum_scatter(shift_three_grad, BOTH, scatter_dimension=0, tiled=True),
        lax.psum_scatter(embed_grad, BOTH, scatter_dimension=1, tiled=True),
        lax.psum_scatter(inner_grad, BOTH, scatter_dimension=0, tiled=True),
        lax.psum_scatter(outer_grad, BOTH, scatter_dimension=1, tiled=True),
    )
    return (
        result.astype(jnp.bfloat16),
        inputs_grad,
        memory_grad,
        query_one_sum,
        key_one_sum,
        value_one_sum,
        output_one_sum,
        query_two_sum,
        key_two_sum,
        value_two_sum,
        output_two_sum,
        gain_one_sum,
        shift_one_sum,
        gain_two_sum,
        shift_two_sum,
        gain_three_sum,
        shift_three_sum,
        feed_in_total,
        feed_out_total,
        down_total,
        up_total,
        embed_sum,
        inner_sum,
        outer_sum,
    )


def place():
    w = lax.axis_index(WIDE); n = lax.axis_index(NARROW)
    return w // 2, w % 2, n // 2, n % 2

def device(a, b, x, c):
    return (a * 2 + b, x * 2 + c)

def greet(peers):
    barrier = pltpu.get_barrier_semaphore()
    for p in peers:
        pl.semaphore_signal(barrier, inc=1, device_id=p, device_id_type=MESH)
    pl.semaphore_wait(barrier, len(peers))

def remote(src, dst, send, recv, dev):
    return pltpu.make_async_remote_copy(src_ref=src, dst_ref=dst, send_sem=send, recv_sem=recv, device_id=dev, device_id_type=MESH)


def dot_left(l, r):
    return lax.dot_general(l, r, (((0,), (0,)), ((), ())), preferred_element_type=f32)

class Copies:
    def __init__(self, send, recv):
        self.send, self.recv, self.count, self.all = send, recv, 0, []
    def __call__(self, src, dst, dev):
        cp = remote(src, dst, self.send.at[self.count], self.recv.at[self.count], dev)
        self.count += 1
        cp.start(); self.all.append(cp)
        return cp
    def local(self, src, dst):
        cp = pltpu.make_async_copy(src, dst, self.send.at[self.count])
        self.count += 1
        cp.start()
        return cp
    def sent(self, some):
        for cp in some:
            cp.wait_send()
            self.all = [o for o in self.all if o is not cp]
    def close(self):
        for cp in self.all: cp.wait_send()


EPSILON = 1e-05
ADAPT_SCALE = 4.0

def dot(l, r):
    return jnp.dot(l, r, preferred_element_type=f32)

def dot_right(l, r):
    return lax.dot_general(l, r, (((1,), (1,)), ((), ())), preferred_element_type=f32)

def gelu_both(v):
    phi = 0.5 + 0.5 * lax.erf(v * 0.7071067811865476)
    return v * phi, phi + v * (0.3989422804014327 * jnp.exp(-0.5 * v * v))

def norm(v):
    center = v - jnp.mean(v, axis=-1, keepdims=True)
    inverse = lax.rsqrt(jnp.mean(center * center, axis=-1, keepdims=True) + EPSILON)
    return center * inverse, inverse

def norm_back(e, n, inverse, factor):
    s = e * factor
    return inverse * (s - jnp.mean(s, axis=-1, keepdims=True) - n * jnp.mean(s * n, axis=-1, keepdims=True))

def feed_part(A, second, vecs, cot, fin_own, fout_own, down_ref, up_ref, inputs, memory, att, flow, crossed, slow, partner, outs, scratch):
    result, gsec, fi_out, fo_out, ay, blow, ngrad, xp0, xatt, xin, xmem, xad = outs
    fin, fout, fi, fo, down, up, rows, brow, hid, slope, gpre, part, q1, q2, q3, bslope, acc, ssem, rsem = scratch
    a, b, x, c = place()
    o = 1 - c
    yp = device(a, 1 - b, x, c)
    zp = device((a + A // 2) % A, b, x, c)
    core, xp, dp = device(a, b, x, o), device(a, b, 1 - x, c), device(a, b, 1 - x, o)
    cp = Copies(ssem, rsem)
    half = fin_own.shape[1]
    loads = [cp.local(fin_own, fin.at[:, pl.ds(0, half)]), cp.local(fout_own, fout.at[pl.ds(0, half)])]
    T, D = second.shape
    NC, R = 2, T // 2
    C = R // NC
    HID = fin.shape[1]; TW = 256
    NT = D // TW
    def span(h): return pl.ds(h * R, R)

    def spread(buf, h):
        zs, ys, passed = [], [], []
        for u in range(NC):
            s = pl.ds(u * C, C)
            zs.append(cp(buf.at[h, 0, s], buf.at[h, 2, s], zp))
        for u in range(NC):
            s = pl.ds(u * C, C)
            ys.append(cp(buf.at[h, 0, s], buf.at[h, 1, s], yp))
        def beside():
            for e in ys: e.wait_recv()
        def forward():
            for u in range(NC):
                s = pl.ds(u * C, C)
                zs[u].wait_recv()
                passed.append(cp(buf.at[h, 2, s], buf.at[h, 3, s], yp))
        def across():
            for e in passed: e.wait_recv()
        return beside, forward, across

    sums, onward = {}, {}
    def send_part(level, h, j, t):
        sums[level, h, j, t] = cp(part.at[h, j, t], (q3 if j == 3 else q1).at[level, h, t], yp)
    def collect(level, h, t):
        sums[level, h, 3, t].wait_recv()
        part[h, 2, t] = part[h, 2, t] + q3[level, h, t]
        onward[level, h, t] = cp(part.at[h, 2, t], q2.at[level, h, t], zp)
    def gather_up(level, h):
        for t in range(NT):
            cols = pl.ds(t * TW, TW)
            sums[level, h, 1, t].wait_recv(); onward[level, h, t].wait_recv()
            acc[h, :, cols] = acc[h, :, cols] + q1[level, h, t].astype(f32) + q2[level, h, t].astype(f32)
        cp.sent([onward[level, h, t] for t in range(NT)] + [sums[level, h, j, t] for j in (1, 3) for t in range(NT)])

    for h in range(2): rows[h, 0] = second[span(h), :].astype(bf16)
    moves = {(0, h): spread(rows, h) for h in range(2)}
    AD = down_ref.shape[1]
    n = x * 2 + c
    nd = pl.ds(pl.multiple_of(n * AD, AD), AD)
    md = pl.ds(pl.multiple_of((2 - 2 * x + c) * AD, AD), AD)
    kept, late = [cp.local(down_ref, down.at[:, nd]), cp.local(up_ref, up.at[nd])], []
    over = [cp(down_ref, down.at[:, nd], xp), cp(up_ref, up.at[nd], xp)]
    near = [cp(down_ref, down.at[:, nd], core), cp(up_ref, up.at[nd], core)]
    def rowsn(ref, m, place): return ref.at[pl.ds(pl.multiple_of(place * m, m), m)]
    def fan(srcs, dst, only=False):
        k = cp.count
        cp.count += 4
        def start(me):
            own, other = srcs[me], srcs[1 - me]
            if own is not None:
                pltpu.make_async_copy(own, rowsn(dst, T, n), ssem.at[k]).start()
                remote(own, rowsn(dst, T, n), ssem.at[k + 1], rsem.at[k + 1], xp).start()
            if other is not None:
                remote(other, rowsn(dst, T, n), ssem.at[k + 2], rsem.at[k + 2], core).start()
                remote(other, rowsn(dst, T, n), ssem.at[k + 3], rsem.at[k + 3], dp).start()
        def finish(me):
            own, other = srcs[me], srcs[1 - me]
            src = own if own is not None else other
            ways = [remote(src, rowsn(dst, T, n), ssem.at[k + i], rsem.at[k + i], d) for i, d in ((1, xp), (2, core), (3, dp))]
            if own is not None:
                pltpu.make_async_copy(own, rowsn(dst, T, n), ssem.at[k]).wait()
                ways[0].wait_send()
                for e in ways: e.wait_recv()
            if other is not None:
                ways[1].wait_send(); ways[2].wait_send()
        pl.when(c == 0)(functools.partial(start, 0))
        pl.when(c == 1)(functools.partial(start, 1))
        def done():
            pl.when(c == 0)(functools.partial(finish, 0))
            pl.when(c == 1)(functools.partial(finish, 1))
        return done
    fans = [fan((crossed, flow), xp0), fan((att, None), xatt)]
    M = memory.shape[0]
    share = []
    for src, dst, m in ((inputs, xin, T), (memory, xmem, M)):
        kept.append(cp.local(src, rowsn(dst, m, n)))
        near.append(cp(src, rowsn(dst, m, n), core))
        share.append((cp(src, rowsn(dst, m, n), xp), rowsn(dst, m, 2 - 2 * x + c)))
    fans.append(fan((slow, None), xad))
    def adapter_weights():
        kept[0].wait(); kept[1].wait()
        for e, ref in zip(over, (down.at[:, md], up.at[md])):
            e.wait_recv()
            late.append(cp(ref, ref, core))
        ready.extend(late[:2])
    ready = []
    def adapter_ready():
        near[0].wait_recv(); near[1].wait_recv()
        for e in ready: e.wait_recv()
    def share_on():
        for e, ref in share:
            e.wait_recv()
            late.append(cp(ref, ref, core))
    def adapter_forward():
        own = rows[:, 0].reshape(T, D)
        for t in range(2):
            cols = pl.ds(t * 256, 256)
            g, s = gelu_both(dot(own, down[:, cols]))
            ay[1, :, cols] = (ADAPT_SCALE * g.astype(bf16).astype(f32)).astype(bf16)
            bslope[:, cols] = s
        def tile(t, _):
            cols = pl.ds(pl.multiple_of(t * 256, 256), 256)
            acc[:, :, cols] = acc[:, :, cols] + dot(ay[1], up[:, cols]).reshape(2, R, 256)
            return 0
        lax.fori_loop(0, D // 256, tile, 0)
    def adapter_back():
        def tile(t, _):
            cols = pl.ds(pl.multiple_of(t * 256, 256), 256)
            gbot = bslope[:, cols] * (ADAPT_SCALE * dot_right(brow[:, 0].reshape(T, D), up[cols, :]))
            ay[0, :, cols] = gbot.astype(bf16)
            return 0
        lax.fori_loop(0, down.shape[1] // 256, tile, 0)
        def tile2(t, _):
            cols = pl.ds(pl.multiple_of(t * 256, 256), 256)
            acc[:, :, cols] = acc[:, :, cols] + dot_right(ay[0], down[cols, :]).reshape(2, R, 256)
            return 0
        lax.fori_loop(0, D // 256, tile2, 0)
    def both(buf, h, g): return buf[h, 2 * g:2 * g + 2].reshape(2 * R, buf.shape[3])
    def put_out(level, h, g, t, p):
        cols = pl.ds(t * TW, TW)
        if g == 0:
            acc[h, :, cols] = p[:R] if level == 0 else acc[h, :, cols] + p[:R]
            part[h, 1, t] = p[R:].astype(bf16)
            send_part(level, h, 1, t)
        else:
            part[h, 3, t] = p[R:].astype(bf16)
            send_part(level, h, 3, t)
            part[h, 2, t] = p[:R].astype(bf16)
    def enter(h, g):
        moves[0, h][2 * g]()
        xv = both(rows, h, g)
        def tile(t, _):
            cols = pl.ds(pl.multiple_of(t * TW, TW), TW)
            e, s = gelu_both(dot(xv, fin[:, cols]))
            hid[h, 2 * g:2 * g + 2, :, cols] = e.astype(bf16).reshape(2, R, TW)
            slope[h, 2 * g:2 * g + 2, :, cols] = s.reshape(2, R, TW)
            return 0
        lax.fori_loop(0, HID // TW, tile, 0)
    def leave(h, g):
        moves[1, h][2 * g]()
        xv = both(brow, h, g)
        def tile(t, _):
            cols = pl.ds(pl.multiple_of(t * TW, TW), TW)
            gh = dot_right(xv, fout[cols, :])
            gpre[h, 2 * g:2 * g + 2, :, cols] = (slope[h, 2 * g:2 * g + 2, :, cols].reshape(2 * R, TW) * gh).astype(bf16).reshape(2, R, TW)
            return 0
        lax.fori_loop(0, HID // TW, tile, 0)
    def out_tile(level, h, g, t):
        cols = pl.ds(t * TW, TW)
        put_out(level, h, g, t, dot_right(both(gpre, h, g), fin[cols, :]) if level else dot(both(hid, h, g), fout[:, cols]))
    fac, off = vecs[4:5, :], vecs[5:6, :]
    def turn(h):
        n3, inv3 = norm(second[span(h), :] + acc[h])
        result[span(h), :] = (n3 * fac + off).astype(bf16)
        e = cot[span(h), :].astype(f32)
        gb = norm_back(e, n3, inv3, fac)
        gbl = gb.astype(bf16)
        brow[h, 0] = gbl
        moves[1, h] = spread(brow, h)
        blow[span(h), :] = gbl
        acc[h] = gb
        gg, gs = jnp.sum(e * n3, axis=0, keepdims=True), jnp.sum(e, axis=0, keepdims=True)
        ngrad[0:1, :] = gg if h == 0 else ngrad[0:1, :] + gg
        ngrad[1:2, :] = gs if h == 0 else ngrad[1:2, :] + gs
    def wtile(t):
        cols = pl.ds(t * TW, TW)
        fi[:, cols] = dot_left(rows[...].reshape(4 * T, D), gpre[:, :, :, cols].reshape(4 * T, TW)).astype(bf16)
        fo[:, cols] = dot_left(hid[...].reshape(4 * T, HID), brow[:, :, :, cols].reshape(4 * T, TW)).astype(bf16)
    for e in loads: e.wait()
    partner()
    enter(1, 0)
    moves[0, 0][1]()
    enter(0, 0)
    moves[0, 1][1]()
    enter(0, 1)
    out_tile(0, 0, 1, 0)
    out_tile(0, 0, 1, 1)
    out_tile(0, 0, 0, 0)
    out_tile(0, 0, 1, 2)
    out_tile(0, 0, 0, 1)
    out_tile(0, 1, 0, 0)
    out_tile(0, 0, 1, 3)
    out_tile(0, 0, 0, 2)
    adapter_weights()
    collect(0, 0, 0)
    collect(0, 0, 1)
    enter(1, 1)
    collect(0, 0, 2)
    adapter_ready()
    out_tile(0, 1, 1, 0)
    out_tile(0, 1, 1, 1)
    out_tile(0, 1, 1, 2)
    collect(0, 0, 3)
    out_tile(0, 1, 0, 1)
    out_tile(0, 0, 0, 3)
    collect(0, 1, 0)
    out_tile(0, 1, 1, 3)
    out_tile(0, 1, 0, 2)
    out_tile(0, 1, 0, 3)
    collect(0, 1, 1)
    adapter_forward()
    collect(0, 1, 2)
    gather_up(0, 0)
    collect(0, 1, 3)
    turn(0)
    gather_up(0, 1)
    turn(1)
    fans.append(fan((None, blow), xad))
    moves[1, 0][1]()
    leave(0, 0)
    leave(1, 0)
    out_tile(1, 0, 0, 0)
    out_tile(1, 0, 0, 1)
    moves[1, 1][1]()
    leave(0, 1)
    out_tile(1, 0, 1, 0)
    share_on()
    out_tile(1, 0, 1, 1)
    out_tile(1, 0, 1, 2)
    out_tile(1, 0, 1, 3)
    out_tile(1, 1, 0, 0)
    out_tile(1, 1, 0, 1)
    out_tile(1, 1, 0, 2)
    collect(1, 0, 0)
    leave(1, 1)
    collect(1, 0, 2)
    out_tile(1, 1, 1, 0)
    collect(1, 0, 1)
    out_tile(1, 1, 1, 1)
    collect(1, 0, 3)
    out_tile(1, 1, 1, 2)
    out_tile(1, 1, 1, 3)
    wtile(0)
    collect(1, 1, 0)
    out_tile(1, 0, 0, 2)
    out_tile(1, 0, 0, 3)
    collect(1, 1, 1)
    collect(1, 1, 2)
    wtile(1)
    out_tile(1, 1, 0, 3)
    collect(1, 1, 3)
    adapter_back()
    gather_up(1, 0)
    gsec[span(0), :] = acc[0]
    wtile(2)
    wtile(3)
    kept += [cp.local(fi, fi_out), cp.local(fo, fo_out)]
    gather_up(1, 1)
    gsec[span(1), :] = acc[1]
    for e in kept[2:]: e.wait()
    for e in near[2:]: e.wait_recv()
    for e in late:
        if not any(e is o for o in ready): e.wait_recv()
    for e in fans: e()
    cp.close()


NEGATIVE = -1000000000.0
PADDED = 32
PREFIX = 30


def lane_half(rows):
    return lax.broadcasted_iota(jnp.int32, (rows, 128), 1) < 64

def split_heads(v):
    low = lane_half(v.shape[0])
    zero = jnp.zeros_like(v)
    return jnp.where(low, v, zero), jnp.where(low, zero, v)


def whole(ref):
    return lambda cols: ref[:, cols]


def norm_back_into(e, n, i, gain, out, ngrad, at):
    ee = e[...]
    nn = n[...]
    out[...] = norm_back(ee, nn, i[...], gain)
    ngrad[at:at + 1, :] = jnp.sum(ee * nn, axis=0, keepdims=True)
    ngrad[at + 1:at + 2, :] = jnp.sum(ee, axis=0, keepdims=True)


def repeat(n):
    row = lax.broadcasted_iota(jnp.int32, (n, 128), 0)
    col = lax.broadcasted_iota(jnp.int32, (n, 128), 1)
    return jnp.where(row == lax.rem(col, n), 1.0, 0.0).astype(bf16)

def columns(t, tile=256):
    return pl.ds(pl.multiple_of(t * tile, tile), tile)

def loop(start, stop, step):
    lax.fori_loop(start, stop, lambda t, z: (step(t), z)[1], 0)

def front_part(A, r, inputs, memory, seg_row, mem_row, embed, inner, outer, norms, ws, fin, fout, fin2, fout2, outs, scratch):
    (wout, tangent, prows_o, vecs_o, q_o, k_o, v_o, probs_o, att_o, first_o, n1_o, i1_o, cq_o, ck_o, cv_o, cprobs_o, crossed_o, slow_o, n2_o, i2_o) = outs
    (g, q, k, v, probs, att, first, flow, n1, i1, cq, ck, cv, cprobs, crossed, second, slow, n2, i2, pen, cpen,
     buf, got, zbuf, r0, r1, prows, nout, vecs, tan, ssem, rsem) = scratch
    a, b, x, c = place()
    core, xp, yp = device(a, b, x, 1 - c), device(a, b, 1 - x, c), device(a, 1 - b, x, c)
    zp = [device((a + j) % A, b, x, c) for j in range(A)]
    za = a + 1 - 2 * (a % 2)
    zq = device(za, b, x, c)
    greet([core, xp, yp, device(a, b, 1 - x, 1 - c)] + zp[1:])
    cp = Copies(ssem, rsem)
    T, D = inputs.shape
    pairs = 4
    small = {}
    def pre0():
        zbuf[a] = jnp.zeros(zbuf.shape[1:], f32)
        zbuf[a, :PREFIX, :] = dot(embed[...], inner[...])
        small["s"] = [cp(zbuf.at[a], zbuf.at[a], zp[j]) for j in range(1, A)]
    pre0()
    def row(a_, b_, x_):
        return pl.multiple_of(((a_ * 2 + b_) * 2 + x_) * 2 * r, 2 * r)
    at = pl.ds(pl.multiple_of(row(a, b, x) + c * r, r), r)
    cut = (pl.ds(0, D // 2), pl.ds(D // 2, D // 2))
    def block(i, h, a_, b_, x_):
        return g.at[2 * i + c, pl.ds(row(a_, b_, x_), 2 * r), cut[h]]
    kept = []
    own, cross = [], []
    base = cp.count
    for i in range(pairs):
        s1, s2, rr = ssem.at[cp.count], ssem.at[cp.count + 1], rsem.at[cp.count]
        cp.count += 2
        def start(keep, give):
            pltpu.make_async_copy(ws[2 * i + keep], g.at[2 * i + keep, at], s2).start()
            remote(ws[2 * i + give], g.at[2 * i + give, at], s1, rr, core).start()
        pl.when(c == 0)(functools.partial(start, 0, 1))
        pl.when(c == 1)(functools.partial(start, 1, 0))
        own.append(pltpu.make_async_copy(ws[2 * i], g.at[2 * i, at], s2))
        cross.append(remote(ws[2 * i], g.at[2 * i, at], s1, rr, core))
    G = norms.shape[0]
    me = ((a * 2 + b) * 2 + x) * 2 + c
    chip = (a * 2 + b) * 2 + x
    def nrows(start, count): return nout.at[pl.ds(pl.multiple_of(start * G, G), count * G)]
    def lanes(start, count): return prows.at[:, pl.ds(pl.multiple_of(start * 128, 128), count * 128)]
    nout[pl.ds(pl.multiple_of(me * G, G), G), :] = dot(norms[...], repeat(norms.shape[1])).astype(bf16)
    peers = (core, xp, yp)
    def settle():
        for e in small["s"]: e.wait_recv()
    def pre1():
        settle()
        t = zbuf[0]
        for n in range(1, A): t = t + zbuf[n]
        buf[0] = t
        small["s"] = [cp(buf.at[0], got.at[0], core)]
    def pre2(n):
        def go():
            settle()
            buf[n] = buf[n - 1] + got[n - 1]
            small["s"] = [cp(buf.at[n], got.at[n], peers[n])]
        return go
    def pre4():
        settle()
        t = jnp.tanh(buf[2] + got[2])
        tan[...] = t
        r0[...] = dot(dot_right(t.astype(bf16), outer[...]).astype(bf16), repeat(outer.shape[0])).astype(bf16)
        small["s"] = [cp(r0, r1, core), cp(nrows(me, 1), nrows(me, 1), core)]
        kept.append(cp.local(tan, tangent))
    def pre5():
        settle()
        lane = lax.broadcasted_iota(jnp.int32, (PADDED, 128), 1)
        prows[:, pl.ds(pl.multiple_of(chip * 128, 128), 128)] = jnp.where((lane // 64) == c, r0[...].astype(f32), r1[...].astype(f32)).astype(bf16)
        small["s"] = [cp(lanes(chip, 1), lanes(chip, 1), xp), cp(nrows(me - c, 2), nrows(me - c, 2), xp)]
    def pre6():
        settle()
        small["s"] = [cp(lanes(chip - x, 2), lanes(chip - x, 2), yp), cp(nrows(me - c - 2 * x, 4), nrows(me - c - 2 * x, 4), yp)]
    def pre7():
        settle()
        small["s"] = [cp(lanes(a * 4, 4), lanes(a * 4, 4), zp[j]) for j in range(1, A)] + [cp(nrows(a * 8, 8), nrows(a * 8, 8), zp[j]) for j in range(1, A)]
    def pre8():
        settle()
        lane = lax.broadcasted_iota(jnp.int32, (G, 128), 1) // 32
        for w in range(2 * A):
            s = nout[pl.ds(w * 4 * G, G), :].astype(f32)
            for n in range(1, 4):
                s = jnp.where(lane == n, nout[pl.ds((w * 4 + n) * G, G), :].astype(f32), s)
            vecs[:, pl.ds(w * 128, 128)] = s[:8]
        kept.append(cp.local(vecs, vecs_o))
        kept.append(cp.local(prows, prows_o))
    H = fin.shape[1]
    feeds, passed = {}, []
    def feed_send(i):
        n = D // 8
        ri = pl.ds(pl.multiple_of(c * (D // 2) + i * n, n), n)
        m = H // 8
        ro = pl.ds(pl.multiple_of(c * (H // 2) + i * m, m), m)
        ro2 = pl.ds(pl.multiple_of(H + c * (H // 2) + i * m, m), m)
        feeds[i] = [(cp(fin.at[ri], fin2.at[ri, pl.ds(H, H)], zq), fin2.at[ri, pl.ds(H, H)]),
                    (cp(fout.at[ro], fout2.at[ro2], zq), fout2.at[ro2])]
    def feed_pass(i):
        for e, ref in feeds[i]:
            e.wait_recv()
            passed.append(cp(ref, ref, core))
    zc, mc, lc, dc = {}, {}, {}, {}
    two, three = (yp, xp), (xp, yp)
    begun = set()
    def fs(i, h):
        if i not in begun:
            begun.add(i)
            own[i].wait(); cross[i].wait()
        mc[i, h, 0] = cp(block(i, h, a, b, x), block(i, h, a, b, x), two[h])
        lc[i, h, 0, 0] = cp(block(i, h, a, b, x), block(i, h, a, b, x), three[h])
    def fz(i, h):
        for j in range(1, A):
            zc[i, h, j] = cp(block(i, h, a, b, x), block(i, h, a, b, x), zp[j])
    def mid(i, h, j):
        aj = (a + A - j) % A
        zc[i, h, j].wait_recv()
        mc[i, h, j] = cp(block(i, h, aj, b, x), block(i, h, aj, b, x), two[h])
        lc[i, h, j, 0] = cp(block(i, h, aj, b, x), block(i, h, aj, b, x), three[h])
    def third(i, h, j):
        aj = (a + A - j) % A
        w = (aj, 1 - b, x) if h == 0 else (aj, b, 1 - x)
        mc[i, h, j].wait_recv()
        lc[i, h, j, 1] = cp(block(i, h, *w), block(i, h, *w), three[h])
    per = D // A
    def finish(i, j):
        aj = (a + A - j) % A
        for h in range(2):
            lc[i, h, j, 0].wait_recv(); lc[i, h, j, 1].wait_recv()
        ref = g.at[2 * i + c, pl.ds(pl.multiple_of(aj * per, per), per)]
        dc[i, j] = cp(ref, ref, core)
    def arrive(i):
        for j in range(A): dc[i, j].wait_recv()
        kept.append(cp.local(g.at[2 * i], wout.at[2 * i]))
        kept.append(cp.local(g.at[2 * i + 1], wout.at[2 * i + 1]))
    def halves(src, w, out):
        def part(n):
            def go():
                xv = src[...]
                def step(t):
                    out[:, columns(t)] = dot(xv, g[w, :, columns(t)]).astype(bf16)
                loop(2 * n, 2 * n + 2, step)
            return go
        return [part(0), part(1)]
    def masks():
        row = lax.broadcasted_iota(jnp.int32, (T, T), 0)
        col = lax.broadcasted_iota(jnp.int32, (T, T), 1)
        across = jnp.broadcast_to(seg_row[...].astype(f32), (T, T))
        down = across.T
        pen[:, :T] = jnp.where((row >= col) & (down == across), 0.0, NEGATIVE)
        lane = lax.broadcasted_iota(jnp.int32, (T, PADDED), 1)
        pen[:, T:] = jnp.where(lane < PREFIX, 0.0, NEGATIVE)
        for n in range(memory.shape[0] // T):
            span = slice(n * T, (n + 1) * T)
            cpen[:, span] = jnp.where(down == mem_row[:, span].astype(f32), 0.0, NEGATIVE)
    def softmax(qv, kk, penalty):
        score = jnp.where(penalty[...] < -1.0, NEGATIVE, dot_right(qv, kk) * 0.125)
        e = jnp.exp(score - jnp.max(score, axis=-1, keepdims=True))
        return (e * (1.0 / jnp.sum(e, axis=-1, keepdims=True))).astype(bf16)
    def own_attend(n):
        def go():
            def step(p):
                cols = columns(p, 128)
                kk = jnp.concatenate([k[:, cols], prows[:, cols]], axis=0)
                vv = jnp.concatenate([v[:, cols], prows[:, pl.ds(pl.multiple_of(D + p * 128, 128), 128)]], axis=0)
                qs, vs = split_heads(q[:, cols]), split_heads(vv)
                total = None
                for s in range(2):
                    prob = softmax(qs[s], kk, pen)
                    probs[2 * p + s] = prob
                    m = dot(prob, vs[s])
                    total = m if total is None else total + m
                att[:, cols] = total.astype(bf16)
            loop(2 * n, 2 * n + 2, step)
        return go
    def cross_scores(n):
        def go():
            def step(p):
                cols = columns(p, 128)
                qs = split_heads(cq[:, cols])
                for s in range(2):
                    cprobs[2 * p + s] = softmax(qs[s], ck[:, cols], cpen)
            loop(2 * n, 2 * n + 2, step)
        return go
    def cross_mix(n):
        def go():
            def step(p):
                cols = columns(p, 128)
                vs = split_heads(cv[:, cols])
                crossed[:, cols] = (dot(cprobs[2 * p], vs[0]) + dot(cprobs[2 * p + 1], vs[1])).astype(bf16)
            loop(4 * n, 4 * n + 4, step)
        return go
    def normed(base, low, w, at, out, nn, ii, olow):
        def part(n):
            def go():
                lv = low[...]
                def step(t):
                    out[:, columns(t)] = base[:, columns(t)].astype(f32) + dot(lv, g[w, :, columns(t)])
                loop(2 * n, 2 * n + 2, step)
            return go
        def last():
            m, inv = norm(out[...])
            nn[...] = m
            ii[...] = inv
            s = m * vecs[at:at + 1, :] + vecs[at + 1:at + 2, :]
            out[...] = s
            olow[...] = s.astype(bf16)
        return [part(0), part(1), last]
    make_q, make_k, make_v = halves(inputs, 0, q), halves(inputs, 1, k), halves(inputs, 2, v)
    make_ck, make_cq, make_cv = halves(memory, 4, ck), halves(flow, 5, cq), halves(memory, 6, cv)
    norm_one, norm_two = normed(inputs, att, 3, 0, first, n1, i1, flow), normed(first, crossed, 7, 2, second, n2, i2, slow)
    fs(0, 0)
    fs(0, 1)
    fz(0, 0)
    fs(1, 1)
    fs(1, 0)
    fz(0, 1)
    fs(3, 0)
    fs(2, 0)
    fz(1, 0)
    fs(2, 1)
    third(0, 1, 0)
    third(1, 1, 0)
    pre1()
    fs(3, 1)
    pre2(1)()
    mid(0, 0, 3)
    mid(0, 1, 1)
    third(0, 0, 0)
    mid(0, 0, 2)
    pre2(2)()
    fz(1, 1)
    mid(0, 1, 3)
    mid(0, 0, 1)
    mid(1, 0, 2)
    finish(0, 0)
    third(0, 0, 2)
    mid(1, 0, 1)
    fz(2, 0)
    pre4()
    pre5()
    third(0, 0, 1)
    mid(1, 1, 1)
    mid(0, 1, 2)
    feed_send(2)
    third(1, 0, 0)
    mid(1, 1, 2)
    third(0, 1, 1)
    mid(1, 1, 3)
    third(0, 1, 2)
    pre6()
    fz(2, 1)
    third(0, 1, 3)
    third(2, 0, 0)
    third(0, 0, 3)
    mid(1, 0, 3)
    mid(2, 1, 1)
    finish(0, 2)
    pre7()
    finish(0, 1)
    fz(3, 0)
    third(1, 0, 1)
    third(1, 1, 2)
    third(1, 0, 2)
    mid(2, 1, 2)
    third(1, 0, 3)
    mid(2, 0, 2)
    fz(3, 1)
    third(1, 1, 1)
    third(1, 1, 3)
    mid(2, 1, 3)
    finish(0, 3)
    finish(1, 0)
    finish(1, 1)
    feed_send(3)
    arrive(0)
    third(2, 1, 0)
    make_q[0]()
    finish(1, 3)
    mid(2, 0, 1)
    mid(2, 0, 3)
    finish(1, 2)
    pre8()
    third(2, 1, 2)
    feed_send(0)
    feed_send(1)
    make_q[1]()
    kept.append(cp.local(q, q_o))
    mid(3, 0, 2)
    third(2, 1, 3)
    arrive(1)
    make_k[0]()
    make_k[1]()
    kept.append(cp.local(k, k_o))
    third(2, 0, 2)
    third(2, 1, 1)
    masks()
    make_v[0]()
    mid(3, 1, 1)
    mid(3, 0, 1)
    third(2, 0, 3)
    third(2, 0, 1)
    feed_pass(2)
    mid(3, 0, 3)
    make_v[1]()
    kept.append(cp.local(v, v_o))
    own_attend(0)()
    mid(3, 1, 2)
    finish(2, 2)
    finish(2, 0)
    own_attend(1)()
    mid(3, 1, 3)
    feed_pass(3)
    own_attend(2)()
    own_attend(3)()
    kept.append(cp.local(probs, probs_o))
    kept.append(cp.local(att, att_o))
    third(3, 1, 1)
    finish(2, 3)
    norm_one[0]()
    finish(2, 1)
    third(3, 0, 1)
    third(3, 0, 0)
    third(3, 1, 0)
    norm_one[1]()
    norm_one[2]()
    kept.append(cp.local(flow, first_o))
    kept.append(cp.local(n1, n1_o))
    kept.append(cp.local(i1, i1_o))
    feed_pass(0)
    arrive(2)
    make_ck[0]()
    third(3, 0, 2)
    third(3, 1, 2)
    make_cq[0]()
    make_cq[1]()
    kept.append(cp.local(cq, cq_o))
    make_ck[1]()
    kept.append(cp.local(ck, ck_o))
    third(3, 1, 3)
    third(3, 0, 3)
    cross_scores(0)()
    finish(3, 1)
    finish(3, 0)
    cross_scores(1)()
    finish(3, 2)
    cross_scores(2)()
    finish(3, 3)
    cross_scores(3)()
    kept.append(cp.local(cprobs, cprobs_o))
    feed_pass(1)
    arrive(3)
    make_cv[0]()
    make_cv[1]()
    kept.append(cp.local(cv, cv_o))
    cross_mix(0)()
    cross_mix(1)()
    kept.append(cp.local(crossed, crossed_o))
    norm_two[0]()
    norm_two[1]()
    norm_two[2]()
    kept.append(cp.local(slow, slow_o))
    kept.append(cp.local(n2, n2_o))
    kept.append(cp.local(i2, i2_o))
    def partner():
        for e in passed: e.wait_recv()
    def finish():
        for e in kept: e.wait()
        cp.close()
    return (second, vecs, att, flow, crossed, slow), partner, finish

def forward_kernel(A, r, inputs, memory, seg_row, mem_row, embed, inner, outer, norms, cot, *refs):
    ws, (fin, fout, down, up), outs, scratch = refs[:8], refs[8:12], refs[12:44], refs[44:]
    fin2, fout2 = scratch[32:34]
    (second, vecs, att, flow, crossed, slow), partner, finish = front_part(A, r, inputs, memory, seg_row, mem_row, embed, inner, outer, norms, ws, fin, fout, fin2, fout2, outs[:20], scratch[:32])
    feed_part(A, second, vecs, cot, fin, fout, down, up, inputs, memory, att, flow, crossed, slow, partner, outs[20:], scratch[32:])
    finish()

def forward(A, r, inputs, memory, seg_row, mem_row, embed, inner, outer, norms, cot, ws, fin, fout, down, up):
    T, D = inputs.shape; M = memory.shape[0]; H = fin.shape[1]; AD = down.shape[1] * 4
    HID = 2 * H
    vm = pl.BlockSpec(memory_space=pltpu.VMEM)
    any_ = pl.BlockSpec(memory_space=pl.ANY)
    sds = jax.ShapeDtypeStruct
    v = lambda *s: pltpu.VMEM(s, bf16)
    vf = lambda *s: pltpu.VMEM(s, f32)
    row, mrow, full, one = sds((T, D), bf16), sds((M, D), bf16), sds((T, D), f32), sds((T, 1), f32)
    S = (PADDED, inner.shape[1])
    probs, cprobs = (16, T, T + PADDED), (16, T, M)
    R = T // 2
    sums = (2, 2, D // 256, R, 256)
    four = sds((4 * T, D), bf16)
    sem = pltpu.SemaphoreType.DMA
    return pl.pallas_call(functools.partial(forward_kernel, A, r),
        out_shape=(sds((8, D, D), bf16), sds(S, f32), sds((PADDED, 2 * D), bf16), sds((8, D), f32), row, row, row, sds(probs, bf16), row, row, full, one, row, mrow, mrow,
            sds(cprobs, bf16), row, row, full, one,
            row, full, sds((D, HID), bf16), sds((HID, D), bf16), sds((2, T, AD), bf16), row, sds((2, D), f32), four, four, four, sds((4 * M, D), bf16), four),
        in_specs=[vm] * 9 + [any_] * 12, out_specs=(any_,) * 20 + (vm,) * 2 + (any_,) * 2 + (vm,) * 3 + (any_,) * 5,
        scratch_shapes=[v(8, D, D), v(T, D), v(T, D), v(T, D), v(*probs), v(T, D), vf(T, D), v(T, D), vf(T, D), vf(T, 1), v(T, D), v(M, D), v(M, D), v(*cprobs), v(T, D),
            vf(T, D), v(T, D), vf(T, D), vf(T, 1), vf(T, T + PADDED), vf(T, M),
            vf(3, *S), vf(3, *S), vf(A, *S), v(PADDED, 128), v(PADDED, 128), v(PADDED, 2 * D), v(8 * A * norms.shape[0], 128), vf(8, D), vf(*S), sem((320,)), sem((320,)),
            v(D, HID), v(HID, D), v(D, HID), v(HID, D), v(D, AD), v(AD, D), v(2, 4, R, D), v(2, 4, R, D), v(2, 4, R, HID), vf(2, 4, R, HID), v(2, 4, R, HID), v(2, 4, D // 256, R, 256),
            v(*sums), v(*sums), v(*sums), vf(T, AD), vf(2, R, D), sem((128,)), sem((128,))],
        compiler_params=pltpu.CompilerParams(collective_id=1, has_side_effects=True, vmem_limit_bytes=60 << 20), name="forward")(
            inputs, memory, seg_row, mem_row, embed, inner, outer, norms, cot, *ws, fin, fout, down, up)


def exact(l, r, dims):
    return lax.dot_general(l, r, (dims, ((), ())), precision=lax.Precision.HIGHEST, preferred_element_type=f32)

def back_kernel(A, r, gsec, n2, i2, vecs, ngrad3, tangent, embed, inner, outer, *refs):
    late, (ay, weights, fi, fo, xp0, xatt, xin, xmem, xad) = refs[:11], refs[11:20]
    back_body(A, r, gsec, n2, i2, vecs, ngrad3, tangent, embed, inner, outer, late, ay, weights, fi, fo, xp0, xatt, xin, xmem, xad, *refs[20:])

def back_body(A, r, gsec, n2, i2, vecs, ngrad3, tangent, embed, inner, outer, late, ay, weights, fi, fo, xp0, xatt, xin, xmem, xad,
                igrad_o, mgrad_o, out, aout, fi_out, fo_out, outer_o, inner_o, embed_o, nsum,
                igrad, mgrad, cq, ck, cv, cprobs, n1, i1, q, k, v, probs, prows, ws, gmid, gfirst, og, mid, dcq, dck, dcv, startl, dq, dk, dv, pg,
                xb, yb, mb, mby, axb, ayb, pb, apb, fib, fob, r1, r2, r3, sb, xs, ra2, ra3, rfi, rfo, rzi, rzo, rxi, rxo, ob, aob, fib2, fob2,
                buf, got, zbuf, nbuf, ngot, nz, w0, w1, w2, w3, s0, s1, s2, nfull, pgl, ssem, rsem):
    a, b, x, c = place()
    o = 1 - c
    core, xp, yp = device(a, b, x, o), device(a, b, 1 - x, c), device(a, 1 - b, x, c)
    dp = device(a, b, 1 - x, o)
    place_n = x * 2 + c
    zp = [device((a + j) % A, b, x, c) for j in range(A)]
    za = a + 1 - 2 * (a % 2)
    zq = device(za, b, x, c)
    peers = (core, xp, yp)
    T, D = gsec.shape
    M = xmem.shape[0] // 4
    HID = fi.shape[1] // 2
    Q = fi.shape[0] // 4
    half = D // 2
    cp = Copies(ssem, rsem)
    loads = {}
    def fetch(slot, w):
        loads[slot] = cp.local(weights.at[w], ws.at[slot])
    loaded = [cp.local(src, dst) for src, dst in zip(late, (cq, ck, cv, cprobs, n1, i1, q, k, v, probs, prows))]
    def ready(start, stop):
        for e in loaded[start:stop]: e.wait()
    fetch(0, 7); fetch(1, 5); fetch(2, 3); fetch(3, 4)
    fown = []
    for xx in range(2):
        dq_ = pl.ds(pl.multiple_of((xx * 2 + c) * Q, Q), Q)
        fown += [cp.local(fi.at[dq_, :], fib.at[xx]), cp.local(fo.at[:, dq_], fob.at[xx])]
    greet([core, xp, yp, dp] + zp[1:])
    waits = {}
    aw = [cp.local(xad, axb).wait]
    xload = cp.count
    cp.count += 4
    def load_x(me):
        pltpu.make_async_copy(xp0, xb.at[0], ssem.at[xload]).start()
        pltpu.make_async_copy(xmem, mb, ssem.at[xload + 1]).start()
        pltpu.make_async_copy(xin if me else xatt, xb.at[1], ssem.at[xload + 2]).start()
        pltpu.make_async_copy(xin, xb.at[2], ssem.at[xload + 3]).start()
    pl.when(c == 0)(functools.partial(load_x, 0))
    pl.when(c == 1)(functools.partial(load_x, 1))
    waits[0] = (pltpu.make_async_copy(xp0, xb.at[0], ssem.at[xload]).wait,)
    waits[1] = (pltpu.make_async_copy(xmem, mb, ssem.at[xload + 1]).wait,)
    waits[2] = (pltpu.make_async_copy(xin, xb.at[1], ssem.at[xload + 2]).wait,)
    waits[3] = (pltpu.make_async_copy(xin, xb.at[2], ssem.at[xload + 3]).wait,)
    def share_adapter():
        quarter = ayb.shape[1]
        k = cp.count
        cp.count += 4
        here, there = pl.ds(pl.multiple_of(x * quarter, quarter), quarter), pl.ds(pl.multiple_of((1 - x) * quarter, quarter), quarter)
        spot = ayb.at[pl.ds(pl.multiple_of(place_n * T, T), T)]
        kept = pltpu.make_async_copy(ay.at[c, :, here], spot, ssem.at[k])
        ways = [remote(ay.at[c, :, there], spot, ssem.at[k + 1], rsem.at[k + 1], xp), remote(ay.at[o, :, here], spot, ssem.at[k + 2], rsem.at[k + 2], core),
                remote(ay.at[o, :, there], spot, ssem.at[k + 3], rsem.at[k + 3], dp)]
        for e in ways: e.start()
        kept.start()
        cp.all.extend(ways)
        aw.extend([kept.wait] + [e.wait_recv for e in ways])
    share_adapter()
    def share(srcs, dst, t):
        m = srcs[0].shape[0]
        k = cp.count
        cp.count += 4
        wide = half // 2
        here = pl.ds(pl.multiple_of(x * half + t * wide, wide), wide)
        there = pl.ds(pl.multiple_of((1 - x) * half + t * wide, wide), wide)
        spot = dst.at[pl.ds(pl.multiple_of(place_n * m, m), m), pl.ds(t * wide, wide)]
        def start(me):
            own, other = srcs[me], srcs[1 - me]
            remote(own.at[:, there], spot, ssem.at[k + 1], rsem.at[k + 1], xp).start()
            remote(other.at[:, there], spot, ssem.at[k + 3], rsem.at[k + 3], dp).start()
            remote(other.at[:, here], spot, ssem.at[k + 2], rsem.at[k + 2], core).start()
            pltpu.make_async_copy(own.at[:, here], spot, ssem.at[k]).start()
        pl.when(c == 0)(functools.partial(start, 0))
        pl.when(c == 1)(functools.partial(start, 1))
        ways = [remote(srcs[0].at[:, here], spot, ssem.at[k + i], rsem.at[k + i], d) for i, d in ((1, xp), (2, core), (3, dp))]
        cp.all.extend(ways)
        return (pltpu.make_async_copy(srcs[0].at[:, here], spot, ssem.at[k]).wait,) + tuple(e.wait_recv for e in ways)
    fcopies = []
    for xx in range(2):
        dq_ = pl.ds(pl.multiple_of((xx * 2 + o) * Q, Q), Q)
        fcopies += [cp(fi.at[dq_, :], rfi.at[xx], core), cp(fo.at[:, dq_], rfo.at[xx], core)]

    zf, xf, outs = [], [], []
    def feed0():
        for e in fown: e.wait()
        for e in fcopies: e.wait_recv()
        for xx in range(2):
            def rows_fi(t):
                s = pl.ds(t * 32, 32)
                fib[xx, s, :] = fib[xx, s, :] + rfi[xx, s, :]
            loop(0, Q // 32, rows_fi)
            def rows_fo(t):
                s = pl.ds(t * 64, 64)
                fob[xx, s, :] = fob[xx, s, :] + rfo[xx, s, :]
            loop(0, 2 * HID // 64, rows_fo)
        zf.extend([cp(fib.at[:, :, pl.ds(HID, HID)], rzi, zq), cp(fob.at[:, pl.ds(HID, HID), :], rzo, zq)])
    def feed1():
        for e in zf: e.wait_recv()
        for xx in range(2):
            def rows_fi(t):
                s = pl.ds(t * 32, 32)
                fib[xx, s, pl.ds(0, HID)] = fib[xx, s, pl.ds(0, HID)] + rzi[xx, s, :]
            loop(0, Q // 32, rows_fi)
            def rows_fo(t):
                s = pl.ds(t * 64, 64)
                fob[xx, s, :] = fob[xx, s, :] + rzo[xx, s, :]
            loop(0, HID // 64, rows_fo)
        xf.extend([cp(fib.at[1 - x, :, pl.ds(0, HID)], rxi, xp), cp(fob.at[1 - x, pl.ds(0, HID), :], rxo, xp)])
    def feed2():
        for e in xf: e.wait_recv()
        def rows_fi(t):
            s = pl.ds(t * 32, 32)
            fib2[s, :] = fib[x, s, pl.ds(0, HID)].astype(f32) + rxi[s, :].astype(f32)
        loop(0, Q // 32, rows_fi)
        def rows_fo(t):
            s = pl.ds(t * 64, 64)
            fob2[s, :] = fob[x, s, :].astype(f32) + rxo[s, :].astype(f32)
        loop(0, HID // 64, rows_fo)
        outs.extend([cp.local(fib2, fi_out).wait, cp.local(fob2, fo_out).wait])

    first, second, third, fourth = {}, {}, {}, {}
    wide = half // 2
    numbers = {}
    for i in range(4):
        for t in range(2):
            numbers[i, t] = cp.count
            cp.count += 1
    def level1(i, t):
        n = numbers[i, t]
        return remote(pb.at[i, t, :, 1 - b], r1.at[i, t], ssem.at[n], rsem.at[n], yp)
    for i in range(4):
        for t in range(2):
            first[i, t] = level1(i, t)
            cp.all.append(first[i, t])
    def share_one(src, dst, t, owner):
        m = src.shape[0]
        k = cp.count
        cp.count += 4
        wide = half // 2
        here = pl.ds(pl.multiple_of(x * half + t * wide, wide), wide)
        there = pl.ds(pl.multiple_of((1 - x) * half + t * wide, wide), wide)
        spot = dst.at[pl.ds(pl.multiple_of(place_n * m, m), m), pl.ds(t * wide, wide)]
        kept = pltpu.make_async_copy(src.at[:, here], spot, ssem.at[k])
        ways = [remote(src.at[:, there], spot, ssem.at[k + 1], rsem.at[k + 1], xp), remote(src.at[:, here], spot, ssem.at[k + 2], rsem.at[k + 2], core),
                remote(src.at[:, there], spot, ssem.at[k + 3], rsem.at[k + 3], dp)]
        def mine():
            ways[0].start()
            kept.start()
        def other():
            ways[2].start()
            ways[1].start()
        pl.when(c == owner)(mine)
        pl.when(c != owner)(other)
        def arrived():
            kept.wait()
            for e in ways: e.wait_recv()
        def sent():
            pl.when(c == owner)(ways[0].wait_send)
            def both():
                ways[1].wait_send()
                ways[2].wait_send()
            pl.when(c != owner)(both)
        ending.append(sent)
        return (arrived,)
    ending = []
    used, filled = set(), set()
    def compute(i, t, owner=None):
        def go():
            if (i, owner) not in used:
                used.add((i, owner))
                for e in waits[i]: e()
            for e in shared[(i, t) if owner is None else (i, t, owner)]: e()
            cols = pl.ds(t * wide, wide)
            n = (0, None, 1, 2)[i]
            def rows(u):
                d = columns(u)
                p = dot_left(mb[:, d], mby[:, cols]) if i == 1 else dot_left(xb[n, :, d], yb[n, :, cols])
                pb[i, t, u] = p.astype(bf16).reshape(2, 2, 2 * r, wide)
            loop(0, A, rows)
            level1(i, t).start()
        if owner is None: go()
        else: pl.when(c == owner)(go)
    def one(i, t):
        def go():
            first[i, t].wait_recv()
            for j in range(1, A):
                aj = (a + j) % A
                pb[i, t, aj, b] = pb[i, t, aj, b] + r1[i, t, aj]
                third[i, t, j] = cp(pb.at[i, t, aj, b], r2.at[i, t, j - 1], zp[j])
            pb[i, t, a, b] = pb[i, t, a, b] + r1[i, t, a]
        return go
    def two(i, t):
        def go():
            for j in range(1, A): third[i, t, j].wait_recv()
            for s in (1 - x, x):
                e = pb[i, t, a, b, s].astype(f32)
                for j in range(1, A): e = e + r2[i, t, j - 1, s].astype(f32)
                sb[i, t, s] = e
            xs[i, t] = sb[i, t, 1 - x].astype(bf16)
            fourth[i, t] = cp(xs.at[i, t], r3.at[i, t], xp)
        return go
    def three(i, t):
        def go():
            fourth[i, t].wait_recv()
            ob[i, :, pl.ds(pl.multiple_of(x * half + t * wide, wide), wide)] = sb[i, t, x]
            ob[i, :, pl.ds(pl.multiple_of((1 - x) * half + t * wide, wide), wide)] = r3[i, t].astype(f32)
            filled.add((i, t))
            if (i, 1 - t) in filled:
                outs.append(cp.local(ob.at[i, pl.ds(pl.multiple_of(c * r, r), r)], out.at[2 * i + c]).wait)
                outs.append(cp(ob.at[i, pl.ds(pl.multiple_of(o * r, r), r)], out.at[2 * i + c], core).wait_recv)
        return go
    def adapt0():
        for e in aw: e()
        def rows(u):
            apb[u] = dot_left(axb[:, columns(u)], ayb[...]).astype(bf16).reshape(2, D // (2 * A), ayb.shape[1])
        loop(0, A, rows)
        second["a"] = cp(apb.at[:, 1 - b], ra2, yp)
    def adapt2():
        second["a"].wait_recv()
        for j in range(1, A):
            aj = (a + j) % A
            apb[aj, b] = apb[aj, b] + ra2[aj]
            third["a", j] = cp(apb.at[aj, b], ra3.at[j - 1], zp[j])
        apb[a, b] = apb[a, b] + ra2[a]
    def adapt3():
        for j in range(1, A): third["a", j].wait_recv()
        t = apb[a, b].astype(f32)
        for j in range(1, A): t = t + ra3[j - 1].astype(f32)
        aob[0] = t[:, :128]
        aob[1] = t[:, 128:]
        outs.append(cp.local(aob.at[c], aout.at[c]).wait)
        outs.append(cp(aob.at[o], aout.at[c], core).wait_recv)
    small = {}
    def lanes(start, count): return pl.ds(pl.multiple_of(start * 128, 128), count * 128)
    def tail_norm0():
        small["n"] = [cp(nbuf.at[0], ngot.at[0], core)]
    def tail0():
        pgl[...] = pg[...].astype(bf16)
        small["w"] = [cp(pgl.at[:, lanes((a + j) % A * 4, 4)], w0.at[j - 1], zp[j]) for j in range(1, A)]
    def tail_norm(n):
        def go():
            for e in small["n"]: e.wait_recv()
            nbuf[n] = nbuf[n - 1] + ngot[n - 1]
            small["n"] = [cp(nbuf.at[n], ngot.at[n], peers[n])]
        return go
    def tail_norm3():
        for e in small["n"]: e.wait_recv()
        nz[a] = nbuf[2] + ngot[2]
        small["n"] = [cp(nz.at[a], nz.at[a], zp[j]) for j in range(1, A)]
    def tail_norm4():
        for e in small["n"]: e.wait_recv()
        t = nz[0]
        for n in range(1, A): t = t + nz[n]
        nfull[...] = t
        quad = nfull[:, pl.ds(pl.multiple_of((a * 2 + b) * 128, 128), 128)]
        piece = quad[:, :r]
        for e in range(1, 4): piece = jnp.where(place_n == e, quad[:, e * r:(e + 1) * r], piece)
        nsum[...] = piece
    def tail1():
        t = pg[:, lanes(a * 4, 4)]
        for j, e in enumerate(small["w"]):
            e.wait_recv()
            t = t + w0[j].astype(f32)
        s0[...] = t
        small["w"] = [cp(s0.at[:, lanes((1 - b) * 2, 2)], w1, yp)]
    def tail2():
        small["w"][0].wait_recv()
        s1[...] = s0[:, lanes(b * 2, 2)] + w1[...]
        small["w"] = [cp(s1.at[:, lanes(1 - x, 1)], w2, xp)]
    def tail3():
        small["w"][0].wait_recv()
        s2[...] = s1[:, lanes(x, 1)] + w2[...]
        small["w"] = [cp(s2, w3, core)]
    def tail4():
        small["w"][0].wait_recv()
        t = s2[...] + w3[...]
        mine = jnp.where(c == 0, t[:, :64], t[:, 64:])
        buf[0] = exact(mine, outer[...].astype(f32), ((1,), (0,)))
        small["w"] = [cp(buf.at[0], got.at[0], core)]
        outer_o[...] = exact(mine, tangent[...].astype(bf16).astype(f32), ((0,), (0,)))
    def tail5(n):
        def go():
            small["w"][0].wait_recv()
            buf[n] = buf[n - 1] + got[n - 1]
            small["w"] = [cp(buf.at[n], got.at[n], peers[n])]
        return go
    def tail6():
        small["w"][0].wait_recv()
        zbuf[a] = (buf[2] + got[2]).astype(bf16)
        small["w"] = [cp(zbuf.at[a], zbuf.at[a], zp[j]) for j in range(1, A)]
    def tail7():
        for e in small["w"]: e.wait_recv()
        t = zbuf[0].astype(f32)
        for n in range(1, A): t = t + zbuf[n].astype(f32)
        tan = tangent[...]
        t = t * (1.0 - tan * tan)
        inner_o[...] = exact(embed[...].astype(f32), t[:PREFIX], ((0,), (0,)))
        embed_o[...] = exact(t[:PREFIX], inner[...].astype(f32), ((1,), (1,)))
    def norm_two():
        norm_back_into(gsec, n2, i2, vecs[2:3, :], gmid, nbuf.at[0], 2)
        mid[...] = gmid[...].astype(bf16)
    def back_project(src, slot, n):
        def go():
            s = src[...]
            loop(2 * n, 2 * n + 2, lambda t: og.__setitem__((slice(None), columns(t)), dot_right(s, ws[slot, columns(t), :]).astype(bf16)))
        return go
    def wait_slot(slot):
        def go(): loads[slot].wait()
        return go
    def pair_back(p, grad, qr, kk, vv, pr):
        cols = columns(p, 128)
        qs, ks, gs = split_heads(qr[:, cols]), split_heads(kk), split_heads(grad[:, cols])
        res = None
        for s in range(2):
            low = pr[2 * p + s]
            prob = low.astype(f32)
            t = prob * dot_right(gs[s], vv)
            ds = (t - prob * jnp.sum(t, axis=-1, keepdims=True)).astype(bf16)
            m = (dot(ds, ks[s]), dot_left(ds, qs[s]), dot_left(low, gs[s]))
            res = m if res is None else tuple(e + f for e, f in zip(res, m))
        return cols, res[0] * 0.125, res[1] * 0.125, res[2]
    def cross_back(n):
        def go():
            def step(p):
                cs = columns(p, 128)
                cols, m1, m2, m3 = pair_back(p, og, cq, ck[:, cs], cv[:, cs], cprobs)
                dcq[:, cols] = m1.astype(bf16)
                dck[:, cols] = m2.astype(bf16)
                dcv[:, cols] = m3.astype(bf16)
            for p in range(2 * n, 2 * n + 2): step(p)
        return go
    def self_back(n):
        def go():
            def step(p):
                cs = columns(p, 128)
                cv_ = pl.ds(pl.multiple_of(D + p * 128, 128), 128)
                kk = jnp.concatenate([k[:, cs], prows[:, cs]], axis=0)
                vv = jnp.concatenate([v[:, cs], prows[:, cv_]], axis=0)
                cols, m1, m2, m3 = pair_back(p, og, q, kk, vv, probs)
                dq[:, cols] = m1.astype(bf16)
                dk[:, cols] = m2[:T].astype(bf16)
                dv[:, cols] = m3[:T].astype(bf16)
                pg[:, cols] = m2[T:]
                pg[:, cv_] = m3[T:]
            for p in range(2 * n, 2 * n + 2): step(p)
        return go
    def first_grad():
        s = dcq[...]
        def step(t):
            gfirst[:, columns(t)] = gmid[:, columns(t)] + dot_right(s, ws[1, columns(t), :])
        loop(0, D // 256, step)
    def norm_one():
        norm_back_into(gfirst, n1, i1, vecs[0:1, :], gmid, nbuf.at[0], 0)
        nbuf[0, 4:6, :] = ngrad3[...]
        nbuf[0, 6:8, :] = jnp.zeros((2, D), f32)
        startl[...] = gmid[...].astype(bf16)
    def memory_part(n):
        def go():
            def step(t):
                mgrad[:, columns(t)] = (dot_right(dck[...], ws[3, columns(t), :]) + dot_right(dcv[...], ws[0, columns(t), :])).astype(bf16)
            loop(2 * n, 2 * n + 2, step)
        return go
    def input_part(n):
        def go():
            def step(t):
                s = gmid[:, columns(t)] + dot_right(dq[...], ws[1, columns(t), :]) + dot_right(dk[...], ws[2, columns(t), :]) + dot_right(dv[...], ws[3, columns(t), :])
                igrad[:, columns(t)] = s.astype(bf16)
            loop(2 * n, 2 * n + 2, step)
        return go
    shared = {}
    def spread(i, srcs, dst):
        for t in range(2): shared[i, t] = share(srcs, dst, t)
    def spread_one(i, src, dst, owner):
        for t in range(2): shared[i, t, owner] = share_one(src, dst, t, owner)
    norm_two()
    spread_one(0, mid, yb.at[0], 0)
    wait_slot(0)()
    back_project(mid, 0, 0)()
    back_project(mid, 0, 1)()
    fetch(0, 6)
    ready(0, 4)
    cross_back(0)()
    feed0()
    adapt0()
    cross_back(1)()
    cross_back(2)()
    cross_back(3)()
    spread_one(0, dcq, yb.at[0], 1)
    wait_slot(1)()
    first_grad()
    fetch(1, 0)
    compute(0, 0, 0)
    spread(1, (dck, dcv), mby)
    ready(4, 6)
    norm_one()
    compute(0, 0, 1)
    adapt2()
    compute(0, 1, 0)
    compute(0, 1, 1)
    wait_slot(2)()
    back_project(startl, 2, 0)()
    spread_one(2, startl, yb.at[1], 0)
    back_project(startl, 2, 1)()
    fetch(2, 1)
    ready(6, 11)
    self_back(0)()
    one(0, 0)()
    compute(1, 0)
    self_back(1)()
    self_back(2)()
    self_back(3)()
    tail_norm0()
    tail0()
    spread(3, (dk, dv), yb.at[2])
    one(0, 1)()
    compute(1, 1)
    one(1, 0)()
    compute(2, 1, 0)
    spread_one(2, dq, yb.at[1], 1)
    feed1()
    wait_slot(3)()
    wait_slot(0)()
    memory_part(0)()
    compute(3, 1)
    tail_norm(1)()
    one(1, 1)()
    tail1()
    compute(2, 1, 1)
    memory_part(1)()
    outs.append(cp.local(mgrad, mgrad_o).wait)
    fetch(3, 2)
    one(3, 1)()
    compute(3, 0)
    wait_slot(1)()
    wait_slot(2)()
    wait_slot(3)()
    input_part(0)()
    tail2()
    compute(2, 0, 0)
    one(2, 1)()
    two(0, 0)()
    adapt3()
    tail3()
    feed2()
    tail4()
    two(0, 1)()
    tail5(1)()
    one(3, 0)()
    compute(2, 0, 1)
    two(1, 0)()
    one(2, 0)()
    tail_norm(2)()
    three(0, 1)()
    two(1, 1)()
    two(2, 1)()
    three(0, 0)()
    tail5(2)()
    three(1, 1)()
    two(3, 0)()
    tail6()
    tail_norm3()
    three(2, 1)()
    two(3, 1)()
    two(2, 0)()
    three(3, 0)()
    input_part(1)()
    outs.append(cp.local(igrad, igrad_o).wait)
    three(1, 0)()
    three(2, 0)()
    three(3, 1)()
    tail7()
    tail_norm4()
    for e in ending: e()
    for e in outs: e()
    cp.close()

def back(A, r, first, late, rest):
    gsec = first[0]
    T, D = gsec.shape; M = rest[7].shape[0] // 4
    fi, fo = rest[2:4]
    Q, H2 = fi.shape[0] // 4, fi.shape[1]
    H = H2 // 2
    half = D // 2
    v = lambda *s: pltpu.VMEM(s, bf16)
    vf = lambda *s: pltpu.VMEM(s, f32)
    any_ = pl.BlockSpec(memory_space=pl.ANY)
    vm = pl.BlockSpec(memory_space=pltpu.VMEM)
    sds = jax.ShapeDtypeStruct
    P_, N = PADDED, (8, D)
    hid = first[-2].shape[1]
    S = (P_, hid)
    return pl.pallas_call(functools.partial(back_kernel, A, r),
        out_shape=(sds((T, D), bf16), sds((M, D), bf16), sds((8, r, D), f32), sds((2, D // (2 * A), 128), f32), sds((Q, H), f32), sds((H, Q), f32),
            sds((64, hid), f32), sds((r, hid), f32), sds((PREFIX, r), f32), sds((8, r), f32)),
        in_specs=[vm] * len(first) + [any_] * (len(late) + len(rest)), out_specs=(any_,) * 6 + (vm,) * 4,
        scratch_shapes=[v(T, D), v(M, D)] + [pltpu.VMEM(e.shape, e.dtype) for e in late] + [v(4, D, D), vf(T, D), vf(T, D), v(T, D), v(T, D), v(T, D), v(M, D), v(M, D), v(T, D), v(T, D), v(T, D), v(T, D), vf(P_, 2 * D),
            v(3, 4 * T, D), v(3, 4 * T, half), v(4 * M, D), v(4 * M, half), v(4 * T, D), v(4 * T, 256),
            v(4, 2, A, 2, 2, 2 * r, half // 2), v(A, 2, D // (2 * A), 256), v(2, Q, H2), v(2, H2, Q),
            v(4, 2, A, 2, 2 * r, half // 2), v(4, 2, A - 1, 2, 2 * r, half // 2), v(4, 2, 2 * r, half // 2), vf(4, 2, 2, 2 * r, half // 2), v(4, 2, 2 * r, half // 2),
            v(A, D // (2 * A), 256), v(A - 1, D // (2 * A), 256),
            v(2, Q, H2), v(2, H2, Q), v(2, Q, H), v(2, H, Q), v(Q, H), v(H, Q),
            vf(4, 2 * r, D), vf(2, D // (2 * A), 128), vf(Q, H), vf(H, Q),
            vf(3, *S), vf(3, *S), v(A, *S), vf(3, *N), vf(3, *N), vf(A, *N), v(A - 1, P_, 512), vf(P_, 256), vf(P_, 128), vf(P_, 128), vf(P_, 512), vf(P_, 256), vf(P_, 128), vf(8, D), v(P_, 2 * D),
            pltpu.SemaphoreType.DMA((224,)), pltpu.SemaphoreType.DMA((224,))],
        compiler_params=pltpu.CompilerParams(collective_id=2, has_side_effects=True, vmem_limit_bytes=63 << 20),
        name="back")(*first, *late, *rest)

def fast_body(A, inputs, memory, cotangent, segments, memory_segments, query_self, key_self, value_self, output_self,
              query_cross, key_cross, value_cross, output_cross, self_gain, self_shift, cross_gain, cross_shift,
              final_gain, final_shift, feed_in, feed_out, adapter_down, adapter_up, prefix_embed, prefix_inner, prefix_outer):
    r = query_self.shape[0]
    blank = jnp.zeros_like(self_gain)
    norms = jnp.stack([self_gain, self_shift, cross_gain, cross_shift, final_gain, final_shift] + [blank] * 10)
    (weights, tangent, prows, vecs, q, k, v, probs, attended, first_low, n1, i1, cq, ck, cv, cprobs, crossed, second_low, n2, i2,
     result, grad_second, fi, fo, ay, branch_low, ngrad3, xp0, xatt, xin, xmem, xad) = forward(
        A, r, inputs, memory, segments.reshape(1, -1), memory_segments.reshape(1, -1), prefix_embed, prefix_inner, prefix_outer.T, norms, cotangent,
        [query_self, key_self, value_self, output_self, key_cross, query_cross, value_cross, output_cross], feed_in, feed_out, adapter_down, adapter_up)
    igrad, mgrad, sums, adapt, fi_sum, fo_sum, outer_grad, inner_grad, embed_grad, ng = back(A, r,
        (grad_second, n2, i2, vecs, ngrad3, tangent, prefix_embed, prefix_inner, prefix_outer.T), (cq, ck, cv, cprobs, n1, i1, q, k, v, probs, prows),
        (ay, weights, fi, fo, xp0, xatt, xin, xmem, xad))
    whole = deliver(result, igrad, mgrad, sums, fi_sum, fo_sum, outer_grad, inner_grad, embed_grad, adapt)
    return whole[:11] + tuple(ng[k] for k in range(6)) + whole[11:17] + (whole[17].T,)


def deliver_kernel(*refs):
    ins, outs, held, (turned, into, out_of) = refs[:10], refs[10:28], refs[28:38], refs[38:]
    loads = [pltpu.make_async_copy(src, dst, into.at[i]) for i, (src, dst) in enumerate(zip(ins, held))]
    for e in loads: e.start()
    order = (5, 6, 7, 4, 1, 2, 3, 0)
    moves = [(3, held[3].at[k], outs[3 + i]) for i, k in enumerate(order)]
    moves += [(i, held[i], outs[i]) for i in range(3)] + [(4, held[4], outs[11]), (5, held[5], outs[12]), (9, held[9].at[0], outs[13]), (9, turned, outs[14])]
    moves += [(8, held[8], outs[15]), (7, held[7], outs[16]), (6, held[6], outs[17])]
    stores, ready = [], set()
    for n, (i, src, dst) in enumerate(moves):
        if i not in ready:
            ready.add(i)
            loads[i].wait()
        if src is turned: turned[...] = held[9][1].T
        stores.append(pltpu.make_async_copy(src, dst, out_of.at[n]))
        stores[-1].start()
    for e in stores: e.wait()


def deliver(result, igrad, mgrad, sums, fi, fo, outer, inner, embed, adapt):
    ins = (result, igrad, mgrad, sums, fi, fo, outer, inner, embed, adapt)
    like = lambda e: jax.ShapeDtypeStruct(e.shape, e.dtype)
    row = jax.ShapeDtypeStruct(sums.shape[1:], f32)
    square = jax.ShapeDtypeStruct(adapt.shape[1:], f32)
    any_ = pl.BlockSpec(memory_space=pl.ANY)
    return pl.pallas_call(deliver_kernel,
        out_shape=(like(result), like(igrad), like(mgrad)) + (row,) * 8 + (like(fi), like(fo), square, square, like(embed), like(inner), like(outer)),
        in_specs=[any_] * 10, out_specs=(any_,) * 18,
        scratch_shapes=[pltpu.VMEM(e.shape, e.dtype) for e in ins] + [pltpu.VMEM(adapt.shape[1:], f32), pltpu.SemaphoreType.DMA((10,)), pltpu.SemaphoreType.DMA((18,))],
        compiler_params=pltpu.CompilerParams(vmem_limit_bytes=60 << 20), name="deliver")(*ins)


def solution(mesh):
    wide, narrow = mesh.shape[WIDE], mesh.shape[NARROW]
    fits = narrow == 4 and wide == 8
    body = functools.partial(fast_body, wide // 2) if fits else plain_body
    return jax.shard_map(
        body,
        mesh=mesh,
        in_specs=(
            P(BOTH, None),
            P(BOTH, None),
            P(BOTH, None),
            P(BOTH),
            P(BOTH),
            P(BOTH, None),
            P(BOTH, None),
            P(BOTH, None),
            P(BOTH, None),
            P(BOTH, None),
            P(BOTH, None),
            P(BOTH, None),
            P(BOTH, None),
            P(BOTH),
            P(BOTH),
            P(BOTH),
            P(BOTH),
            P(BOTH),
            P(BOTH),
            P(None, WIDE),
            P(WIDE, None),
            P(None, NARROW),
            P(NARROW, None),
            P(None, BOTH),
            P(BOTH, None),
            P(None, BOTH),
        ),
        out_specs=(
            P(BOTH, None),
            P(BOTH, None),
            P(BOTH, None),
            P(BOTH, None),
            P(BOTH, None),
            P(BOTH, None),
            P(BOTH, None),
            P(BOTH, None),
            P(BOTH, None),
            P(BOTH, None),
            P(BOTH, None),
            P(BOTH),
            P(BOTH),
            P(BOTH),
            P(BOTH),
            P(BOTH),
            P(BOTH),
            P(NARROW, WIDE),
            P(WIDE, NARROW),
            P(WIDE, NARROW),
            P(NARROW, WIDE),
            P(None, BOTH),
            P(BOTH, None),
            P(None, BOTH),
        ),
        check_vma=False,
    )
```

```python
import functools
from functools import reduce

import jax
import jax.numpy as jnp
from jax import lax
from jax.experimental import pallas as pl
from jax.experimental.pallas import tpu as pltpu
from jax.sharding import PartitionSpec as P

MESH = pl.DeviceIdType.MESH
bf16, f32 = jnp.bfloat16, jnp.float32
WIDE, NARROW = "wide", "narrow"
BOTH = (WIDE, NARROW)


HEADS = 16
HEAD = 64
PREFIX = 30


HIGHEST = lax.Precision.HIGHEST
EPSILON = 1e-05
MASKED = -1000000000.0
ADAPT_SCALE = 4.0


def matmul(left, right):
    return jnp.dot(left, right, preferred_element_type=jnp.float32)


def left_product(left, right):
    return lax.dot_general(
        left, right, (((0,), (0,)), ((), ())), preferred_element_type=jnp.float32
    )


def right_product(left, right):
    return lax.dot_general(
        left, right, (((1,), (1,)), ((), ())), preferred_element_type=jnp.float32
    )


def exact_left(left, right):
    return lax.dot_general(
        left, right, (((0,), (0,)), ((), ())), precision=HIGHEST, preferred_element_type=jnp.float32
    )


def exact_right(left, right):
    return lax.dot_general(
        left, right, (((1,), (1,)), ((), ())), precision=HIGHEST, preferred_element_type=jnp.float32
    )


def norm_forward(values, factor, offset):
    average = jnp.mean(values, axis=-1, keepdims=True)
    center = values - average
    inverse = lax.rsqrt(jnp.mean(center * center, axis=-1, keepdims=True) + EPSILON)
    normed = center * inverse
    return (normed * factor + offset, normed, inverse)


def norm_backward(grad_out, normed, inverse, factor):
    scaled = grad_out * factor
    grad_in = inverse * (
        scaled
        - jnp.mean(scaled, axis=-1, keepdims=True)
        - normed * jnp.mean(scaled * normed, axis=-1, keepdims=True)
    )
    return (grad_in, jnp.sum(grad_out * normed, axis=0), jnp.sum(grad_out, axis=0))


def head_view(rows):
    return rows.reshape(rows.shape[0], HEADS, HEAD)


def scored(queries, key_rows, allowed):
    raw = jnp.einsum(
        "shd,khd->hsk", head_view(queries), head_view(key_rows), preferred_element_type=jnp.float32
    )
    return jnp.where(allowed[None], raw * HEAD ** (-0.5), MASKED)


def attend_forward(queries, parts):
    scores = [scored(queries, member[0], member[2]) for member in parts]
    largest = reduce(jnp.maximum, [jnp.max(matrix, axis=-1, keepdims=True) for matrix in scores])
    total = reduce(
        jnp.add, [jnp.sum(jnp.exp(matrix - largest), axis=-1, keepdims=True) for matrix in scores]
    )
    logsum = largest + jnp.log(total)
    mixed = reduce(
        jnp.add,
        [
            jnp.einsum(
                "hsk,khd->shd",
                jnp.exp(matrix - logsum).astype(jnp.bfloat16),
                head_view(member[1]),
                preferred_element_type=jnp.float32,
            )
            for matrix, member in zip(scores, parts)
        ],
    )
    return (mixed.reshape(queries.shape[0], HEADS * HEAD), logsum)


def attend_backward(queries, parts, logsum, grad_low):
    grad_heads = head_view(grad_low)
    chances = [jnp.exp(scored(queries, member[0], member[2]) - logsum) for member in parts]
    slopes = [
        jnp.einsum(
            "shd,khd->hsk", grad_heads, head_view(member[1]), preferred_element_type=jnp.float32
        )
        for member in parts
    ]
    row_dot = reduce(
        jnp.add,
        [jnp.sum(chance * slope, axis=-1, keepdims=True) for chance, slope in zip(chances, slopes)],
    )
    scale = HEAD ** (-0.5)
    grad_query = jnp.zeros((queries.shape[0], HEADS, HEAD), jnp.float32)
    results = []
    for member, chance, slope in zip(parts, chances, slopes):
        dscore = (chance * (slope - row_dot)).astype(jnp.bfloat16)
        grad_query = grad_query + jnp.einsum(
            "hsk,khd->shd", dscore, head_view(member[0]), preferred_element_type=jnp.float32
        )
        grad_key = (
            jnp.einsum(
                "hsk,shd->khd", dscore, head_view(queries), preferred_element_type=jnp.float32
            )
            * scale
        )
        grad_value = jnp.einsum(
            "hsk,shd->khd",
            chance.astype(jnp.bfloat16),
            grad_heads,
            preferred_element_type=jnp.float32,
        )
        results.append(
            (
                grad_key.reshape(grad_key.shape[0], HEADS * HEAD),
                grad_value.reshape(grad_value.shape[0], HEADS * HEAD),
            )
        )
    return ((grad_query * scale).reshape(queries.shape[0], HEADS * HEAD), results)


def gelu_back(pre_values, grad_values):
    return jax.vjp(lambda inner: jax.nn.gelu(inner, approximate=False), pre_values)[1](grad_values)[
        0
    ]


def plain_body(
    inputs,
    memory,
    cotangent,
    segments,
    memory_segments,
    query_self,
    key_self,
    value_self,
    output_self,
    query_cross,
    key_cross,
    value_cross,
    output_cross,
    self_gain,
    self_shift,
    cross_gain,
    cross_shift,
    final_gain,
    final_shift,
    feed_in,
    feed_out,
    adapter_down,
    adapter_up,
    prefix_embed,
    prefix_inner,
    prefix_outer,
):
    (
        query_one,
        key_one,
        value_one,
        output_one,
        query_two,
        key_two,
        value_two,
        output_two,
        gain_one,
        shift_one,
        gain_two,
        shift_two,
        gain_three,
        shift_three,
        embed_full,
        inner_full,
        outer_full,
    ) = (
        lax.all_gather(query_self, BOTH, axis=0, tiled=True),
        lax.all_gather(key_self, BOTH, axis=0, tiled=True),
        lax.all_gather(value_self, BOTH, axis=0, tiled=True),
        lax.all_gather(output_self, BOTH, axis=0, tiled=True),
        lax.all_gather(query_cross, BOTH, axis=0, tiled=True),
        lax.all_gather(key_cross, BOTH, axis=0, tiled=True),
        lax.all_gather(value_cross, BOTH, axis=0, tiled=True),
        lax.all_gather(output_cross, BOTH, axis=0, tiled=True),
        lax.all_gather(self_gain, BOTH, axis=0, tiled=True),
        lax.all_gather(self_shift, BOTH, axis=0, tiled=True),
        lax.all_gather(cross_gain, BOTH, axis=0, tiled=True),
        lax.all_gather(cross_shift, BOTH, axis=0, tiled=True),
        lax.all_gather(final_gain, BOTH, axis=0, tiled=True),
        lax.all_gather(final_shift, BOTH, axis=0, tiled=True),
        lax.all_gather(prefix_embed, BOTH, axis=1, tiled=True),
        lax.all_gather(prefix_inner, BOTH, axis=0, tiled=True),
        lax.all_gather(prefix_outer, BOTH, axis=1, tiled=True),
    )
    factor_one = gain_one.astype(jnp.float32)
    factor_two = gain_two.astype(jnp.float32)
    factor_three = gain_three.astype(jnp.float32)
    length = inputs.shape[0]
    width = inputs.shape[1]
    places = jnp.arange(length)
    causal = places[:, None] >= places[None, :]
    local_mask = (segments[:, None] == segments[None, :]) & causal
    prefix_mask = jnp.ones((length, PREFIX), jnp.bool_)
    cross_mask = segments[:, None] == memory_segments[None, :]
    tangent = jnp.tanh(matmul(embed_full, inner_full))
    tangent_low = tangent.astype(jnp.bfloat16)
    prefix_rows = matmul(tangent_low, outer_full).astype(jnp.bfloat16)
    prefix_keys = prefix_rows[:, :width]
    prefix_values = prefix_rows[:, width:]
    queries = matmul(inputs, query_one).astype(jnp.bfloat16)
    key_rows = matmul(inputs, key_one).astype(jnp.bfloat16)
    value_rows = matmul(inputs, value_one).astype(jnp.bfloat16)
    self_parts = ((prefix_keys, prefix_values, prefix_mask), (key_rows, value_rows, local_mask))
    attended, self_logsum = attend_forward(queries, self_parts)
    attended_low = attended.astype(jnp.bfloat16)
    first, normed_one, inverse_one = norm_forward(
        inputs.astype(jnp.float32) + matmul(attended_low, output_one),
        factor_one,
        shift_one.astype(jnp.float32),
    )
    first_low = first.astype(jnp.bfloat16)
    cross_queries = matmul(first_low, query_two).astype(jnp.bfloat16)
    cross_keys = matmul(memory, key_two).astype(jnp.bfloat16)
    cross_values = matmul(memory, value_two).astype(jnp.bfloat16)
    cross_parts = ((cross_keys, cross_values, cross_mask),)
    crossed, cross_logsum = attend_forward(cross_queries, cross_parts)
    crossed_low = crossed.astype(jnp.bfloat16)
    second, normed_two, inverse_two = norm_forward(
        first + matmul(crossed_low, output_two), factor_two, shift_two.astype(jnp.float32)
    )
    second_low = second.astype(jnp.bfloat16)
    feed_rows = lax.all_gather(second_low, WIDE, axis=0, tiled=True)
    hidden_pre = matmul(feed_rows, feed_in)
    hidden_low = jax.nn.gelu(hidden_pre, approximate=False).astype(jnp.bfloat16)
    feed_sum = lax.psum_scatter(
        matmul(hidden_low, feed_out), WIDE, scatter_dimension=0, tiled=True
    )
    adapt_rows = lax.all_gather(second_low, NARROW, axis=0, tiled=True)
    bottle_pre = matmul(adapt_rows, adapter_down)
    bottle_low = jax.nn.gelu(bottle_pre, approximate=False).astype(jnp.bfloat16)
    adapt_sum = lax.psum_scatter(
        matmul(bottle_low, adapter_up).astype(jnp.bfloat16),
        NARROW,
        scatter_dimension=0,
        tiled=True,
    ).astype(jnp.float32)
    branch = feed_sum + ADAPT_SCALE * adapt_sum
    result, normed_three, inverse_three = norm_forward(
        second + branch, factor_three, shift_three.astype(jnp.float32)
    )
    grad_branch, gain_three_grad, shift_three_grad = norm_backward(
        cotangent.astype(jnp.float32), normed_three, inverse_three, factor_three
    )
    branch_low = grad_branch.astype(jnp.bfloat16)
    branch_rows = lax.all_gather(branch_low, WIDE, axis=0, tiled=True)
    grad_hidden = right_product(branch_rows, feed_out)
    grad_pre = gelu_back(hidden_pre, grad_hidden).astype(jnp.bfloat16)
    grad_out_part = left_product(hidden_low, branch_rows)
    grad_in_part = left_product(feed_rows, grad_pre)
    grad_feed = lax.psum_scatter(
        right_product(grad_pre, feed_in), WIDE, scatter_dimension=0, tiled=True
    )
    feed_in_total, feed_out_total = (
        lax.psum_scatter(
            grad_in_part.astype(jnp.bfloat16), NARROW, scatter_dimension=0, tiled=True
        ).astype(jnp.float32),
        lax.psum_scatter(
            grad_out_part.astype(jnp.bfloat16), NARROW, scatter_dimension=1, tiled=True
        ).astype(jnp.float32),
    )
    branch_narrow = lax.all_gather(branch_low, NARROW, axis=0, tiled=True)
    grad_bottle = ADAPT_SCALE * right_product(branch_narrow, adapter_up)
    grad_bottle_pre = gelu_back(bottle_pre, grad_bottle).astype(jnp.bfloat16)
    grad_up_part = ADAPT_SCALE * left_product(bottle_low, branch_narrow)
    grad_down_part = left_product(adapt_rows, grad_bottle_pre)
    grad_adapt = lax.psum_scatter(
        right_product(grad_bottle_pre, adapter_down).astype(jnp.bfloat16),
        NARROW,
        scatter_dimension=0,
        tiled=True,
    ).astype(jnp.float32)
    down_total, up_total = (
        lax.psum_scatter(grad_down_part, WIDE, scatter_dimension=0, tiled=True),
        lax.psum_scatter(grad_up_part, WIDE, scatter_dimension=1, tiled=True),
    )
    grad_second = grad_branch + grad_feed + grad_adapt
    grad_mid, gain_two_grad, shift_two_grad = norm_backward(
        grad_second, normed_two, inverse_two, factor_two
    )
    mid_low = grad_mid.astype(jnp.bfloat16)
    output_two_grad = left_product(crossed_low, mid_low)
    crossed_grad = right_product(mid_low, output_two).astype(jnp.bfloat16)
    cross_query_grad, cross_results = attend_backward(
        cross_queries, cross_parts, cross_logsum, crossed_grad
    )
    cross_query_low = cross_query_grad.astype(jnp.bfloat16)
    cross_key_low = cross_results[0][0].astype(jnp.bfloat16)
    cross_value_low = cross_results[0][1].astype(jnp.bfloat16)
    query_two_grad = left_product(first_low, cross_query_low)
    key_two_grad = left_product(memory, cross_key_low)
    value_two_grad = left_product(memory, cross_value_low)
    memory_grad = (
        right_product(cross_key_low, key_two) + right_product(cross_value_low, value_two)
    ).astype(jnp.bfloat16)
    grad_first = grad_mid + right_product(cross_query_low, query_two)
    grad_start, gain_one_grad, shift_one_grad = norm_backward(
        grad_first, normed_one, inverse_one, factor_one
    )
    start_low = grad_start.astype(jnp.bfloat16)
    output_one_grad = left_product(attended_low, start_low)
    attended_grad = right_product(start_low, output_one).astype(jnp.bfloat16)
    self_query_grad, self_results = attend_backward(queries, self_parts, self_logsum, attended_grad)
    self_query_low = self_query_grad.astype(jnp.bfloat16)
    self_key_low = self_results[1][0].astype(jnp.bfloat16)
    self_value_low = self_results[1][1].astype(jnp.bfloat16)
    query_one_grad = left_product(inputs, self_query_low)
    key_one_grad = left_product(inputs, self_key_low)
    value_one_grad = left_product(inputs, self_value_low)
    inputs_grad = (
        grad_start
        + right_product(self_query_low, query_one)
        + right_product(self_key_low, key_one)
        + right_product(self_value_low, value_one)
    ).astype(jnp.bfloat16)
    prefix_grad = jnp.concatenate([self_results[0][0], self_results[0][1]], axis=1)
    outer_grad = exact_left(tangent_low.astype(jnp.float32), prefix_grad)
    tangent_grad = exact_right(prefix_grad, outer_full.astype(jnp.float32)) * (
        1.0 - tangent * tangent
    )
    inner_grad = exact_left(embed_full.astype(jnp.float32), tangent_grad)
    embed_grad = exact_right(tangent_grad, inner_full.astype(jnp.float32))
    (
        query_one_sum,
        key_one_sum,
        value_one_sum,
        output_one_sum,
        query_two_sum,
        key_two_sum,
        value_two_sum,
        output_two_sum,
        gain_one_sum,
        shift_one_sum,
        gain_two_sum,
        shift_two_sum,
        gain_three_sum,
        shift_three_sum,
        embed_sum,
        inner_sum,
        outer_sum,
    ) = (
        lax.psum_scatter(query_one_grad, BOTH, scatter_dimension=0, tiled=True),
        lax.psum_scatter(key_one_grad, BOTH, scatter_dimension=0, tiled=True),
        lax.psum_scatter(value_one_grad, BOTH, scatter_dimension=0, tiled=True),
        lax.psum_scatter(output_one_grad, BOTH, scatter_dimension=0, tiled=True),
        lax.psum_scatter(query_two_grad, BOTH, scatter_dimension=0, tiled=True),
        lax.psum_scatter(key_two_grad, BOTH, scatter_dimension=0, tiled=True),
        lax.psum_scatter(value_two_grad, BOTH, scatter_dimension=0, tiled=True),
        lax.psum_scatter(output_two_grad, BOTH, scatter_dimension=0, tiled=True),
        lax.psum_scatter(gain_one_grad, BOTH, scatter_dimension=0, tiled=True),
        lax.psum_scatter(shift_one_grad, BOTH, scatter_dimension=0, tiled=True),
        lax.psum_scatter(gain_two_grad, BOTH, scatter_dimension=0, tiled=True),
        lax.psum_scatter(shift_two_grad, BOTH, scatter_dimension=0, tiled=True),
        lax.psum_scatter(gain_three_grad, BOTH, scatter_dimension=0, tiled=True),
        lax.psum_scatter(shift_three_grad, BOTH, scatter_dimension=0, tiled=True),
        lax.psum_scatter(embed_grad, BOTH, scatter_dimension=1, tiled=True),
        lax.psum_scatter(inner_grad, BOTH, scatter_dimension=0, tiled=True),
        lax.psum_scatter(outer_grad, BOTH, scatter_dimension=1, tiled=True),
    )
    return (
        result.astype(jnp.bfloat16),
        inputs_grad,
        memory_grad,
        query_one_sum,
        key_one_sum,
        value_one_sum,
        output_one_sum,
        query_two_sum,
        key_two_sum,
        value_two_sum,
        output_two_sum,
        gain_one_sum,
        shift_one_sum,
        gain_two_sum,
        shift_two_sum,
        gain_three_sum,
        shift_three_sum,
        feed_in_total,
        feed_out_total,
        down_total,
        up_total,
        embed_sum,
        inner_sum,
        outer_sum,
    )


def place():
    w = lax.axis_index(WIDE); n = lax.axis_index(NARROW)
    return w // 2, w % 2, n // 2, n % 2

def device(a, b, x, c):
    return (a * 2 + b, x * 2 + c)

def greet(peers):
    barrier = pltpu.get_barrier_semaphore()
    for p in peers:
        pl.semaphore_signal(barrier, inc=1, device_id=p, device_id_type=MESH)
    pl.semaphore_wait(barrier, len(peers))

def remote(src, dst, send, recv, dev):
    return pltpu.make_async_remote_copy(src_ref=src, dst_ref=dst, send_sem=send, recv_sem=recv, device_id=dev, device_id_type=MESH)


def dot_left(l, r):
    return lax.dot_general(l, r, (((0,), (0,)), ((), ())), preferred_element_type=f32)

class Copies:
    def __init__(self, send, recv):
        self.send, self.recv, self.count, self.all = send, recv, 0, []
    def __call__(self, src, dst, dev):
        cp = remote(src, dst, self.send.at[self.count], self.recv.at[self.count], dev)
        self.count += 1
        cp.start(); self.all.append(cp)
        return cp
    def local(self, src, dst):
        cp = pltpu.make_async_copy(src, dst, self.send.at[self.count])
        self.count += 1
        cp.start()
        return cp
    def sent(self, some):
        for cp in some:
            cp.wait_send()
            self.all = [o for o in self.all if o is not cp]
    def close(self):
        for cp in self.all: cp.wait_send()


EPSILON = 1e-05
ADAPT_SCALE = 4.0

def dot(l, r):
    return jnp.dot(l, r, preferred_element_type=f32)

def dot_right(l, r):
    return lax.dot_general(l, r, (((1,), (1,)), ((), ())), preferred_element_type=f32)

def gelu_both(v):
    phi = 0.5 + 0.5 * lax.erf(v * 0.7071067811865476)
    return v * phi, phi + v * (0.3989422804014327 * jnp.exp(-0.5 * v * v))

def norm(v):
    center = v - jnp.mean(v, axis=-1, keepdims=True)
    inverse = lax.rsqrt(jnp.mean(center * center, axis=-1, keepdims=True) + EPSILON)
    return center * inverse, inverse

def norm_back(e, n, inverse, factor):
    s = e * factor
    return inverse * (s - jnp.mean(s, axis=-1, keepdims=True) - n * jnp.mean(s * n, axis=-1, keepdims=True))

def feed_part(A, second, vecs, cot, fin_own, fout_own, down_ref, up_ref, inputs, memory, att, flow, crossed, slow, partner, outs, scratch):
    result, gsec, fi_out, fo_out, ay, blow, ngrad, xp0, xatt, xin, xmem, xad = outs
    fin, fout, fi, fo, down, up, rows, brow, hid, slope, gpre, part, q1, q2, q3, bslope, acc, ssem, rsem = scratch
    a, b, x, c = place()
    o = 1 - c
    yp = device(a, 1 - b, x, c)
    zp = device((a + A // 2) % A, b, x, c)
    core, xp, dp = device(a, b, x, o), device(a, b, 1 - x, c), device(a, b, 1 - x, o)
    cp = Copies(ssem, rsem)
    half = fin_own.shape[1]
    loads = [cp.local(fin_own, fin.at[:, pl.ds(0, half)]), cp.local(fout_own, fout.at[pl.ds(0, half)])]
    T, D = second.shape
    NC, R = 2, T // 2
    C = R // NC
    HID = fin.shape[1]; TW = 256
    NT = D // TW
    def span(h): return pl.ds(h * R, R)

    def spread(buf, h):
        zs, ys, passed = [], [], []
        for u in range(NC):
            s = pl.ds(u * C, C)
            zs.append(cp(buf.at[h, 0, s], buf.at[h, 2, s], zp))
        for u in range(NC):
            s = pl.ds(u * C, C)
            ys.append(cp(buf.at[h, 0, s], buf.at[h, 1, s], yp))
        def beside():
            for e in ys: e.wait_recv()
        def forward():
            for u in range(NC):
                s = pl.ds(u * C, C)
                zs[u].wait_recv()
                passed.append(cp(buf.at[h, 2, s], buf.at[h, 3, s], yp))
        def across():
            for e in passed: e.wait_recv()
        return beside, forward, across

    sums, onward = {}, {}
    def send_part(level, h, j, t):
        sums[level, h, j, t] = cp(part.at[h, j, t], (q3 if j == 3 else q1).at[level, h, t], yp)
    def collect(level, h, t):
        sums[level, h, 3, t].wait_recv()
        part[h, 2, t] = part[h, 2, t] + q3[level, h, t]
        onward[level, h, t] = cp(part.at[h, 2, t], q2.at[level, h, t], zp)
    def gather_up(level, h):
        for t in range(NT):
            cols = pl.ds(t * TW, TW)
            sums[level, h, 1, t].wait_recv(); onward[level, h, t].wait_recv()
            acc[h, :, cols] = acc[h, :, cols] + q1[level, h, t].astype(f32) + q2[level, h, t].astype(f32)
        cp.sent([onward[level, h, t] for t in range(NT)] + [sums[level, h, j, t] for j in (1, 3) for t in range(NT)])

    for h in range(2): rows[h, 0] = second[span(h), :].astype(bf16)
    moves = {(0, h): spread(rows, h) for h in range(2)}
    AD = down_ref.shape[1]
    n = x * 2 + c
    nd = pl.ds(pl.multiple_of(n * AD, AD), AD)
    md = pl.ds(pl.multiple_of((2 - 2 * x + c) * AD, AD), AD)
    kept, late = [cp.local(down_ref, down.at[:, nd]), cp.local(up_ref, up.at[nd])], []
    over = [cp(down_ref, down.at[:, nd], xp), cp(up_ref, up.at[nd], xp)]
    near = [cp(down_ref, down.at[:, nd], core), cp(up_ref, up.at[nd], core)]
    def rowsn(ref, m, place): return ref.at[pl.ds(pl.multiple_of(place * m, m), m)]
    def fan(srcs, dst, only=False):
        k = cp.count
        cp.count += 4
        def start(me):
            own, other = srcs[me], srcs[1 - me]
            if own is not None:
                pltpu.make_async_copy(own, rowsn(dst, T, n), ssem.at[k]).start()
                remote(own, rowsn(dst, T, n), ssem.at[k + 1], rsem.at[k + 1], xp).start()
            if other is not None:
                remote(other, rowsn(dst, T, n), ssem.at[k + 2], rsem.at[k + 2], core).start()
                remote(other, rowsn(dst, T, n), ssem.at[k + 3], rsem.at[k + 3], dp).start()
        def finish(me):
            own, other = srcs[me], srcs[1 - me]
            src = own if own is not None else other
            ways = [remote(src, rowsn(dst, T, n), ssem.at[k + i], rsem.at[k + i], d) for i, d in ((1, xp), (2, core), (3, dp))]
            if own is not None:
                pltpu.make_async_copy(own, rowsn(dst, T, n), ssem.at[k]).wait()
                ways[0].wait_send()
                for e in ways: e.wait_recv()
            if other is not None:
                ways[1].wait_send(); ways[2].wait_send()
        pl.when(c == 0)(functools.partial(start, 0))
        pl.when(c == 1)(functools.partial(start, 1))
        def done():
            pl.when(c == 0)(functools.partial(finish, 0))
            pl.when(c == 1)(functools.partial(finish, 1))
        return done
    fans = [fan((crossed, flow), xp0), fan((att, None), xatt)]
    M = memory.shape[0]
    share = []
    for src, dst, m in ((inputs, xin, T), (memory, xmem, M)):
        kept.append(cp.local(src, rowsn(dst, m, n)))
        near.append(cp(src, rowsn(dst, m, n), core))
        share.append((cp(src, rowsn(dst, m, n), xp), rowsn(dst, m, 2 - 2 * x + c)))
    fans.append(fan((slow, None), xad))
    def adapter_weights():
        kept[0].wait(); kept[1].wait()
        for e, ref in zip(over, (down.at[:, md], up.at[md])):
            e.wait_recv()
            late.append(cp(ref, ref, core))
        ready.extend(late[:2])
    ready = []
    def adapter_ready():
        near[0].wait_recv(); near[1].wait_recv()
        for e in ready: e.wait_recv()
    def share_on():
        for e, ref in share:
            e.wait_recv()
            late.append(cp(ref, ref, core))
    def adapter_forward():
        own = rows[:, 0].reshape(T, D)
        for t in range(2):
            cols = pl.ds(t * 256, 256)
            g, s = gelu_both(dot(own, down[:, cols]))
            ay[1, :, cols] = (ADAPT_SCALE * g.astype(bf16).astype(f32)).astype(bf16)
            bslope[:, cols] = s
        def tile(t, _):
            cols = pl.ds(pl.multiple_of(t * 256, 256), 256)
            acc[:, :, cols] = acc[:, :, cols] + dot(ay[1], up[:, cols]).reshape(2, R, 256)
            return 0
        lax.fori_loop(0, D // 256, tile, 0)
    def adapter_back():
        def tile(t, _):
            cols = pl.ds(pl.multiple_of(t * 256, 256), 256)
            gbot = bslope[:, cols] * (ADAPT_SCALE * dot_right(brow[:, 0].reshape(T, D), up[cols, :]))
            ay[0, :, cols] = gbot.astype(bf16)
            return 0
        lax.fori_loop(0, down.shape[1] // 256, tile, 0)
        def tile2(t, _):
            cols = pl.ds(pl.multiple_of(t * 256, 256), 256)
            acc[:, :, cols] = acc[:, :, cols] + dot_right(ay[0], down[cols, :]).reshape(2, R, 256)
            return 0
        lax.fori_loop(0, D // 256, tile2, 0)
    def both(buf, h, g): return buf[h, 2 * g:2 * g + 2].reshape(2 * R, buf.shape[3])
    def put_out(level, h, g, t, p):
        cols = pl.ds(t * TW, TW)
        if g == 0:
            acc[h, :, cols] = p[:R] if level == 0 else acc[h, :, cols] + p[:R]
            part[h, 1, t] = p[R:].astype(bf16)
            send_part(level, h, 1, t)
        else:
            part[h, 3, t] = p[R:].astype(bf16)
            send_part(level, h, 3, t)
            part[h, 2, t] = p[:R].astype(bf16)
    def enter(h, g):
        moves[0, h][2 * g]()
        xv = both(rows, h, g)
        def tile(t, _):
            cols = pl.ds(pl.multiple_of(t * TW, TW), TW)
            e, s = gelu_both(dot(xv, fin[:, cols]))
            hid[h, 2 * g:2 * g + 2, :, cols] = e.astype(bf16).reshape(2, R, TW)
            slope[h, 2 * g:2 * g + 2, :, cols] = s.reshape(2, R, TW)
            return 0
        lax.fori_loop(0, HID // TW, tile, 0)
    def leave(h, g):
        moves[1, h][2 * g]()
        xv = both(brow, h, g)
        def tile(t, _):
            cols = pl.ds(pl.multiple_of(t * TW, TW), TW)
            gh = dot_right(xv, fout[cols, :])
            gpre[h, 2 * g:2 * g + 2, :, cols] = (slope[h, 2 * g:2 * g + 2, :, cols].reshape(2 * R, TW) * gh).astype(bf16).reshape(2, R, TW)
            return 0
        lax.fori_loop(0, HID // TW, tile, 0)
    def out_tile(level, h, g, t):
        cols = pl.ds(t * TW, TW)
        put_out(level, h, g, t, dot_right(both(gpre, h, g), fin[cols, :]) if level else dot(both(hid, h, g), fout[:, cols]))
    fac, off = vecs[4:5, :], vecs[5:6, :]
    def turn(h):
        n3, inv3 = norm(second[span(h), :] + acc[h])
        result[span(h), :] = (n3 * fac + off).astype(bf16)
        e = cot[span(h), :].astype(f32)
        gb = norm_back(e, n3, inv3, fac)
        gbl = gb.astype(bf16)
        brow[h, 0] = gbl
        moves[1, h] = spread(brow, h)
        blow[span(h), :] = gbl
        acc[h] = gb
        gg, gs = jnp.sum(e * n3, axis=0, keepdims=True), jnp.sum(e, axis=0, keepdims=True)
        ngrad[0:1, :] = gg if h == 0 else ngrad[0:1, :] + gg
        ngrad[1:2, :] = gs if h == 0 else ngrad[1:2, :] + gs
    def wtile(t):
        cols = pl.ds(t * TW, TW)
        fi[:, cols] = dot_left(rows[...].reshape(4 * T, D), gpre[:, :, :, cols].reshape(4 * T, TW)).astype(bf16)
        fo[:, cols] = dot_left(hid[...].reshape(4 * T, HID), brow[:, :, :, cols].reshape(4 * T, TW)).astype(bf16)
    for e in loads: e.wait()
    partner()
    enter(1, 0)
    moves[0, 0][1]()
    enter(0, 0)
    moves[0, 1][1]()
    enter(0, 1)
    out_tile(0, 0, 1, 0)
    out_tile(0, 0, 1, 1)
    out_tile(0, 0, 0, 0)
    out_tile(0, 0, 1, 2)
    out_tile(0, 0, 0, 1)
    out_tile(0, 1, 0, 0)
    out_tile(0, 0, 1, 3)
    out_tile(0, 0, 0, 2)
    adapter_weights()
    collect(0, 0, 0)
    collect(0, 0, 1)
    enter(1, 1)
    collect(0, 0, 2)
    adapter_ready()
    out_tile(0, 1, 1, 0)
    out_tile(0, 1, 1, 1)
    out_tile(0, 1, 1, 2)
    collect(0, 0, 3)
    out_tile(0, 1, 0, 1)
    out_tile(0, 0, 0, 3)
    collect(0, 1, 0)
    out_tile(0, 1, 1, 3)
    out_tile(0, 1, 0, 2)
    out_tile(0, 1, 0, 3)
    collect(0, 1, 1)
    adapter_forward()
    collect(0, 1, 2)
    gather_up(0, 0)
    collect(0, 1, 3)
    turn(0)
    gather_up(0, 1)
    turn(1)
    fans.append(fan((None, blow), xad))
    moves[1, 0][1]()
    leave(0, 0)
    leave(1, 0)
    out_tile(1, 0, 0, 0)
    out_tile(1, 0, 0, 1)
    moves[1, 1][1]()
    leave(0, 1)
    out_tile(1, 0, 1, 0)
    share_on()
    out_tile(1, 0, 1, 1)
    out_tile(1, 0, 1, 2)
    out_tile(1, 0, 1, 3)
    out_tile(1, 1, 0, 0)
    out_tile(1, 1, 0, 1)
    out_tile(1, 1, 0, 2)
    collect(1, 0, 0)
    leave(1, 1)
    collect(1, 0, 2)
    out_tile(1, 1, 1, 0)
    collect(1, 0, 1)
    out_tile(1, 1, 1, 1)
    collect(1, 0, 3)
    out_tile(1, 1, 1, 2)
    out_tile(1, 1, 1, 3)
    wtile(0)
    collect(1, 1, 0)
    out_tile(1, 0, 0, 2)
    out_tile(1, 0, 0, 3)
    collect(1, 1, 1)
    collect(1, 1, 2)
    wtile(1)
    out_tile(1, 1, 0, 3)
    collect(1, 1, 3)
    adapter_back()
    gather_up(1, 0)
    gsec[span(0), :] = acc[0]
    wtile(2)
    wtile(3)
    kept += [cp.local(fi, fi_out), cp.local(fo, fo_out)]
    gather_up(1, 1)
    gsec[span(1), :] = acc[1]
    for e in kept[2:]: e.wait()
    for e in near[2:]: e.wait_recv()
    for e in late:
        if not any(e is o for o in ready): e.wait_recv()
    for e in fans: e()
    cp.close()


NEGATIVE = -1000000000.0
PADDED = 32
PREFIX = 30


def lane_half(rows):
    return lax.broadcasted_iota(jnp.int32, (rows, 128), 1) < 64

def split_heads(v):
    low = lane_half(v.shape[0])
    zero = jnp.zeros_like(v)
    return jnp.where(low, v, zero), jnp.where(low, zero, v)


def whole(ref):
    return lambda cols: ref[:, cols]


def norm_back_into(e, n, i, gain, out, ngrad, at):
    ee = e[...]
    nn = n[...]
    out[...] = norm_back(ee, nn, i[...], gain)
    ngrad[at:at + 1, :] = jnp.sum(ee * nn, axis=0, keepdims=True)
    ngrad[at + 1:at + 2, :] = jnp.sum(ee, axis=0, keepdims=True)


def repeat(n):
    row = lax.broadcasted_iota(jnp.int32, (n, 128), 0)
    col = lax.broadcasted_iota(jnp.int32, (n, 128), 1)
    return jnp.where(row == lax.rem(col, n), 1.0, 0.0).astype(bf16)

def columns(t, tile=256):
    return pl.ds(pl.multiple_of(t * tile, tile), tile)

def loop(start, stop, step):
    lax.fori_loop(start, stop, lambda t, z: (step(t), z)[1], 0)

def front_part(A, r, inputs, memory, seg_row, mem_row, embed, inner, outer, norms, ws, fin, fout, fin2, fout2, outs, scratch):
    (wout, tangent, prows_o, vecs_o, q_o, k_o, v_o, probs_o, att_o, first_o, n1_o, i1_o, cq_o, ck_o, cv_o, cprobs_o, crossed_o, slow_o, n2_o, i2_o) = outs
    (g, q, k, v, probs, att, first, flow, n1, i1, cq, ck, cv, cprobs, crossed, second, slow, n2, i2, pen, cpen,
     buf, got, zbuf, r0, r1, prows, nout, vecs, tan, ssem, rsem) = scratch
    a, b, x, c = place()
    core, xp, yp = device(a, b, x, 1 - c), device(a, b, 1 - x, c), device(a, 1 - b, x, c)
    zp = [device((a + j) % A, b, x, c) for j in range(A)]
    za = a + 1 - 2 * (a % 2)
    zq = device(za, b, x, c)
    greet([core, xp, yp, device(a, b, 1 - x, 1 - c)] + zp[1:])
    cp = Copies(ssem, rsem)
    T, D = inputs.shape
    pairs = 4
    small = {}
    def pre0():
        zbuf[a] = jnp.zeros(zbuf.shape[1:], f32)
        zbuf[a, :PREFIX, :] = dot(embed[...], inner[...])
        small["s"] = [cp(zbuf.at[a], zbuf.at[a], zp[j]) for j in range(1, A)]
    pre0()
    def row(a_, b_, x_):
        return pl.multiple_of(((a_ * 2 + b_) * 2 + x_) * 2 * r, 2 * r)
    at = pl.ds(pl.multiple_of(row(a, b, x) + c * r, r), r)
    cut = (pl.ds(0, D // 2), pl.ds(D // 2, D // 2))
    def block(i, h, a_, b_, x_):
        return g.at[2 * i + c, pl.ds(row(a_, b_, x_), 2 * r), cut[h]]
    kept = []
    own, cross = [], []
    base = cp.count
    for i in range(pairs):
        s1, s2, rr = ssem.at[cp.count], ssem.at[cp.count + 1], rsem.at[cp.count]
        cp.count += 2
        def start(keep, give):
            pltpu.make_async_copy(ws[2 * i + keep], g.at[2 * i + keep, at], s2).start()
            remote(ws[2 * i + give], g.at[2 * i + give, at], s1, rr, core).start()
        pl.when(c == 0)(functools.partial(start, 0, 1))
        pl.when(c == 1)(functools.partial(start, 1, 0))
        own.append(pltpu.make_async_copy(ws[2 * i], g.at[2 * i, at], s2))
        cross.append(remote(ws[2 * i], g.at[2 * i, at], s1, rr, core))
    G = norms.shape[0]
    me = ((a * 2 + b) * 2 + x) * 2 + c
    chip = (a * 2 + b) * 2 + x
    def nrows(start, count): return nout.at[pl.ds(pl.multiple_of(start * G, G), count * G)]
    def lanes(start, count): return prows.at[:, pl.ds(pl.multiple_of(start * 128, 128), count * 128)]
    nout[pl.ds(pl.multiple_of(me * G, G), G), :] = dot(norms[...], repeat(norms.shape[1])).astype(bf16)
    peers = (core, xp, yp)
    def settle():
        for e in small["s"]: e.wait_recv()
    def pre1():
        settle()
        t = zbuf[0]
        for n in range(1, A): t = t + zbuf[n]
        buf[0] = t
        small["s"] = [cp(buf.at[0], got.at[0], core)]
    def pre2(n):
        def go():
            settle()
            buf[n] = buf[n - 1] + got[n - 1]
            small["s"] = [cp(buf.at[n], got.at[n], peers[n])]
        return go
    def pre4():
        settle()
        t = jnp.tanh(buf[2] + got[2])
        tan[...] = t
        r0[...] = dot(dot_right(t.astype(bf16), outer[...]).astype(bf16), repeat(outer.shape[0])).astype(bf16)
        small["s"] = [cp(r0, r1, core), cp(nrows(me, 1), nrows(me, 1), core)]
        kept.append(cp.local(tan, tangent))
    def pre5():
        settle()
        lane = lax.broadcasted_iota(jnp.int32, (PADDED, 128), 1)
        prows[:, pl.ds(pl.multiple_of(chip * 128, 128), 128)] = jnp.where((lane // 64) == c, r0[...].astype(f32), r1[...].astype(f32)).astype(bf16)
        small["s"] = [cp(lanes(chip, 1), lanes(chip, 1), xp), cp(nrows(me - c, 2), nrows(me - c, 2), xp)]
    def pre6():
        settle()
        small["s"] = [cp(lanes(chip - x, 2), lanes(chip - x, 2), yp), cp(nrows(me - c - 2 * x, 4), nrows(me - c - 2 * x, 4), yp)]
    def pre7():
        settle()
        small["s"] = [cp(lanes(a * 4, 4), lanes(a * 4, 4), zp[j]) for j in range(1, A)] + [cp(nrows(a * 8, 8), nrows(a * 8, 8), zp[j]) for j in range(1, A)]
    def pre8():
        settle()
        lane = lax.broadcasted_iota(jnp.int32, (G, 128), 1) // 32
        for w in range(2 * A):
            s = nout[pl.ds(w * 4 * G, G), :].astype(f32)
            for n in range(1, 4):
                s = jnp.where(lane == n, nout[pl.ds((w * 4 + n) * G, G), :].astype(f32), s)
            vecs[:, pl.ds(w * 128, 128)] = s[:8]
        kept.append(cp.local(vecs, vecs_o))
        kept.append(cp.local(prows, prows_o))
    H = fin.shape[1]
    feeds, passed = {}, []
    def feed_send(i):
        n = D // 8
        ri = pl.ds(pl.multiple_of(c * (D // 2) + i * n, n), n)
        m = H // 8
        ro = pl.ds(pl.multiple_of(c * (H // 2) + i * m, m), m)
        ro2 = pl.ds(pl.multiple_of(H + c * (H // 2) + i * m, m), m)
        feeds[i] = [(cp(fin.at[ri], fin2.at[ri, pl.ds(H, H)], zq), fin2.at[ri, pl.ds(H, H)]),
                    (cp(fout.at[ro], fout2.at[ro2], zq), fout2.at[ro2])]
    def feed_pass(i):
        for e, ref in feeds[i]:
            e.wait_recv()
            passed.append(cp(ref, ref, core))
    zc, mc, lc, dc = {}, {}, {}, {}
    two, three = (yp, xp), (xp, yp)
    begun = set()
    def fs(i, h):
        if i not in begun:
            begun.add(i)
            own[i].wait(); cross[i].wait()
        mc[i, h, 0] = cp(block(i, h, a, b, x), block(i, h, a, b, x), two[h])
        lc[i, h, 0, 0] = cp(block(i, h, a, b, x), block(i, h, a, b, x), three[h])
    def fz(i, h):
        for j in range(1, A):
            zc[i, h, j] = cp(block(i, h, a, b, x), block(i, h, a, b, x), zp[j])
    def mid(i, h, j):
        aj = (a + A - j) % A
        zc[i, h, j].wait_recv()
        mc[i, h, j] = cp(block(i, h, aj, b, x), block(i, h, aj, b, x), two[h])
        lc[i, h, j, 0] = cp(block(i, h, aj, b, x), block(i, h, aj, b, x), three[h])
    def third(i, h, j):
        aj = (a + A - j) % A
        w = (aj, 1 - b, x) if h == 0 else (aj, b, 1 - x)
        mc[i, h, j].wait_recv()
        lc[i, h, j, 1] = cp(block(i, h, *w), block(i, h, *w), three[h])
    per = D // A
    def finish(i, j):
        aj = (a + A - j) % A
        for h in range(2):
            lc[i, h, j, 0].wait_recv(); lc[i, h, j, 1].wait_recv()
        ref = g.at[2 * i + c, pl.ds(pl.multiple_of(aj * per, per), per)]
        dc[i, j] = cp(ref, ref, core)
    def arrive(i):
        for j in range(A): dc[i, j].wait_recv()
        kept.append(cp.local(g.at[2 * i], wout.at[2 * i]))
        kept.append(cp.local(g.at[2 * i + 1], wout.at[2 * i + 1]))
    def halves(src, w, out):
        def part(n):
            def go():
                xv = src[...]
                def step(t):
                    out[:, columns(t)] = dot(xv, g[w, :, columns(t)]).astype(bf16)
                loop(2 * n, 2 * n + 2, step)
            return go
        return [part(0), part(1)]
    def masks():
        row = lax.broadcasted_iota(jnp.int32, (T, T), 0)
        col = lax.broadcasted_iota(jnp.int32, (T, T), 1)
        across = jnp.broadcast_to(seg_row[...].astype(f32), (T, T))
        down = across.T
        pen[:, :T] = jnp.where((row >= col) & (down == across), 0.0, NEGATIVE)
        lane = lax.broadcasted_iota(jnp.int32, (T, PADDED), 1)
        pen[:, T:] = jnp.where(lane < PREFIX, 0.0, NEGATIVE)
        for n in range(memory.shape[0] // T):
            span = slice(n * T, (n + 1) * T)
            cpen[:, span] = jnp.where(down == mem_row[:, span].astype(f32), 0.0, NEGATIVE)
    def softmax(qv, kk, penalty):
        score = jnp.where(penalty[...] < -1.0, NEGATIVE, dot_right(qv, kk) * 0.125)
        e = jnp.exp(score - jnp.max(score, axis=-1, keepdims=True))
        return (e * (1.0 / jnp.sum(e, axis=-1, keepdims=True))).astype(bf16)
    def own_attend(n):
        def go():
            def step(p):
                cols = columns(p, 128)
                kk = jnp.concatenate([k[:, cols], prows[:, cols]], axis=0)
                vv = jnp.concatenate([v[:, cols], prows[:, pl.ds(pl.multiple_of(D + p * 128, 128), 128)]], axis=0)
                qs, vs = split_heads(q[:, cols]), split_heads(vv)
                total = None
                for s in range(2):
                    prob = softmax(qs[s], kk, pen)
                    probs[2 * p + s] = prob
                    m = dot(prob, vs[s])
                    total = m if total is None else total + m
                att[:, cols] = total.astype(bf16)
            loop(2 * n, 2 * n + 2, step)
        return go
    def cross_scores(n):
        def go():
            def step(p):
                cols = columns(p, 128)
                qs = split_heads(cq[:, cols])
                for s in range(2):
                    cprobs[2 * p + s] = softmax(qs[s], ck[:, cols], cpen)
            loop(2 * n, 2 * n + 2, step)
        return go
    def cross_mix(n):
        def go():
            def step(p):
                cols = columns(p, 128)
                vs = split_heads(cv[:, cols])
                crossed[:, cols] = (dot(cprobs[2 * p], vs[0]) + dot(cprobs[2 * p + 1], vs[1])).astype(bf16)
            loop(4 * n, 4 * n + 4, step)
        return go
    def normed(base, low, w, at, out, nn, ii, olow):
        def part(n):
            def go():
                lv = low[...]
                def step(t):
                    out[:, columns(t)] = base[:, columns(t)].astype(f32) + dot(lv, g[w, :, columns(t)])
                loop(2 * n, 2 * n + 2, step)
            return go
        def last():
            m, inv = norm(out[...])
            nn[...] = m
            ii[...] = inv
            s = m * vecs[at:at + 1, :] + vecs[at + 1:at + 2, :]
            out[...] = s
            olow[...] = s.astype(bf16)
        return [part(0), part(1), last]
    make_q, make_k, make_v = halves(inputs, 0, q), halves(inputs, 1, k), halves(inputs, 2, v)
    make_ck, make_cq, make_cv = halves(memory, 4, ck), halves(flow, 5, cq), halves(memory, 6, cv)
    norm_one, norm_two = normed(inputs, att, 3, 0, first, n1, i1, flow), normed(first, crossed, 7, 2, second, n2, i2, slow)
    fs(0, 0)
    fs(0, 1)
    fs(1, 1)
    fs(3, 0)
    fs(1, 0)
    fz(1, 1)
    fz(0, 0)
    fs(2, 0)
    pre1()
    third(3, 0, 0)
    pre2(1)()
    mid(1, 1, 1)
    fs(2, 1)
    mid(1, 1, 2)
    fz(1, 0)
    third(0, 1, 0)
    pre2(2)()
    feed_send(0)
    mid(1, 1, 3)
    third(0, 0, 0)
    third(1, 1, 1)
    fs(3, 1)
    pre4()
    mid(0, 0, 2)
    mid(0, 0, 1)
    fz(0, 1)
    mid(1, 0, 2)
    mid(1, 0, 3)
    pre5()
    mid(1, 0, 1)
    mid(0, 0, 3)
    third(1, 0, 0)
    third(1, 0, 2)
    mid(0, 1, 1)
    fz(2, 0)
    mid(0, 1, 3)
    mid(0, 1, 2)
    third(0, 0, 3)
    feed_send(2)
    third(1, 1, 0)
    pre6()
    third(1, 1, 2)
    third(0, 0, 1)
    third(0, 0, 2)
    fz(2, 1)
    third(0, 1, 1)
    mid(2, 0, 3)
    fz(3, 1)
    third(0, 1, 3)
    mid(2, 0, 2)
    finish(0, 1)
    pre7()
    third(0, 1, 2)
    finish(0, 0)
    third(1, 1, 3)
    mid(2, 0, 1)
    third(1, 0, 3)
    mid(2, 1, 2)
    third(1, 0, 1)
    third(3, 1, 0)
    finish(1, 2)
    feed_pass(0)
    mid(2, 1, 3)
    mid(2, 1, 1)
    finish(0, 3)
    finish(0, 2)
    finish(1, 3)
    fz(3, 0)
    third(2, 0, 0)
    mid(3, 1, 1)
    third(2, 1, 0)
    arrive(0)
    third(2, 0, 2)
    feed_send(1)
    third(2, 0, 1)
    make_q[0]()
    feed_send(3)
    make_q[1]()
    kept.append(cp.local(q, q_o))
    finish(1, 1)
    make_k[0]()
    finish(1, 0)
    pre8()
    make_k[1]()
    kept.append(cp.local(k, k_o))
    third(2, 1, 2)
    mid(3, 0, 1)
    masks()
    arrive(1)
    third(2, 1, 3)
    make_v[0]()
    make_v[1]()
    kept.append(cp.local(v, v_o))
    third(2, 1, 1)
    third(2, 0, 3)
    own_attend(0)()
    feed_pass(2)
    finish(2, 0)
    own_attend(1)()
    finish(2, 2)
    mid(3, 0, 2)
    mid(3, 1, 3)
    own_attend(2)()
    own_attend(3)()
    kept.append(cp.local(probs, probs_o))
    kept.append(cp.local(att, att_o))
    mid(3, 1, 2)
    feed_pass(1)
    finish(2, 3)
    mid(3, 0, 3)
    finish(2, 1)
    norm_one[0]()
    third(3, 1, 1)
    norm_one[1]()
    norm_one[2]()
    kept.append(cp.local(flow, first_o))
    kept.append(cp.local(n1, n1_o))
    kept.append(cp.local(i1, i1_o))
    third(3, 0, 1)
    finish(3, 0)
    third(3, 0, 2)
    arrive(2)
    make_ck[0]()
    third(3, 1, 2)
    make_cq[0]()
    feed_pass(3)
    make_cq[1]()
    kept.append(cp.local(cq, cq_o))
    third(3, 0, 3)
    third(3, 1, 3)
    make_ck[1]()
    kept.append(cp.local(ck, ck_o))
    finish(3, 1)
    cross_scores(0)()
    finish(3, 2)
    cross_scores(1)()
    finish(3, 3)
    cross_scores(2)()
    cross_scores(3)()
    kept.append(cp.local(cprobs, cprobs_o))
    arrive(3)
    make_cv[0]()
    make_cv[1]()
    kept.append(cp.local(cv, cv_o))
    cross_mix(0)()
    cross_mix(1)()
    kept.append(cp.local(crossed, crossed_o))
    norm_two[0]()
    norm_two[1]()
    norm_two[2]()
    kept.append(cp.local(slow, slow_o))
    kept.append(cp.local(n2, n2_o))
    kept.append(cp.local(i2, i2_o))
    def partner():
        for e in passed: e.wait_recv()
    def finish():
        for e in kept: e.wait()
        cp.close()
    return (second, vecs, att, flow, crossed, slow), partner, finish

def forward_kernel(A, r, inputs, memory, seg_row, mem_row, embed, inner, outer, norms, cot, *refs):
    ws, (fin, fout, down, up), outs, scratch = refs[:8], refs[8:12], refs[12:44], refs[44:]
    fin2, fout2 = scratch[32:34]
    (second, vecs, att, flow, crossed, slow), partner, finish = front_part(A, r, inputs, memory, seg_row, mem_row, embed, inner, outer, norms, ws, fin, fout, fin2, fout2, outs[:20], scratch[:32])
    feed_part(A, second, vecs, cot, fin, fout, down, up, inputs, memory, att, flow, crossed, slow, partner, outs[20:], scratch[32:])
    finish()

def forward(A, r, inputs, memory, seg_row, mem_row, embed, inner, outer, norms, cot, ws, fin, fout, down, up):
    T, D = inputs.shape; M = memory.shape[0]; H = fin.shape[1]; AD = down.shape[1] * 4
    HID = 2 * H
    vm = pl.BlockSpec(memory_space=pltpu.VMEM)
    any_ = pl.BlockSpec(memory_space=pl.ANY)
    sds = jax.ShapeDtypeStruct
    v = lambda *s: pltpu.VMEM(s, bf16)
    vf = lambda *s: pltpu.VMEM(s, f32)
    row, mrow, full, one = sds((T, D), bf16), sds((M, D), bf16), sds((T, D), f32), sds((T, 1), f32)
    S = (PADDED, inner.shape[1])
    probs, cprobs = (16, T, T + PADDED), (16, T, M)
    R = T // 2
    sums = (2, 2, D // 256, R, 256)
    four = sds((4 * T, D), bf16)
    sem = pltpu.SemaphoreType.DMA
    return pl.pallas_call(functools.partial(forward_kernel, A, r),
        out_shape=(sds((8, D, D), bf16), sds(S, f32), sds((PADDED, 2 * D), bf16), sds((8, D), f32), row, row, row, sds(probs, bf16), row, row, full, one, row, mrow, mrow,
            sds(cprobs, bf16), row, row, full, one,
            row, full, sds((D, HID), bf16), sds((HID, D), bf16), sds((2, T, AD), bf16), row, sds((2, D), f32), four, four, four, sds((4 * M, D), bf16), four),
        in_specs=[vm] * 9 + [any_] * 12, out_specs=(any_,) * 20 + (vm,) * 2 + (any_,) * 2 + (vm,) * 3 + (any_,) * 5,
        scratch_shapes=[v(8, D, D), v(T, D), v(T, D), v(T, D), v(*probs), v(T, D), vf(T, D), v(T, D), vf(T, D), vf(T, 1), v(T, D), v(M, D), v(M, D), v(*cprobs), v(T, D),
            vf(T, D), v(T, D), vf(T, D), vf(T, 1), vf(T, T + PADDED), vf(T, M),
            vf(3, *S), vf(3, *S), vf(A, *S), v(PADDED, 128), v(PADDED, 128), v(PADDED, 2 * D), v(8 * A * norms.shape[0], 128), vf(8, D), vf(*S), sem((320,)), sem((320,)),
            v(D, HID), v(HID, D), v(D, HID), v(HID, D), v(D, AD), v(AD, D), v(2, 4, R, D), v(2, 4, R, D), v(2, 4, R, HID), vf(2, 4, R, HID), v(2, 4, R, HID), v(2, 4, D // 256, R, 256),
            v(*sums), v(*sums), v(*sums), vf(T, AD), vf(2, R, D), sem((128,)), sem((128,))],
        compiler_params=pltpu.CompilerParams(collective_id=1, has_side_effects=True, vmem_limit_bytes=60 << 20), name="forward")(
            inputs, memory, seg_row, mem_row, embed, inner, outer, norms, cot, *ws, fin, fout, down, up)


def exact(l, r, dims):
    return lax.dot_general(l, r, (dims, ((), ())), precision=lax.Precision.HIGHEST, preferred_element_type=f32)

def back_kernel(A, r, gsec, n2, i2, vecs, ngrad3, tangent, embed, inner, outer, *refs):
    late, (ay, weights, fi, fo, xp0, xatt, xin, xmem, xad) = refs[:11], refs[11:20]
    back_body(A, r, gsec, n2, i2, vecs, ngrad3, tangent, embed, inner, outer, late, ay, weights, fi, fo, xp0, xatt, xin, xmem, xad, *refs[20:])

def back_body(A, r, gsec, n2, i2, vecs, ngrad3, tangent, embed, inner, outer, late, ay, weights, fi, fo, xp0, xatt, xin, xmem, xad,
                igrad_o, mgrad_o, out, aout, fi_out, fo_out, outer_o, inner_o, embed_o, nsum,
                igrad, mgrad, cq, ck, cv, cprobs, n1, i1, q, k, v, probs, prows, ws, gmid, gfirst, og, mid, dcq, dck, dcv, startl, dq, dk, dv, pg,
                xb, yb, mb, mby, axb, ayb, pb, apb, fib, fob, r1, r2, r3, sb, xs, ra2, ra3, rfi, rfo, rzi, rzo, rxi, rxo, ob, aob, fib2, fob2,
                buf, got, zbuf, nbuf, ngot, nz, w0, w1, w2, w3, s0, s1, s2, nfull, pgl, ssem, rsem):
    a, b, x, c = place()
    o = 1 - c
    core, xp, yp = device(a, b, x, o), device(a, b, 1 - x, c), device(a, 1 - b, x, c)
    dp = device(a, b, 1 - x, o)
    place_n = x * 2 + c
    zp = [device((a + j) % A, b, x, c) for j in range(A)]
    za = a + 1 - 2 * (a % 2)
    zq = device(za, b, x, c)
    peers = (core, xp, yp)
    T, D = gsec.shape
    M = xmem.shape[0] // 4
    HID = fi.shape[1] // 2
    Q = fi.shape[0] // 4
    half = D // 2
    cp = Copies(ssem, rsem)
    loads = {}
    def fetch(slot, w):
        loads[slot] = cp.local(weights.at[w], ws.at[slot])
    loaded = [cp.local(src, dst) for src, dst in zip(late, (cq, ck, cv, cprobs, n1, i1, q, k, v, probs, prows))]
    def ready(start, stop):
        for e in loaded[start:stop]: e.wait()
    fetch(0, 7); fetch(1, 5); fetch(2, 3); fetch(3, 4)
    fown = []
    for xx in range(2):
        dq_ = pl.ds(pl.multiple_of((xx * 2 + c) * Q, Q), Q)
        fown += [cp.local(fi.at[dq_, :], fib.at[xx]), cp.local(fo.at[:, dq_], fob.at[xx])]
    greet([core, xp, yp, dp] + zp[1:])
    waits = {}
    aw = [cp.local(xad, axb).wait]
    xload = cp.count
    cp.count += 4
    def load_x(me):
        pltpu.make_async_copy(xp0, xb.at[0], ssem.at[xload]).start()
        pltpu.make_async_copy(xmem, mb, ssem.at[xload + 1]).start()
        pltpu.make_async_copy(xin if me else xatt, xb.at[1], ssem.at[xload + 2]).start()
        pltpu.make_async_copy(xin, xb.at[2], ssem.at[xload + 3]).start()
    pl.when(c == 0)(functools.partial(load_x, 0))
    pl.when(c == 1)(functools.partial(load_x, 1))
    waits[0] = (pltpu.make_async_copy(xp0, xb.at[0], ssem.at[xload]).wait,)
    waits[1] = (pltpu.make_async_copy(xmem, mb, ssem.at[xload + 1]).wait,)
    waits[2] = (pltpu.make_async_copy(xin, xb.at[1], ssem.at[xload + 2]).wait,)
    waits[3] = (pltpu.make_async_copy(xin, xb.at[2], ssem.at[xload + 3]).wait,)
    def share_adapter():
        quarter = ayb.shape[1]
        k = cp.count
        cp.count += 4
        here, there = pl.ds(pl.multiple_of(x * quarter, quarter), quarter), pl.ds(pl.multiple_of((1 - x) * quarter, quarter), quarter)
        spot = ayb.at[pl.ds(pl.multiple_of(place_n * T, T), T)]
        kept = pltpu.make_async_copy(ay.at[c, :, here], spot, ssem.at[k])
        ways = [remote(ay.at[c, :, there], spot, ssem.at[k + 1], rsem.at[k + 1], xp), remote(ay.at[o, :, here], spot, ssem.at[k + 2], rsem.at[k + 2], core),
                remote(ay.at[o, :, there], spot, ssem.at[k + 3], rsem.at[k + 3], dp)]
        for e in ways: e.start()
        kept.start()
        cp.all.extend(ways)
        aw.extend([kept.wait] + [e.wait_recv for e in ways])
    share_adapter()
    def share(srcs, dst, t):
        m = srcs[0].shape[0]
        k = cp.count
        cp.count += 4
        wide = half // 2
        here = pl.ds(pl.multiple_of(x * half + t * wide, wide), wide)
        there = pl.ds(pl.multiple_of((1 - x) * half + t * wide, wide), wide)
        spot = dst.at[pl.ds(pl.multiple_of(place_n * m, m), m), pl.ds(t * wide, wide)]
        def start(me):
            own, other = srcs[me], srcs[1 - me]
            remote(own.at[:, there], spot, ssem.at[k + 1], rsem.at[k + 1], xp).start()
            remote(other.at[:, there], spot, ssem.at[k + 3], rsem.at[k + 3], dp).start()
            remote(other.at[:, here], spot, ssem.at[k + 2], rsem.at[k + 2], core).start()
            pltpu.make_async_copy(own.at[:, here], spot, ssem.at[k]).start()
        pl.when(c == 0)(functools.partial(start, 0))
        pl.when(c == 1)(functools.partial(start, 1))
        ways = [remote(srcs[0].at[:, here], spot, ssem.at[k + i], rsem.at[k + i], d) for i, d in ((1, xp), (2, core), (3, dp))]
        cp.all.extend(ways)
        return (pltpu.make_async_copy(srcs[0].at[:, here], spot, ssem.at[k]).wait,) + tuple(e.wait_recv for e in ways)
    fcopies = []
    for xx in range(2):
        dq_ = pl.ds(pl.multiple_of((xx * 2 + o) * Q, Q), Q)
        fcopies += [cp(fi.at[dq_, :], rfi.at[xx], core), cp(fo.at[:, dq_], rfo.at[xx], core)]

    zf, xf, outs = [], [], []
    def feed0():
        for e in fown: e.wait()
        for e in fcopies: e.wait_recv()
        for xx in range(2):
            def rows_fi(t):
                s = pl.ds(t * 32, 32)
                fib[xx, s, :] = fib[xx, s, :] + rfi[xx, s, :]
            loop(0, Q // 32, rows_fi)
            def rows_fo(t):
                s = pl.ds(t * 64, 64)
                fob[xx, s, :] = fob[xx, s, :] + rfo[xx, s, :]
            loop(0, 2 * HID // 64, rows_fo)
        zf.extend([cp(fib.at[:, :, pl.ds(HID, HID)], rzi, zq), cp(fob.at[:, pl.ds(HID, HID), :], rzo, zq)])
    def feed1():
        for e in zf: e.wait_recv()
        for xx in range(2):
            def rows_fi(t):
                s = pl.ds(t * 32, 32)
                fib[xx, s, pl.ds(0, HID)] = fib[xx, s, pl.ds(0, HID)] + rzi[xx, s, :]
            loop(0, Q // 32, rows_fi)
            def rows_fo(t):
                s = pl.ds(t * 64, 64)
                fob[xx, s, :] = fob[xx, s, :] + rzo[xx, s, :]
            loop(0, HID // 64, rows_fo)
        xf.extend([cp(fib.at[1 - x, :, pl.ds(0, HID)], rxi, xp), cp(fob.at[1 - x, pl.ds(0, HID), :], rxo, xp)])
    def feed2():
        for e in xf: e.wait_recv()
        def rows_fi(t):
            s = pl.ds(t * 32, 32)
            fib2[s, :] = fib[x, s, pl.ds(0, HID)].astype(f32) + rxi[s, :].astype(f32)
        loop(0, Q // 32, rows_fi)
        def rows_fo(t):
            s = pl.ds(t * 64, 64)
            fob2[s, :] = fob[x, s, :].astype(f32) + rxo[s, :].astype(f32)
        loop(0, HID // 64, rows_fo)
        outs.extend([cp.local(fib2, fi_out).wait, cp.local(fob2, fo_out).wait])

    first, second, third, fourth = {}, {}, {}, {}
    wide = half // 2
    numbers = {}
    for i in range(4):
        for t in range(2):
            numbers[i, t] = cp.count
            cp.count += 1
    def level1(i, t):
        n = numbers[i, t]
        return remote(pb.at[i, t, :, 1 - b], r1.at[i, t], ssem.at[n], rsem.at[n], yp)
    for i in range(4):
        for t in range(2):
            first[i, t] = level1(i, t)
            cp.all.append(first[i, t])
    def share_one(src, dst, t, owner):
        m = src.shape[0]
        k = cp.count
        cp.count += 4
        wide = half // 2
        here = pl.ds(pl.multiple_of(x * half + t * wide, wide), wide)
        there = pl.ds(pl.multiple_of((1 - x) * half + t * wide, wide), wide)
        spot = dst.at[pl.ds(pl.multiple_of(place_n * m, m), m), pl.ds(t * wide, wide)]
        kept = pltpu.make_async_copy(src.at[:, here], spot, ssem.at[k])
        ways = [remote(src.at[:, there], spot, ssem.at[k + 1], rsem.at[k + 1], xp), remote(src.at[:, here], spot, ssem.at[k + 2], rsem.at[k + 2], core),
                remote(src.at[:, there], spot, ssem.at[k + 3], rsem.at[k + 3], dp)]
        def mine():
            ways[0].start()
            kept.start()
        def other():
            ways[2].start()
            ways[1].start()
        pl.when(c == owner)(mine)
        pl.when(c != owner)(other)
        def arrived():
            kept.wait()
            for e in ways: e.wait_recv()
        def sent():
            pl.when(c == owner)(ways[0].wait_send)
            def both():
                ways[1].wait_send()
                ways[2].wait_send()
            pl.when(c != owner)(both)
        ending.append(sent)
        return (arrived,)
    ending = []
    used, filled = set(), set()
    def compute(i, t, owner=None):
        def go():
            if (i, owner) not in used:
                used.add((i, owner))
                for e in waits[i]: e()
            for e in shared[(i, t) if owner is None else (i, t, owner)]: e()
            cols = pl.ds(t * wide, wide)
            n = (0, None, 1, 2)[i]
            def rows(u):
                d = columns(u)
                p = dot_left(mb[:, d], mby[:, cols]) if i == 1 else dot_left(xb[n, :, d], yb[n, :, cols])
                pb[i, t, u] = p.astype(bf16).reshape(2, 2, 2 * r, wide)
            loop(0, A, rows)
            level1(i, t).start()
        if owner is None: go()
        else: pl.when(c == owner)(go)
    def one(i, t):
        def go():
            first[i, t].wait_recv()
            for j in range(1, A):
                aj = (a + j) % A
                pb[i, t, aj, b] = pb[i, t, aj, b] + r1[i, t, aj]
                third[i, t, j] = cp(pb.at[i, t, aj, b], r2.at[i, t, j - 1], zp[j])
            pb[i, t, a, b] = pb[i, t, a, b] + r1[i, t, a]
        return go
    def two(i, t):
        def go():
            for j in range(1, A): third[i, t, j].wait_recv()
            for s in (1 - x, x):
                e = pb[i, t, a, b, s].astype(f32)
                for j in range(1, A): e = e + r2[i, t, j - 1, s].astype(f32)
                sb[i, t, s] = e
            xs[i, t] = sb[i, t, 1 - x].astype(bf16)
            fourth[i, t] = cp(xs.at[i, t], r3.at[i, t], xp)
        return go
    def three(i, t):
        def go():
            fourth[i, t].wait_recv()
            ob[i, :, pl.ds(pl.multiple_of(x * half + t * wide, wide), wide)] = sb[i, t, x]
            ob[i, :, pl.ds(pl.multiple_of((1 - x) * half + t * wide, wide), wide)] = r3[i, t].astype(f32)
            filled.add((i, t))
            if (i, 1 - t) in filled:
                outs.append(cp.local(ob.at[i, pl.ds(pl.multiple_of(c * r, r), r)], out.at[2 * i + c]).wait)
                outs.append(cp(ob.at[i, pl.ds(pl.multiple_of(o * r, r), r)], out.at[2 * i + c], core).wait_recv)
        return go
    def adapt0():
        for e in aw: e()
        def rows(u):
            apb[u] = dot_left(axb[:, columns(u)], ayb[...]).astype(bf16).reshape(2, D // (2 * A), ayb.shape[1])
        loop(0, A, rows)
        second["a"] = cp(apb.at[:, 1 - b], ra2, yp)
    def adapt2():
        second["a"].wait_recv()
        for j in range(1, A):
            aj = (a + j) % A
            apb[aj, b] = apb[aj, b] + ra2[aj]
            third["a", j] = cp(apb.at[aj, b], ra3.at[j - 1], zp[j])
        apb[a, b] = apb[a, b] + ra2[a]
    def adapt3():
        for j in range(1, A): third["a", j].wait_recv()
        t = apb[a, b].astype(f32)
        for j in range(1, A): t = t + ra3[j - 1].astype(f32)
        aob[0] = t[:, :128]
        aob[1] = t[:, 128:]
        outs.append(cp.local(aob.at[c], aout.at[c]).wait)
        outs.append(cp(aob.at[o], aout.at[c], core).wait_recv)
    small = {}
    def lanes(start, count): return pl.ds(pl.multiple_of(start * 128, 128), count * 128)
    def tail_norm0():
        small["n"] = [cp(nbuf.at[0], ngot.at[0], core)]
    def tail0():
        pgl[...] = pg[...].astype(bf16)
        small["w"] = [cp(pgl.at[:, lanes((a + j) % A * 4, 4)], w0.at[j - 1], zp[j]) for j in range(1, A)]
    def tail_norm(n):
        def go():
            for e in small["n"]: e.wait_recv()
            nbuf[n] = nbuf[n - 1] + ngot[n - 1]
            small["n"] = [cp(nbuf.at[n], ngot.at[n], peers[n])]
        return go
    def tail_norm3():
        for e in small["n"]: e.wait_recv()
        nz[a] = nbuf[2] + ngot[2]
        small["n"] = [cp(nz.at[a], nz.at[a], zp[j]) for j in range(1, A)]
    def tail_norm4():
        for e in small["n"]: e.wait_recv()
        t = nz[0]
        for n in range(1, A): t = t + nz[n]
        nfull[...] = t
        quad = nfull[:, pl.ds(pl.multiple_of((a * 2 + b) * 128, 128), 128)]
        piece = quad[:, :r]
        for e in range(1, 4): piece = jnp.where(place_n == e, quad[:, e * r:(e + 1) * r], piece)
        nsum[...] = piece
    def tail1():
        t = pg[:, lanes(a * 4, 4)]
        for j, e in enumerate(small["w"]):
            e.wait_recv()
            t = t + w0[j].astype(f32)
        s0[...] = t
        small["w"] = [cp(s0.at[:, lanes((1 - b) * 2, 2)], w1, yp)]
    def tail2():
        small["w"][0].wait_recv()
        s1[...] = s0[:, lanes(b * 2, 2)] + w1[...]
        small["w"] = [cp(s1.at[:, lanes(1 - x, 1)], w2, xp)]
    def tail3():
        small["w"][0].wait_recv()
        s2[...] = s1[:, lanes(x, 1)] + w2[...]
        small["w"] = [cp(s2, w3, core)]
    def tail4():
        small["w"][0].wait_recv()
        t = s2[...] + w3[...]
        mine = jnp.where(c == 0, t[:, :64], t[:, 64:])
        buf[0] = exact(mine, outer[...].astype(f32), ((1,), (0,)))
        small["w"] = [cp(buf.at[0], got.at[0], core)]
        outer_o[...] = exact(mine, tangent[...].astype(bf16).astype(f32), ((0,), (0,)))
    def tail5(n):
        def go():
            small["w"][0].wait_recv()
            buf[n] = buf[n - 1] + got[n - 1]
            small["w"] = [cp(buf.at[n], got.at[n], peers[n])]
        return go
    def tail6():
        small["w"][0].wait_recv()
        zbuf[a] = (buf[2] + got[2]).astype(bf16)
        small["w"] = [cp(zbuf.at[a], zbuf.at[a], zp[j]) for j in range(1, A)]
    def tail7():
        for e in small["w"]: e.wait_recv()
        t = zbuf[0].astype(f32)
        for n in range(1, A): t = t + zbuf[n].astype(f32)
        tan = tangent[...]
        t = t * (1.0 - tan * tan)
        inner_o[...] = exact(embed[...].astype(f32), t[:PREFIX], ((0,), (0,)))
        embed_o[...] = exact(t[:PREFIX], inner[...].astype(f32), ((1,), (1,)))
    def norm_two():
        norm_back_into(gsec, n2, i2, vecs[2:3, :], gmid, nbuf.at[0], 2)
        mid[...] = gmid[...].astype(bf16)
    def back_project(src, slot, n):
        def go():
            s = src[...]
            loop(2 * n, 2 * n + 2, lambda t: og.__setitem__((slice(None), columns(t)), dot_right(s, ws[slot, columns(t), :]).astype(bf16)))
        return go
    def wait_slot(slot):
        def go(): loads[slot].wait()
        return go
    def pair_back(p, grad, qr, kk, vv, pr):
        cols = columns(p, 128)
        qs, ks, gs = split_heads(qr[:, cols]), split_heads(kk), split_heads(grad[:, cols])
        res = None
        for s in range(2):
            low = pr[2 * p + s]
            prob = low.astype(f32)
            t = prob * dot_right(gs[s], vv)
            ds = (t - prob * jnp.sum(t, axis=-1, keepdims=True)).astype(bf16)
            m = (dot(ds, ks[s]), dot_left(ds, qs[s]), dot_left(low, gs[s]))
            res = m if res is None else tuple(e + f for e, f in zip(res, m))
        return cols, res[0] * 0.125, res[1] * 0.125, res[2]
    def cross_back(n):
        def go():
            def step(p):
                cs = columns(p, 128)
                cols, m1, m2, m3 = pair_back(p, og, cq, ck[:, cs], cv[:, cs], cprobs)
                dcq[:, cols] = m1.astype(bf16)
                dck[:, cols] = m2.astype(bf16)
                dcv[:, cols] = m3.astype(bf16)
            for p in range(2 * n, 2 * n + 2): step(p)
        return go
    def self_back(n):
        def go():
            def step(p):
                cs = columns(p, 128)
                cv_ = pl.ds(pl.multiple_of(D + p * 128, 128), 128)
                kk = jnp.concatenate([k[:, cs], prows[:, cs]], axis=0)
                vv = jnp.concatenate([v[:, cs], prows[:, cv_]], axis=0)
                cols, m1, m2, m3 = pair_back(p, og, q, kk, vv, probs)
                dq[:, cols] = m1.astype(bf16)
                dk[:, cols] = m2[:T].astype(bf16)
                dv[:, cols] = m3[:T].astype(bf16)
                pg[:, cols] = m2[T:]
                pg[:, cv_] = m3[T:]
            for p in range(2 * n, 2 * n + 2): step(p)
        return go
    def first_grad():
        s = dcq[...]
        def step(t):
            gfirst[:, columns(t)] = gmid[:, columns(t)] + dot_right(s, ws[1, columns(t), :])
        loop(0, D // 256, step)
    def norm_one():
        norm_back_into(gfirst, n1, i1, vecs[0:1, :], gmid, nbuf.at[0], 0)
        nbuf[0, 4:6, :] = ngrad3[...]
        nbuf[0, 6:8, :] = jnp.zeros((2, D), f32)
        startl[...] = gmid[...].astype(bf16)
    def memory_part(n):
        def go():
            def step(t):
                mgrad[:, columns(t)] = (dot_right(dck[...], ws[3, columns(t), :]) + dot_right(dcv[...], ws[0, columns(t), :])).astype(bf16)
            loop(2 * n, 2 * n + 2, step)
        return go
    def input_part(n):
        def go():
            def step(t):
                s = gmid[:, columns(t)] + dot_right(dq[...], ws[1, columns(t), :]) + dot_right(dk[...], ws[2, columns(t), :]) + dot_right(dv[...], ws[3, columns(t), :])
                igrad[:, columns(t)] = s.astype(bf16)
            loop(2 * n, 2 * n + 2, step)
        return go
    shared = {}
    def spread(i, srcs, dst):
        for t in range(2): shared[i, t] = share(srcs, dst, t)
    def spread_one(i, src, dst, owner):
        for t in range(2): shared[i, t, owner] = share_one(src, dst, t, owner)
    norm_two()
    spread_one(0, mid, yb.at[0], 0)
    wait_slot(0)()
    back_project(mid, 0, 0)()
    back_project(mid, 0, 1)()
    fetch(0, 6)
    ready(0, 4)
    cross_back(0)()
    feed0()
    adapt0()
    cross_back(1)()
    cross_back(2)()
    cross_back(3)()
    spread_one(0, dcq, yb.at[0], 1)
    wait_slot(1)()
    first_grad()
    fetch(1, 0)
    compute(0, 0, 0)
    spread(1, (dck, dcv), mby)
    ready(4, 6)
    norm_one()
    compute(0, 0, 1)
    adapt2()
    compute(0, 1, 0)
    compute(0, 1, 1)
    wait_slot(2)()
    back_project(startl, 2, 0)()
    spread_one(2, startl, yb.at[1], 0)
    back_project(startl, 2, 1)()
    fetch(2, 1)
    ready(6, 11)
    self_back(0)()
    one(0, 0)()
    compute(1, 0)
    self_back(1)()
    self_back(2)()
    self_back(3)()
    tail_norm0()
    tail0()
    spread(3, (dk, dv), yb.at[2])
    one(0, 1)()
    compute(1, 1)
    one(1, 0)()
    compute(2, 1, 0)
    spread_one(2, dq, yb.at[1], 1)
    feed1()
    wait_slot(3)()
    wait_slot(0)()
    memory_part(0)()
    compute(3, 1)
    tail_norm(1)()
    one(1, 1)()
    tail1()
    compute(2, 1, 1)
    memory_part(1)()
    outs.append(cp.local(mgrad, mgrad_o).wait)
    fetch(3, 2)
    one(3, 1)()
    compute(3, 0)
    wait_slot(1)()
    wait_slot(2)()
    wait_slot(3)()
    input_part(0)()
    tail2()
    compute(2, 0, 0)
    one(2, 1)()
    two(0, 0)()
    adapt3()
    tail3()
    feed2()
    tail4()
    two(0, 1)()
    tail5(1)()
    one(3, 0)()
    compute(2, 0, 1)
    two(1, 0)()
    one(2, 0)()
    tail_norm(2)()
    three(0, 1)()
    two(1, 1)()
    two(2, 1)()
    three(0, 0)()
    tail5(2)()
    three(1, 1)()
    two(3, 0)()
    tail6()
    tail_norm3()
    three(2, 1)()
    two(3, 1)()
    two(2, 0)()
    three(3, 0)()
    input_part(1)()
    outs.append(cp.local(igrad, igrad_o).wait)
    three(1, 0)()
    three(2, 0)()
    three(3, 1)()
    tail7()
    tail_norm4()
    for e in ending: e()
    for e in outs: e()
    cp.close()

def back(A, r, first, late, rest):
    gsec = first[0]
    T, D = gsec.shape; M = rest[7].shape[0] // 4
    fi, fo = rest[2:4]
    Q, H2 = fi.shape[0] // 4, fi.shape[1]
    H = H2 // 2
    half = D // 2
    v = lambda *s: pltpu.VMEM(s, bf16)
    vf = lambda *s: pltpu.VMEM(s, f32)
    any_ = pl.BlockSpec(memory_space=pl.ANY)
    vm = pl.BlockSpec(memory_space=pltpu.VMEM)
    sds = jax.ShapeDtypeStruct
    P_, N = PADDED, (8, D)
    hid = first[-2].shape[1]
    S = (P_, hid)
    return pl.pallas_call(functools.partial(back_kernel, A, r),
        out_shape=(sds((T, D), bf16), sds((M, D), bf16), sds((8, r, D), f32), sds((2, D // (2 * A), 128), f32), sds((Q, H), f32), sds((H, Q), f32),
            sds((64, hid), f32), sds((r, hid), f32), sds((PREFIX, r), f32), sds((8, r), f32)),
        in_specs=[vm] * len(first) + [any_] * (len(late) + len(rest)), out_specs=(any_,) * 6 + (vm,) * 4,
        scratch_shapes=[v(T, D), v(M, D)] + [pltpu.VMEM(e.shape, e.dtype) for e in late] + [v(4, D, D), vf(T, D), vf(T, D), v(T, D), v(T, D), v(T, D), v(M, D), v(M, D), v(T, D), v(T, D), v(T, D), v(T, D), vf(P_, 2 * D),
            v(3, 4 * T, D), v(3, 4 * T, half), v(4 * M, D), v(4 * M, half), v(4 * T, D), v(4 * T, 256),
            v(4, 2, A, 2, 2, 2 * r, half // 2), v(A, 2, D // (2 * A), 256), v(2, Q, H2), v(2, H2, Q),
            v(4, 2, A, 2, 2 * r, half // 2), v(4, 2, A - 1, 2, 2 * r, half // 2), v(4, 2, 2 * r, half // 2), vf(4, 2, 2, 2 * r, half // 2), v(4, 2, 2 * r, half // 2),
            v(A, D // (2 * A), 256), v(A - 1, D // (2 * A), 256),
            v(2, Q, H2), v(2, H2, Q), v(2, Q, H), v(2, H, Q), v(Q, H), v(H, Q),
            vf(4, 2 * r, D), vf(2, D // (2 * A), 128), vf(Q, H), vf(H, Q),
            vf(3, *S), vf(3, *S), v(A, *S), vf(3, *N), vf(3, *N), vf(A, *N), v(A - 1, P_, 512), vf(P_, 256), vf(P_, 128), vf(P_, 128), vf(P_, 512), vf(P_, 256), vf(P_, 128), vf(8, D), v(P_, 2 * D),
            pltpu.SemaphoreType.DMA((224,)), pltpu.SemaphoreType.DMA((224,))],
        compiler_params=pltpu.CompilerParams(collective_id=2, has_side_effects=True, vmem_limit_bytes=63 << 20),
        name="back")(*first, *late, *rest)

def fast_body(A, inputs, memory, cotangent, segments, memory_segments, query_self, key_self, value_self, output_self,
              query_cross, key_cross, value_cross, output_cross, self_gain, self_shift, cross_gain, cross_shift,
              final_gain, final_shift, feed_in, feed_out, adapter_down, adapter_up, prefix_embed, prefix_inner, prefix_outer):
    r = query_self.shape[0]
    blank = jnp.zeros_like(self_gain)
    norms = jnp.stack([self_gain, self_shift, cross_gain, cross_shift, final_gain, final_shift] + [blank] * 10)
    (weights, tangent, prows, vecs, q, k, v, probs, attended, first_low, n1, i1, cq, ck, cv, cprobs, crossed, second_low, n2, i2,
     result, grad_second, fi, fo, ay, branch_low, ngrad3, xp0, xatt, xin, xmem, xad) = forward(
        A, r, inputs, memory, segments.reshape(1, -1), memory_segments.reshape(1, -1), prefix_embed, prefix_inner, prefix_outer.T, norms, cotangent,
        [query_self, key_self, value_self, output_self, key_cross, query_cross, value_cross, output_cross], feed_in, feed_out, adapter_down, adapter_up)
    igrad, mgrad, sums, adapt, fi_sum, fo_sum, outer_grad, inner_grad, embed_grad, ng = back(A, r,
        (grad_second, n2, i2, vecs, ngrad3, tangent, prefix_embed, prefix_inner, prefix_outer.T), (cq, ck, cv, cprobs, n1, i1, q, k, v, probs, prows),
        (ay, weights, fi, fo, xp0, xatt, xin, xmem, xad))
    whole = deliver(result, igrad, mgrad, sums, fi_sum, fo_sum, outer_grad, inner_grad, embed_grad, adapt)
    return whole[:11] + tuple(ng[k] for k in range(6)) + whole[11:17] + (whole[17].T,)


def deliver_kernel(*refs):
    ins, outs, held, (turned, into, out_of) = refs[:10], refs[10:28], refs[28:38], refs[38:]
    loads = [pltpu.make_async_copy(src, dst, into.at[i]) for i, (src, dst) in enumerate(zip(ins, held))]
    for e in loads: e.start()
    order = (5, 6, 7, 4, 1, 2, 3, 0)
    moves = [(3, held[3].at[k], outs[3 + i]) for i, k in enumerate(order)]
    moves += [(i, held[i], outs[i]) for i in range(3)] + [(4, held[4], outs[11]), (5, held[5], outs[12]), (9, held[9].at[0], outs[13]), (9, turned, outs[14])]
    moves += [(8, held[8], outs[15]), (7, held[7], outs[16]), (6, held[6], outs[17])]
    stores, ready = [], set()
    for n, (i, src, dst) in enumerate(moves):
        if i not in ready:
            ready.add(i)
            loads[i].wait()
        if src is turned: turned[...] = held[9][1].T
        stores.append(pltpu.make_async_copy(src, dst, out_of.at[n]))
        stores[-1].start()
    for e in stores: e.wait()


def deliver(result, igrad, mgrad, sums, fi, fo, outer, inner, embed, adapt):
    ins = (result, igrad, mgrad, sums, fi, fo, outer, inner, embed, adapt)
    like = lambda e: jax.ShapeDtypeStruct(e.shape, e.dtype)
    row = jax.ShapeDtypeStruct(sums.shape[1:], f32)
    square = jax.ShapeDtypeStruct(adapt.shape[1:], f32)
    any_ = pl.BlockSpec(memory_space=pl.ANY)
    return pl.pallas_call(deliver_kernel,
        out_shape=(like(result), like(igrad), like(mgrad)) + (row,) * 8 + (like(fi), like(fo), square, square, like(embed), like(inner), like(outer)),
        in_specs=[any_] * 10, out_specs=(any_,) * 18,
        scratch_shapes=[pltpu.VMEM(e.shape, e.dtype) for e in ins] + [pltpu.VMEM(adapt.shape[1:], f32), pltpu.SemaphoreType.DMA((10,)), pltpu.SemaphoreType.DMA((18,))],
        compiler_params=pltpu.CompilerParams(vmem_limit_bytes=60 << 20), name="deliver")(*ins)


def solution(mesh):
    wide, narrow = mesh.shape[WIDE], mesh.shape[NARROW]
    fits = narrow == 4 and wide == 8
    body = functools.partial(fast_body, wide // 2) if fits else plain_body
    return jax.shard_map(
        body,
        mesh=mesh,
        in_specs=(
            P(BOTH, None),
            P(BOTH, None),
            P(BOTH, None),
            P(BOTH),
            P(BOTH),
            P(BOTH, None),
            P(BOTH, None),
            P(BOTH, None),
            P(BOTH, None),
            P(BOTH, None),
            P(BOTH, None),
            P(BOTH, None),
            P(BOTH, None),
            P(BOTH),
            P(BOTH),
            P(BOTH),
            P(BOTH),
            P(BOTH),
            P(BOTH),
            P(None, WIDE),
            P(WIDE, None),
            P(None, NARROW),
            P(NARROW, None),
            P(None, BOTH),
            P(BOTH, None),
            P(None, BOTH),
        ),
        out_specs=(
            P(BOTH, None),
            P(BOTH, None),
            P(BOTH, None),
            P(BOTH, None),
            P(BOTH, None),
            P(BOTH, None),
            P(BOTH, None),
            P(BOTH, None),
            P(BOTH, None),
            P(BOTH, None),
            P(BOTH, None),
            P(BOTH),
            P(BOTH),
            P(BOTH),
            P(BOTH),
            P(BOTH),
            P(BOTH),
            P(NARROW, WIDE),
            P(WIDE, NARROW),
            P(WIDE, NARROW),
            P(NARROW, WIDE),
            P(None, BOTH),
            P(BOTH, None),
            P(None, BOTH),
        ),
        check_vma=False,
    )
```
